128 devices in a mesh: dp: 16 (over z, x_hi, core), head: 8 (over y, x_lo).
Axes of the slice: x: 4 (x_hi: 2, x_lo: 2; x = x_hi * 2 + x_lo), y: 4, z: 4, core: 2. Of those that a mesh axis runs over, the one named last changes fastest.
Arguments:
- hidden_in: bfloat16 [8192, 2048], P('dp'), may hold values from -6 to 6
- norm_gain: float32 [2048], replicated, may hold values from 0.5 to 1.5
- w_query: bfloat16 [2048, 2048], P('dp', 'head'), may hold values from -0.125 to 0.125
- w_forget: bfloat16 [2048, 2048], P('dp', 'head'), may hold values from -0.125 to 0.125
- w_input: bfloat16 [2048, 2048], P('dp', 'head'), may hold values from -0.125 to 0.125
- w_outgate: bfloat16 [2048, 2048], P('dp', 'head'), may hold values from -0.125 to 0.125
- lower_bounds: float32 [24, 2048], P(None, 'head'), may hold values from -20 to 1
- layer_index: int32 [1], replicated, may hold values from 1 to 23
- group_gain: float32 [128], replicated, may hold values from 0.5 to 1.5
- w_output: bfloat16 [2048, 2048], P('head', 'dp'), may hold values from -0.25 to 0.25
- ffn_gain: float32 [2048], replicated, may hold values from 0.5 to 1.5
- w_gate: bfloat16 [2048, 5632], P('dp', 'head'), may hold values from -0.125 to 0.125
- w_up: bfloat16 [2048, 5632], P('dp', 'head'), may hold values from -0.125 to 0.125
- w_down: bfloat16 [5632, 2048], P('head', 'dp'), may hold values from -0.15625 to 0.15625
- seq_lengths: int32 [12], replicated, may hold values from 1 to 7840, as said below
- grad_out: bfloat16 [8192, 2048], P('dp'), may hold values from -6 to 6
Outputs:
- block_out: bfloat16 [8192, 2048], P(('dp', 'head'))
- grad_in: float32 [8192, 2048], P(('dp', 'head'))
- grad_norm_gain: float32 [2048], replicated
- grad_query: float32 [2048, 2048], P('dp', 'head')
- grad_forget: float32 [2048, 2048], P('dp', 'head')
- grad_input: float32 [2048, 2048], P('dp', 'head')
- grad_outgate: float32 [2048, 2048], P('dp', 'head')
- grad_bounds: float32 [24, 2048], P(None, 'head')
- grad_group_gain: float32 [128], replicated
- grad_output: float32 [2048, 2048], P('head', 'dp')
- grad_ffn_gain: float32 [2048], replicated
- grad_gate: float32 [2048, 5632], P('dp', 'head')
- grad_up: float32 [2048, 5632], P('dp', 'head')
- grad_down: float32 [5632, 2048], P('head', 'dp')
- forget_mean: float32 [1], replicated
The draws below stay inside these ranges and needn't reach their ends.
Inputs may be any that keep to these rules, and one draw needn't show every extreme that they name: `seq_lengths`: 12 positive lengths, in order of the packed tokens, summing to 8192; one of them, at a position drawn from the seed, is the longest.
All inputs are finite; a program needn't handle non-finite values.
Results may differ from the reference program's by a relative error of at most 0.029.
Values may be sent and summed in bfloat16 or wider, within the bound.
A program may use at most 128 MiB of HBM per device.

```python
import jax
import jax.numpy as jnp
from jax import lax

D = 2048
KDIM = 128
FF = 5632
LAYERS = 24
HEADS = 16
TOK_DEV = 512
BLOCK = 64
NSEQ = 12
TOKENS = 8192


def draw_seq_lengths(key, part):
    key = jax.random.fold_in(key, 11)
    cut_key, place_key = jax.random.split(key, 2)
    rest = (NSEQ - 1) * max(2, TOK_DEV // 16)
    order = jax.random.permutation(cut_key, rest - 1).astype(jnp.int32)
    cuts = jnp.sort(order[:NSEQ - 2] + 1).astype(jnp.int32)
    edges = jnp.concatenate([jnp.zeros((1,), jnp.int32), cuts, jnp.full((1,), rest, jnp.int32)])
    pieces = (edges[1:] - edges[:-1]).astype(jnp.int32)
    place = jax.random.randint(place_key, (), 0, NSEQ).astype(jnp.int32)
    slots = jnp.arange(NSEQ, dtype=jnp.int32)
    earlier = jnp.concatenate([pieces, jnp.zeros((1,), jnp.int32)])
    later = jnp.concatenate([jnp.zeros((1,), jnp.int32), pieces])
    shifted = jnp.where(slots < place, earlier, later)
    return jnp.where(slots == place, jnp.int32(TOKENS - rest), shifted).astype(jnp.int32)


def bound_row(unit, slow_heads, shrink):
    slow_log = jnp.log(0.25 / TOKENS) + unit * jnp.log(8.0)
    fast_log = jnp.log(0.02) + unit * jnp.log(4.0)
    return jnp.where(slow_heads, slow_log, fast_log) - jnp.log(shrink)


def draw_lower_bounds(key, part):
    key = jax.random.fold_in(key, 23)
    pick_key, first_key, rest_key = jax.random.split(key, 3)
    slow_share = 0.5
    slow_heads = jnp.repeat(jax.random.bernoulli(pick_key, slow_share, (D // KDIM,)), KDIM)
    first_unit = jax.random.uniform(first_key, (D,), jnp.float32)
    rest_unit = jax.random.uniform(rest_key, (LAYERS - 2, D), jnp.float32)
    first_row = bound_row(first_unit, slow_heads, 1.0)[None]
    kept_row = jnp.zeros((1, D), jnp.float32)
    rest_rows = bound_row(rest_unit, slow_heads[None], float(LAYERS))
    return jnp.concatenate([first_row, kept_row, rest_rows], axis=0).astype(jnp.float32)


def steps_of(stream_key, shape, cuts, low, high):
    level, own = 1.0, jax.random.fold_in(stream_key, 6)
    for axis_at, blocks in cuts:
        steps = jnp.exp(jax.random.uniform(jax.random.fold_in(own, axis_at), (blocks,), jnp.float32, low / len(cuts), high / len(cuts)))
        level = level * jnp.repeat(steps, shape[axis_at] // blocks).reshape([-1 if axis == axis_at else 1 for axis in range(len(shape))])
    return level


def normal_values(own_key, extent, deviation, most, shards=(), kind=jnp.bfloat16):
    entries = deviation * jax.random.normal(own_key, extent, jnp.float32)
    if shards:
        entries = entries * steps_of(own_key, extent, shards, -0.22, 0.18)
    return jnp.clip(entries, -most, most).astype(kind)


def setup_inputs(seed: int = 0) -> dict:
    streams_of = jax.random.split(jax.random.key(seed), 17)
    hidden_in = normal_values(streams_of[0], (TOKENS, D), 1.0, 6.0, ((0, 16),))
    norm_gain = jnp.clip(1.0 + 0.1 * jax.random.normal(streams_of[1], (D,), jnp.float32), 0.5, 1.5)
    w_query = normal_values(streams_of[2], (D, D), D ** -0.5, 0.125, ((0, 16), (1, 8)))
    w_forget = normal_values(streams_of[3], (D, D), D ** -0.5, 0.125, ((0, 16), (1, 8)))
    w_input = normal_values(streams_of[4], (D, D), D ** -0.5, 0.125, ((0, 16), (1, 8)))
    w_outgate = normal_values(streams_of[5], (D, D), D ** -0.5, 0.125, ((0, 16), (1, 8)))
    lower_bounds = draw_lower_bounds(jax.random.fold_in(streams_of[16], 71), 0)
    layer_index = jax.random.randint(streams_of[7], (1,), 1, LAYERS).astype(jnp.int32)
    group_gain = jnp.clip(1.0 + 0.1 * jax.random.normal(streams_of[8], (KDIM,), jnp.float32), 0.5, 1.5)
    w_output = normal_values(streams_of[9], (D, D), (D // 4) ** -0.5, 0.25, ((0, 8), (1, 16)))
    ffn_gain = jnp.clip(1.0 + 0.1 * jax.random.normal(streams_of[10], (D,), jnp.float32), 0.5, 1.5)
    w_gate = normal_values(streams_of[11], (D, FF), D ** -0.5, 0.125, ((0, 16), (1, 8)))
    w_up = normal_values(streams_of[12], (D, FF), D ** -0.5, 0.125, ((0, 16), (1, 8)))
    w_down = normal_values(streams_of[13], (FF, D), (FF // 4) ** -0.5, 0.15625, ((0, 8), (1, 16)))
    seq_lengths = draw_seq_lengths(jax.random.fold_in(streams_of[16], 71), 0)
    grad_out = normal_values(streams_of[15], (TOKENS, D), 1.0, 6.0, ((0, 16),))
    return dict(hidden_in=hidden_in, norm_gain=norm_gain, w_query=w_query, w_forget=w_forget, w_input=w_input, w_outgate=w_outgate, lower_bounds=lower_bounds, layer_index=layer_index, group_gain=group_gain, w_output=w_output, ffn_gain=ffn_gain, w_gate=w_gate, w_up=w_up, w_down=w_down, seq_lengths=seq_lengths, grad_out=grad_out)


@jax.custom_vjp
def low(v):
    return lax.optimization_barrier(v.astype(jnp.bfloat16)).astype(jnp.float32)

@jax.custom_vjp
def low_back(v):
    return v

def low_keep(v):
    return (low(v), None)

def low_pass(kept, grad):
    return (grad,)

def back_keep(v):
    return (v, None)

def back_low(kept, grad):
    return (low(grad),)
low.defvjp(low_keep, low_pass)
low_back.defvjp(back_keep, back_low)
epsilon = 1e-06
topmost_precision = lax.Precision.HIGHEST

def matmul_high(first, second):
    return jnp.dot(first, second, precision=topmost_precision, preferred_element_type=jnp.float32)

def rms_scale(value_rows, weight):
    return value_rows * lax.rsqrt(lax.optimization_barrier(jnp.mean(value_rows * value_rows, axis=-1, keepdims=True)) + epsilon) * weight

def block_step(carry, block):
    recurrent_state, before = carry
    query, keys, value_rows, log_forget, segment = block
    span = segment.shape[0]
    running = jnp.cumsum(log_forget, axis=0)
    ending = running[span - 1]
    causal = lax.broadcasted_iota(jnp.int32, (span, span), 0) >= lax.broadcasted_iota(jnp.int32, (span, span), 1)
    linked = (causal & (segment[:, None] == segment[None, :])).astype(jnp.float32)
    lifted = query * jnp.exp(running - ending[None])
    lowered = keys * jnp.exp(ending[None] - running)
    scores = jnp.einsum('thk,shk->hts', lifted, lowered, precision=topmost_precision) * linked[None]
    inner = jnp.einsum('hts,shv->thv', scores, value_rows, precision=topmost_precision)
    carried = (segment == before).astype(jnp.float32)[:, None, None]
    reach_extent = query * jnp.exp(running) * carried
    outer_product = jnp.einsum('fmp,mpu->fmu', reach_extent, recurrent_state, precision=topmost_precision)
    final = segment[span - 1]
    tail_rows = lowered * (segment == final).astype(jnp.float32)[:, None, None]
    recurrent_state = recurrent_state * (jnp.exp(ending) * carried[span - 1])[:, :, None]
    recurrent_state = recurrent_state + jnp.einsum('jem,jel->eml', tail_rows, value_rows, precision=topmost_precision)
    return ((recurrent_state, final), inner + outer_product)

def run_blocks(segment, before, query, keys, value_rows, log_forget, recurrent_state):
    count = query.shape[0] // BLOCK
    heads_here = query.shape[1] // KDIM

    def shaped(array):
        return array.reshape(count, BLOCK, heads_here, KDIM)
    carry, outputs = lax.scan(jax.checkpoint(block_step), (recurrent_state, before), (shaped(query), shaped(keys), shaped(value_rows), shaped(log_forget), segment.reshape(count, BLOCK)))
    return (outputs.reshape(query.shape[0], heads_here, KDIM), carry[0])

def reference(hidden_in, norm_gain, w_query, w_forget, w_input, w_outgate, lower_bounds, layer_index, group_gain, w_output, ffn_gain, w_gate, w_up, w_down, seq_lengths, grad_out):
    starts = (jnp.cumsum(seq_lengths) - seq_lengths).astype(jnp.int32)
    position = jnp.arange(TOKENS, dtype=jnp.int32)
    segment = (lax.optimization_barrier(jnp.sum((starts[None, :] <= position[:, None]).astype(jnp.int32), axis=1)) - 1).astype(jnp.int32)
    depth = jnp.arange(LAYERS, dtype=jnp.int32)[:, None]
    picked = ((depth >= 1) & (depth <= layer_index[0])).astype(jnp.float32)

    def forward(inputs, gain_in, weight_query, weight_forget, weight_input, weight_outgate, bound_params, gain_group, weight_output, gain_mid, weight_gate, weight_up, weight_down):
        normed_in = low(rms_scale(inputs, gain_in))
        query_raw = low_back(matmul_high(normed_in, weight_query))
        forget_raw = low_back(matmul_high(normed_in, weight_forget))
        input_raw = low_back(matmul_high(normed_in, weight_input))
        outgate_raw = low_back(matmul_high(normed_in, weight_outgate))
        soft_bounds = jax.nn.softmax(bound_params, axis=0)
        bound = lax.optimization_barrier(jnp.sum(soft_bounds * picked, axis=0))
        forget = bound + (1.0 - bound) * jax.nn.sigmoid(forget_raw)
        query = low(jax.nn.silu(query_raw))
        keys = low(1.0 - forget)
        value_rows = low(input_raw)
        log_forget = jnp.log(forget)
        zero_state = jnp.zeros((HEADS, KDIM, KDIM), jnp.float32)
        mixed_output, final_state = run_blocks(segment, jnp.int32(-1), query, keys, value_rows, log_forget, zero_state)
        mixed_output = low_back(mixed_output)
        group_normed = rms_scale(mixed_output, gain_group).reshape(TOKENS, D)
        gated = low(group_normed * jax.nn.silu(outgate_raw))
        branch = low_back(matmul_high(gated, weight_output))
        residual = inputs + branch
        normed_mid = low(rms_scale(residual, gain_mid))
        gate_act = low_back(matmul_high(normed_mid, weight_gate))
        up_act = low_back(matmul_high(normed_mid, weight_up))
        hidden = low(jax.nn.silu(gate_act) * up_act)
        return (residual + matmul_high(hidden, weight_down), jnp.mean(forget))
    floats = (hidden_in.astype(jnp.float32), norm_gain, w_query.astype(jnp.float32), w_forget.astype(jnp.float32), w_input.astype(jnp.float32), w_outgate.astype(jnp.float32), lower_bounds, group_gain, w_output.astype(jnp.float32), ffn_gain, w_gate.astype(jnp.float32), w_up.astype(jnp.float32), w_down.astype(jnp.float32))
    result, pull_back, forget_mean = jax.vjp(forward, *floats, has_aux=True)
    grads = pull_back(grad_out.astype(jnp.float32))
    return (result.astype(jnp.bfloat16), grads[0], grads[1], grads[2], grads[3], grads[4], grads[5], grads[6], grads[7], grads[8], grads[9], grads[10], grads[11], grads[12], jnp.reshape(forget_mean, (1,)))
```

```python
from functools import partial

import jax
import jax.numpy as jnp
from jax import lax
from jax.experimental import pallas as pl
from jax.experimental.pallas import tpu as pltpu
from jax.sharding import PartitionSpec as P

D = 2048
KDIM = 128
CHUNK = 128
TOK = 512
CHUNKS = TOK // CHUNK
HERE = 256
FFH = 704
NSEQ = 12
NHEAD = 8
ROWS = TOK // NHEAD
EPS = 1e-06
F32 = jnp.float32
BF16 = jnp.bfloat16
MESH = pl.DeviceIdType.MESH
VM = pl.BlockSpec(memory_space=pltpu.VMEM)
SM = pl.BlockSpec(memory_space=pltpu.SMEM)
HB = pl.BlockSpec(memory_space=pl.ANY)


class Spot:
    def __init__(self):
        self.dp = lax.axis_index("dp")
        self.head = lax.axis_index("head")
        self.core = lax.rem(self.dp, 2)
        self.chip = lax.div(self.dp, 2)
        self.xh = lax.rem(self.chip, 2)
        self.z = lax.div(self.chip, 2)

    def at(self, dz, xh, core):
        return (lax.rem(self.z + dz, 4) * 2 + xh) * 2 + core

    @property
    def sibling(self):
        return {"dp": self.chip * 2 + 1 - self.core}

    def chips(self):
        return [{"dp": lax.rem(self.chip + k, 8) * 2 + self.core} for k in range(1, 8)]

    def heads(self):
        return [{"head": lax.rem(self.head + k, NHEAD)} for k in range(1, NHEAD)]


def greet(ids):
    barrier = pltpu.get_barrier_semaphore()
    for one in ids:
        pl.semaphore_signal(barrier, inc=1, device_id=one, device_id_type=MESH)
    pl.semaphore_wait(barrier, len(ids))


def rcopy(src, dst, send, recv, where):
    return pltpu.make_async_remote_copy(
        src_ref=src, dst_ref=dst, send_sem=send, recv_sem=recv, device_id=where, device_id_type=MESH
    )


GATHER_SENDS = 17


class Gather:
    def __init__(self, spot, g, send, recv, half):
        self.spot, self.g, self.s, self.r, self.h = spot, g, send, recv, half

    def block(self, d, start=0, rows=128):
        return self.g.at[pl.ds(pl.multiple_of(d * 128 + start, 64), rows), :]

    def push(self, d, to, k):
        rcopy(self.block(d), self.block(d), self.s.at[k], self.r.at[d], {"dp": to}).start()

    def push_half(self, d, to, k, xh, part):
        b = self.block(d, part * 64, 64)
        rcopy(b, b, self.s.at[k], self.h.at[2 * xh + part], {"dp": to}).start()

    def arrived(self, d):
        b = self.block(d)
        rcopy(b, b, self.s.at[0], self.r.at[d], self.spot.sibling).wait_recv()

    def arrived_halves(self, d, xh):
        for part in range(2):
            b = self.block(d, part * 64, 64)
            rcopy(b, b, self.s.at[0], self.h.at[2 * xh + part], self.spot.sibling).wait_recv()

    def first(self):
        p = self.spot
        self.push(p.dp, p.at(0, 1 - p.xh, p.core), 0)
        self.push(p.dp, p.at(1, p.xh, p.core), 1)
        self.push(p.dp, p.at(3, p.xh, p.core), 2)
        self.push(p.dp, p.at(0, p.xh, 1 - p.core), 3)

    def second(self):
        p = self.spot
        b = p.at(0, 1 - p.xh, p.core)
        self.arrived(b)
        self.push(b, p.at(1, p.xh, p.core), 4)
        self.push(b, p.at(3, p.xh, p.core), 5)
        self.push(b, p.at(0, p.xh, 1 - p.core), 6)

    def third(self):
        p = self.spot
        for i, h in enumerate((p.xh, 1 - p.xh)):
            b = p.at(3, h, p.core)
            self.arrived(b)
            self.push_half(b, p.at(1, p.xh, p.core), 7 + i, h, 0)
            self.push(b, p.at(0, p.xh, 1 - p.core), 9 + i)
            b = p.at(1, h, p.core)
            self.arrived(b)
            self.push_half(b, p.at(3, p.xh, p.core), 11 + i, h, 1)
            self.push(b, p.at(0, p.xh, 1 - p.core), 13 + i)

    def fourth(self):
        p = self.spot
        for i, h in enumerate((p.xh, 1 - p.xh)):
            b = p.at(2, h, p.core)
            self.arrived_halves(b, h)
            self.push(b, p.at(0, p.xh, 1 - p.core), 15 + i)

    def last(self):
        p = self.spot
        for dz in range(4):
            for h in range(2):
                self.arrived(p.at(dz, h, 1 - p.core))
        half = self.block(0, 0, 64)
        for k in range(GATHER_SENDS):
            b = half if k in (7, 8, 11, 12) else self.block(0)
            rcopy(b, b, self.s.at[k], self.r.at[0], p.sibling).wait_send()


def gather_semaphores():
    return [
        pltpu.SemaphoreType.DMA((GATHER_SENDS,)),
        pltpu.SemaphoreType.DMA((16,)),
        pltpu.SemaphoreType.DMA((4,)),
    ]


NN = (((1,), (0,)), ((), ()))
NT = (((1,), (1,)), ((), ()))
TN = (((0,), (0,)), ((), ()))


def mm(a, b, dims):
    return lax.dot_general(a, b, dims, preferred_element_type=F32)


def halves(a):
    high = a.astype(BF16)
    return high, (a - high.astype(F32)).astype(BF16)


def mm2(a, b, dims):
    return mm(a[0], b, dims) + mm(a[1], b, dims)


def mm3(a, b, dims):
    return mm(a[0], b[0], dims) + (mm(a[0], b[1], dims) + mm(a[1], b[0], dims))


def triangle(lower):
    rows = lax.broadcasted_iota(jnp.int32, (CHUNK, CHUNK), 0)
    columns = lax.broadcasted_iota(jnp.int32, (CHUNK, CHUNK), 1)
    return (rows >= columns if lower else rows <= columns).astype(BF16)


def summed_rows(lower, x):
    high = x.astype(BF16)
    rest = x - high.astype(F32)
    middle = rest.astype(BF16)
    low = (rest - middle.astype(F32)).astype(BF16)
    t = triangle(lower)
    return mm(t, high, NN) + (mm(t, middle, NN) + mm(t, low, NN))


class Segments:
    def __init__(self, spot, seq):
        self.starts = []
        total = jnp.int32(0)
        for i in range(NSEQ):
            self.starts.append(total)
            total = total + seq[i]
        self.first = spot.dp * TOK

    def of(self, position):
        found = jnp.where(position >= self.starts[0], 1, 0)
        for s in self.starts[1:]:
            found = found + jnp.where(position >= s, 1, 0)
        return found - 1

    def column(self, c):
        return self.of(self.first + c * CHUNK + lax.broadcasted_iota(jnp.int32, (CHUNK, KDIM), 0))

    def row(self, c):
        return self.of(self.first + c * CHUNK + lax.broadcasted_iota(jnp.int32, (CHUNK, KDIM), 1))

    def before(self, c):
        return self.of(self.first + c * CHUNK - 1)

    def final(self, c):
        return self.of(self.first + (c + 1) * CHUNK - 1)


def lower_bound(lb, layer):
    x = lb[...]
    e = jnp.exp(x - jnp.max(x, axis=0, keepdims=True))
    soft = e / jnp.sum(e, axis=0, keepdims=True)
    depth = lax.broadcasted_iota(jnp.int32, x.shape, 0)
    picked = jnp.where((depth >= 1) & (depth <= layer), 1.0, 0.0)
    return soft, picked, jnp.sum(soft * picked, axis=0, keepdims=True)


def sigmoid(x):
    return lax.logistic(x)


def slope(x, s):
    return s * (1.0 + x * (1.0 - s))


class Exchange:
    def __init__(self, spot, msg, sib, slots, give, take, send, recv, backward):
        self.p, self.msg, self.sib, self.slots = spot, msg, sib, slots
        self.give, self.take, self.s, self.r, self.back = give, take, send, recv, backward

    def to_sibling(self):
        p = self.p
        rcopy(self.msg.at[1 - p.core], self.sib, self.s.at[7], self.r.at[8], p.sibling).start()

    def to_chips(self):
        p = self.p
        rcopy(self.sib, self.sib, self.s.at[7], self.r.at[8], p.sibling).wait_recv()
        mine, other = self.msg[p.core], self.sib[...]
        zero = p.core == 0
        one, two = jnp.where(zero, mine, other), jnp.where(zero, other, mine)
        near, far = (two, one) if self.back else (one, two)
        self.near = near
        state = near[0:128] * far[128:129] + far[0:128]
        self.slots[p.chip, 0:128, :] = state
        self.slots[p.chip, 128:136, :] = near[128:136] * far[128:136]
        for k, to in enumerate(p.chips()):
            rcopy(self.slots.at[p.chip], self.slots.at[p.chip], self.s.at[k], self.r.at[p.chip], to).start()

    def result(self, out):
        p = self.p
        for k in range(1, 8):
            chip = lax.rem(p.chip + k, 8)
            rcopy(self.slots.at[chip], self.slots.at[chip], self.s.at[0], self.r.at[chip], p.sibling).wait_recv()
        state = jnp.zeros((128, 128), F32)
        for k in range(7, 0, -1) if self.back else range(7):
            m = self.slots[k]
            after = state * m[128:129] + m[0:128]
            state = jnp.where(k > p.chip if self.back else k < p.chip, after, state)
        second = state * self.near[128:129] + self.near[0:128]
        is_first = p.core == (1 if self.back else 0)
        self.give[...] = jnp.where(is_first, second, state)
        move = rcopy(self.give, self.take, self.s.at[8], self.r.at[9], p.sibling)
        move.start()
        out[p.core] = jnp.where(is_first, state, second)
        move.wait_recv()
        out[1 - p.core] = self.take[...]

    def finish(self):
        p = self.p
        for k in range(7):
            rcopy(self.slots.at[0], self.slots.at[0], self.s.at[k], self.r.at[0], p.sibling).wait_send()
        rcopy(self.sib, self.sib, self.s.at[7], self.r.at[8], p.sibling).wait_send()
        rcopy(self.give, self.take, self.s.at[8], self.r.at[9], p.sibling).wait_send()


def exchange_scratch():
    return [
        pltpu.VMEM((2, 136, 128), F32),
        pltpu.VMEM((136, 128), F32),
        pltpu.VMEM((8, 136, 128), F32),
        pltpu.VMEM((128, 128), F32),
        pltpu.VMEM((128, 128), F32),
        pltpu.SemaphoreType.DMA((9,)),
        pltpu.SemaphoreType.DMA((10,)),
    ]


def gates(raw, bound, rows):
    query_raw = raw[rows, 0:256]
    logistic = sigmoid(raw[rows, 256:512])
    forget = bound + (1.0 - bound) * logistic
    query = (query_raw * sigmoid(query_raw)).astype(BF16)
    keys = (1.0 - forget).astype(BF16)
    values = raw[rows, 512:768].astype(BF16)
    return logistic, forget, query, keys, values


def mixer_forward(
    hid, gain, wq, wf, wi, wo, wt, lb, layer, seq, group_gain,
    raw, xn, gated, mixed, states, run, total, w_out, wt_out,
    w, wt_all, inner_update, decay, incoming,
    msg, sib, slots, give, take, ex_send, ex_recv,
    gs, gr, gh, hs, hr, hh, local_sem,
):
    p = Spot()
    greet(p.chips() + [p.sibling])
    mine = pl.ds(pl.multiple_of(p.dp * 128, 128), 128)
    for k, one in enumerate((wq, wf, wi, wo)):
        w[mine, 256 * k : 256 * (k + 1)] = one[...]
    gather = Gather(p, w, gs, gr, gh)
    gather.first()
    wt_all[mine, :] = wt[...]
    later = Gather(p, wt_all, hs, hr, hh)

    @pl.loop(0, 8)
    def _(i):
        rows = pl.ds(pl.multiple_of(i * 64, 64), 64)
        x = hid[rows, :].astype(F32)
        scale = lax.rsqrt(jnp.mean(x * x, axis=-1, keepdims=True) + EPS)
        xn[rows, :] = (x * scale * gain[...]).astype(BF16)

    gather.second()
    gather.third()
    gather.fourth()
    later.first()
    gather.last()
    keep = pltpu.make_async_copy(w, w_out, local_sem.at[0])
    keep.start()

    @pl.loop(0, 4)
    def _(j):
        columns = pl.ds(pl.multiple_of(j * 256, 256), 256)
        raw[:, columns] = mm(xn[...], w[:, columns], NN)

    later.second()
    segments = Segments(p, seq)
    bound = lower_bound(lb, layer[0])[2]
    forget_total = jnp.zeros((1, HERE), F32)
    for c in range(CHUNKS):
        rows = slice(c * CHUNK, (c + 1) * CHUNK)
        logistic, forget, query, keys, values = gates(raw, bound, rows)
        forget_total = forget_total + jnp.sum(forget, axis=0, keepdims=True)
        running = summed_rows(True, jnp.log(forget))
        run[rows, :] = running
        middle, ending = running[63:64], running[127:128]
        lifted = query.astype(F32) * jnp.exp(running - middle)
        lowered = keys.astype(F32) * jnp.exp(middle - running)
        tail = keys.astype(F32) * jnp.exp(ending - running)
        column, row = segments.column(c), segments.row(c)
        linked = (column == row) & (
            lax.broadcasted_iota(jnp.int32, (CHUNK, CHUNK), 0)
            >= lax.broadcasted_iota(jnp.int32, (CHUNK, CHUNK), 1)
        )
        final = segments.final(c)
        carried_last = jnp.where(final == segments.before(c), 1.0, 0.0)
        decay[c : c + 1, :] = jnp.exp(ending) * carried_last
        ends = jnp.where(column == final, 1.0, 0.0)
        for h in range(2):
            lanes = slice(h * 128, (h + 1) * 128)
            scores = mm3(halves(lifted[:, lanes]), halves(lowered[:, lanes]), NT)
            scores = jnp.where(linked, scores, 0.0)
            mixed[rows, lanes] = mm2(halves(scores), values[:, lanes], NN)
            high, low = halves(tail[:, lanes] * ends)
            inner_update[h, c] = mm(values[:, lanes], high, TN) + mm(values[:, lanes], low, TN)
    total[...] = forget_total
    for h in range(2):
        lanes = slice(h * 128, (h + 1) * 128)
        state, rate = inner_update[h, 0], decay[0:1, lanes]
        for c in range(1, CHUNKS):
            state = state * decay[c : c + 1, lanes] + inner_update[h, c]
            rate = rate * decay[c : c + 1, lanes]
        msg[h, 0:128, :] = state
        msg[h, 128:136, :] = jnp.broadcast_to(rate, (8, 128))
    exchange = Exchange(p, msg, sib, slots, give, take, ex_send, ex_recv, False)
    exchange.to_sibling()
    exchange.to_chips()
    later.third()
    later.fourth()
    exchange.result(incoming)
    for h in range(2):
        lanes = slice(h * 128, (h + 1) * 128)
        state = incoming[h]
        states[h, 0] = state
        for c in range(CHUNKS):
            state = state * decay[c : c + 1, lanes] + inner_update[h, c]
            states[h, c + 1] = state

    @pl.loop(0, CHUNKS)
    def _(c):
        rows = pl.ds(pl.multiple_of(c * CHUNK, CHUNK), CHUNK)
        carried = jnp.where(segments.column(c) == segments.before(c), 1.0, 0.0)
        for h in range(2):
            lanes = slice(h * 128, (h + 1) * 128)
            query_raw = raw[rows, h * 128 : (h + 1) * 128]
            query = (query_raw * sigmoid(query_raw)).astype(BF16).astype(F32)
            reach = query * jnp.exp(run[rows, lanes]) * carried
            x = mixed[rows, lanes] + mm3(halves(reach), halves(states[h, c]), NT)
            mixed[rows, lanes] = x
            scale = lax.rsqrt(jnp.mean(x * x, axis=-1, keepdims=True) + EPS)
            gate = raw[rows, 768 + h * 128 : 768 + (h + 1) * 128]
            gated[rows, lanes] = (x * scale * group_gain[...] * (gate * sigmoid(gate))).astype(BF16)

    later.last()
    keep_later = pltpu.make_async_copy(wt_all, wt_out, local_sem.at[1])
    keep_later.start()
    exchange.finish()
    keep.wait()
    keep_later.wait()


def call_mixer_forward(hid, gain, wq, wf, wi, wo, wt, lb, layer, seq, group_gain):
    out = jax.ShapeDtypeStruct
    return pl.pallas_call(
        mixer_forward,
        name="mixer_forward",
        out_shape=(
            out((TOK, 1024), F32),
            out((TOK, D), BF16),
            out((TOK, HERE), BF16),
            out((TOK, HERE), F32),
            out((2, CHUNKS + 1, 128, 128), F32),
            out((TOK, HERE), F32),
            out((1, HERE), F32),
            out((D, 1024), BF16),
            out((D, HERE), BF16),
        ),
        in_specs=[VM] * 8 + [SM, SM, VM],
        out_specs=(VM,) * 7 + (HB, HB),
        scratch_shapes=[
            pltpu.VMEM((D, 1024), BF16),
            pltpu.VMEM((D, HERE), BF16),
            pltpu.VMEM((2, CHUNKS, 128, 128), F32),
            pltpu.VMEM((8, HERE), F32),
            pltpu.VMEM((2, 128, 128), F32),
            *exchange_scratch(),
            *gather_semaphores(),
            *gather_semaphores(),
            pltpu.SemaphoreType.DMA((2,)),
        ],
        compiler_params=pltpu.CompilerParams(
            collective_id=0, has_side_effects=True, vmem_limit_bytes=56 * 1024 * 1024
        ),
    )(hid, gain, wq, wf, wi, wo, wt, lb, layer, seq, group_gain)

class HeadSum:
    def __init__(self, spot, ps, slots, send, recv):
        self.p, self.ps, self.slots, self.s, self.r = spot, ps, slots, send, recv

    def send(self):
        p = self.p
        for k in range(1, NHEAD):
            h = lax.rem(p.head + k, NHEAD)
            rcopy(self.ps.at[h], self.slots.at[p.head], self.s.at[k], self.r.at[p.head], {"head": h}).start()

    def collect(self):
        p = self.p
        self.slots[p.head] = self.ps[p.head]
        for k in range(1, NHEAD):
            h = lax.rem(p.head + k, NHEAD)
            rcopy(self.slots.at[h], self.slots.at[h], self.s.at[0], self.r.at[h], p.sibling).wait_recv()

    def rows(self, rows):
        total = self.slots[0, rows, :].astype(F32)
        for h in range(1, NHEAD):
            total = total + self.slots[h, rows, :].astype(F32)
        return total

    def finish(self):
        for k in range(1, NHEAD):
            rcopy(self.ps.at[0], self.slots.at[0], self.s.at[k], self.r.at[0], self.p.sibling).wait_send()


class HeadGather:
    def __init__(self, spot, full, send, recv):
        self.p, self.full, self.s, self.r = spot, full, send, recv

    def block(self, h):
        return self.full.at[pl.ds(pl.multiple_of(h * ROWS, ROWS), ROWS), :]

    def send(self):
        p = self.p
        for k in range(1, NHEAD):
            h = lax.rem(p.head + k, NHEAD)
            rcopy(self.block(p.head), self.block(p.head), self.s.at[k], self.r.at[p.head], {"head": h}).start()

    def collect(self):
        p = self.p
        for k in range(1, NHEAD):
            h = lax.rem(p.head + k, NHEAD)
            rcopy(self.block(h), self.block(h), self.s.at[0], self.r.at[h], p.sibling).wait_recv()

    def finish(self):
        for k in range(1, NHEAD):
            rcopy(self.block(0), self.block(0), self.s.at[k], self.r.at[0], self.p.sibling).wait_send()


def eight():
    return [pltpu.SemaphoreType.DMA((8,)), pltpu.SemaphoreType.DMA((8,))]


def branch(
    gated, wt, hid, gain, wg, wu, wd,
    hn_out, resid, wg_out, wu_out, wd_out,
    ps, slots, hn, g0, g1, g2, rs_s, rs_r, ag_s, ag_r,
    s0, r0, h0, s1, r1, h1, s2, r2, h2, local_sem,
):
    p = Spot()
    greet(p.chips() + [p.sibling] + p.heads())
    mine = pl.ds(pl.multiple_of(p.dp * 128, 128), 128)
    gathers = [Gather(p, g0, s0, r0, h0), Gather(p, g1, s1, r1, h1), Gather(p, g2, s2, r2, h2)]
    for one, full in zip((wg, wu, wd), (g0, g1, g2)):
        full[mine, :] = one[...]
    for g in gathers:
        g.first()

    @pl.loop(0, 8)
    def _(j):
        columns = pl.ds(pl.multiple_of(j * 256, 256), 256)
        part = mm(gated[...], wt[columns, :], NT).astype(BF16)
        for h in range(NHEAD):
            ps[h, :, columns] = part[h * ROWS : (h + 1) * ROWS]

    scatter = HeadSum(p, ps, slots, rs_s, rs_r)
    scatter.send()
    for g in gathers:
        g.second()
    for g in gathers:
        g.third()
    scatter.collect()
    own = pl.multiple_of(p.head * ROWS, ROWS)

    @pl.loop(0, 4)
    def _(i):
        rows = pl.ds(pl.multiple_of(i * 16, 16), 16)
        here = pl.ds(pl.multiple_of(own + i * 16, 16), 16)
        x = hid[here, :].astype(F32) + scatter.rows(rows)
        resid[rows, :] = x
        scale = lax.rsqrt(jnp.mean(x * x, axis=-1, keepdims=True) + EPS)
        hn[here, :] = (x * scale * gain[...]).astype(BF16)

    spread = HeadGather(p, hn, ag_s, ag_r)
    spread.send()
    for g in gathers:
        g.fourth()
    outs = []
    for k, (g, full, out) in enumerate(zip(gathers, (g0, g1, g2), (wg_out, wu_out, wd_out))):
        g.last()
        move = pltpu.make_async_copy(full, out, local_sem.at[k])
        move.start()
        outs.append(move)
    spread.collect()
    move = pltpu.make_async_copy(hn, hn_out, local_sem.at[3])
    move.start()
    outs.append(move)
    scatter.finish()
    spread.finish()
    for move in outs:
        move.wait()


def call_branch(gated, wt, hid, gain, wg, wu, wd):
    out = jax.ShapeDtypeStruct
    return pl.pallas_call(
        branch,
        name="branch",
        out_shape=(
            out((TOK, D), BF16),
            out((ROWS, D), F32),
            out((D, FFH), BF16),
            out((D, FFH), BF16),
            out((D, FFH), BF16),
        ),
        in_specs=[VM] * 7,
        out_specs=(HB, VM, HB, HB, HB),
        scratch_shapes=[
            pltpu.VMEM((NHEAD, ROWS, D), BF16),
            pltpu.VMEM((NHEAD, ROWS, D), BF16),
            pltpu.VMEM((TOK, D), BF16),
            *[pltpu.VMEM((D, FFH), BF16)] * 3,
            *eight(),
            *eight(),
            *gather_semaphores(),
            *gather_semaphores(),
            *gather_semaphores(),
            pltpu.SemaphoreType.DMA((4,)),
        ],
        compiler_params=pltpu.CompilerParams(
            collective_id=1, has_side_effects=True, vmem_limit_bytes=56 * 1024 * 1024
        ),
    )(gated, wt, hid, gain, wg, wu, wd)


class DpSum:
    def __init__(self, spot, gs, cr, zr, xs, xr, send, recv):
        self.p, self.gs, self.cr, self.zr, self.xs, self.xr = spot, gs, cr, zr, xs, xr
        self.s, self.r = send, recv

    def pair(self, i):
        p = self.p
        two = pl.ds(2 * i, 2)
        return rcopy(self.gs.at[1 - p.core, two], self.cr.at[two], self.s.at[i], self.r.at[i], p.sibling)

    def to_sibling(self):
        for i in range(4):
            self.pair(i).start()

    def across(self, d):
        p = self.p
        z = lax.rem(p.z + d, 4)
        where = {"dp": (z * 2 + p.xh) * 2 + p.core}
        return rcopy(self.gs.at[p.core, pl.ds(z * 2, 2)], self.zr.at[d - 1], self.s.at[3 + d], self.r.at[3 + d], where)

    def to_z(self):
        p = self.p
        for i in range(4):
            self.pair(i).wait_recv()

        @pl.loop(0, 8)
        def _(k):
            self.gs[p.core, k] = (self.gs[p.core, k].astype(F32) + self.cr[k].astype(F32)).astype(BF16)

        for d in (1, 3, 2):
            self.across(d).start()

    def last_move(self):
        p = self.p
        where = {"dp": (p.z * 2 + 1 - p.xh) * 2 + p.core}
        return rcopy(self.xs, self.xr, self.s.at[7], self.r.at[7], where)

    def to_x(self, put):
        p = self.p
        for d in (1, 3, 2):
            self.across(d).wait_recv()

        def total(h):
            one = self.gs[p.core, 2 * p.z + h].astype(F32)
            for i in range(3):
                one = one + self.zr[i, h].astype(F32)
            return one

        self.xs[...] = total(1 - p.xh).astype(BF16)
        self.last_move().start()
        put(total(p.xh))

    def end(self, add):
        self.last_move().wait_recv()
        add(self.xr[...].astype(F32))

    def finish(self):
        for i in range(4):
            self.pair(i).wait_send()
        for d in (1, 3, 2):
            self.across(d).wait_send()
        self.last_move().wait_send()


def dp_sum_scratch(n):
    return [
        pltpu.VMEM((2, 8, 128, n), BF16),
        pltpu.VMEM((8, 128, n), BF16),
        pltpu.VMEM((3, 2, 128, n), BF16),
        pltpu.VMEM((128, n), BF16),
        pltpu.VMEM((128, n), BF16),
        *eight(),
    ]


def outer_products(left, right, gs):
    @pl.loop(0, 8)
    def _(k):
        columns = pl.ds(pl.multiple_of(k * 256, 256), 256)
        both = mm(left[:, columns], right[...], TN).astype(BF16)
        gs[0, k] = both[0:128]
        gs[1, k] = both[128:256]


def write(ref):
    def put(x):
        ref[...] = x

    return put


def accumulate(ref):
    def add(x):
        ref[...] += x

    return add


def feed_forward(
    hn, dy, wg_in, wu_in, wd_in, resid, gain,
    down, d_resid, db_out, gain_terms, out_gate, out_up, out_down,
    wg, wu, wd, hidden, dg, du, ps, slots, db, rs_s, rs_r, ag_s, ag_r,
    a0, a1, a2, a3, a4, a5, a6, b0, b1, b2, b3, b4, b5, b6, c0, c1, c2, c3, c4, c5, c6, local_sem,
):
    loads = []
    for k, (one, full) in enumerate(((wg_in, wg), (wu_in, wu), (wd_in, wd))):
        move = pltpu.make_async_copy(one, full, local_sem.at[k])
        move.start()
        loads.append(move)
    p = Spot()
    partners = [{"dp": p.at(k, p.xh, p.core)} for k in (1, 2, 3)]
    partners += [{"dp": p.at(0, 1 - p.xh, p.core)}, p.sibling]
    greet(partners + p.heads())
    for move in loads:
        move.wait()
    for low, high in ((0, 256), (256, 512), (512, FFH)):
        gate = mm(hn[...], wg[:, low:high], NN)
        up = mm(hn[...], wu[:, low:high], NN)
        dh = mm(dy[...], wd[:, low:high], NN)
        s = sigmoid(gate)
        silu = gate * s
        hidden[:, low:high] = (silu * up).astype(BF16)
        dg[:, low:high] = (dh * up * slope(gate, s)).astype(BF16)
        du[:, low:high] = (dh * silu).astype(BF16)

    @pl.loop(0, 8)
    def _(j):
        columns = pl.ds(pl.multiple_of(j * 256, 256), 256)
        part = (mm(dg[...], wg[columns, :], NT) + mm(du[...], wu[columns, :], NT)).astype(BF16)
        for h in range(NHEAD):
            ps[h, :, columns] = part[h * ROWS : (h + 1) * ROWS]

    scatter = HeadSum(p, ps, slots, rs_s, rs_r)
    scatter.send()
    sums = [
        DpSum(p, a0, a1, a2, a3, a4, a5, a6),
        DpSum(p, b0, b1, b2, b3, b4, b5, b6),
        DpSum(p, c0, c1, c2, c3, c4, c5, c6),
    ]
    outer_products(hn, dg, a0)
    sums[0].to_sibling()
    outer_products(hn, du, b0)
    sums[0].to_z()
    sums[1].to_sibling()
    outer_products(dy, hidden, c0)
    sums[1].to_z()
    sums[2].to_sibling()

    @pl.loop(0, 8)
    def _(j):
        columns = pl.ds(pl.multiple_of(j * 256, 256), 256)
        part = mm(hidden[...], wd[columns, :], NT).astype(BF16)
        for h in range(NHEAD):
            down[h, :, columns] = part[h * ROWS : (h + 1) * ROWS]

    sums[2].to_z()
    scatter.collect()
    own = pl.multiple_of(p.head * ROWS, ROWS)
    gain_terms[...] = jnp.zeros_like(gain_terms)

    @pl.loop(0, 4)
    def _(i):
        rows = pl.ds(pl.multiple_of(i * 16, 16), 16)
        here = pl.ds(pl.multiple_of(own + i * 16, 16), 16)
        grad, x = scatter.rows(rows), resid[rows, :]
        inverse = lax.rsqrt(jnp.mean(x * x, axis=-1, keepdims=True) + EPS)
        scaled, normed = grad * gain[...], x * inverse
        back = inverse * (scaled - normed * jnp.mean(scaled * normed, axis=-1, keepdims=True))
        gain_terms[...] += jnp.sum(grad * normed, axis=0, keepdims=True)
        both = dy[here, :].astype(F32) + back
        d_resid[rows, :] = both
        db[here, :] = both.astype(BF16)

    spread = HeadGather(p, db, ag_s, ag_r)
    spread.send()
    results = (out_gate, out_up, out_down)
    for one, out in zip(sums, results):
        one.to_x(write(out))
    for one, out in zip(sums, results):
        one.end(accumulate(out))
    spread.collect()
    move = pltpu.make_async_copy(db, db_out, local_sem.at[0])
    move.start()
    scatter.finish()
    spread.finish()
    for one in sums:
        one.finish()
    move.wait()


def call_feed_forward(hn, dy, wg, wu, wd, resid, gain):
    out = jax.ShapeDtypeStruct
    return pl.pallas_call(
        feed_forward,
        name="feed_forward",
        out_shape=(
            out((NHEAD, ROWS, D), BF16),
            out((ROWS, D), F32),
            out((TOK, D), BF16),
            out((1, D), F32),
            out((128, FFH), F32),
            out((128, FFH), F32),
            out((128, FFH), F32),
        ),
        in_specs=[VM, VM, HB, HB, HB, VM, VM],
        out_specs=(VM, VM, HB, VM, VM, VM, VM),
        scratch_shapes=[
            *[pltpu.VMEM((D, FFH), BF16)] * 3,
            *[pltpu.VMEM((TOK, FFH), BF16)] * 3,
            pltpu.VMEM((NHEAD, ROWS, D), BF16),
            pltpu.VMEM((NHEAD, ROWS, D), BF16),
            pltpu.VMEM((TOK, D), BF16),
            *eight(),
            *eight(),
            *dp_sum_scratch(FFH),
            *dp_sum_scratch(FFH),
            *dp_sum_scratch(FFH),
            pltpu.SemaphoreType.DMA((3,)),
        ],
        compiler_params=pltpu.CompilerParams(
            collective_id=2, has_side_effects=True, vmem_limit_bytes=60 * 1024 * 1024
        ),
    )(hn, dy, wg, wu, wd, resid, gain)


VEC = 40


class Total:
    def __init__(self, spot, vec, h_slots, c_slots, own, other, h_s, h_r, c_s, c_r, k_s, k_r):
        self.p, self.vec, self.hs, self.cs, self.own, self.other = spot, vec, h_slots, c_slots, own, other
        self.h_s, self.h_r, self.c_s, self.c_r, self.k_s, self.k_r = h_s, h_r, c_s, c_r, k_s, k_r

    def send(self):
        p = self.p
        self.hs[p.head] = self.vec[...]
        for k in range(1, NHEAD):
            h = lax.rem(p.head + k, NHEAD)
            rcopy(self.hs.at[p.head], self.hs.at[p.head], self.h_s.at[k], self.h_r.at[p.head], {"head": h}).start()

    def middle(self):
        p = self.p
        for k in range(1, NHEAD):
            h = lax.rem(p.head + k, NHEAD)
            rcopy(self.hs.at[h], self.hs.at[h], self.h_s.at[0], self.h_r.at[h], p.sibling).wait_recv()
        total = self.hs[0]
        for h in range(1, NHEAD):
            total = total + self.hs[h]
        per_head = lax.broadcasted_iota(jnp.int32, (VEC, 128), 0) >= 34
        self.cs[p.chip] = jnp.where(per_head, self.vec[...], total)
        for k, to in enumerate(p.chips()):
            rcopy(self.cs.at[p.chip], self.cs.at[p.chip], self.c_s.at[k], self.c_r.at[p.chip], to).start()

    def result(self):
        p = self.p
        for k in range(1, 8):
            chip = lax.rem(p.chip + k, 8)
            rcopy(self.cs.at[chip], self.cs.at[chip], self.c_s.at[0], self.c_r.at[chip], p.sibling).wait_recv()
        total = self.cs[0]
        for k in range(1, 8):
            total = total + self.cs[k]
        self.own[...] = total
        move = rcopy(self.own, self.other, self.k_s, self.k_r, p.sibling)
        move.start()
        move.wait_recv()
        return total + self.other[...]

    def finish(self):
        p = self.p
        for k in range(1, NHEAD):
            rcopy(self.hs.at[0], self.hs.at[0], self.h_s.at[k], self.h_r.at[0], p.sibling).wait_send()
        for k in range(7):
            rcopy(self.cs.at[0], self.cs.at[0], self.c_s.at[k], self.c_r.at[0], p.sibling).wait_send()
        rcopy(self.own, self.other, self.k_s, self.k_r, p.sibling).wait_send()


def mixer_backward(
    db, wt, raw, run, mixed, states, gated, xn, w_in, d_resid, hid, down, resid, ffn_terms, total,
    gain, group_gain, lb, layer, seq,
    block_out, grad_in, out_query, out_forget, out_input, out_outgate, out_output, out_bounds,
    out_norm, out_group, out_ffn, out_mean,
    w, draw, d_mixed, d_query, d_keys, d_values, back_update, decay, incoming, ps, slots, slots2, vec,
    msg, sib, slots3, give, take, ex_send, ex_recv, rs_s, rs_r, rs2_s, rs2_r,
    a0, a1, a2, a3, a4, a5, a6, b0, b1, b2, b3, b4, b5, b6, c0, c1, c2, c3, c4, c5, c6,
    t0, t1, t2, t3, t4, t5, t6, t7, t8, t9, result_a, result_b, group_total, bound_total, local_sem,
):
    load = pltpu.make_async_copy(w_in, w, local_sem.at[0])
    load.start()
    p = Spot()
    greet(p.chips() + [p.sibling] + p.heads())
    scatter = HeadSum(p, down, slots, rs_s, rs_r)
    scatter.send()
    segments = Segments(p, seq)
    soft, picked, bound = lower_bound(lb, layer[0])
    group_total[...] = jnp.zeros_like(group_total)

    @pl.loop(0, CHUNKS)
    def _(c):
        rows = pl.ds(pl.multiple_of(c * CHUNK, CHUNK), CHUNK)
        d_gated = mm(db[rows, :], wt[...], NN)
        before, final = segments.before(c), segments.final(c)
        carried = jnp.where(segments.column(c) == before, 1.0, 0.0)
        running = run[rows, :]
        rate = jnp.exp(running[127:128]) * jnp.where(final == before, 1.0, 0.0)
        decay[c] = jnp.broadcast_to(rate, (8, HERE))
        for h in range(2):
            lanes = slice(h * 128, (h + 1) * 128)
            x, grad = mixed[rows, lanes], d_gated[:, lanes]
            gate = raw[rows, 768 + h * 128 : 768 + (h + 1) * 128]
            s = sigmoid(gate)
            inverse = lax.rsqrt(jnp.mean(x * x, axis=-1, keepdims=True) + EPS)
            normed = x * inverse
            draw[rows, 768 + h * 128 : 768 + (h + 1) * 128] = (
                grad * (normed * group_gain[...]) * slope(gate, s)
            ).astype(BF16)
            inner = grad * (gate * s)
            scaled = inner * group_gain[...]
            back = inverse * (scaled - normed * jnp.mean(scaled * normed, axis=-1, keepdims=True))
            group_total[...] += jnp.sum(inner * normed, axis=0, keepdims=True)
            back = back.astype(BF16)
            d_mixed[rows, lanes] = back
            query_raw = raw[rows, lanes]
            query = (query_raw * sigmoid(query_raw)).astype(BF16).astype(F32)
            high, low = halves(query * jnp.exp(running[:, lanes]) * carried)
            back_update[h, c] = mm(back, high, TN) + mm(back, low, TN)

    for h in range(2):
        lanes = slice(h * 128, (h + 1) * 128)
        state, rate = back_update[h, CHUNKS - 1], decay[CHUNKS - 1, 0:1, lanes]
        for c in range(CHUNKS - 2, -1, -1):
            state = state * decay[c, 0:1, lanes] + back_update[h, c]
            rate = rate * decay[c, 0:1, lanes]
        msg[h, 0:128, :] = state
        msg[h, 128:136, :] = jnp.broadcast_to(rate, (8, 128))
    exchange = Exchange(p, msg, sib, slots3, give, take, ex_send, ex_recv, True)
    exchange.to_sibling()
    exchange.to_chips()

    @pl.loop(0, CHUNKS)
    def _(c):
        rows = pl.ds(pl.multiple_of(c * CHUNK, CHUNK), CHUNK)
        running = run[rows, :]
        middle = running[63:64]
        _, _, query, keys, values = gates(raw, bound, rows)
        up, down_ = jnp.exp(running - middle), jnp.exp(middle - running)
        lifted = query.astype(F32) * up
        lowered = keys.astype(F32) * down_
        column, row = segments.column(c), segments.row(c)
        carried = jnp.where(column == segments.before(c), 1.0, 0.0)
        linked = (column == row) & (
            lax.broadcasted_iota(jnp.int32, (CHUNK, CHUNK), 0)
            >= lax.broadcasted_iota(jnp.int32, (CHUNK, CHUNK), 1)
        )
        for h in range(2):
            lanes = slice(h * 128, (h + 1) * 128)
            lift, lower = halves(lifted[:, lanes]), halves(lowered[:, lanes])
            scores = halves(jnp.where(linked, mm3(lift, lower, NT), 0.0))
            grad = d_mixed[rows, lanes]
            d_scores = halves(jnp.where(linked, mm(grad, values[:, lanes], NT), 0.0))
            d_values[rows, lanes] = mm(scores[0], grad, TN) + mm(scores[1], grad, TN)
            state = halves(states[h, c])
            outer = mm(grad, state[0], NN) + mm(grad, state[1], NN)
            d_query[rows, lanes] = mm3(d_scores, lower, NN) * up[:, lanes] + outer * jnp.exp(running[:, lanes]) * carried
            d_keys[rows, lanes] = mm3(d_scores, lift, TN) * down_[:, lanes]

    sums = [
        DpSum(p, a0, a1, a2, a3, a4, a5, a6),
        DpSum(p, b0, b1, b2, b3, b4, b5, b6),
        DpSum(p, c0, c1, c2, c3, c4, c5, c6),
    ]
    outer_products(db, gated, c0)
    sums[2].to_sibling()
    exchange.result(incoming)
    sums[2].to_z()
    bound_total[...] = jnp.zeros_like(bound_total)

    @pl.loop(0, CHUNKS)
    def _(i):
        c = CHUNKS - 1 - i
        rows = pl.ds(pl.multiple_of(c * CHUNK, CHUNK), CHUNK)
        running = run[rows, :]
        logistic, forget, query, keys, values = gates(raw, bound, rows)
        keys = keys.astype(F32)
        fade = jnp.exp(running[127:128] - running)
        column, final = segments.column(c), segments.final(c)
        ends = jnp.where(column == final, 1.0, 0.0)
        for h in range(2):
            lanes = slice(h * 128, (h + 1) * 128)
            state = incoming[h]
            pair = halves(state)
            tail = halves(keys[:, lanes] * fade[:, lanes] * ends)
            value_grad = d_values[rows, lanes] + mm3(tail, pair, NT)
            draw[rows, 512 + h * 128 : 512 + (h + 1) * 128] = value_grad.astype(BF16)
            lift = mm(values[:, lanes], pair[0], NN) + mm(values[:, lanes], pair[1], NN)
            key_grad = d_keys[rows, lanes] + lift * fade[:, lanes] * ends
            at_end = jnp.sum(states[h, c + 1] * state, axis=0, keepdims=True)
            query_grad = d_query[rows, lanes]
            step = query[:, lanes].astype(F32) * query_grad - keys[:, lanes] * key_grad
            log_grad = summed_rows(False, step) + at_end
            forget_grad = log_grad / forget[:, lanes] - key_grad
            rest = 1.0 - logistic[:, lanes]
            draw[rows, 256 + h * 128 : 256 + (h + 1) * 128] = (
                forget_grad * (1.0 - bound[:, lanes]) * logistic[:, lanes] * rest
            ).astype(BF16)
            bound_total[:, lanes] += jnp.sum(forget_grad * rest, axis=0, keepdims=True)
            query_raw = raw[rows, lanes]
            draw[rows, lanes] = (query_grad * slope(query_raw, sigmoid(query_raw))).astype(BF16)
            incoming[h] = state * decay[c, 0:1, lanes] + back_update[h, c]

    load.wait()

    @pl.loop(0, 8)
    def _(j):
        columns = pl.ds(pl.multiple_of(j * 256, 256), 256)
        part = mm(draw[...], w[columns, :], NT).astype(BF16)
        for h in range(NHEAD):
            ps[h, :, columns] = part[h * ROWS : (h + 1) * ROWS]

    scatter2 = HeadSum(p, ps, slots2, rs2_s, rs2_r)
    scatter2.send()
    outer_products(xn, draw.at[:, 0:512], a0)
    sums[0].to_sibling()
    outer_products(xn, draw.at[:, 512:1024], b0)
    sums[0].to_z()
    sums[1].to_sibling()
    scatter.collect()

    @pl.loop(0, 4)
    def _(i):
        rows = pl.ds(pl.multiple_of(i * 16, 16), 16)
        block_out[rows, :] = (resid[rows, :] + scatter.rows(rows)).astype(BF16)

    sums[1].to_z()
    sums[2].to_x(write(out_output))
    scatter2.collect()
    own = pl.multiple_of(p.head * ROWS, ROWS)
    out_norm[...] = jnp.zeros_like(out_norm)

    @pl.loop(0, 4)
    def _(i):
        rows = pl.ds(pl.multiple_of(i * 16, 16), 16)
        here = pl.ds(pl.multiple_of(own + i * 16, 16), 16)
        grad, x = scatter2.rows(rows), hid[here, :].astype(F32)
        inverse = lax.rsqrt(jnp.mean(x * x, axis=-1, keepdims=True) + EPS)
        scaled, normed = grad * gain[...], x * inverse
        back = inverse * (scaled - normed * jnp.mean(scaled * normed, axis=-1, keepdims=True))
        out_norm[...] += jnp.sum(grad * normed, axis=0, keepdims=True)
        grad_in[rows, :] = d_resid[rows, :] + back

    vec[...] = jnp.zeros_like(vec)
    for i in range(16):
        vec[i : i + 1, :] = out_norm[:, i * 128 : (i + 1) * 128]
        vec[16 + i : 17 + i, :] = ffn_terms[:, i * 128 : (i + 1) * 128]
    vec[32:33, :] = group_total[...]
    vec[33:34, :] = total[:, 0:128] + total[:, 128:256]
    vec[34:35, :] = bound_total[:, 0:128]
    vec[35:36, :] = bound_total[:, 128:256]
    everywhere = Total(p, vec, t0, t1, t2, t3, t4, t5, t6, t7, t8.at[0], t9.at[0])
    everywhere.send()
    sums[2].end(accumulate(out_output))
    everywhere.middle()
    sums[0].to_x(write(result_a))
    sums[1].to_x(write(result_b))
    vec[...] = everywhere.result()
    for i in range(16):
        out_norm[:, i * 128 : (i + 1) * 128] = vec[i : i + 1, :]
        out_ffn[:, i * 128 : (i + 1) * 128] = vec[16 + i : 17 + i, :]
    out_group[...] = vec[32:33, :]
    mean = jnp.sum(vec[33:34, :], axis=-1, keepdims=True) / float(8192 * D)
    out_mean[...] = jnp.broadcast_to(mean, (1, 128))
    for h in range(2):
        lanes = slice(h * 128, (h + 1) * 128)
        out_bounds[:, lanes] = soft[:, lanes] * (picked[:, lanes] - bound[:, lanes]) * vec[34 + h : 35 + h, :]
    sums[0].end(accumulate(result_a))
    out_query[...] = result_a[:, 0:256]
    out_forget[...] = result_a[:, 256:512]
    sums[1].end(accumulate(result_b))
    out_input[...] = result_b[:, 0:256]
    out_outgate[...] = result_b[:, 256:512]
    scatter.finish()
    scatter2.finish()
    exchange.finish()
    everywhere.finish()
    for one in sums:
        one.finish()


def call_mixer_backward(*arrays):
    out = jax.ShapeDtypeStruct
    return pl.pallas_call(
        mixer_backward,
        name="mixer_backward",
        out_shape=(
            out((ROWS, D), BF16),
            out((ROWS, D), F32),
            out((128, HERE), F32),
            out((128, HERE), F32),
            out((128, HERE), F32),
            out((128, HERE), F32),
            out((128, HERE), F32),
            out((24, HERE), F32),
            out((1, D), F32),
            out((1, KDIM), F32),
            out((1, D), F32),
            out((1, 128), F32),
        ),
        in_specs=[VM] * 8 + [HB] + [VM] * 9 + [SM, SM],
        out_specs=(VM,) * 12,
        scratch_shapes=[
            pltpu.VMEM((D, 1024), BF16),
            pltpu.VMEM((TOK, 1024), BF16),
            pltpu.VMEM((TOK, HERE), BF16),
            *[pltpu.VMEM((TOK, HERE), F32)] * 3,
            pltpu.VMEM((2, CHUNKS, 128, 128), F32),
            pltpu.VMEM((CHUNKS, 8, HERE), F32),
            pltpu.VMEM((2, 128, 128), F32),
            *[pltpu.VMEM((NHEAD, ROWS, D), BF16)] * 3,
            pltpu.VMEM((VEC, 128), F32),
            *exchange_scratch(),
            *eight(),
            *eight(),
            *dp_sum_scratch(512),
            *dp_sum_scratch(512),
            *dp_sum_scratch(HERE),
            pltpu.VMEM((8, VEC, 128), F32),
            pltpu.VMEM((8, VEC, 128), F32),
            pltpu.VMEM((VEC, 128), F32),
            pltpu.VMEM((VEC, 128), F32),
            *eight(),
            *eight(),
            pltpu.SemaphoreType.DMA((1,)),
            pltpu.SemaphoreType.DMA((1,)),
            pltpu.VMEM((128, 512), F32),
            pltpu.VMEM((128, 512), F32),
            pltpu.VMEM((1, 128), F32),
            pltpu.VMEM((1, HERE), F32),
            pltpu.SemaphoreType.DMA((1,)),
        ],
        compiler_params=pltpu.CompilerParams(
            collective_id=3, has_side_effects=True, vmem_limit_bytes=60 * 1024 * 1024
        ),
    )(*arrays)


def local(
    hidden_in, norm_gain, w_query, w_forget, w_input, w_outgate, lower_bounds, layer_index, group_gain,
    w_output, ffn_gain, w_gate, w_up, w_down, seq_lengths, grad_out,
):
    norm_row, ffn_row, group_row = norm_gain.reshape(1, D), ffn_gain.reshape(1, D), group_gain.reshape(1, KDIM)
    raw, xn, gated, mixed, states, run, total, w_all, wt_all = call_mixer_forward(
        hidden_in, norm_row, w_query, w_forget, w_input, w_outgate, w_output.T,
        lower_bounds, layer_index, seq_lengths, group_row,
    )
    hn, resid, wg, wu, wd = call_branch(gated, wt_all, hidden_in, ffn_row, w_gate, w_up, w_down.T)
    down, d_resid, db, ffn_terms, grad_gate, grad_up, grad_down = call_feed_forward(
        hn, grad_out, wg, wu, wd, resid, ffn_row
    )
    (
        block_out, grad_in, grad_query, grad_forget, grad_input, grad_outgate, grad_output, grad_bounds,
        grad_norm, grad_group, grad_ffn, mean,
    ) = call_mixer_backward(
        db, wt_all, raw, run, mixed, states, gated, xn, w_all, d_resid, hidden_in, down, resid, ffn_terms, total,
        norm_row, group_row, lower_bounds, layer_index, seq_lengths,
    )
    return (
        block_out,
        grad_in,
        grad_norm.reshape(D),
        grad_query,
        grad_forget,
        grad_input,
        grad_outgate,
        grad_bounds,
        grad_group.reshape(KDIM),
        grad_output.T,
        grad_ffn.reshape(D),
        grad_gate,
        grad_up,
        grad_down.T,
        mean[0, 0:1],
    )


def solution(mesh):
    return jax.shard_map(
        local,
        mesh=mesh,
        in_specs=(
            P("dp", None),
            P(),
            P("dp", "head"),
            P("dp", "head"),
            P("dp", "head"),
            P("dp", "head"),
            P(None, "head"),
            P(),
            P(),
            P("head", "dp"),
            P(),
            P("dp", "head"),
            P("dp", "head"),
            P("head", "dp"),
            P(),
            P("dp", None),
        ),
        out_specs=(
            P(("dp", "head"), None),
            P(("dp", "head"), None),
            P(),
            P("dp", "head"),
            P("dp", "head"),
            P("dp", "head"),
            P("dp", "head"),
            P(None, "head"),
            P(),
            P("head", "dp"),
            P(),
            P("dp", "head"),
            P("dp", "head"),
            P("head", "dp"),
            P(),
        ),
        check_vma=False,
    )
```

```python
from functools import partial

import jax
import jax.numpy as jnp
from jax import lax
from jax.experimental import pallas as pl
from jax.experimental.pallas import tpu as pltpu
from jax.sharding import PartitionSpec as P

D = 2048
KDIM = 128
CHUNK = 128
TOK = 512
CHUNKS = TOK // CHUNK
HERE = 256
FFH = 704
NSEQ = 12
NHEAD = 8
ROWS = TOK // NHEAD
EPS = 1e-06
F32 = jnp.float32
BF16 = jnp.bfloat16
MESH = pl.DeviceIdType.MESH
VM = pl.BlockSpec(memory_space=pltpu.VMEM)
SM = pl.BlockSpec(memory_space=pltpu.SMEM)
HB = pl.BlockSpec(memory_space=pl.ANY)


class Spot:
    def __init__(self):
        self.dp = lax.axis_index("dp")
        self.head = lax.axis_index("head")
        self.core = lax.rem(self.dp, 2)
        self.chip = lax.div(self.dp, 2)
        self.xh = lax.rem(self.chip, 2)
        self.z = lax.div(self.chip, 2)

    def at(self, dz, xh, core):
        return (lax.rem(self.z + dz, 4) * 2 + xh) * 2 + core

    @property
    def sibling(self):
        return {"dp": self.chip * 2 + 1 - self.core}

    def chips(self):
        return [{"dp": lax.rem(self.chip + k, 8) * 2 + self.core} for k in range(1, 8)]

    def heads(self):
        return [{"head": lax.rem(self.head + k, NHEAD)} for k in range(1, NHEAD)]


def greet(ids):
    barrier = pltpu.get_barrier_semaphore()
    for one in ids:
        pl.semaphore_signal(barrier, inc=1, device_id=one, device_id_type=MESH)
    pl.semaphore_wait(barrier, len(ids))


def rcopy(src, dst, send, recv, where):
    return pltpu.make_async_remote_copy(
        src_ref=src, dst_ref=dst, send_sem=send, recv_sem=recv, device_id=where, device_id_type=MESH
    )


GATHER_SENDS = 17


class Gather:
    def __init__(self, spot, g, send, recv, half, columns=0):
        self.spot, self.g, self.s, self.r, self.h = spot, g, send, recv, half
        self.columns, self.middle = columns, (columns or 128) // 2

    def block(self, d, start=0, rows=0):
        if self.columns:
            rows = rows or self.columns
            return self.g.at[pl.ds(start, rows), pl.ds(pl.multiple_of(d * 128, 128), 128)]
        return self.g.at[pl.ds(pl.multiple_of(d * 128 + start, 64), rows or 128), :]

    def push(self, d, to, k):
        rcopy(self.block(d), self.block(d), self.s.at[k], self.r.at[d], {"dp": to}).start()

    def push_half(self, d, to, k, xh, part):
        b = self.block(d, part * self.middle, self.middle)
        rcopy(b, b, self.s.at[k], self.h.at[2 * xh + part], {"dp": to}).start()

    def arrived(self, d):
        b = self.block(d)
        rcopy(b, b, self.s.at[0], self.r.at[d], self.spot.sibling).wait_recv()

    def arrived_halves(self, d, xh):
        for part in range(2):
            b = self.block(d, part * self.middle, self.middle)
            rcopy(b, b, self.s.at[0], self.h.at[2 * xh + part], self.spot.sibling).wait_recv()

    def first(self):
        p = self.spot
        self.push(p.dp, p.at(0, 1 - p.xh, p.core), 0)
        self.push(p.dp, p.at(1, p.xh, p.core), 1)
        self.push(p.dp, p.at(3, p.xh, p.core), 2)
        self.push(p.dp, p.at(0, p.xh, 1 - p.core), 3)

    def second(self):
        p = self.spot
        b = p.at(0, 1 - p.xh, p.core)
        self.arrived(b)
        self.push(b, p.at(1, p.xh, p.core), 4)
        self.push(b, p.at(3, p.xh, p.core), 5)
        self.push(b, p.at(0, p.xh, 1 - p.core), 6)

    def third(self):
        p = self.spot
        for i, h in enumerate((p.xh, 1 - p.xh)):
            b = p.at(3, h, p.core)
            self.arrived(b)
            self.push_half(b, p.at(1, p.xh, p.core), 7 + i, h, 0)
            self.push(b, p.at(0, p.xh, 1 - p.core), 9 + i)
            b = p.at(1, h, p.core)
            self.arrived(b)
            self.push_half(b, p.at(3, p.xh, p.core), 11 + i, h, 1)
            self.push(b, p.at(0, p.xh, 1 - p.core), 13 + i)

    def fourth(self):
        p = self.spot
        for i, h in enumerate((p.xh, 1 - p.xh)):
            b = p.at(2, h, p.core)
            self.arrived_halves(b, h)
            self.push(b, p.at(0, p.xh, 1 - p.core), 15 + i)

    def last(self):
        p = self.spot
        for dz in range(4):
            for h in range(2):
                self.arrived(p.at(dz, h, 1 - p.core))
        half = self.block(0, 0, self.middle)
        for k in range(GATHER_SENDS):
            b = half if k in (7, 8, 11, 12) else self.block(0)
            rcopy(b, b, self.s.at[k], self.r.at[0], p.sibling).wait_send()


def gather_semaphores():
    return [
        pltpu.SemaphoreType.DMA((GATHER_SENDS,)),
        pltpu.SemaphoreType.DMA((16,)),
        pltpu.SemaphoreType.DMA((4,)),
    ]


NN = (((1,), (0,)), ((), ()))
NT = (((1,), (1,)), ((), ()))
TN = (((0,), (0,)), ((), ()))


def mm(a, b, dims):
    return lax.dot_general(a, b, dims, preferred_element_type=F32)


def halves(a):
    high = a.astype(BF16)
    return high, (a - high.astype(F32)).astype(BF16)


def mm2(a, b, dims):
    return mm(a[0], b, dims) + mm(a[1], b, dims)


def mm3(a, b, dims):
    return mm(a[0], b[0], dims) + (mm(a[0], b[1], dims) + mm(a[1], b[0], dims))


def triangle(lower):
    rows = lax.broadcasted_iota(jnp.int32, (CHUNK, CHUNK), 0)
    columns = lax.broadcasted_iota(jnp.int32, (CHUNK, CHUNK), 1)
    return (rows >= columns if lower else rows <= columns).astype(BF16)


def summed_rows(lower, x):
    high = x.astype(BF16)
    rest = x - high.astype(F32)
    middle = rest.astype(BF16)
    low = (rest - middle.astype(F32)).astype(BF16)
    t = triangle(lower)
    return mm(t, high, NN) + (mm(t, middle, NN) + mm(t, low, NN))


class Segments:
    def __init__(self, spot, seq):
        self.starts = []
        total = jnp.int32(0)
        for i in range(NSEQ):
            self.starts.append(total)
            total = total + seq[i]
        self.first = spot.dp * TOK

    def of(self, position):
        found = jnp.where(position >= self.starts[0], 1, 0)
        for s in self.starts[1:]:
            found = found + jnp.where(position >= s, 1, 0)
        return found - 1

    def column(self, c):
        return self.of(self.first + c * CHUNK + lax.broadcasted_iota(jnp.int32, (CHUNK, KDIM), 0))

    def row(self, c):
        return self.of(self.first + c * CHUNK + lax.broadcasted_iota(jnp.int32, (CHUNK, KDIM), 1))

    def before(self, c):
        return self.of(self.first + c * CHUNK - 1)

    def final(self, c):
        return self.of(self.first + (c + 1) * CHUNK - 1)


def lower_bound(lb, layer):
    x = lb[...]
    e = jnp.exp(x - jnp.max(x, axis=0, keepdims=True))
    soft = e / jnp.sum(e, axis=0, keepdims=True)
    depth = lax.broadcasted_iota(jnp.int32, x.shape, 0)
    picked = jnp.where((depth >= 1) & (depth <= layer), 1.0, 0.0)
    return soft, picked, jnp.sum(soft * picked, axis=0, keepdims=True)


def sigmoid(x):
    return lax.logistic(x)


def slope(x, s):
    return s * (1.0 + x * (1.0 - s))


class Exchange:
    def __init__(self, spot, msg, sib, slots, give, take, send, recv, backward):
        self.p, self.msg, self.sib, self.slots = spot, msg, sib, slots
        self.give, self.take, self.s, self.r, self.back = give, take, send, recv, backward

    def to_sibling(self):
        p = self.p
        rcopy(self.msg.at[1 - p.core], self.sib, self.s.at[7], self.r.at[8], p.sibling).start()

    def to_chips(self):
        p = self.p
        rcopy(self.sib, self.sib, self.s.at[7], self.r.at[8], p.sibling).wait_recv()
        mine, other = self.msg[p.core], self.sib[...]
        zero = p.core == 0
        one, two = jnp.where(zero, mine, other), jnp.where(zero, other, mine)
        near, far = (two, one) if self.back else (one, two)
        self.near = near
        state = near[0:128] * far[128:129] + far[0:128]
        self.slots[p.chip, 0:128, :] = state
        self.slots[p.chip, 128:136, :] = near[128:136] * far[128:136]
        for k, to in enumerate(p.chips()):
            rcopy(self.slots.at[p.chip], self.slots.at[p.chip], self.s.at[k], self.r.at[p.chip], to).start()

    def result(self, out):
        p = self.p
        for k in range(1, 8):
            chip = lax.rem(p.chip + k, 8)
            rcopy(self.slots.at[chip], self.slots.at[chip], self.s.at[0], self.r.at[chip], p.sibling).wait_recv()
        state = jnp.zeros((128, 128), F32)
        for k in range(7, 0, -1) if self.back else range(7):
            m = self.slots[k]
            after = state * m[128:129] + m[0:128]
            state = jnp.where(k > p.chip if self.back else k < p.chip, after, state)
        second = state * self.near[128:129] + self.near[0:128]
        is_first = p.core == (1 if self.back else 0)
        self.give[...] = jnp.where(is_first, second, state)
        move = rcopy(self.give, self.take, self.s.at[8], self.r.at[9], p.sibling)
        move.start()
        out[p.core] = jnp.where(is_first, state, second)
        move.wait_recv()
        out[1 - p.core] = self.take[...]

    def finish(self):
        p = self.p
        for k in range(7):
            rcopy(self.slots.at[0], self.slots.at[0], self.s.at[k], self.r.at[0], p.sibling).wait_send()
        rcopy(self.sib, self.sib, self.s.at[7], self.r.at[8], p.sibling).wait_send()
        rcopy(self.give, self.take, self.s.at[8], self.r.at[9], p.sibling).wait_send()


def exchange_scratch():
    return [
        pltpu.VMEM((2, 136, 128), F32),
        pltpu.VMEM((136, 128), F32),
        pltpu.VMEM((8, 136, 128), F32),
        pltpu.VMEM((128, 128), F32),
        pltpu.VMEM((128, 128), F32),
        pltpu.SemaphoreType.DMA((9,)),
        pltpu.SemaphoreType.DMA((10,)),
    ]


def gates(raw, bound, rows):
    query_raw = raw[rows, 0:256]
    logistic = sigmoid(raw[rows, 256:512])
    forget = bound + (1.0 - bound) * logistic
    query = (query_raw * sigmoid(query_raw)).astype(BF16)
    keys = (1.0 - forget).astype(BF16)
    values = raw[rows, 512:768].astype(BF16)
    return logistic, forget, query, keys, values


def eighth(ref, h):
    return ref.at[pl.ds(pl.multiple_of(h * ROWS, ROWS), ROWS), :]


class HeadSum:
    def __init__(self, spot, ps, slots, send, recv):
        self.p, self.ps, self.slots, self.s, self.r = spot, ps, slots, send, recv

    def send(self):
        p = self.p
        for k in range(1, NHEAD):
            h = lax.rem(p.head + k, NHEAD)
            rcopy(eighth(self.ps, h), eighth(self.slots, p.head), self.s.at[k], self.r.at[p.head], {"head": h}).start()

    def collect(self):
        p = self.p
        mine = pl.ds(pl.multiple_of(p.head * ROWS, ROWS), ROWS)
        self.slots[mine, :] = self.ps[mine, :]
        for k in range(1, NHEAD):
            h = lax.rem(p.head + k, NHEAD)
            one = eighth(self.slots, h)
            rcopy(one, one, self.s.at[0], self.r.at[h], p.sibling).wait_recv()

    def rows(self, start, count):
        total = None
        for h in range(NHEAD):
            one = self.slots[pl.ds(pl.multiple_of(h * ROWS + start, 16), count), :].astype(F32)
            total = one if total is None else total + one
        return total

    def finish(self):
        for k in range(1, NHEAD):
            one = eighth(self.ps, 0)
            rcopy(one, one, self.s.at[k], self.r.at[0], self.p.sibling).wait_send()


class HeadGather:
    def __init__(self, spot, full, send, recv):
        self.p, self.full, self.s, self.r = spot, full, send, recv

    def block(self, h):
        return self.full.at[pl.ds(pl.multiple_of(h * ROWS, ROWS), ROWS), :]

    def send(self):
        p = self.p
        for k in range(1, NHEAD):
            h = lax.rem(p.head + k, NHEAD)
            rcopy(self.block(p.head), self.block(p.head), self.s.at[k], self.r.at[p.head], {"head": h}).start()

    def collect(self):
        p = self.p
        for k in range(1, NHEAD):
            h = lax.rem(p.head + k, NHEAD)
            rcopy(self.block(h), self.block(h), self.s.at[0], self.r.at[h], p.sibling).wait_recv()

    def finish(self):
        for k in range(1, NHEAD):
            rcopy(self.block(0), self.block(0), self.s.at[k], self.r.at[0], self.p.sibling).wait_send()


def eight():
    return [pltpu.SemaphoreType.DMA((8,)), pltpu.SemaphoreType.DMA((8,))]


class DpSum:
    def __init__(self, spot, rows, gs, cr, zr, xs, xr, send, recv):
        n = pl.ds(0, rows)
        self.rows, self.p = rows, spot
        self.gs, self.cr, self.zr = gs.at[:, :, n, :], cr.at[:, n, :], zr.at[:, :, n, :]
        self.xs, self.xr, self.s, self.r = xs.at[n, :], xr.at[n, :], send, recv

    def pair(self, i):
        p = self.p
        two = pl.ds(2 * i, 2)
        return rcopy(self.gs.at[1 - p.core, two], self.cr.at[two], self.s.at[i], self.r.at[i], p.sibling)

    def to_sibling(self):
        for i in range(4):
            self.pair(i).start()

    def across(self, d):
        p = self.p
        z = lax.rem(p.z + d, 4)
        where = {"dp": (z * 2 + p.xh) * 2 + p.core}
        return rcopy(self.gs.at[p.core, pl.ds(z * 2, 2)], self.zr.at[d - 1], self.s.at[3 + d], self.r.at[3 + d], where)

    def to_z(self):
        p = self.p
        for i in range(4):
            self.pair(i).wait_recv()

        @pl.loop(0, 8)
        def _(k):
            self.gs[p.core, k] = (self.gs[p.core, k].astype(F32) + self.cr[k].astype(F32)).astype(BF16)

        for d in (1, 3, 2):
            self.across(d).start()

    def last_move(self):
        p = self.p
        where = {"dp": (p.z * 2 + 1 - p.xh) * 2 + p.core}
        return rcopy(self.xs, self.xr, self.s.at[7], self.r.at[7], where)

    def to_x(self, put):
        p = self.p
        for d in (1, 3, 2):
            self.across(d).wait_recv()

        def total(h):
            one = self.gs[p.core, 2 * p.z + h].astype(F32)
            for i in range(3):
                one = one + self.zr[i, h].astype(F32)
            return one

        self.xs[...] = total(1 - p.xh).astype(BF16)
        self.last_move().start()
        put(total(p.xh))

    def end(self, add):
        self.last_move().wait_recv()
        add(self.xr[...].astype(F32))

    def finish(self):
        for i in range(4):
            self.pair(i).wait_send()
        for d in (1, 3, 2):
            self.across(d).wait_send()
        self.last_move().wait_send()


def dp_sum_scratch(rows):
    return [
        pltpu.VMEM((2, 8, rows, 128), BF16),
        pltpu.VMEM((8, rows, 128), BF16),
        pltpu.VMEM((3, 2, rows, 128), BF16),
        pltpu.VMEM((rows, 128), BF16),
        pltpu.VMEM((rows, 128), BF16),
        *eight(),
    ]


def products(left_turned, right, gs):
    @pl.loop(0, 8)
    def _(k):
        columns = pl.ds(pl.multiple_of(k * 256, 256), 256)
        both = mm(left_turned[...], right[:, columns], NN).astype(BF16)
        gs[0, k] = both[:, 0:128]
        gs[1, k] = both[:, 128:256]


def products_turned(left, right, gs):
    @pl.loop(0, 8)
    def _(k):
        columns = pl.ds(pl.multiple_of(k * 256, 256), 256)
        both = mm(left[:, columns], right[...], TN).astype(BF16)
        for q in range(4):
            gs[0, k, 128 * q : 128 * (q + 1), :] = both[0:128, 128 * q : 128 * (q + 1)]
            gs[1, k, 128 * q : 128 * (q + 1), :] = both[128:256, 128 * q : 128 * (q + 1)]


def write(ref):
    def put(x):
        ref[...] = x

    return put


def accumulate(ref):
    def add(x):
        ref[...] += x

    return add


VEC = 40


class Total:
    def __init__(self, spot, vec, h_slots, c_slots, own, other, h_s, h_r, c_s, c_r, k_s, k_r):
        self.p, self.vec, self.hs, self.cs, self.own, self.other = spot, vec, h_slots, c_slots, own, other
        self.h_s, self.h_r, self.c_s, self.c_r, self.k_s, self.k_r = h_s, h_r, c_s, c_r, k_s, k_r

    def send(self):
        p = self.p
        self.hs[p.head] = self.vec[...]
        for k in range(1, NHEAD):
            h = lax.rem(p.head + k, NHEAD)
            rcopy(self.hs.at[p.head], self.hs.at[p.head], self.h_s.at[k], self.h_r.at[p.head], {"head": h}).start()

    def middle(self):
        p = self.p
        for k in range(1, NHEAD):
            h = lax.rem(p.head + k, NHEAD)
            rcopy(self.hs.at[h], self.hs.at[h], self.h_s.at[0], self.h_r.at[h], p.sibling).wait_recv()
        total = self.hs[0]
        for h in range(1, NHEAD):
            total = total + self.hs[h]
        per_head = lax.broadcasted_iota(jnp.int32, (VEC, 128), 0) >= 34
        self.cs[p.chip] = jnp.where(per_head, self.vec[...], total)
        for k, to in enumerate(p.chips()):
            rcopy(self.cs.at[p.chip], self.cs.at[p.chip], self.c_s.at[k], self.c_r.at[p.chip], to).start()

    def result(self):
        p = self.p
        for k in range(1, 8):
            chip = lax.rem(p.chip + k, 8)
            rcopy(self.cs.at[chip], self.cs.at[chip], self.c_s.at[0], self.c_r.at[chip], p.sibling).wait_recv()
        total = self.cs[0]
        for k in range(1, 8):
            total = total + self.cs[k]
        self.own[...] = total
        move = rcopy(self.own, self.other, self.k_s, self.k_r, p.sibling)
        move.start()
        move.wait_recv()
        return total + self.other[...]

    def finish(self):
        p = self.p
        for k in range(1, NHEAD):
            rcopy(self.hs.at[0], self.hs.at[0], self.h_s.at[k], self.h_r.at[0], p.sibling).wait_send()
        for k in range(7):
            rcopy(self.cs.at[0], self.cs.at[0], self.c_s.at[k], self.c_r.at[0], p.sibling).wait_send()
        rcopy(self.own, self.other, self.k_s, self.k_r, p.sibling).wait_send()


def forward(
    hid, gain, wq, wf, wi, wo, w_output, lb, layer, seq, group_gain, ffn_gain, wg, wu, wd,
    raw, xn_out, gated, mixed, states, run, total, w_out, wt_out, hn_out, resid, wg_out, wu_out, wd_out,
    xn, w, wt, g0, g1, g2, hn, ps, slots, inner_update, decay, incoming,
    msg, sib, slots3, give, take, ex_send, ex_recv, rs_s, rs_r, ag_s, ag_r,
    ws, wr, wh, os, or_, oh, s0, r0, h0, s1, r1, h1, s2, r2, h2, local_sem,
):
    p = Spot()
    mine = pl.ds(pl.multiple_of(p.dp * 128, 128), 128)
    for k, one in enumerate((wq, wf, wi, wo)):
        w[mine, 256 * k : 256 * (k + 1)] = one[...]
    greet(p.chips() + [p.sibling] + p.heads())
    gather = Gather(p, w, ws, wr, wh)
    gather.first()
    wt[:, mine] = w_output[...]
    later = Gather(p, wt, os, or_, oh, HERE)
    for one, full in zip((wg, wu, wd), (g0, g1, g2)):
        full[:, mine] = one[...]
    gathers = [Gather(p, g0, s0, r0, h0, FFH), Gather(p, g1, s1, r1, h1, FFH), Gather(p, g2, s2, r2, h2, FFH)]

    @pl.loop(0, 8)
    def _(i):
        rows = pl.ds(pl.multiple_of(i * 64, 64), 64)
        x = hid[rows, :].astype(F32)
        scale = lax.rsqrt(jnp.mean(x * x, axis=-1, keepdims=True) + EPS)
        xn[rows, :] = (x * scale * gain[...]).astype(BF16)

    keeps = []

    def keep(source, out):
        move = pltpu.make_async_copy(source, out, local_sem.at[len(keeps)])
        move.start()
        keeps.append(move)

    keep(xn, xn_out)
    gather.second()
    gather.third()
    gather.fourth()
    later.first()
    gathers[0].first()
    gather.last()
    keep(w, w_out)

    @pl.loop(0, 4)
    def _(j):
        columns = pl.ds(pl.multiple_of(j * 256, 256), 256)
        raw[:, columns] = mm(xn[...], w[:, columns], NN)

    later.second()
    segments = Segments(p, seq)
    bound = lower_bound(lb, layer[0])[2]
    total[...] = jnp.zeros_like(total)

    @pl.loop(0, CHUNKS)
    def _(c):
        rows = pl.ds(pl.multiple_of(c * CHUNK, CHUNK), CHUNK)
        logistic, forget, query, keys, values = gates(raw, bound, rows)
        total[...] += jnp.sum(forget, axis=0, keepdims=True)
        running = summed_rows(True, jnp.log(forget))
        run[rows, :] = running
        middle, ending = running[63:64], running[127:128]
        lifted = query.astype(F32) * jnp.exp(running - middle)
        lowered = keys.astype(F32) * jnp.exp(middle - running)
        tail = keys.astype(F32) * jnp.exp(ending - running)
        column, row = segments.column(c), segments.row(c)
        linked = (column == row) & (
            lax.broadcasted_iota(jnp.int32, (CHUNK, CHUNK), 0)
            >= lax.broadcasted_iota(jnp.int32, (CHUNK, CHUNK), 1)
        )
        final = segments.final(c)
        rate = jnp.exp(ending) * jnp.where(final == segments.before(c), 1.0, 0.0)
        decay[c] = jnp.broadcast_to(rate, (8, HERE))
        ends = jnp.where(column == final, 1.0, 0.0)
        for h in range(2):
            lanes = slice(h * 128, (h + 1) * 128)
            scores = mm3(halves(lifted[:, lanes]), halves(lowered[:, lanes]), NT)
            scores = jnp.where(linked, scores, 0.0)
            mixed[rows, lanes] = mm2(halves(scores), values[:, lanes], NN)
            high, low = halves(tail[:, lanes] * ends)
            inner_update[h, c] = mm(values[:, lanes], high, TN) + mm(values[:, lanes], low, TN)

    for h in range(2):
        lanes = slice(h * 128, (h + 1) * 128)
        state, rate = inner_update[h, 0], decay[0, 0:1, lanes]
        for c in range(1, CHUNKS):
            state = state * decay[c, 0:1, lanes] + inner_update[h, c]
            rate = rate * decay[c, 0:1, lanes]
        msg[h, 0:128, :] = state
        msg[h, 128:136, :] = jnp.broadcast_to(rate, (8, 128))
    exchange = Exchange(p, msg, sib, slots3, give, take, ex_send, ex_recv, False)
    exchange.to_sibling()
    exchange.to_chips()
    later.third()
    gathers[1].first()
    gathers[2].first()
    gathers[0].second()
    later.fourth()
    exchange.result(incoming)
    for h in range(2):
        lanes = slice(h * 128, (h + 1) * 128)
        state = incoming[h]
        states[h, 0] = state
        for c in range(CHUNKS):
            state = state * decay[c, 0:1, lanes] + inner_update[h, c]
            states[h, c + 1] = state

    @pl.loop(0, CHUNKS)
    def _(c):
        rows = pl.ds(pl.multiple_of(c * CHUNK, CHUNK), CHUNK)
        carried = jnp.where(segments.column(c) == segments.before(c), 1.0, 0.0)
        for h in range(2):
            lanes = slice(h * 128, (h + 1) * 128)
            query_raw = raw[rows, h * 128 : (h + 1) * 128]
            query = (query_raw * sigmoid(query_raw)).astype(BF16).astype(F32)
            reach = query * jnp.exp(run[rows, lanes]) * carried
            x = mixed[rows, lanes] + mm3(halves(reach), halves(states[h, c]), NT)
            mixed[rows, lanes] = x
            scale = lax.rsqrt(jnp.mean(x * x, axis=-1, keepdims=True) + EPS)
            gate = raw[rows, 768 + h * 128 : 768 + (h + 1) * 128]
            gated[rows, lanes] = (x * scale * group_gain[...] * (gate * sigmoid(gate))).astype(BF16)

    gathers[1].second()
    gathers[2].second()
    later.last()
    keep(wt, wt_out)

    @pl.loop(0, 8)
    def _(j):
        columns = pl.ds(pl.multiple_of(j * 256, 256), 256)
        ps[:, columns] = mm(gated[...], wt[:, columns], NN).astype(BF16)

    scatter = HeadSum(p, ps, slots, rs_s, rs_r)
    scatter.send()
    for g in gathers:
        g.third()
    for g in gathers:
        g.fourth()
    scatter.collect()
    own = pl.multiple_of(p.head * ROWS, ROWS)

    @pl.loop(0, 4)
    def _(i):
        rows = pl.ds(pl.multiple_of(i * 16, 16), 16)
        here = pl.ds(pl.multiple_of(own + i * 16, 16), 16)
        x = hid[here, :].astype(F32) + scatter.rows(i * 16, 16)
        resid[rows, :] = x
        scale = lax.rsqrt(jnp.mean(x * x, axis=-1, keepdims=True) + EPS)
        hn[here, :] = (x * scale * ffn_gain[...]).astype(BF16)

    spread = HeadGather(p, hn, ag_s, ag_r)
    spread.send()
    for g, full, out in zip(gathers, (g0, g1, g2), (wg_out, wu_out, wd_out)):
        g.last()
        keep(full, out)
    exchange.finish()
    scatter.finish()
    spread.collect()
    keep(hn, hn_out)
    spread.finish()
    for move in keeps:
        move.wait()


def call_forward(*arrays):
    out = jax.ShapeDtypeStruct
    return pl.pallas_call(
        forward,
        name="forward",
        out_shape=(
            out((TOK, 1024), F32),
            out((TOK, D), BF16),
            out((TOK, HERE), BF16),
            out((TOK, HERE), F32),
            out((2, CHUNKS + 1, 128, 128), F32),
            out((TOK, HERE), F32),
            out((1, HERE), F32),
            out((D, 1024), BF16),
            out((HERE, D), BF16),
            out((TOK, D), BF16),
            out((ROWS, D), F32),
            out((FFH, D), BF16),
            out((FFH, D), BF16),
            out((FFH, D), BF16),
        ),
        in_specs=[VM] * 8 + [SM, SM] + [VM] * 5,
        out_specs=(VM, HB, VM, VM, VM, VM, VM, HB, HB, HB, VM, HB, HB, HB),
        scratch_shapes=[
            pltpu.VMEM((TOK, D), BF16),
            pltpu.VMEM((D, 1024), BF16),
            pltpu.VMEM((HERE, D), BF16),
            *[pltpu.VMEM((FFH, D), BF16)] * 3,
            *[pltpu.VMEM((TOK, D), BF16)] * 3,
            pltpu.VMEM((2, CHUNKS, 128, 128), F32),
            pltpu.VMEM((CHUNKS, 8, HERE), F32),
            pltpu.VMEM((2, 128, 128), F32),
            *exchange_scratch(),
            *eight(),
            *eight(),
            *gather_semaphores(),
            *gather_semaphores(),
            *gather_semaphores(),
            *gather_semaphores(),
            *gather_semaphores(),
            pltpu.SemaphoreType.DMA((7,)),
        ],
        compiler_params=pltpu.CompilerParams(
            collective_id=0, has_side_effects=True, vmem_limit_bytes=58 * 1024 * 1024
        ),
    )(*arrays)


def backward(
    hn_in, dy_in, wg_in, wu_in, wd_in, resid, ffn_gain, wt, raw_in, run, mixed, states, gated, xn_in, w_in, hid,
    total, gain, group_gain, lb, layer, seq,
    block_out, grad_in, out_query, out_forget, out_input, out_outgate, out_output, out_bounds,
    out_norm, out_group, out_ffn, out_mean, out_gate, out_up, out_down,
    hn, dy, wg, wu, wd, hidden, dg, du, hidden_t, dg_t, du_t, gated_t, ps, slots, db, d_resid, hid_rows, raw,
    draw, d_mixed, d_query, d_keys, d_values, back_update, decay, incoming, vec,
    norm_terms, ffn_terms, group_total, bound_total,
    msg, sib, slots3, give, take, ex_send, ex_recv, rs_s, rs_r, ag_s, ag_r, rs1_s, rs1_r, rs2_s, rs2_r,
    a0, a1, a2, a3, a4, a5, a6, b0, b1, b2, b3, b4, b5, b6, c0, c1, c2, c3, c4, c5, c6,
    e0, e1, e2, e3, e4, e5, e6, f3, f4, f5, f6, g3, g4, g5, g6,
    t0, t1, t2, t3, t4, t5, t6, t7, t8, t9, local_sem,
):
    def load(source, to, k):
        move = pltpu.make_async_copy(source, to, local_sem.at[k])
        move.start()
        return move

    def quarter(ref, j):
        return ref.at[pl.ds(256 * j, 256), :]

    def place(ref, j):
        row, column = lax.rem(j, 2) * 256, lax.div(j, 2) * 1024
        return ref.at[pl.ds(pl.multiple_of(row, 256), 256), pl.ds(pl.multiple_of(column, 1024), 1024)]

    p = Spot()
    own = pl.multiple_of(p.head * ROWS, ROWS)
    loads = [load(one, full, k) for k, (one, full) in enumerate(((wg_in, wg), (hn_in, hn), (wu_in, wu), (wd_in, wd), (dy_in, dy)))]
    late = [load(hid.at[pl.ds(own, ROWS), :], hid_rows, 5), load(raw_in, raw, 6)]
    greet(p.chips() + [p.sibling] + p.heads())
    for move in loads:
        move.wait()
    for low, high in ((0, 256), (256, 512), (512, FFH)):
        gate = mm(hn[...], wg[low:high, :], NT)
        up = mm(hn[...], wu[low:high, :], NT)
        dh = mm(dy[...], wd[low:high, :], NT)
        s = sigmoid(gate)
        silu = gate * s
        hidden[:, low:high] = (silu * up).astype(BF16)
        dg[:, low:high] = (dh * up * slope(gate, s)).astype(BF16)
        du[:, low:high] = (dh * silu).astype(BF16)

    @pl.loop(0, 8)
    def _(j):
        columns = pl.ds(pl.multiple_of(j * 256, 256), 256)
        ps[:, columns] = (mm(dg[...], wg[:, columns], NN) + mm(du[...], wu[:, columns], NN)).astype(BF16)

    scatter = HeadSum(p, ps, slots, rs_s, rs_r)
    scatter.send()
    sums = [
        DpSum(p, FFH, a0, a1, a2, a3, a4, a5, a6),
        DpSum(p, FFH, b0, b1, b2, b3, b4, b5, b6),
        DpSum(p, FFH, c0, c1, c2, c3, c4, c5, c6),
    ]
    dg_t[...] = dg[...].T
    products(dg_t, hn, a0)
    sums[0].to_sibling()
    du_t[...] = du[...].T
    products(du_t, hn, b0)
    sums[0].to_z()
    sums[1].to_sibling()
    hidden_t[...] = hidden[...].T
    products(hidden_t, dy, c0)
    sums[1].to_z()
    sums[2].to_sibling()

    @pl.loop(0, 8)
    def _(j):
        columns = pl.ds(pl.multiple_of(j * 256, 256), 256)
        wu[0:TOK, columns] = mm(hidden[...], wd[:, columns], NN).astype(BF16)

    sums[2].to_z()
    late.append(load(xn_in, hn, 7))
    late += [load(quarter(w_in, j), place(wd, j), 8 + j) for j in range(4)]
    scatter.collect()
    ffn_terms[...] = jnp.zeros_like(ffn_terms)

    @pl.loop(0, 4)
    def _(i):
        rows = pl.ds(pl.multiple_of(i * 16, 16), 16)
        here = pl.ds(pl.multiple_of(own + i * 16, 16), 16)
        grad, x = scatter.rows(i * 16, 16), resid[rows, :]
        inverse = lax.rsqrt(jnp.mean(x * x, axis=-1, keepdims=True) + EPS)
        scaled, normed = grad * ffn_gain[...], x * inverse
        back = inverse * (scaled - normed * jnp.mean(scaled * normed, axis=-1, keepdims=True))
        ffn_terms[...] += jnp.sum(grad * normed, axis=0, keepdims=True)
        both = dy[here, :].astype(F32) + back
        d_resid[rows, :] = both
        db[here, :] = both.astype(BF16)

    spread = HeadGather(p, db, ag_s, ag_r)
    spread.send()
    late += [load(quarter(w_in, 4 + j), place(dy, j), 12 + j) for j in range(4)]
    segments = Segments(p, seq)
    soft, picked, bound = lower_bound(lb, layer[0])
    group_total[...] = jnp.zeros_like(group_total)
    scatter.finish()
    gated_t[...] = gated[...].T
    for move in late:
        move.wait()
    spread.collect()
    scatter1 = HeadSum(p, wu, wg, rs1_s, rs1_r)
    scatter1.send()

    @pl.loop(0, CHUNKS)
    def _(c):
        rows = pl.ds(pl.multiple_of(c * CHUNK, CHUNK), CHUNK)
        d_gated = mm(db[rows, :], wt[...], NT)
        before, final = segments.before(c), segments.final(c)
        carried = jnp.where(segments.column(c) == before, 1.0, 0.0)
        running = run[rows, :]
        rate = jnp.exp(running[127:128]) * jnp.where(final == before, 1.0, 0.0)
        decay[c] = jnp.broadcast_to(rate, (8, HERE))
        for h in range(2):
            lanes = slice(h * 128, (h + 1) * 128)
            x, grad = mixed[rows, lanes], d_gated[:, lanes]
            gate = raw[rows, 768 + h * 128 : 768 + (h + 1) * 128]
            s = sigmoid(gate)
            inverse = lax.rsqrt(jnp.mean(x * x, axis=-1, keepdims=True) + EPS)
            normed = x * inverse
            draw[rows, 768 + h * 128 : 768 + (h + 1) * 128] = (
                grad * (normed * group_gain[...]) * slope(gate, s)
            ).astype(BF16)
            inner = grad * (gate * s)
            scaled = inner * group_gain[...]
            back = inverse * (scaled - normed * jnp.mean(scaled * normed, axis=-1, keepdims=True))
            group_total[...] += jnp.sum(inner * normed, axis=0, keepdims=True)
            back = back.astype(BF16)
            d_mixed[rows, lanes] = back
            query_raw = raw[rows, lanes]
            query = (query_raw * sigmoid(query_raw)).astype(BF16).astype(F32)
            high, low = halves(query * jnp.exp(running[:, lanes]) * carried)
            back_update[h, c] = mm(back, high, TN) + mm(back, low, TN)

    for h in range(2):
        lanes = slice(h * 128, (h + 1) * 128)
        state, rate = back_update[h, CHUNKS - 1], decay[CHUNKS - 1, 0:1, lanes]
        for c in range(CHUNKS - 2, -1, -1):
            state = state * decay[c, 0:1, lanes] + back_update[h, c]
            rate = rate * decay[c, 0:1, lanes]
        msg[h, 0:128, :] = state
        msg[h, 128:136, :] = jnp.broadcast_to(rate, (8, 128))
    exchange = Exchange(p, msg, sib, slots3, give, take, ex_send, ex_recv, True)
    exchange.to_sibling()
    results = (out_gate, out_up, out_down)
    for one, out in zip(sums, results):
        one.to_x(write(out))
    exchange.to_chips()

    @pl.loop(0, CHUNKS)
    def _(c):
        rows = pl.ds(pl.multiple_of(c * CHUNK, CHUNK), CHUNK)
        running = run[rows, :]
        middle = running[63:64]
        _, _, query, keys, values = gates(raw, bound, rows)
        up, down_ = jnp.exp(running - middle), jnp.exp(middle - running)
        lifted = query.astype(F32) * up
        lowered = keys.astype(F32) * down_
        column, row = segments.column(c), segments.row(c)
        carried = jnp.where(column == segments.before(c), 1.0, 0.0)
        linked = (column == row) & (
            lax.broadcasted_iota(jnp.int32, (CHUNK, CHUNK), 0)
            >= lax.broadcasted_iota(jnp.int32, (CHUNK, CHUNK), 1)
        )
        for h in range(2):
            lanes = slice(h * 128, (h + 1) * 128)
            lift, lower = halves(lifted[:, lanes]), halves(lowered[:, lanes])
            scores = halves(jnp.where(linked, mm3(lift, lower, NT), 0.0))
            grad = d_mixed[rows, lanes]
            d_scores = halves(jnp.where(linked, mm(grad, values[:, lanes], NT), 0.0))
            d_values[rows, lanes] = mm(scores[0], grad, TN) + mm(scores[1], grad, TN)
            state = halves(states[h, c])
            outer = mm(grad, state[0], NN) + mm(grad, state[1], NN)
            d_query[rows, lanes] = mm3(d_scores, lower, NN) * up[:, lanes] + outer * jnp.exp(running[:, lanes]) * carried
            d_keys[rows, lanes] = mm3(d_scores, lift, TN) * down_[:, lanes]

    for one, out in zip(sums, results):
        one.end(accumulate(out))
    third = DpSum(p, HERE, e0, e1, e2, e3, e4, e5, e6)
    products(gated_t, db, e0)
    third.to_sibling()
    exchange.result(incoming)
    third.to_z()
    bound_total[...] = jnp.zeros_like(bound_total)

    @pl.loop(0, CHUNKS)
    def _(i):
        c = CHUNKS - 1 - i
        rows = pl.ds(pl.multiple_of(c * CHUNK, CHUNK), CHUNK)
        running = run[rows, :]
        logistic, forget, query, keys, values = gates(raw, bound, rows)
        keys = keys.astype(F32)
        fade = jnp.exp(running[127:128] - running)
        column, final = segments.column(c), segments.final(c)
        ends = jnp.where(column == final, 1.0, 0.0)
        for h in range(2):
            lanes = slice(h * 128, (h + 1) * 128)
            state = incoming[h]
            pair = halves(state)
            tail = halves(keys[:, lanes] * fade[:, lanes] * ends)
            value_grad = d_values[rows, lanes] + mm3(tail, pair, NT)
            draw[rows, 512 + h * 128 : 512 + (h + 1) * 128] = value_grad.astype(BF16)
            lift = mm(values[:, lanes], pair[0], NN) + mm(values[:, lanes], pair[1], NN)
            key_grad = d_keys[rows, lanes] + lift * fade[:, lanes] * ends
            at_end = jnp.sum(states[h, c + 1] * state, axis=0, keepdims=True)
            query_grad = d_query[rows, lanes]
            step = query[:, lanes].astype(F32) * query_grad - keys[:, lanes] * key_grad
            log_grad = summed_rows(False, step) + at_end
            forget_grad = log_grad / forget[:, lanes] - key_grad
            rest = 1.0 - logistic[:, lanes]
            draw[rows, 256 + h * 128 : 256 + (h + 1) * 128] = (
                forget_grad * (1.0 - bound[:, lanes]) * logistic[:, lanes] * rest
            ).astype(BF16)
            bound_total[:, lanes] += jnp.sum(forget_grad * rest, axis=0, keepdims=True)
            query_raw = raw[rows, lanes]
            draw[rows, lanes] = (query_grad * slope(query_raw, sigmoid(query_raw))).astype(BF16)
            incoming[h] = state * decay[c, 0:1, lanes] + back_update[h, c]

    for first_column, part in ((0, wd), (1024, dy)):

        @pl.loop(0, 4)
        def _(j):
            columns = pl.ds(pl.multiple_of(first_column + j * 256, 256), 256)
            ps[:, columns] = mm(draw[...], place(part, j)[...], NT).astype(BF16)

    scatter2 = HeadSum(p, ps, slots, rs2_s, rs2_r)
    scatter2.send()
    for one in sums:
        one.finish()
    first = DpSum(p, 512, a0, a1, a2, f3, f4, f5, f6)
    second = DpSum(p, 512, b0, b1, b2, g3, g4, g5, g6)
    products_turned(hn, draw.at[:, 0:512], a0)
    first.to_sibling()
    products_turned(hn, draw.at[:, 512:1024], b0)
    first.to_z()
    second.to_sibling()
    scatter1.collect()

    @pl.loop(0, 4)
    def _(i):
        rows = pl.ds(pl.multiple_of(i * 16, 16), 16)
        block_out[rows, :] = (resid[rows, :] + scatter1.rows(i * 16, 16)).astype(BF16)

    second.to_z()
    third.to_x(write(out_output))
    scatter2.collect()
    norm_terms[...] = jnp.zeros_like(norm_terms)

    @pl.loop(0, 4)
    def _(i):
        rows = pl.ds(pl.multiple_of(i * 16, 16), 16)
        grad, x = scatter2.rows(i * 16, 16), hid_rows[rows, :].astype(F32)
        inverse = lax.rsqrt(jnp.mean(x * x, axis=-1, keepdims=True) + EPS)
        scaled, normed = grad * gain[...], x * inverse
        back = inverse * (scaled - normed * jnp.mean(scaled * normed, axis=-1, keepdims=True))
        norm_terms[...] += jnp.sum(grad * normed, axis=0, keepdims=True)
        grad_in[rows, :] = d_resid[rows, :] + back

    vec[...] = jnp.zeros_like(vec)
    for i in range(16):
        vec[i : i + 1, :] = norm_terms[:, i * 128 : (i + 1) * 128]
        vec[16 + i : 17 + i, :] = ffn_terms[:, i * 128 : (i + 1) * 128]
    vec[32:33, :] = group_total[...]
    vec[33:34, :] = total[:, 0:128] + total[:, 128:256]
    vec[34:35, :] = bound_total[:, 0:128]
    vec[35:36, :] = bound_total[:, 128:256]
    everywhere = Total(p, vec, t0, t1, t2, t3, t4, t5, t6, t7, t8.at[0], t9.at[0])
    everywhere.send()
    third.end(accumulate(out_output))
    everywhere.middle()

    def put_first(x):
        out_query[:, 0:128], out_query[:, 128:256] = x[0:128], x[128:256]
        out_forget[:, 0:128], out_forget[:, 128:256] = x[256:384], x[384:512]

    def put_second(x):
        out_input[:, 0:128], out_input[:, 128:256] = x[0:128], x[128:256]
        out_outgate[:, 0:128], out_outgate[:, 128:256] = x[256:384], x[384:512]

    def add_to(low, high):
        def add(x):
            low[:, 0:128] += x[0:128]
            low[:, 128:256] += x[128:256]
            high[:, 0:128] += x[256:384]
            high[:, 128:256] += x[384:512]

        return add

    first.to_x(put_first)
    second.to_x(put_second)
    all_of = everywhere.result()
    out_norm[...] = all_of[0:16]
    out_ffn[...] = all_of[16:32]
    out_group[...] = all_of[32:33]
    mean = jnp.sum(all_of[33:34], axis=-1, keepdims=True) / float(8192 * D)
    out_mean[...] = jnp.broadcast_to(mean, (1, 128))
    for h in range(2):
        lanes = slice(h * 128, (h + 1) * 128)
        out_bounds[:, lanes] = soft[:, lanes] * (picked[:, lanes] - bound[:, lanes]) * all_of[34 + h : 35 + h]
    first.end(add_to(out_query, out_forget))
    second.end(add_to(out_input, out_outgate))
    spread.finish()
    scatter1.finish()
    scatter2.finish()
    exchange.finish()
    everywhere.finish()
    for one in (first, second, third):
        one.finish()


OUTS = (
    ((ROWS, D), BF16),
    ((ROWS, D), F32),
    ((128, HERE), F32),
    ((128, HERE), F32),
    ((128, HERE), F32),
    ((128, HERE), F32),
    ((HERE, 128), F32),
    ((24, HERE), F32),
    ((16, 128), F32),
    ((1, KDIM), F32),
    ((16, 128), F32),
    ((1, 128), F32),
    ((FFH, 128), F32),
    ((FFH, 128), F32),
    ((FFH, 128), F32),
)


def call_backward(*arrays):
    sums = dp_sum_scratch(FFH)
    again = [pltpu.VMEM((512, 128), BF16)] * 2 + eight()
    return pl.pallas_call(
        backward,
        name="backward",
        out_shape=[jax.ShapeDtypeStruct(*one) for one in OUTS],
        in_specs=[HB, HB, HB, HB, HB, VM, VM, VM, HB, VM, VM, VM, VM, HB, HB, HB, VM, VM, VM, VM, SM, SM],
        out_specs=[VM] * len(OUTS),
        scratch_shapes=[
            *[pltpu.VMEM((TOK, D), BF16)] * 2,
            *[pltpu.VMEM((FFH, D), BF16)] * 3,
            *[pltpu.VMEM((TOK, FFH), BF16)] * 3,
            *[pltpu.VMEM((FFH, TOK), BF16)] * 3,
            pltpu.VMEM((HERE, TOK), BF16),
            *[pltpu.VMEM((TOK, D), BF16)] * 3,
            pltpu.VMEM((ROWS, D), F32),
            pltpu.VMEM((ROWS, D), BF16),
            pltpu.VMEM((TOK, 1024), F32),
            pltpu.VMEM((TOK, 1024), BF16),
            pltpu.VMEM((TOK, HERE), BF16),
            *[pltpu.VMEM((TOK, HERE), F32)] * 3,
            pltpu.VMEM((2, CHUNKS, 128, 128), F32),
            pltpu.VMEM((CHUNKS, 8, HERE), F32),
            pltpu.VMEM((2, 128, 128), F32),
            pltpu.VMEM((VEC, 128), F32),
            pltpu.VMEM((1, D), F32),
            pltpu.VMEM((1, D), F32),
            pltpu.VMEM((1, 128), F32),
            pltpu.VMEM((1, HERE), F32),
            *exchange_scratch(),
            *eight(),
            *eight(),
            *eight(),
            *eight(),
            *sums,
            *sums,
            *sums,
            *dp_sum_scratch(HERE),
            *again,
            *again,
            pltpu.VMEM((8, VEC, 128), F32),
            pltpu.VMEM((8, VEC, 128), F32),
            pltpu.VMEM((VEC, 128), F32),
            pltpu.VMEM((VEC, 128), F32),
            *eight(),
            *eight(),
            pltpu.SemaphoreType.DMA((1,)),
            pltpu.SemaphoreType.DMA((1,)),
            pltpu.SemaphoreType.DMA((16,)),
        ],
        compiler_params=pltpu.CompilerParams(
            collective_id=1, has_side_effects=True, vmem_limit_bytes=60 * 1024 * 1024
        ),
    )(*arrays)


def results(*refs):
    half = len(refs) // 2
    for one, out in zip(refs[:half], refs[half:]):
        out[...] = one[...]


def call_results(arrays):
    return pl.pallas_call(
        results,
        name="results",
        out_shape=[jax.ShapeDtypeStruct(*one) for one in OUTS],
        in_specs=[VM] * len(OUTS),
        out_specs=[VM] * len(OUTS),
    )(*arrays)


def local(
    hidden_in, norm_gain, w_query, w_forget, w_input, w_outgate, lower_bounds, layer_index, group_gain,
    w_output, ffn_gain, w_gate, w_up, w_down, seq_lengths, grad_out,
):
    norm_row, ffn_row, group_row = norm_gain.reshape(1, D), ffn_gain.reshape(1, D), group_gain.reshape(1, KDIM)
    raw, xn, gated, mixed, states, run, total, w_all, wt_all, hn, resid, wg, wu, wd = call_forward(
        hidden_in, norm_row, w_query, w_forget, w_input, w_outgate, w_output, lower_bounds, layer_index, seq_lengths,
        group_row, ffn_row, w_gate.T, w_up.T, w_down,
    )
    (
        block_out, grad_in, grad_query, grad_forget, grad_input, grad_outgate, grad_output, grad_bounds,
        grad_norm, grad_group, grad_ffn, mean, grad_gate, grad_up, grad_down,
    ) = call_results(call_backward(
        hn, grad_out, wg, wu, wd, resid, ffn_row, wt_all, raw, run, mixed, states, gated, xn, w_all, hidden_in,
        total, norm_row, group_row, lower_bounds, layer_index, seq_lengths,
    ))
    return (
        block_out,
        grad_in,
        grad_norm.reshape(D),
        grad_query,
        grad_forget,
        grad_input,
        grad_outgate,
        grad_bounds,
        grad_group.reshape(KDIM),
        grad_output,
        grad_ffn.reshape(D),
        grad_gate.T,
        grad_up.T,
        grad_down,
        mean[0, 0:1],
    )


def solution(mesh):
    return jax.shard_map(
        local,
        mesh=mesh,
        in_specs=(
            P("dp", None),
            P(),
            P("dp", "head"),
            P("dp", "head"),
            P("dp", "head"),
            P("dp", "head"),
            P(None, "head"),
            P(),
            P(),
            P("head", "dp"),
            P(),
            P("dp", "head"),
            P("dp", "head"),
            P("head", "dp"),
            P(),
            P("dp", None),
        ),
        out_specs=(
            P(("dp", "head"), None),
            P(("dp", "head"), None),
            P(),
            P("dp", "head"),
            P("dp", "head"),
            P("dp", "head"),
            P("dp", "head"),
            P(None, "head"),
            P(),
            P("head", "dp"),
            P(),
            P("dp", "head"),
            P("dp", "head"),
            P("head", "dp"),
            P(),
        ),
        check_vma=False,
    )
```

```python
from functools import partial

import jax
import jax.numpy as jnp
from jax import lax
from jax.experimental import pallas as pl
from jax.experimental.pallas import tpu as pltpu
from jax.sharding import PartitionSpec as P

D = 2048
KDIM = 128
CHUNK = 128
TOK = 512
CHUNKS = TOK // CHUNK
HERE = 256
FFH = 704
NSEQ = 12
NHEAD = 8
ROWS = TOK // NHEAD
EPS = 1e-06
F32 = jnp.float32
BF16 = jnp.bfloat16
MESH = pl.DeviceIdType.MESH
VM = pl.BlockSpec(memory_space=pltpu.VMEM)
SM = pl.BlockSpec(memory_space=pltpu.SMEM)
HB = pl.BlockSpec(memory_space=pl.ANY)


class Spot:
    def __init__(self):
        self.dp = lax.axis_index("dp")
        self.head = lax.axis_index("head")
        self.core = lax.rem(self.dp, 2)
        self.chip = lax.div(self.dp, 2)
        self.xh = lax.rem(self.chip, 2)
        self.z = lax.div(self.chip, 2)
        self.xl = lax.rem(self.head, 2)
        self.y = lax.div(self.head, 2)

    def at(self, dz, xh, core):
        return (lax.rem(self.z + dz, 4) * 2 + xh) * 2 + core

    def y_at(self, k):
        return lax.rem(self.y + k, 4)

    @property
    def beside(self):
        return {"head": self.y * 2 + 1 - self.xl}

    def lines(self):
        return [self.beside] + [{"head": self.y_at(k) * 2 + self.xl} for k in (1, 2, 3)]

    @property
    def sibling(self):
        return {"dp": self.chip * 2 + 1 - self.core}

    def chips(self):
        return [{"dp": lax.rem(self.chip + k, 8) * 2 + self.core} for k in range(1, 8)]

    def heads(self):
        return [{"head": lax.rem(self.head + k, NHEAD)} for k in range(1, NHEAD)]


def greet(ids):
    barrier = pltpu.get_barrier_semaphore()
    for one in ids:
        pl.semaphore_signal(barrier, inc=1, device_id=one, device_id_type=MESH)
    pl.semaphore_wait(barrier, len(ids))


def rcopy(src, dst, send, recv, where):
    return pltpu.make_async_remote_copy(
        src_ref=src, dst_ref=dst, send_sem=send, recv_sem=recv, device_id=where, device_id_type=MESH
    )


GATHER_SENDS = 17


class Gather:
    def __init__(self, spot, g, send, recv, half, columns=0):
        self.spot, self.g, self.s, self.r, self.h = spot, g, send, recv, half
        self.columns, self.middle = columns, (columns or 128) // 2

    def block(self, d, start=0, rows=0):
        if self.columns:
            rows = rows or self.columns
            return self.g.at[pl.ds(start, rows), pl.ds(pl.multiple_of(d * 128, 128), 128)]
        return self.g.at[pl.ds(pl.multiple_of(d * 128 + start, 64), rows or 128), :]

    def push(self, d, to, k):
        rcopy(self.block(d), self.block(d), self.s.at[k], self.r.at[d], {"dp": to}).start()

    def push_half(self, d, to, k, xh, part):
        b = self.block(d, part * self.middle, self.middle)
        rcopy(b, b, self.s.at[k], self.h.at[2 * xh + part], {"dp": to}).start()

    def arrived(self, d):
        b = self.block(d)
        rcopy(b, b, self.s.at[0], self.r.at[d], self.spot.sibling).wait_recv()

    def arrived_halves(self, d, xh):
        for part in range(2):
            b = self.block(d, part * self.middle, self.middle)
            rcopy(b, b, self.s.at[0], self.h.at[2 * xh + part], self.spot.sibling).wait_recv()

    def first(self):
        p = self.spot
        self.push(p.dp, p.at(0, 1 - p.xh, p.core), 0)
        self.push(p.dp, p.at(1, p.xh, p.core), 1)
        self.push(p.dp, p.at(3, p.xh, p.core), 2)
        self.push(p.dp, p.at(0, p.xh, 1 - p.core), 3)

    def second(self):
        p = self.spot
        b = p.at(0, 1 - p.xh, p.core)
        self.arrived(b)
        self.push(b, p.at(1, p.xh, p.core), 4)
        self.push(b, p.at(3, p.xh, p.core), 5)
        self.push(b, p.at(0, p.xh, 1 - p.core), 6)

    def third(self):
        p = self.spot
        for i, h in enumerate((p.xh, 1 - p.xh)):
            b = p.at(3, h, p.core)
            self.arrived(b)
            self.push_half(b, p.at(1, p.xh, p.core), 7 + i, h, 0)
            self.push(b, p.at(0, p.xh, 1 - p.core), 9 + i)
            b = p.at(1, h, p.core)
            self.arrived(b)
            self.push_half(b, p.at(3, p.xh, p.core), 11 + i, h, 1)
            self.push(b, p.at(0, p.xh, 1 - p.core), 13 + i)

    def fourth(self):
        p = self.spot
        for i, h in enumerate((p.xh, 1 - p.xh)):
            b = p.at(2, h, p.core)
            self.arrived_halves(b, h)
            self.push(b, p.at(0, p.xh, 1 - p.core), 15 + i)

    def last(self):
        p = self.spot
        for dz in range(4):
            for h in range(2):
                self.arrived(p.at(dz, h, 1 - p.core))
        half = self.block(0, 0, self.middle)
        for k in range(GATHER_SENDS):
            b = half if k in (7, 8, 11, 12) else self.block(0)
            rcopy(b, b, self.s.at[k], self.r.at[0], p.sibling).wait_send()


def gather_semaphores():
    return [
        pltpu.SemaphoreType.DMA((GATHER_SENDS,)),
        pltpu.SemaphoreType.DMA((16,)),
        pltpu.SemaphoreType.DMA((4,)),
    ]


NN = (((1,), (0,)), ((), ()))
NT = (((1,), (1,)), ((), ()))
TN = (((0,), (0,)), ((), ()))


def mm(a, b, dims):
    return lax.dot_general(a, b, dims, preferred_element_type=F32)


def halves(a):
    high = a.astype(BF16)
    return high, (a - high.astype(F32)).astype(BF16)


def mm2(a, b, dims):
    return mm(a[0], b, dims) + mm(a[1], b, dims)


def mm3(a, b, dims):
    return mm(a[0], b[0], dims) + (mm(a[0], b[1], dims) + mm(a[1], b[0], dims))


def triangle(lower):
    rows = lax.broadcasted_iota(jnp.int32, (CHUNK, CHUNK), 0)
    columns = lax.broadcasted_iota(jnp.int32, (CHUNK, CHUNK), 1)
    return (rows >= columns if lower else rows <= columns).astype(BF16)


def summed_rows(lower, x):
    high = x.astype(BF16)
    rest = x - high.astype(F32)
    middle = rest.astype(BF16)
    low = (rest - middle.astype(F32)).astype(BF16)
    t = triangle(lower)
    return mm(t, high, NN) + (mm(t, middle, NN) + mm(t, low, NN))


class Segments:
    def __init__(self, spot, seq):
        self.starts = []
        total = jnp.int32(0)
        for i in range(NSEQ):
            self.starts.append(total)
            total = total + seq[i]
        self.first = spot.dp * TOK

    def of(self, position):
        found = jnp.where(position >= self.starts[0], 1, 0)
        for s in self.starts[1:]:
            found = found + jnp.where(position >= s, 1, 0)
        return found - 1

    def column(self, c):
        return self.of(self.first + c * CHUNK + lax.broadcasted_iota(jnp.int32, (CHUNK, KDIM), 0))

    def row(self, c):
        return self.of(self.first + c * CHUNK + lax.broadcasted_iota(jnp.int32, (CHUNK, KDIM), 1))

    def before(self, c):
        return self.of(self.first + c * CHUNK - 1)

    def final(self, c):
        return self.of(self.first + (c + 1) * CHUNK - 1)


def lower_bound(lb, layer):
    x = lb[...]
    e = jnp.exp(x - jnp.max(x, axis=0, keepdims=True))
    soft = e / jnp.sum(e, axis=0, keepdims=True)
    depth = lax.broadcasted_iota(jnp.int32, x.shape, 0)
    picked = jnp.where((depth >= 1) & (depth <= layer), 1.0, 0.0)
    return soft, picked, jnp.sum(soft * picked, axis=0, keepdims=True)


def sigmoid(x):
    return lax.logistic(x)


def slope(x, s):
    return s * (1.0 + x * (1.0 - s))


class Exchange:
    def __init__(self, spot, msg, sib, slots, give, take, send, recv, backward):
        self.p, self.msg, self.sib, self.slots = spot, msg, sib, slots
        self.give, self.take, self.s, self.r, self.back = give, take, send, recv, backward

    def to_sibling(self):
        p = self.p
        rcopy(self.msg.at[1 - p.core], self.sib, self.s.at[7], self.r.at[8], p.sibling).start()

    def to_chips(self):
        p = self.p
        rcopy(self.sib, self.sib, self.s.at[7], self.r.at[8], p.sibling).wait_recv()
        mine, other = self.msg[p.core], self.sib[...]
        zero = p.core == 0
        one, two = jnp.where(zero, mine, other), jnp.where(zero, other, mine)
        near, far = (two, one) if self.back else (one, two)
        self.near = near
        state = near[0:128] * far[128:129] + far[0:128]
        self.slots[p.chip, 0:128, :] = state
        self.slots[p.chip, 128:136, :] = near[128:136] * far[128:136]
        for k, to in enumerate(p.chips()):
            rcopy(self.slots.at[p.chip], self.slots.at[p.chip], self.s.at[k], self.r.at[p.chip], to).start()

    def result(self, out):
        p = self.p
        for k in range(1, 8):
            chip = lax.rem(p.chip + k, 8)
            rcopy(self.slots.at[chip], self.slots.at[chip], self.s.at[0], self.r.at[chip], p.sibling).wait_recv()
        state = jnp.zeros((128, 128), F32)
        for k in range(7, 0, -1) if self.back else range(7):
            m = self.slots[k]
            after = state * m[128:129] + m[0:128]
            state = jnp.where(k > p.chip if self.back else k < p.chip, after, state)
        second = state * self.near[128:129] + self.near[0:128]
        is_first = p.core == (1 if self.back else 0)
        self.give[...] = jnp.where(is_first, second, state)
        move = rcopy(self.give, self.take, self.s.at[8], self.r.at[9], p.sibling)
        move.start()
        out[p.core] = jnp.where(is_first, state, second)
        move.wait_recv()
        out[1 - p.core] = self.take[...]

    def finish(self):
        p = self.p
        for k in range(7):
            rcopy(self.slots.at[0], self.slots.at[0], self.s.at[k], self.r.at[0], p.sibling).wait_send()
        rcopy(self.sib, self.sib, self.s.at[7], self.r.at[8], p.sibling).wait_send()
        rcopy(self.give, self.take, self.s.at[8], self.r.at[9], p.sibling).wait_send()


def exchange_scratch():
    return [
        pltpu.VMEM((2, 136, 128), F32),
        pltpu.VMEM((136, 128), F32),
        pltpu.VMEM((8, 136, 128), F32),
        pltpu.VMEM((128, 128), F32),
        pltpu.VMEM((128, 128), F32),
        pltpu.SemaphoreType.DMA((9,)),
        pltpu.SemaphoreType.DMA((10,)),
    ]


def gates(raw, bound, rows):
    query_raw = raw[rows, 0:256]
    logistic = sigmoid(raw[rows, 256:512])
    forget = bound + (1.0 - bound) * logistic
    query = (query_raw * sigmoid(query_raw)).astype(BF16)
    keys = (1.0 - forget).astype(BF16)
    values = raw[rows, 512:768].astype(BF16)
    return logistic, forget, query, keys, values


HALF = D // 2


class HeadSum:
    def __init__(self, spot, ps, slots, send, recv):
        self.p, self.ps, self.slots, self.s, self.r = spot, ps, slots, send, recv

    def left_of(self, start, rows=ROWS):
        return self.slots.at[pl.ds(start, rows), pl.ds(0, HALF)]

    def right_of(self, start, rows=ROWS):
        return self.slots.at[pl.ds(start, rows), pl.ds(HALF, HALF)]

    def part(self, h, rows, right):
        return self.ps.at[pl.ds(pl.multiple_of(h * ROWS, ROWS), rows), pl.ds(HALF if right else 0, HALF)]

    def left_x(self, k):
        p = self.p
        h = p.y_at(k) * 2 + 1 - p.xl
        return rcopy(self.part(h, ROWS, False), self.left_of(64 * k), self.s.at[k], self.r.at[k], p.beside)

    def left_y(self, k):
        p = self.p
        to = {"head": p.y_at(k) * 2 + p.xl}
        return rcopy(self.left_of(64 * k), self.left_of(192 + 64 * k), self.s.at[3 + k], self.r.at[3 + k], to)

    def right_y(self, k):
        p = self.p
        to = {"head": p.y_at(k) * 2 + p.xl}
        return rcopy(
            self.part(p.y_at(k) * 2, 128, True), self.right_of(128 * k - 128, 128), self.s.at[6 + k], self.r.at[6 + k], to
        )

    def right_x(self):
        return rcopy(self.right_of(384), self.right_of(448), self.s.at[10], self.r.at[10], self.p.beside)

    def send_left(self):
        for k in (2, 1, 3, 0):
            self.left_x(k).start()

    def send_right(self):
        for k in (2, 1, 3):
            self.right_y(k).start()

    def send(self):
        self.send_right()
        self.send_left()

    def middle(self):
        p = self.p
        for k in (2, 1, 3, 0):
            self.left_x(k).wait_recv()
            mine = self.part(p.y_at(k) * 2 + p.xl, ROWS, False)
            one = self.left_of(64 * k)
            one[...] = (one[...].astype(F32) + mine[...].astype(F32)).astype(BF16)
            if k:
                self.left_y(k).start()
        for k in (1, 3, 2):
            self.right_y(k).wait_recv()

        def total(xl):
            one = self.part(p.y * 2 + xl, ROWS, True)[...].astype(F32)
            for k in range(3):
                rows = pl.ds(pl.multiple_of(128 * k + xl * ROWS, ROWS), ROWS)
                one = one + self.slots[rows, HALF:].astype(F32)
            return one.astype(BF16)

        self.slots[384:448, HALF:] = total(1 - p.xl)
        self.right_x().start()
        self.slots[448:512, 0:HALF] = total(p.xl)

    def collect(self):
        for k in (1, 3, 2):
            self.left_y(k).wait_recv()
        self.right_x().wait_recv()

    def rows(self, start, count):
        def at(row, left):
            rows = pl.ds(pl.multiple_of(row + start, 16), count)
            return self.slots[rows, 0:HALF].astype(F32) if left else self.slots[rows, HALF:].astype(F32)

        left = (at(0, True) + at(256, True)) + (at(320, True) + at(384, True))
        return jnp.concatenate([left, at(448, True) + at(448, False)], axis=1)

    def finish(self):
        for k in range(4):
            self.left_x(k).wait_send()
        for k in (1, 2, 3):
            self.left_y(k).wait_send()
            self.right_y(k).wait_send()
        self.right_x().wait_send()


class LateHeadSum:
    def __init__(self, spot, ps, slots, send, recv):
        self.p, self.ps, self.slots, self.s, self.r = spot, ps, slots, send, recv

    def block(self, ref, start, rows=ROWS):
        return ref.at[pl.ds(pl.multiple_of(start, ROWS), rows), :]

    def along_y(self, k):
        p = self.p
        y = p.y_at(k)
        return rcopy(
            self.block(self.ps, y * 128, 128), self.block(self.slots, 128 * k - 128, 128),
            self.s.at[k], self.r.at[k], {"head": y * 2 + p.xl},
        )

    def along_x(self):
        return rcopy(self.block(self.slots, 384), self.block(self.slots, 448), self.s.at[0], self.r.at[0], self.p.beside)

    def send(self):
        for k in (2, 1, 3):
            self.along_y(k).start()

    def part(self, xl, start, count):
        p = self.p
        one = self.ps[pl.ds(pl.multiple_of((p.y * 2 + xl) * ROWS + start, 16), count), :].astype(F32)
        for k in range(3):
            rows = pl.ds(pl.multiple_of(128 * k + xl * ROWS + start, 16), count)
            one = one + self.slots[rows, :].astype(F32)
        return one

    def middle(self):
        for k in (1, 3, 2):
            self.along_y(k).wait_recv()

        @pl.loop(0, 4)
        def _(i):
            rows = pl.ds(pl.multiple_of(384 + i * 16, 16), 16)
            self.slots[rows, :] = self.part(1 - self.p.xl, i * 16, 16).astype(BF16)

        self.along_x().start()

    def collect(self):
        self.along_x().wait_recv()

    def rows(self, start, count):
        rows = pl.ds(pl.multiple_of(448 + start, 16), count)
        return self.part(self.p.xl, start, count) + self.slots[rows, :].astype(F32)

    def finish(self):
        for k in (1, 2, 3):
            self.along_y(k).wait_send()
        self.along_x().wait_send()


class HeadGather:
    def __init__(self, spot, full, send, recv):
        self.p, self.full, self.s, self.r = spot, full, send, recv

    def block(self, h, right):
        return self.full.at[pl.ds(pl.multiple_of(h * ROWS, ROWS), ROWS), pl.ds(HALF if right else 0, HALF)]

    def along_y(self, k, xl, right, i):
        p = self.p
        b = self.block(p.y * 2 + xl, right)
        return rcopy(b, b, self.s.at[i + k], self.r.at[i + k], {"head": p.y_at(k) * 2 + p.xl})

    def beside(self, k, right, i):
        p = self.p
        b = self.block(p.y_at(k) * 2 + p.xl, right)
        return rcopy(b, b, self.s.at[i + k], self.r.at[i + k], p.beside)

    def send(self):
        p = self.p
        self.beside(0, False, 0).start()
        for k in (2, 1, 3):
            self.along_y(k, p.xl, True, 0).start()
        self.beside(0, True, 4).start()
        for k in (2, 1, 3):
            self.along_y(k, p.xl, False, 8).start()

    def middle(self):
        p = self.p
        self.beside(0, False, 0).wait_recv()
        for k in (2, 1, 3):
            self.along_y(k, 1 - p.xl, False, 11).start()
        for k in (1, 3, 2):
            self.along_y(4 - k, p.xl, True, 0).wait_recv()
            self.beside(k, True, 4).start()

    def collect(self):
        p = self.p
        self.beside(0, True, 4).wait_recv()
        for k in (1, 3, 2):
            self.along_y(k, p.xl, False, 8).wait_recv()
            self.along_y(k, 1 - p.xl, False, 11).wait_recv()
            self.beside(k, True, 4).wait_recv()

    def finish(self):
        p = self.p
        self.beside(0, False, 0).wait_send()
        for k in range(4):
            self.beside(k, True, 4).wait_send()
        for k in (1, 2, 3):
            self.along_y(k, p.xl, True, 0).wait_send()
            self.along_y(k, p.xl, False, 8).wait_send()
            self.along_y(k, 1 - p.xl, False, 11).wait_send()


def sixteen():
    return [pltpu.SemaphoreType.DMA((16,)), pltpu.SemaphoreType.DMA((16,))]


def eight():
    return [pltpu.SemaphoreType.DMA((8,)), pltpu.SemaphoreType.DMA((8,))]


class DpSum:
    def __init__(self, spot, rows, gs, cr, zr, xs, xr, send, recv):
        n = pl.ds(0, rows)
        self.rows, self.p = rows, spot
        self.gs, self.cr, self.zr = gs.at[:, :, n, :], cr.at[:, n, :], zr.at[:, :, n, :]
        self.xs, self.xr, self.s, self.r = xs.at[n, :], xr.at[n, :], send, recv

    def pair(self, i):
        p = self.p
        two = pl.ds(2 * i, 2)
        return rcopy(self.gs.at[1 - p.core, two], self.cr.at[two], self.s.at[i], self.r.at[i], p.sibling)

    def to_sibling(self):
        for i in range(4):
            self.pair(i).start()

    def half(self, part):
        return pl.ds(part * (self.rows // 2), self.rows // 2)

    def along_z(self, d, block, part, slot, i):
        p = self.p
        z = lax.rem(p.z + block, 4)
        where = {"dp": (lax.rem(p.z + d, 4) * 2 + p.xh) * 2 + p.core}
        source = self.gs.at[p.core, pl.ds(z * 2, 2), self.half(part), :]
        return rcopy(source, self.zr.at[slot, :, self.half(part), :], self.s.at[4 + i], self.r.at[4 + i], where)

    def far(self, part):
        return self.along_z(3 if part else 1, 2, part, 2, part)

    def near(self, part):
        return self.along_z(3, 3, 0, 1, 2) if part else self.along_z(1, 1, 1, 0, 3)

    def joined(self, part):
        return self.along_z(3, 3, 1, 1, 4) if part else self.along_z(1, 1, 0, 0, 5)

    def to_z(self):
        p = self.p
        for i in range(4):
            self.pair(i).wait_recv()

        @pl.loop(0, 8)
        def _(k):
            self.gs[p.core, k] = (self.gs[p.core, k].astype(F32) + self.cr[k].astype(F32)).astype(BF16)

        for part in range(2):
            self.far(part).start()
        for part in range(2):
            self.near(part).start()

    def join(self):
        p = self.p
        for part in range(2):
            self.far(part).wait_recv()
            z = lax.rem(p.z + (3 if part else 1), 4)
            for h in range(2):
                mine = self.gs.at[p.core, z * 2 + h, self.half(part), :]
                other = self.zr.at[2, h, self.half(part), :]
                mine[...] = (mine[...].astype(F32) + other[...].astype(F32)).astype(BF16)
            self.joined(part).start()

    def last_move(self):
        p = self.p
        where = {"dp": (p.z * 2 + 1 - p.xh) * 2 + p.core}
        return rcopy(self.xs, self.xr, self.s.at[10], self.r.at[10], where)

    def to_x(self, put):
        p = self.p
        for part in range(2):
            self.near(part).wait_recv()
            self.joined(part).wait_recv()

        def total(h):
            one = self.gs[p.core, 2 * p.z + h].astype(F32)
            for i in range(2):
                one = one + self.zr[i, h].astype(F32)
            return one

        self.xs[...] = total(1 - p.xh).astype(BF16)
        self.last_move().start()
        put(total(p.xh))

    def end(self, add):
        self.last_move().wait_recv()
        add(self.xr[...].astype(F32))

    def finish(self):
        for i in range(4):
            self.pair(i).wait_send()
        for part in range(2):
            self.far(part).wait_send()
            self.near(part).wait_send()
            self.joined(part).wait_send()
        self.last_move().wait_send()


def dp_sum_scratch(rows):
    return [
        pltpu.VMEM((2, 8, rows, 128), BF16),
        pltpu.VMEM((8, rows, 128), BF16),
        pltpu.VMEM((3, 2, rows, 128), BF16),
        pltpu.VMEM((rows, 128), BF16),
        pltpu.VMEM((rows, 128), BF16),
        *sixteen(),
    ]


def products(left_turned, right, gs):
    @pl.loop(0, 8)
    def _(k):
        columns = pl.ds(pl.multiple_of(k * 256, 256), 256)
        both = mm(left_turned[...], right[:, columns], NN).astype(BF16)
        gs[0, k] = both[:, 0:128]
        gs[1, k] = both[:, 128:256]


def products_turned(left, right, gs):
    @pl.loop(0, 8)
    def _(k):
        columns = pl.ds(pl.multiple_of(k * 256, 256), 256)
        both = mm(left[:, columns], right[...], TN).astype(BF16)
        for q in range(4):
            gs[0, k, 128 * q : 128 * (q + 1), :] = both[0:128, 128 * q : 128 * (q + 1)]
            gs[1, k, 128 * q : 128 * (q + 1), :] = both[128:256, 128 * q : 128 * (q + 1)]


def write(ref):
    def put(x):
        ref[...] = x

    return put


def accumulate(ref):
    def add(x):
        ref[...] += x

    return add


VEC = 40


class Total:
    def __init__(self, spot, vec, h_slots, c_slots, own, other, h_s, h_r, c_s, c_r, k_s, k_r):
        self.p, self.vec, self.hs, self.cs, self.own, self.other = spot, vec, h_slots, c_slots, own, other
        self.h_s, self.h_r, self.c_s, self.c_r, self.k_s, self.k_r = h_s, h_r, c_s, c_r, k_s, k_r

    def send(self):
        p = self.p
        self.hs[p.head] = self.vec[...]
        for k in range(1, NHEAD):
            h = lax.rem(p.head + k, NHEAD)
            rcopy(self.hs.at[p.head], self.hs.at[p.head], self.h_s.at[k], self.h_r.at[p.head], {"head": h}).start()

    def middle(self):
        p = self.p
        for k in range(1, NHEAD):
            h = lax.rem(p.head + k, NHEAD)
            rcopy(self.hs.at[h], self.hs.at[h], self.h_s.at[0], self.h_r.at[h], p.sibling).wait_recv()
        total = self.hs[0]
        for h in range(1, NHEAD):
            total = total + self.hs[h]
        per_head = lax.broadcasted_iota(jnp.int32, (VEC, 128), 0) >= 34
        self.cs[p.chip] = jnp.where(per_head, self.vec[...], total)
        for k, to in enumerate(p.chips()):
            rcopy(self.cs.at[p.chip], self.cs.at[p.chip], self.c_s.at[k], self.c_r.at[p.chip], to).start()

    def result(self):
        p = self.p
        for k in range(1, 8):
            chip = lax.rem(p.chip + k, 8)
            rcopy(self.cs.at[chip], self.cs.at[chip], self.c_s.at[0], self.c_r.at[chip], p.sibling).wait_recv()
        total = self.cs[0]
        for k in range(1, 8):
            total = total + self.cs[k]
        self.own[...] = total
        move = rcopy(self.own, self.other, self.k_s, self.k_r, p.sibling)
        move.start()
        move.wait_recv()
        return total + self.other[...]

    def finish(self):
        p = self.p
        for k in range(1, NHEAD):
            rcopy(self.hs.at[0], self.hs.at[0], self.h_s.at[k], self.h_r.at[0], p.sibling).wait_send()
        for k in range(7):
            rcopy(self.cs.at[0], self.cs.at[0], self.c_s.at[k], self.c_r.at[0], p.sibling).wait_send()
        rcopy(self.own, self.other, self.k_s, self.k_r, p.sibling).wait_send()


def forward(
    hid, gain, wq, wf, wi, wo, w_output, lb, layer, seq, group_gain, ffn_gain, wg, wu, wd,
    raw, xn_out, gated, mixed, states, run, total, w_out, wt_out, hn_out, resid, wg_out, wu_out, wd_out,
    xn, w, wt, g0, g1, g2, hn, ps, slots, inner_update, decay, incoming,
    msg, sib, slots3, give, take, ex_send, ex_recv, rs_s, rs_r, ag_s, ag_r,
    ws, wr, wh, os, or_, oh, s0, r0, h0, s1, r1, h1, s2, r2, h2, local_sem,
):
    p = Spot()
    mine = pl.ds(pl.multiple_of(p.dp * 128, 128), 128)
    for k, one in enumerate((wq, wf, wi, wo)):
        w[mine, 256 * k : 256 * (k + 1)] = one[...]
    greet(p.chips() + [p.sibling] + p.lines())
    gather = Gather(p, w, ws, wr, wh)
    gather.first()
    wt[:, mine] = w_output[...]
    later = Gather(p, wt, os, or_, oh, HERE)
    for one, full in zip((wg, wu, wd), (g0, g1, g2)):
        full[:, mine] = one[...]
    gathers = [Gather(p, g0, s0, r0, h0, FFH), Gather(p, g1, s1, r1, h1, FFH), Gather(p, g2, s2, r2, h2, FFH)]

    @pl.loop(0, 8)
    def _(i):
        rows = pl.ds(pl.multiple_of(i * 64, 64), 64)
        x = hid[rows, :].astype(F32)
        scale = lax.rsqrt(jnp.mean(x * x, axis=-1, keepdims=True) + EPS)
        xn[rows, :] = (x * scale * gain[...]).astype(BF16)

    keeps = []

    def keep(source, out):
        move = pltpu.make_async_copy(source, out, local_sem.at[len(keeps)])
        move.start()
        keeps.append(move)

    keep(xn, xn_out)
    gather.second()
    gather.third()
    gather.fourth()
    later.first()
    gathers[0].first()
    gather.last()
    keep(w, w_out)

    @pl.loop(0, 4)
    def _(j):
        columns = pl.ds(pl.multiple_of(j * 256, 256), 256)
        raw[:, columns] = mm(xn[...], w[:, columns], NN)

    later.second()
    segments = Segments(p, seq)
    bound = lower_bound(lb, layer[0])[2]
    total[...] = jnp.zeros_like(total)

    @pl.loop(0, CHUNKS)
    def _(c):
        rows = pl.ds(pl.multiple_of(c * CHUNK, CHUNK), CHUNK)
        logistic, forget, query, keys, values = gates(raw, bound, rows)
        total[...] += jnp.sum(forget, axis=0, keepdims=True)
        running = summed_rows(True, jnp.log(forget))
        run[rows, :] = running
        middle, ending = running[63:64], running[127:128]
        lifted = query.astype(F32) * jnp.exp(running - middle)
        lowered = keys.astype(F32) * jnp.exp(middle - running)
        tail = keys.astype(F32) * jnp.exp(ending - running)
        column, row = segments.column(c), segments.row(c)
        linked = (column == row) & (
            lax.broadcasted_iota(jnp.int32, (CHUNK, CHUNK), 0)
            >= lax.broadcasted_iota(jnp.int32, (CHUNK, CHUNK), 1)
        )
        final = segments.final(c)
        rate = jnp.exp(ending) * jnp.where(final == segments.before(c), 1.0, 0.0)
        decay[c] = jnp.broadcast_to(rate, (8, HERE))
        ends = jnp.where(column == final, 1.0, 0.0)
        for h in range(2):
            lanes = slice(h * 128, (h + 1) * 128)
            scores = mm3(halves(lifted[:, lanes]), halves(lowered[:, lanes]), NT)
            scores = jnp.where(linked, scores, 0.0)
            mixed[rows, lanes] = mm2(halves(scores), values[:, lanes], NN)
            high, low = halves(tail[:, lanes] * ends)
            inner_update[h, c] = mm(values[:, lanes], high, TN) + mm(values[:, lanes], low, TN)

    for h in range(2):
        lanes = slice(h * 128, (h + 1) * 128)
        state, rate = inner_update[h, 0], decay[0, 0:1, lanes]
        for c in range(1, CHUNKS):
            state = state * decay[c, 0:1, lanes] + inner_update[h, c]
            rate = rate * decay[c, 0:1, lanes]
        msg[h, 0:128, :] = state
        msg[h, 128:136, :] = jnp.broadcast_to(rate, (8, 128))
    exchange = Exchange(p, msg, sib, slots3, give, take, ex_send, ex_recv, False)
    exchange.to_sibling()
    exchange.to_chips()
    later.third()
    gathers[1].first()
    gathers[2].first()
    gathers[0].second()
    later.fourth()
    exchange.result(incoming)
    for h in range(2):
        lanes = slice(h * 128, (h + 1) * 128)
        state = incoming[h]
        states[h, 0] = state
        for c in range(CHUNKS):
            state = state * decay[c, 0:1, lanes] + inner_update[h, c]
            states[h, c + 1] = state

    @pl.loop(0, CHUNKS)
    def _(c):
        rows = pl.ds(pl.multiple_of(c * CHUNK, CHUNK), CHUNK)
        carried = jnp.where(segments.column(c) == segments.before(c), 1.0, 0.0)
        for h in range(2):
            lanes = slice(h * 128, (h + 1) * 128)
            query_raw = raw[rows, h * 128 : (h + 1) * 128]
            query = (query_raw * sigmoid(query_raw)).astype(BF16).astype(F32)
            reach = query * jnp.exp(run[rows, lanes]) * carried
            x = mixed[rows, lanes] + mm3(halves(reach), halves(states[h, c]), NT)
            mixed[rows, lanes] = x
            scale = lax.rsqrt(jnp.mean(x * x, axis=-1, keepdims=True) + EPS)
            gate = raw[rows, 768 + h * 128 : 768 + (h + 1) * 128]
            gated[rows, lanes] = (x * scale * group_gain[...] * (gate * sigmoid(gate))).astype(BF16)

    gathers[1].second()
    gathers[2].second()
    later.last()
    keep(wt, wt_out)

    scatter = HeadSum(p, ps, slots, rs_s, rs_r)
    for start, send in ((HALF, scatter.send_right), (0, scatter.send_left)):

        @pl.loop(0, 4)
        def _(j):
            columns = pl.ds(pl.multiple_of(start + j * 256, 256), 256)
            ps[:, columns] = mm(gated[...], wt[:, columns], NN).astype(BF16)

        send()
    for g in gathers:
        g.third()
    scatter.middle()
    for g in gathers:
        g.fourth()
    scatter.collect()
    own = pl.multiple_of(p.head * ROWS, ROWS)

    @pl.loop(0, 4)
    def _(i):
        rows = pl.ds(pl.multiple_of(i * 16, 16), 16)
        here = pl.ds(pl.multiple_of(own + i * 16, 16), 16)
        x = hid[here, :].astype(F32) + scatter.rows(i * 16, 16)
        resid[rows, :] = x
        scale = lax.rsqrt(jnp.mean(x * x, axis=-1, keepdims=True) + EPS)
        hn[here, :] = (x * scale * ffn_gain[...]).astype(BF16)

    spread = HeadGather(p, hn, ag_s, ag_r)
    spread.send()
    spread.middle()
    for g, full, out in zip(gathers, (g0, g1, g2), (wg_out, wu_out, wd_out)):
        g.last()
        keep(full, out)
    exchange.finish()
    scatter.finish()
    spread.collect()
    keep(hn, hn_out)
    spread.finish()
    for move in keeps:
        move.wait()


def call_forward(*arrays):
    out = jax.ShapeDtypeStruct
    return pl.pallas_call(
        forward,
        name="forward",
        out_shape=(
            out((TOK, 1024), F32),
            out((TOK, D), BF16),
            out((TOK, HERE), BF16),
            out((TOK, HERE), F32),
            out((2, CHUNKS + 1, 128, 128), F32),
            out((TOK, HERE), F32),
            out((1, HERE), F32),
            out((D, 1024), BF16),
            out((HERE, D), BF16),
            out((TOK, D), BF16),
            out((ROWS, D), F32),
            out((FFH, D), BF16),
            out((FFH, D), BF16),
            out((FFH, D), BF16),
        ),
        in_specs=[VM] * 8 + [SM, SM] + [VM] * 5,
        out_specs=(VM, HB, VM, VM, VM, VM, VM, HB, HB, HB, VM, HB, HB, HB),
        scratch_shapes=[
            pltpu.VMEM((TOK, D), BF16),
            pltpu.VMEM((D, 1024), BF16),
            pltpu.VMEM((HERE, D), BF16),
            *[pltpu.VMEM((FFH, D), BF16)] * 3,
            *[pltpu.VMEM((TOK, D), BF16)] * 3,
            pltpu.VMEM((2, CHUNKS, 128, 128), F32),
            pltpu.VMEM((CHUNKS, 8, HERE), F32),
            pltpu.VMEM((2, 128, 128), F32),
            *exchange_scratch(),
            *sixteen(),
            *sixteen(),
            *gather_semaphores(),
            *gather_semaphores(),
            *gather_semaphores(),
            *gather_semaphores(),
            *gather_semaphores(),
            pltpu.SemaphoreType.DMA((7,)),
        ],
        compiler_params=pltpu.CompilerParams(
            collective_id=0, has_side_effects=True, vmem_limit_bytes=58 * 1024 * 1024
        ),
    )(*arrays)


def backward(
    hn_in, dy_in, wg_in, wu_in, wd_in, resid, ffn_gain, wt, raw_in, run, mixed, states, gated, xn_in, w_in, hid,
    total, gain, group_gain, lb, layer, seq,
    block_out, grad_in, out_query, out_forget, out_input, out_outgate, out_output, out_bounds,
    out_norm, out_group, out_ffn, out_mean, out_gate, out_up, out_down,
    hn, dy, wg, wu, wd, hidden, dg, du, hidden_t, dg_t, du_t, gated_t, ps, slots, db, d_resid, hid_rows, raw,
    draw, d_mixed, d_query, d_keys, d_values, back_update, decay, incoming, vec,
    norm_terms, ffn_terms, group_total, bound_total,
    msg, sib, slots3, give, take, ex_send, ex_recv, rs_s, rs_r, ag_s, ag_r, rs1_s, rs1_r, rs2_s, rs2_r,
    a0, a1, a2, a3, a4, a5, a6, b0, b1, b2, b3, b4, b5, b6, c0, c1, c2, c3, c4, c5, c6,
    e0, e1, e2, e3, e4, e5, e6, f3, f4, f5, f6, g3, g4, g5, g6,
    t0, t1, t2, t3, t4, t5, t6, t7, t8, t9, local_sem,
):
    def load(source, to, k):
        move = pltpu.make_async_copy(source, to, local_sem.at[k])
        move.start()
        return move

    def quarter(ref, j):
        return ref.at[pl.ds(256 * j, 256), :]

    def place(ref, j):
        row, column = lax.rem(j, 2) * 256, lax.div(j, 2) * 1024
        return ref.at[pl.ds(pl.multiple_of(row, 256), 256), pl.ds(pl.multiple_of(column, 1024), 1024)]

    p = Spot()
    own = pl.multiple_of(p.head * ROWS, ROWS)
    loads = [load(one, full, k) for k, (one, full) in enumerate(((wg_in, wg), (hn_in, hn), (wu_in, wu), (wd_in, wd), (dy_in, dy)))]
    late = [load(hid.at[pl.ds(own, ROWS), :], hid_rows, 5), load(raw_in, raw, 6)]
    greet(p.chips() + [p.sibling] + p.heads())
    for move in loads:
        move.wait()
    for low, high in ((0, 256), (256, 512), (512, FFH)):
        gate = mm(hn[...], wg[low:high, :], NT)
        up = mm(hn[...], wu[low:high, :], NT)
        dh = mm(dy[...], wd[low:high, :], NT)
        s = sigmoid(gate)
        silu = gate * s
        hidden[:, low:high] = (silu * up).astype(BF16)
        dg[:, low:high] = (dh * up * slope(gate, s)).astype(BF16)
        du[:, low:high] = (dh * silu).astype(BF16)

    scatter = HeadSum(p, ps, slots, rs_s, rs_r)
    for start, send in ((HALF, scatter.send_right), (0, scatter.send_left)):

        @pl.loop(0, 4)
        def _(j):
            columns = pl.ds(pl.multiple_of(start + j * 256, 256), 256)
            ps[:, columns] = (mm(dg[...], wg[:, columns], NN) + mm(du[...], wu[:, columns], NN)).astype(BF16)

        send()
    sums = [
        DpSum(p, FFH, a0, a1, a2, a3, a4, a5, a6),
        DpSum(p, FFH, b0, b1, b2, b3, b4, b5, b6),
        DpSum(p, FFH, c0, c1, c2, c3, c4, c5, c6),
    ]
    dg_t[...] = dg[...].T
    products(dg_t, hn, a0)
    sums[0].to_sibling()
    du_t[...] = du[...].T
    products(du_t, hn, b0)
    sums[0].to_z()
    sums[1].to_sibling()
    scatter.middle()
    hidden_t[...] = hidden[...].T
    products(hidden_t, dy, c0)
    sums[1].to_z()
    sums[2].to_sibling()
    sums[0].join()

    @pl.loop(0, 8)
    def _(j):
        columns = pl.ds(pl.multiple_of(j * 256, 256), 256)
        wu[0:TOK, columns] = mm(hidden[...], wd[:, columns], NN).astype(BF16)

    sums[2].to_z()
    late.append(load(xn_in, hn, 7))
    late += [load(quarter(w_in, j), place(wd, j), 8 + j) for j in range(4)]
    scatter.collect()
    ffn_terms[...] = jnp.zeros_like(ffn_terms)

    @pl.loop(0, 4)
    def _(i):
        rows = pl.ds(pl.multiple_of(i * 16, 16), 16)
        here = pl.ds(pl.multiple_of(own + i * 16, 16), 16)
        grad, x = scatter.rows(i * 16, 16), resid[rows, :]
        inverse = lax.rsqrt(jnp.mean(x * x, axis=-1, keepdims=True) + EPS)
        scaled, normed = grad * ffn_gain[...], x * inverse
        back = inverse * (scaled - normed * jnp.mean(scaled * normed, axis=-1, keepdims=True))
        ffn_terms[...] += jnp.sum(grad * normed, axis=0, keepdims=True)
        both = dy[here, :].astype(F32) + back
        d_resid[rows, :] = both
        db[here, :] = both.astype(BF16)

    scatter.finish()
    spread = HeadGather(p, db, ag_s, ag_r)
    spread.send()
    spread.middle()
    sums[1].join()
    late += [load(quarter(w_in, 4 + j), place(dy, j), 12 + j) for j in range(4)]
    segments = Segments(p, seq)
    soft, picked, bound = lower_bound(lb, layer[0])
    group_total[...] = jnp.zeros_like(group_total)
    gated_t[...] = gated[...].T
    for move in late:
        move.wait()
    sums[2].join()
    spread.collect()
    scatter1 = LateHeadSum(p, wu, wg, rs1_s, rs1_r)
    scatter1.send()

    @pl.loop(0, CHUNKS)
    def _(c):
        rows = pl.ds(pl.multiple_of(c * CHUNK, CHUNK), CHUNK)
        d_gated = mm(db[rows, :], wt[...], NT)
        before, final = segments.before(c), segments.final(c)
        carried = jnp.where(segments.column(c) == before, 1.0, 0.0)
        running = run[rows, :]
        rate = jnp.exp(running[127:128]) * jnp.where(final == before, 1.0, 0.0)
        decay[c] = jnp.broadcast_to(rate, (8, HERE))
        for h in range(2):
            lanes = slice(h * 128, (h + 1) * 128)
            x, grad = mixed[rows, lanes], d_gated[:, lanes]
            gate = raw[rows, 768 + h * 128 : 768 + (h + 1) * 128]
            s = sigmoid(gate)
            inverse = lax.rsqrt(jnp.mean(x * x, axis=-1, keepdims=True) + EPS)
            normed = x * inverse
            draw[rows, 768 + h * 128 : 768 + (h + 1) * 128] = (
                grad * (normed * group_gain[...]) * slope(gate, s)
            ).astype(BF16)
            inner = grad * (gate * s)
            scaled = inner * group_gain[...]
            back = inverse * (scaled - normed * jnp.mean(scaled * normed, axis=-1, keepdims=True))
            group_total[...] += jnp.sum(inner * normed, axis=0, keepdims=True)
            back = back.astype(BF16)
            d_mixed[rows, lanes] = back
            query_raw = raw[rows, lanes]
            query = (query_raw * sigmoid(query_raw)).astype(BF16).astype(F32)
            high, low = halves(query * jnp.exp(running[:, lanes]) * carried)
            back_update[h, c] = mm(back, high, TN) + mm(back, low, TN)

    for h in range(2):
        lanes = slice(h * 128, (h + 1) * 128)
        state, rate = back_update[h, CHUNKS - 1], decay[CHUNKS - 1, 0:1, lanes]
        for c in range(CHUNKS - 2, -1, -1):
            state = state * decay[c, 0:1, lanes] + back_update[h, c]
            rate = rate * decay[c, 0:1, lanes]
        msg[h, 0:128, :] = state
        msg[h, 128:136, :] = jnp.broadcast_to(rate, (8, 128))
    exchange = Exchange(p, msg, sib, slots3, give, take, ex_send, ex_recv, True)
    exchange.to_sibling()
    results = (out_gate, out_up, out_down)
    for one, out in zip(sums, results):
        one.to_x(write(out))
    exchange.to_chips()

    @pl.loop(0, CHUNKS)
    def _(c):
        rows = pl.ds(pl.multiple_of(c * CHUNK, CHUNK), CHUNK)
        running = run[rows, :]
        middle = running[63:64]
        _, _, query, keys, values = gates(raw, bound, rows)
        up, down_ = jnp.exp(running - middle), jnp.exp(middle - running)
        lifted = query.astype(F32) * up
        lowered = keys.astype(F32) * down_
        column, row = segments.column(c), segments.row(c)
        carried = jnp.where(column == segments.before(c), 1.0, 0.0)
        linked = (column == row) & (
            lax.broadcasted_iota(jnp.int32, (CHUNK, CHUNK), 0)
            >= lax.broadcasted_iota(jnp.int32, (CHUNK, CHUNK), 1)
        )
        for h in range(2):
            lanes = slice(h * 128, (h + 1) * 128)
            lift, lower = halves(lifted[:, lanes]), halves(lowered[:, lanes])
            scores = halves(jnp.where(linked, mm3(lift, lower, NT), 0.0))
            grad = d_mixed[rows, lanes]
            d_scores = halves(jnp.where(linked, mm(grad, values[:, lanes], NT), 0.0))
            d_values[rows, lanes] = mm(scores[0], grad, TN) + mm(scores[1], grad, TN)
            state = halves(states[h, c])
            outer = mm(grad, state[0], NN) + mm(grad, state[1], NN)
            d_query[rows, lanes] = mm3(d_scores, lower, NN) * up[:, lanes] + outer * jnp.exp(running[:, lanes]) * carried
            d_keys[rows, lanes] = mm3(d_scores, lift, TN) * down_[:, lanes]

    for one, out in zip(sums, results):
        one.end(accumulate(out))
    third = DpSum(p, HERE, e0, e1, e2, e3, e4, e5, e6)
    products(gated_t, db, e0)
    third.to_sibling()
    exchange.result(incoming)
    third.to_z()
    third.join()
    bound_total[...] = jnp.zeros_like(bound_total)

    @pl.loop(0, CHUNKS)
    def _(i):
        c = CHUNKS - 1 - i
        rows = pl.ds(pl.multiple_of(c * CHUNK, CHUNK), CHUNK)
        running = run[rows, :]
        logistic, forget, query, keys, values = gates(raw, bound, rows)
        keys = keys.astype(F32)
        fade = jnp.exp(running[127:128] - running)
        column, final = segments.column(c), segments.final(c)
        ends = jnp.where(column == final, 1.0, 0.0)
        for h in range(2):
            lanes = slice(h * 128, (h + 1) * 128)
            state = incoming[h]
            pair = halves(state)
            tail = halves(keys[:, lanes] * fade[:, lanes] * ends)
            value_grad = d_values[rows, lanes] + mm3(tail, pair, NT)
            draw[rows, 512 + h * 128 : 512 + (h + 1) * 128] = value_grad.astype(BF16)
            lift = mm(values[:, lanes], pair[0], NN) + mm(values[:, lanes], pair[1], NN)
            key_grad = d_keys[rows, lanes] + lift * fade[:, lanes] * ends
            at_end = jnp.sum(states[h, c + 1] * state, axis=0, keepdims=True)
            query_grad = d_query[rows, lanes]
            step = query[:, lanes].astype(F32) * query_grad - keys[:, lanes] * key_grad
            log_grad = summed_rows(False, step) + at_end
            forget_grad = log_grad / forget[:, lanes] - key_grad
            rest = 1.0 - logistic[:, lanes]
            draw[rows, 256 + h * 128 : 256 + (h + 1) * 128] = (
                forget_grad * (1.0 - bound[:, lanes]) * logistic[:, lanes] * rest
            ).astype(BF16)
            bound_total[:, lanes] += jnp.sum(forget_grad * rest, axis=0, keepdims=True)
            query_raw = raw[rows, lanes]
            draw[rows, lanes] = (query_grad * slope(query_raw, sigmoid(query_raw))).astype(BF16)
            incoming[h] = state * decay[c, 0:1, lanes] + back_update[h, c]

    scatter2 = HeadSum(p, ps, slots, rs2_s, rs2_r)
    for start, part, send in ((HALF, dy, scatter2.send_right), (0, wd, scatter2.send_left)):

        @pl.loop(0, 4)
        def _(j):
            columns = pl.ds(pl.multiple_of(start + j * 256, 256), 256)
            ps[:, columns] = mm(draw[...], place(part, j)[...], NT).astype(BF16)

        send()
    for one in sums:
        one.finish()
    first = DpSum(p, 512, a0, a1, a2, f3, f4, f5, f6)
    second = DpSum(p, 512, b0, b1, b2, g3, g4, g5, g6)
    products_turned(hn, draw.at[:, 0:512], a0)
    first.to_sibling()
    products_turned(hn, draw.at[:, 512:1024], b0)
    first.to_z()
    second.to_sibling()
    scatter1.middle()
    scatter2.middle()
    second.to_z()
    scatter1.collect()

    @pl.loop(0, 4)
    def _(i):
        rows = pl.ds(pl.multiple_of(i * 16, 16), 16)
        block_out[rows, :] = (resid[rows, :] + scatter1.rows(i * 16, 16)).astype(BF16)

    first.join()
    third.to_x(write(out_output))
    scatter2.collect()
    norm_terms[...] = jnp.zeros_like(norm_terms)

    @pl.loop(0, 4)
    def _(i):
        rows = pl.ds(pl.multiple_of(i * 16, 16), 16)
        grad, x = scatter2.rows(i * 16, 16), hid_rows[rows, :].astype(F32)
        inverse = lax.rsqrt(jnp.mean(x * x, axis=-1, keepdims=True) + EPS)
        scaled, normed = grad * gain[...], x * inverse
        back = inverse * (scaled - normed * jnp.mean(scaled * normed, axis=-1, keepdims=True))
        norm_terms[...] += jnp.sum(grad * normed, axis=0, keepdims=True)
        grad_in[rows, :] = d_resid[rows, :] + back

    vec[...] = jnp.zeros_like(vec)
    for i in range(16):
        vec[i : i + 1, :] = norm_terms[:, i * 128 : (i + 1) * 128]
        vec[16 + i : 17 + i, :] = ffn_terms[:, i * 128 : (i + 1) * 128]
    vec[32:33, :] = group_total[...]
    vec[33:34, :] = total[:, 0:128] + total[:, 128:256]
    vec[34:35, :] = bound_total[:, 0:128]
    vec[35:36, :] = bound_total[:, 128:256]
    everywhere = Total(p, vec, t0, t1, t2, t3, t4, t5, t6, t7, t8.at[0], t9.at[0])
    everywhere.send()
    second.join()
    third.end(accumulate(out_output))
    everywhere.middle()

    def put_first(x):
        out_query[:, 0:128], out_query[:, 128:256] = x[0:128], x[128:256]
        out_forget[:, 0:128], out_forget[:, 128:256] = x[256:384], x[384:512]

    def put_second(x):
        out_input[:, 0:128], out_input[:, 128:256] = x[0:128], x[128:256]
        out_outgate[:, 0:128], out_outgate[:, 128:256] = x[256:384], x[384:512]

    def add_to(low, high):
        def add(x):
            low[:, 0:128] += x[0:128]
            low[:, 128:256] += x[128:256]
            high[:, 0:128] += x[256:384]
            high[:, 128:256] += x[384:512]

        return add

    first.to_x(put_first)
    second.to_x(put_second)
    all_of = everywhere.result()
    out_norm[...] = all_of[0:16]
    out_ffn[...] = all_of[16:32]
    out_group[...] = all_of[32:33]
    mean = jnp.sum(all_of[33:34], axis=-1, keepdims=True) / float(8192 * D)
    out_mean[...] = jnp.broadcast_to(mean, (1, 128))
    for h in range(2):
        lanes = slice(h * 128, (h + 1) * 128)
        out_bounds[:, lanes] = soft[:, lanes] * (picked[:, lanes] - bound[:, lanes]) * all_of[34 + h : 35 + h]
    first.end(add_to(out_query, out_forget))
    second.end(add_to(out_input, out_outgate))
    spread.finish()
    scatter1.finish()
    scatter2.finish()
    exchange.finish()
    everywhere.finish()
    for one in (first, second, third):
        one.finish()


OUTS = (
    ((ROWS, D), BF16),
    ((ROWS, D), F32),
    ((128, HERE), F32),
    ((128, HERE), F32),
    ((128, HERE), F32),
    ((128, HERE), F32),
    ((HERE, 128), F32),
    ((24, HERE), F32),
    ((16, 128), F32),
    ((1, KDIM), F32),
    ((16, 128), F32),
    ((1, 128), F32),
    ((FFH, 128), F32),
    ((FFH, 128), F32),
    ((FFH, 128), F32),
)


def call_backward(*arrays):
    sums = dp_sum_scratch(FFH)
    again = [pltpu.VMEM((512, 128), BF16)] * 2 + sixteen()
    return pl.pallas_call(
        backward,
        name="backward",
        out_shape=[jax.ShapeDtypeStruct(*one) for one in OUTS],
        in_specs=[HB, HB, HB, HB, HB, VM, VM, VM, HB, VM, VM, VM, VM, HB, HB, HB, VM, VM, VM, VM, SM, SM],
        out_specs=[VM] * len(OUTS),
        scratch_shapes=[
            *[pltpu.VMEM((TOK, D), BF16)] * 2,
            *[pltpu.VMEM((FFH, D), BF16)] * 3,
            *[pltpu.VMEM((TOK, FFH), BF16)] * 3,
            *[pltpu.VMEM((FFH, TOK), BF16)] * 3,
            pltpu.VMEM((HERE, TOK), BF16),
            *[pltpu.VMEM((TOK, D), BF16)] * 3,
            pltpu.VMEM((ROWS, D), F32),
            pltpu.VMEM((ROWS, D), BF16),
            pltpu.VMEM((TOK, 1024), F32),
            pltpu.VMEM((TOK, 1024), BF16),
            pltpu.VMEM((TOK, HERE), BF16),
            *[pltpu.VMEM((TOK, HERE), F32)] * 3,
            pltpu.VMEM((2, CHUNKS, 128, 128), F32),
            pltpu.VMEM((CHUNKS, 8, HERE), F32),
            pltpu.VMEM((2, 128, 128), F32),
            pltpu.VMEM((VEC, 128), F32),
            pltpu.VMEM((1, D), F32),
            pltpu.VMEM((1, D), F32),
            pltpu.VMEM((1, 128), F32),
            pltpu.VMEM((1, HERE), F32),
            *exchange_scratch(),
            *sixteen(),
            *sixteen(),
            *eight(),
            *sixteen(),
            *sums,
            *sums,
            *sums,
            *dp_sum_scratch(HERE),
            *again,
            *again,
            pltpu.VMEM((8, VEC, 128), F32),
            pltpu.VMEM((8, VEC, 128), F32),
            pltpu.VMEM((VEC, 128), F32),
            pltpu.VMEM((VEC, 128), F32),
            *eight(),
            *eight(),
            pltpu.SemaphoreType.DMA((1,)),
            pltpu.SemaphoreType.DMA((1,)),
            pltpu.SemaphoreType.DMA((16,)),
        ],
        compiler_params=pltpu.CompilerParams(
            collective_id=1, has_side_effects=True, vmem_limit_bytes=60 * 1024 * 1024
        ),
    )(*arrays)


def results(*refs):
    half = len(refs) // 2
    for one, out in zip(refs[:half], refs[half:]):
        out[...] = one[...]


def call_results(arrays):
    return pl.pallas_call(
        results,
        name="results",
        out_shape=[jax.ShapeDtypeStruct(*one) for one in OUTS],
        in_specs=[VM] * len(OUTS),
        out_specs=[VM] * len(OUTS),
    )(*arrays)


def local(
    hidden_in, norm_gain, w_query, w_forget, w_input, w_outgate, lower_bounds, layer_index, group_gain,
    w_output, ffn_gain, w_gate, w_up, w_down, seq_lengths, grad_out,
):
    norm_row, ffn_row, group_row = norm_gain.reshape(1, D), ffn_gain.reshape(1, D), group_gain.reshape(1, KDIM)
    raw, xn, gated, mixed, states, run, total, w_all, wt_all, hn, resid, wg, wu, wd = call_forward(
        hidden_in, norm_row, w_query, w_forget, w_input, w_outgate, w_output, lower_bounds, layer_index, seq_lengths,
        group_row, ffn_row, w_gate.T, w_up.T, w_down,
    )
    (
        block_out, grad_in, grad_query, grad_forget, grad_input, grad_outgate, grad_output, grad_bounds,
        grad_norm, grad_group, grad_ffn, mean, grad_gate, grad_up, grad_down,
    ) = call_results(call_backward(
        hn, grad_out, wg, wu, wd, resid, ffn_row, wt_all, raw, run, mixed, states, gated, xn, w_all, hidden_in,
        total, norm_row, group_row, lower_bounds, layer_index, seq_lengths,
    ))
    return (
        block_out,
        grad_in,
        grad_norm.reshape(D),
        grad_query,
        grad_forget,
        grad_input,
        grad_outgate,
        grad_bounds,
        grad_group.reshape(KDIM),
        grad_output,
        grad_ffn.reshape(D),
        grad_gate.T,
        grad_up.T,
        grad_down,
        mean[0, 0:1],
    )


def solution(mesh):
    return jax.shard_map(
        local,
        mesh=mesh,
        in_specs=(
            P("dp", None),
            P(),
            P("dp", "head"),
            P("dp", "head"),
            P("dp", "head"),
            P("dp", "head"),
            P(None, "head"),
            P(),
            P(),
            P("head", "dp"),
            P(),
            P("dp", "head"),
            P("dp", "head"),
            P("head", "dp"),
            P(),
            P("dp", None),
        ),
        out_specs=(
            P(("dp", "head"), None),
            P(("dp", "head"), None),
            P(),
            P("dp", "head"),
            P("dp", "head"),
            P("dp", "head"),
            P("dp", "head"),
            P(None, "head"),
            P(),
            P("head", "dp"),
            P(),
            P("dp", "head"),
            P("dp", "head"),
            P("head", "dp"),
            P(),
        ),
        check_vma=False,
    )
```

```python
from functools import partial

import jax
import jax.numpy as jnp
from jax import lax
from jax.experimental import pallas as pl
from jax.experimental.pallas import tpu as pltpu
from jax.sharding import PartitionSpec as P

D = 2048
KDIM = 128
CHUNK = 128
TOK = 512
CHUNKS = TOK // CHUNK
HERE = 256
FFH = 704
NSEQ = 12
NHEAD = 8
ROWS = TOK // NHEAD
EPS = 1e-06
F32 = jnp.float32
BF16 = jnp.bfloat16
MESH = pl.DeviceIdType.MESH
VM = pl.BlockSpec(memory_space=pltpu.VMEM)
SM = pl.BlockSpec(memory_space=pltpu.SMEM)
HB = pl.BlockSpec(memory_space=pl.ANY)


class Spot:
    def __init__(self):
        self.dp = lax.axis_index("dp")
        self.head = lax.axis_index("head")
        self.core = lax.rem(self.dp, 2)
        self.chip = lax.div(self.dp, 2)
        self.xh = lax.rem(self.chip, 2)
        self.z = lax.div(self.chip, 2)
        self.xl = lax.rem(self.head, 2)
        self.y = lax.div(self.head, 2)

    def at(self, dz, xh, core):
        return (lax.rem(self.z + dz, 4) * 2 + xh) * 2 + core

    def y_at(self, k):
        return lax.rem(self.y + k, 4)

    @property
    def beside(self):
        return {"head": self.y * 2 + 1 - self.xl}

    def lines(self):
        return [self.beside] + [{"head": self.y_at(k) * 2 + self.xl} for k in (1, 2, 3)]

    @property
    def sibling(self):
        return {"dp": self.chip * 2 + 1 - self.core}

    def chips(self):
        return [{"dp": lax.rem(self.chip + k, 8) * 2 + self.core} for k in range(1, 8)]

    def heads(self):
        return [{"head": lax.rem(self.head + k, NHEAD)} for k in range(1, NHEAD)]


def greet(ids):
    barrier = pltpu.get_barrier_semaphore()
    for one in ids:
        pl.semaphore_signal(barrier, inc=1, device_id=one, device_id_type=MESH)
    return lambda: pl.semaphore_wait(barrier, len(ids))


def rcopy(src, dst, send, recv, where):
    return pltpu.make_async_remote_copy(
        src_ref=src, dst_ref=dst, send_sem=send, recv_sem=recv, device_id=where, device_id_type=MESH
    )


GATHER_SENDS = 17


class Gather:
    def __init__(self, spot, g, send, recv, half, columns=0):
        self.spot, self.g, self.s, self.r, self.h = spot, g, send, recv, half
        self.columns, self.middle = columns, (columns or 128) // 2

    def block(self, d, start=0, rows=0):
        if self.columns:
            rows = rows or self.columns
            return self.g.at[pl.ds(start, rows), pl.ds(pl.multiple_of(d * 128, 128), 128)]
        return self.g.at[pl.ds(pl.multiple_of(d * 128 + start, 64), rows or 128), :]

    def push(self, d, to, k):
        rcopy(self.block(d), self.block(d), self.s.at[k], self.r.at[d], {"dp": to}).start()

    def push_half(self, d, to, k, xh, part):
        b = self.block(d, part * self.middle, self.middle)
        rcopy(b, b, self.s.at[k], self.h.at[2 * xh + part], {"dp": to}).start()

    def arrived(self, d):
        b = self.block(d)
        rcopy(b, b, self.s.at[0], self.r.at[d], self.spot.sibling).wait_recv()

    def arrived_halves(self, d, xh):
        for part in range(2):
            b = self.block(d, part * self.middle, self.middle)
            rcopy(b, b, self.s.at[0], self.h.at[2 * xh + part], self.spot.sibling).wait_recv()

    def first(self):
        p = self.spot
        self.push(p.dp, p.at(0, 1 - p.xh, p.core), 0)
        self.push(p.dp, p.at(1, p.xh, p.core), 1)
        self.push(p.dp, p.at(3, p.xh, p.core), 2)
        self.push(p.dp, p.at(0, p.xh, 1 - p.core), 3)

    def second(self):
        p = self.spot
        b = p.at(0, 1 - p.xh, p.core)
        self.arrived(b)
        self.push(b, p.at(1, p.xh, p.core), 4)
        self.push(b, p.at(3, p.xh, p.core), 5)
        self.push(b, p.at(0, p.xh, 1 - p.core), 6)

    def third(self):
        p = self.spot
        for i, h in enumerate((p.xh, 1 - p.xh)):
            b = p.at(3, h, p.core)
            self.arrived(b)
            self.push_half(b, p.at(1, p.xh, p.core), 7 + i, h, 0)
            self.push(b, p.at(0, p.xh, 1 - p.core), 9 + i)
            b = p.at(1, h, p.core)
            self.arrived(b)
            self.push_half(b, p.at(3, p.xh, p.core), 11 + i, h, 1)
            self.push(b, p.at(0, p.xh, 1 - p.core), 13 + i)

    def fourth(self):
        p = self.spot
        for i, h in enumerate((p.xh, 1 - p.xh)):
            b = p.at(2, h, p.core)
            self.arrived_halves(b, h)
            self.push(b, p.at(0, p.xh, 1 - p.core), 15 + i)

    def last(self):
        p = self.spot
        for dz in range(4):
            for h in range(2):
                self.arrived(p.at(dz, h, 1 - p.core))
        half = self.block(0, 0, self.middle)
        for k in range(GATHER_SENDS):
            b = half if k in (7, 8, 11, 12) else self.block(0)
            rcopy(b, b, self.s.at[k], self.r.at[0], p.sibling).wait_send()


def gather_semaphores():
    return [
        pltpu.SemaphoreType.DMA((GATHER_SENDS,)),
        pltpu.SemaphoreType.DMA((16,)),
        pltpu.SemaphoreType.DMA((4,)),
    ]


NN = (((1,), (0,)), ((), ()))
NT = (((1,), (1,)), ((), ()))
TN = (((0,), (0,)), ((), ()))


def mm(a, b, dims):
    return lax.dot_general(a, b, dims, preferred_element_type=F32)


def halves(a):
    high = a.astype(BF16)
    return high, (a - high.astype(F32)).astype(BF16)


def mm2(a, b, dims):
    return mm(a[0], b, dims) + mm(a[1], b, dims)


def mm3(a, b, dims):
    return mm(a[0], b[0], dims) + (mm(a[0], b[1], dims) + mm(a[1], b[0], dims))


def triangle(lower):
    rows = lax.broadcasted_iota(jnp.int32, (CHUNK, CHUNK), 0)
    columns = lax.broadcasted_iota(jnp.int32, (CHUNK, CHUNK), 1)
    return (rows >= columns if lower else rows <= columns).astype(BF16)


def summed_rows(lower, x):
    high = x.astype(BF16)
    rest = x - high.astype(F32)
    middle = rest.astype(BF16)
    low = (rest - middle.astype(F32)).astype(BF16)
    t = triangle(lower)
    return mm(t, high, NN) + (mm(t, middle, NN) + mm(t, low, NN))


class Segments:
    def __init__(self, spot, seq):
        self.starts = []
        total = jnp.int32(0)
        for i in range(NSEQ):
            self.starts.append(total)
            total = total + seq[i]
        self.first = spot.dp * TOK

    def of(self, position):
        found = jnp.where(position >= self.starts[0], 1, 0)
        for s in self.starts[1:]:
            found = found + jnp.where(position >= s, 1, 0)
        return found - 1

    def column(self, c):
        return self.of(self.first + c * CHUNK + lax.broadcasted_iota(jnp.int32, (CHUNK, KDIM), 0))

    def row(self, c):
        return self.of(self.first + c * CHUNK + lax.broadcasted_iota(jnp.int32, (CHUNK, KDIM), 1))

    def before(self, c):
        return self.of(self.first + c * CHUNK - 1)

    def final(self, c):
        return self.of(self.first + (c + 1) * CHUNK - 1)


def lower_bound(lb, layer):
    x = lb[...]
    e = jnp.exp(x - jnp.max(x, axis=0, keepdims=True))
    soft = e / jnp.sum(e, axis=0, keepdims=True)
    depth = lax.broadcasted_iota(jnp.int32, x.shape, 0)
    picked = jnp.where((depth >= 1) & (depth <= layer), 1.0, 0.0)
    return soft, picked, jnp.sum(soft * picked, axis=0, keepdims=True)


def sigmoid(x):
    return lax.logistic(x)


def slope(x, s):
    return s * (1.0 + x * (1.0 - s))


class Exchange:
    def __init__(self, spot, msg, sib, slots, give, take, send, recv, backward):
        self.p, self.msg, self.sib, self.slots = spot, msg, sib, slots
        self.give, self.take, self.s, self.r, self.back = give, take, send, recv, backward

    def to_sibling(self):
        p = self.p
        rcopy(self.msg.at[1 - p.core], self.sib, self.s.at[7], self.r.at[8], p.sibling).start()

    def to_chips(self):
        p = self.p
        rcopy(self.sib, self.sib, self.s.at[7], self.r.at[8], p.sibling).wait_recv()
        mine, other = self.msg[p.core], self.sib[...]
        zero = p.core == 0
        one, two = jnp.where(zero, mine, other), jnp.where(zero, other, mine)
        near, far = (two, one) if self.back else (one, two)
        self.near = near
        state = near[0:128] * far[128:129] + far[0:128]
        rate = near[128:136] * far[128:136]
        high = rate.astype(BF16).astype(F32)
        self.slots[p.chip, 0:128, :] = state.astype(BF16)
        self.slots[p.chip, 128:144, :] = jnp.concatenate([high, rate - high], axis=0).astype(BF16)
        for k, to in enumerate(p.chips()):
            rcopy(self.slots.at[p.chip], self.slots.at[p.chip], self.s.at[k], self.r.at[p.chip], to).start()

    def result(self, out):
        p = self.p
        for k in range(1, 8):
            chip = lax.rem(p.chip + k, 8)
            rcopy(self.slots.at[chip], self.slots.at[chip], self.s.at[0], self.r.at[chip], p.sibling).wait_recv()
        state = jnp.zeros((128, 128), F32)
        for k in range(7, 0, -1) if self.back else range(7):
            m = self.slots[k].astype(F32)
            after = state * (m[128:129] + m[136:137]) + m[0:128]
            state = jnp.where(k > p.chip if self.back else k < p.chip, after, state)
        second = state * self.near[128:129] + self.near[0:128]
        is_first = p.core == (1 if self.back else 0)
        self.give[...] = jnp.where(is_first, second, state)
        move = rcopy(self.give, self.take, self.s.at[8], self.r.at[9], p.sibling)
        move.start()
        out[p.core] = jnp.where(is_first, state, second)
        move.wait_recv()
        out[1 - p.core] = self.take[...]

    def finish(self):
        p = self.p
        for k in range(7):
            rcopy(self.slots.at[0], self.slots.at[0], self.s.at[k], self.r.at[0], p.sibling).wait_send()
        rcopy(self.sib, self.sib, self.s.at[7], self.r.at[8], p.sibling).wait_send()
        rcopy(self.give, self.take, self.s.at[8], self.r.at[9], p.sibling).wait_send()


def exchange_scratch():
    return [
        pltpu.VMEM((2, 136, 128), F32),
        pltpu.VMEM((136, 128), F32),
        pltpu.VMEM((8, 144, 128), BF16),
        pltpu.VMEM((128, 128), F32),
        pltpu.VMEM((128, 128), F32),
        pltpu.SemaphoreType.DMA((9,)),
        pltpu.SemaphoreType.DMA((10,)),
    ]


def gates(raw, bound, rows):
    query_raw = raw[rows, 0:256]
    logistic = sigmoid(raw[rows, 256:512])
    forget = bound + (1.0 - bound) * logistic
    query = (query_raw * sigmoid(query_raw)).astype(BF16)
    keys = (1.0 - forget).astype(BF16)
    values = raw[rows, 512:768].astype(BF16)
    return logistic, forget, query, keys, values


HALF = D // 2


class HeadSum:
    def __init__(self, spot, ps, slots, send, recv):
        self.p, self.ps, self.slots, self.s, self.r = spot, ps, slots, send, recv

    def left_of(self, start, rows=ROWS):
        return self.slots.at[pl.ds(start, rows), pl.ds(0, HALF)]

    def right_of(self, start, rows=ROWS):
        return self.slots.at[pl.ds(start, rows), pl.ds(HALF, HALF)]

    def part(self, h, rows, right):
        return self.ps.at[pl.ds(pl.multiple_of(h * ROWS, ROWS), rows), pl.ds(HALF if right else 0, HALF)]

    def left_x(self, k):
        p = self.p
        h = p.y_at(k) * 2 + 1 - p.xl
        return rcopy(self.part(h, ROWS, False), self.left_of(64 * k), self.s.at[k], self.r.at[k], p.beside)

    def left_y(self, k):
        p = self.p
        to = {"head": p.y_at(k) * 2 + p.xl}
        return rcopy(self.left_of(64 * k), self.left_of(192 + 64 * k), self.s.at[3 + k], self.r.at[3 + k], to)

    def right_y(self, k):
        p = self.p
        to = {"head": p.y_at(k) * 2 + p.xl}
        return rcopy(
            self.part(p.y_at(k) * 2, 128, True), self.right_of(128 * k - 128, 128), self.s.at[6 + k], self.r.at[6 + k], to
        )

    def right_x(self):
        return rcopy(self.right_of(384), self.right_of(448), self.s.at[10], self.r.at[10], self.p.beside)

    def send_left(self):
        for k in (2, 1, 3, 0):
            self.left_x(k).start()

    def send_right(self):
        for k in (2, 1, 3):
            self.right_y(k).start()

    def send(self):
        self.send_right()
        self.send_left()

    def middle(self):
        p = self.p
        for k in (2, 1, 3, 0):
            self.left_x(k).wait_recv()
            mine = self.part(p.y_at(k) * 2 + p.xl, ROWS, False)
            one = self.left_of(64 * k)
            one[...] = (one[...].astype(F32) + mine[...].astype(F32)).astype(BF16)
            if k:
                self.left_y(k).start()
        for k in (1, 3, 2):
            self.right_y(k).wait_recv()

        def total(xl):
            one = self.part(p.y * 2 + xl, ROWS, True)[...].astype(F32)
            for k in range(3):
                rows = pl.ds(pl.multiple_of(128 * k + xl * ROWS, ROWS), ROWS)
                one = one + self.slots[rows, HALF:].astype(F32)
            return one.astype(BF16)

        self.slots[384:448, HALF:] = total(1 - p.xl)
        self.right_x().start()
        self.slots[448:512, 0:HALF] = total(p.xl)

    def collect(self):
        for k in (1, 3, 2):
            self.left_y(k).wait_recv()
        self.right_x().wait_recv()

    def rows(self, start, count):
        def at(row, left):
            rows = pl.ds(pl.multiple_of(row + start, 16), count)
            return self.slots[rows, 0:HALF].astype(F32) if left else self.slots[rows, HALF:].astype(F32)

        left = (at(0, True) + at(256, True)) + (at(320, True) + at(384, True))
        return jnp.concatenate([left, at(448, True) + at(448, False)], axis=1)

    def finish(self):
        for k in range(4):
            self.left_x(k).wait_send()
        for k in (1, 2, 3):
            self.left_y(k).wait_send()
            self.right_y(k).wait_send()
        self.right_x().wait_send()


class LateHeadSum:
    def __init__(self, spot, ps, slots, send, recv):
        self.p, self.ps, self.slots, self.s, self.r = spot, ps, slots, send, recv

    def block(self, ref, start, rows=ROWS):
        return ref.at[pl.ds(pl.multiple_of(start, ROWS), rows), :]

    def along_y(self, k):
        p = self.p
        y = p.y_at(k)
        return rcopy(
            self.block(self.ps, y * 128, 128), self.block(self.slots, 128 * k - 128, 128),
            self.s.at[k], self.r.at[k], {"head": y * 2 + p.xl},
        )

    def along_x(self):
        return rcopy(self.block(self.slots, 384), self.block(self.slots, 448), self.s.at[0], self.r.at[0], self.p.beside)

    def send(self):
        for k in (2, 1, 3):
            self.along_y(k).start()

    def part(self, xl, start, count):
        p = self.p
        one = self.ps[pl.ds(pl.multiple_of((p.y * 2 + xl) * ROWS + start, 16), count), :].astype(F32)
        for k in range(3):
            rows = pl.ds(pl.multiple_of(128 * k + xl * ROWS + start, 16), count)
            one = one + self.slots[rows, :].astype(F32)
        return one

    def middle(self):
        for k in (1, 3, 2):
            self.along_y(k).wait_recv()

        @pl.loop(0, 4)
        def _(i):
            rows = pl.ds(pl.multiple_of(384 + i * 16, 16), 16)
            self.slots[rows, :] = self.part(1 - self.p.xl, i * 16, 16).astype(BF16)

        self.along_x().start()

    def collect(self):
        self.along_x().wait_recv()

    def rows(self, start, count):
        rows = pl.ds(pl.multiple_of(448 + start, 16), count)
        return self.part(self.p.xl, start, count) + self.slots[rows, :].astype(F32)

    def finish(self):
        for k in (1, 2, 3):
            self.along_y(k).wait_send()
        self.along_x().wait_send()


class HeadGather:
    def __init__(self, spot, full, send, recv):
        self.p, self.full, self.s, self.r = spot, full, send, recv

    def block(self, h, right):
        return self.full.at[pl.ds(pl.multiple_of(h * ROWS, ROWS), ROWS), pl.ds(HALF if right else 0, HALF)]

    def along_y(self, k, xl, right, i):
        p = self.p
        b = self.block(p.y * 2 + xl, right)
        return rcopy(b, b, self.s.at[i + k], self.r.at[i + k], {"head": p.y_at(k) * 2 + p.xl})

    def beside(self, k, right, i):
        p = self.p
        b = self.block(p.y_at(k) * 2 + p.xl, right)
        return rcopy(b, b, self.s.at[i + k], self.r.at[i + k], p.beside)

    def send(self):
        p = self.p
        self.beside(0, False, 0).start()
        for k in (2, 1, 3):
            self.along_y(k, p.xl, True, 0).start()
        self.beside(0, True, 4).start()
        for k in (2, 1, 3):
            self.along_y(k, p.xl, False, 8).start()

    def middle(self):
        p = self.p
        self.beside(0, False, 0).wait_recv()
        for k in (2, 1, 3):
            self.along_y(k, 1 - p.xl, False, 11).start()
        for k in (1, 3, 2):
            self.along_y(4 - k, p.xl, True, 0).wait_recv()
            self.beside(k, True, 4).start()

    def collect(self):
        p = self.p
        self.beside(0, True, 4).wait_recv()
        for k in (1, 3, 2):
            self.along_y(k, p.xl, False, 8).wait_recv()
            self.along_y(k, 1 - p.xl, False, 11).wait_recv()
            self.beside(k, True, 4).wait_recv()

    def finish(self):
        p = self.p
        self.beside(0, False, 0).wait_send()
        for k in range(4):
            self.beside(k, True, 4).wait_send()
        for k in (1, 2, 3):
            self.along_y(k, p.xl, True, 0).wait_send()
            self.along_y(k, p.xl, False, 8).wait_send()
            self.along_y(k, 1 - p.xl, False, 11).wait_send()


def sixteen():
    return [pltpu.SemaphoreType.DMA((16,)), pltpu.SemaphoreType.DMA((16,))]


def eight():
    return [pltpu.SemaphoreType.DMA((8,)), pltpu.SemaphoreType.DMA((8,))]


class DpSum:
    def __init__(self, spot, rows, gs, cr, zr, xs, xr, send, recv):
        n = pl.ds(0, rows)
        self.rows, self.p = rows, spot
        self.gs, self.cr, self.zr = gs.at[:, :, n, :], cr.at[:, n, :], zr.at[:, :, n, :]
        self.xs, self.xr, self.s, self.r = xs.at[n, :], xr.at[n, :], send, recv

    def pair(self, i):
        p = self.p
        two = pl.ds(2 * i, 2)
        return rcopy(self.gs.at[1 - p.core, two], self.cr.at[two], self.s.at[i], self.r.at[i], p.sibling)

    def to_sibling(self):
        for i in range(4):
            self.pair(i).start()

    def half(self, part):
        return pl.ds(part * (self.rows // 2), self.rows // 2)

    def along_z(self, d, block, part, slot, i):
        p = self.p
        z = lax.rem(p.z + block, 4)
        where = {"dp": (lax.rem(p.z + d, 4) * 2 + p.xh) * 2 + p.core}
        source = self.gs.at[p.core, pl.ds(z * 2, 2), self.half(part), :]
        return rcopy(source, self.zr.at[slot, :, self.half(part), :], self.s.at[4 + i], self.r.at[4 + i], where)

    def far(self, part):
        return self.along_z(3 if part else 1, 2, part, 2, part)

    def near(self, part):
        return self.along_z(3, 3, 0, 1, 2) if part else self.along_z(1, 1, 1, 0, 3)

    def joined(self, part):
        return self.along_z(3, 3, 1, 1, 4) if part else self.along_z(1, 1, 0, 0, 5)

    def to_z(self):
        p = self.p
        for i in range(4):
            self.pair(i).wait_recv()

        @pl.loop(0, 8)
        def _(k):
            self.gs[p.core, k] = (self.gs[p.core, k].astype(F32) + self.cr[k].astype(F32)).astype(BF16)

        for part in range(2):
            self.far(part).start()
        for part in range(2):
            self.near(part).start()

    def join(self):
        p = self.p
        for part in range(2):
            self.far(part).wait_recv()
            z = lax.rem(p.z + (3 if part else 1), 4)
            for h in range(2):
                mine = self.gs.at[p.core, z * 2 + h, self.half(part), :]
                other = self.zr.at[2, h, self.half(part), :]
                mine[...] = (mine[...].astype(F32) + other[...].astype(F32)).astype(BF16)
            self.joined(part).start()

    def last_move(self):
        p = self.p
        where = {"dp": (p.z * 2 + 1 - p.xh) * 2 + p.core}
        return rcopy(self.xs, self.xr, self.s.at[10], self.r.at[10], where)

    def to_x(self, put):
        p = self.p
        for part in range(2):
            self.near(part).wait_recv()
            self.joined(part).wait_recv()

        def total(h):
            one = self.gs[p.core, 2 * p.z + h].astype(F32)
            for i in range(2):
                one = one + self.zr[i, h].astype(F32)
            return one

        self.xs[...] = total(1 - p.xh).astype(BF16)
        self.last_move().start()
        put(total(p.xh))

    def end(self, add):
        self.last_move().wait_recv()
        add(self.xr[...].astype(F32))

    def finish(self):
        for i in range(4):
            self.pair(i).wait_send()
        for part in range(2):
            self.far(part).wait_send()
            self.near(part).wait_send()
            self.joined(part).wait_send()
        self.last_move().wait_send()


def dp_sum_scratch(rows):
    return [
        pltpu.VMEM((2, 8, rows, 128), BF16),
        pltpu.VMEM((8, rows, 128), BF16),
        pltpu.VMEM((3, 2, rows, 128), BF16),
        pltpu.VMEM((rows, 128), BF16),
        pltpu.VMEM((rows, 128), BF16),
        *sixteen(),
    ]


def products(left_turned, right, gs):
    @pl.loop(0, 8)
    def _(k):
        columns = pl.ds(pl.multiple_of(k * 256, 256), 256)
        both = mm(left_turned[...], right[:, columns], NN).astype(BF16)
        gs[0, k] = both[:, 0:128]
        gs[1, k] = both[:, 128:256]


def products_turned(left, first, second, gs):
    @pl.loop(0, 8)
    def _(k):
        turned = left[:, pl.ds(pl.multiple_of(k * 256, 256), 256)]
        for i, right in enumerate((first, second)):
            both = mm(turned, right[...], TN).astype(BF16)
            for q in range(2):
                rows = slice(256 * i + 128 * q, 256 * i + 128 * (q + 1))
                gs[0, k, rows, :] = both[0:128, 128 * q : 128 * (q + 1)]
                gs[1, k, rows, :] = both[128:256, 128 * q : 128 * (q + 1)]


def write(ref):
    def put(x):
        ref[...] = x

    return put


def accumulate(ref):
    def add(x):
        ref[...] += x

    return add


VEC = 40


class Total:
    def __init__(self, spot, vec, h_slots, c_slots, own, other, h_s, h_r, c_s, c_r, k_s, k_r):
        self.p, self.vec, self.hs, self.cs, self.own, self.other = spot, vec, h_slots, c_slots, own, other
        self.h_s, self.h_r, self.c_s, self.c_r, self.k_s, self.k_r = h_s, h_r, c_s, c_r, k_s, k_r

    def send(self):
        p = self.p
        self.cs[p.chip] = self.vec[...]
        for k, to in enumerate(p.chips()):
            rcopy(self.cs.at[p.chip], self.cs.at[p.chip], self.c_s.at[k], self.c_r.at[p.chip], to).start()

    def middle(self):
        p = self.p
        for k in range(1, 8):
            chip = lax.rem(p.chip + k, 8)
            rcopy(self.cs.at[chip], self.cs.at[chip], self.c_s.at[0], self.c_r.at[chip], p.sibling).wait_recv()
        total = self.cs[0]
        for k in range(1, 8):
            total = total + self.cs[k]
        self.own[...] = total
        rcopy(self.own, self.other, self.k_s, self.k_r, p.sibling).start()

    def late(self):
        p = self.p
        rcopy(self.own, self.other, self.k_s, self.k_r, p.sibling).wait_recv()
        self.hs[p.head] = self.own[...] + self.other[...]
        for k in range(1, NHEAD):
            h = lax.rem(p.head + k, NHEAD)
            rcopy(self.hs.at[p.head], self.hs.at[p.head], self.h_s.at[k], self.h_r.at[p.head], {"head": h}).start()

    def result(self):
        p = self.p
        for k in range(1, NHEAD):
            h = lax.rem(p.head + k, NHEAD)
            rcopy(self.hs.at[h], self.hs.at[h], self.h_s.at[0], self.h_r.at[h], p.sibling).wait_recv()
        total = self.hs[0]
        for h in range(1, NHEAD):
            total = total + self.hs[h]
        per_head = lax.broadcasted_iota(jnp.int32, (VEC, 128), 0) >= 34
        return jnp.where(per_head, self.hs[p.head], total)

    def finish(self):
        p = self.p
        for k in range(1, NHEAD):
            rcopy(self.hs.at[0], self.hs.at[0], self.h_s.at[k], self.h_r.at[0], p.sibling).wait_send()
        for k in range(7):
            rcopy(self.cs.at[0], self.cs.at[0], self.c_s.at[k], self.c_r.at[0], p.sibling).wait_send()
        rcopy(self.own, self.other, self.k_s, self.k_r, p.sibling).wait_send()


def forward(
    hid, gain, wq, wf, wi, wo, w_output, lb, layer, seq, group_gain, ffn_gain, wg, wu, wd,
    raw, xn_out, gated, mixed, states, run, total, w_out, wt_out, hn_out, resid, wg_out, wu_out, wd_out,
    xn, w, wt, g0, g1, g2, hn, ps, slots, inner_update, decay, incoming,
    msg, sib, slots3, give, take, ex_send, ex_recv, rs_s, rs_r, ag_s, ag_r,
    ws, wr, wh, os, or_, oh, s0, r0, h0, s1, r1, h1, s2, r2, h2, local_sem,
):
    p = Spot()
    arrive = greet(p.chips() + [p.sibling] + p.lines())
    mine = pl.ds(pl.multiple_of(p.dp * 128, 128), 128)
    for k, one in enumerate((wq, wf, wi, wo)):
        w[mine, 256 * k : 256 * (k + 1)] = one[...]
    arrive()
    gather = Gather(p, w, ws, wr, wh)
    gather.first()
    wt[:, mine] = w_output[...]
    later = Gather(p, wt, os, or_, oh, HERE)
    for one, full in zip((wg, wu, wd), (g0, g1, g2)):
        full[:, mine] = one[...]
    gathers = [Gather(p, g0, s0, r0, h0, FFH), Gather(p, g1, s1, r1, h1, FFH), Gather(p, g2, s2, r2, h2, FFH)]

    @pl.loop(0, 8)
    def _(i):
        rows = pl.ds(pl.multiple_of(i * 64, 64), 64)
        x = hid[rows, :].astype(F32)
        scale = lax.rsqrt(jnp.mean(x * x, axis=-1, keepdims=True) + EPS)
        xn[rows, :] = (x * scale * gain[...]).astype(BF16)

    keeps = []

    def keep(source, out):
        move = pltpu.make_async_copy(source, out, local_sem.at[len(keeps)])
        move.start()
        keeps.append(move)

    keep(xn, xn_out)
    gather.second()
    gather.third()
    gather.fourth()
    later.first()
    gathers[0].first()
    gather.last()
    keep(w, w_out)

    @pl.loop(0, 4)
    def _(j):
        columns = pl.ds(pl.multiple_of(j * 256, 256), 256)
        raw[:, columns] = mm(xn[...], w[:, columns], NN)

    later.second()
    segments = Segments(p, seq)
    bound = lower_bound(lb, layer[0])[2]
    total[...] = jnp.zeros_like(total)

    @pl.loop(0, CHUNKS)
    def _(c):
        rows = pl.ds(pl.multiple_of(c * CHUNK, CHUNK), CHUNK)
        logistic, forget, query, keys, values = gates(raw, bound, rows)
        total[...] += jnp.sum(forget, axis=0, keepdims=True)
        running = summed_rows(True, jnp.log(forget))
        run[rows, :] = running
        middle, ending = running[63:64], running[127:128]
        lifted = query.astype(F32) * jnp.exp(running - middle)
        lowered = keys.astype(F32) * jnp.exp(middle - running)
        tail = keys.astype(F32) * jnp.exp(ending - running)
        column, row = segments.column(c), segments.row(c)
        linked = (column == row) & (
            lax.broadcasted_iota(jnp.int32, (CHUNK, CHUNK), 0)
            >= lax.broadcasted_iota(jnp.int32, (CHUNK, CHUNK), 1)
        )
        final = segments.final(c)
        rate = jnp.exp(ending) * jnp.where(final == segments.before(c), 1.0, 0.0)
        decay[c] = jnp.broadcast_to(rate, (8, HERE))
        ends = jnp.where(column == final, 1.0, 0.0)
        for h in range(2):
            lanes = slice(h * 128, (h + 1) * 128)
            scores = mm3(halves(lifted[:, lanes]), halves(lowered[:, lanes]), NT)
            scores = jnp.where(linked, scores, 0.0)
            mixed[rows, lanes] = mm2(halves(scores), values[:, lanes], NN)
            high, low = halves(tail[:, lanes] * ends)
            inner_update[h, c] = mm(values[:, lanes], high, TN) + mm(values[:, lanes], low, TN)

    for h in range(2):
        lanes = slice(h * 128, (h + 1) * 128)
        state, rate = inner_update[h, 0], decay[0, 0:1, lanes]
        for c in range(1, CHUNKS):
            state = state * decay[c, 0:1, lanes] + inner_update[h, c]
            rate = rate * decay[c, 0:1, lanes]
        msg[h, 0:128, :] = state
        msg[h, 128:136, :] = jnp.broadcast_to(rate, (8, 128))
    exchange = Exchange(p, msg, sib, slots3, give, take, ex_send, ex_recv, False)
    exchange.to_sibling()
    exchange.to_chips()
    later.third()
    gathers[1].first()
    gathers[2].first()
    gathers[0].second()
    later.fourth()
    exchange.result(incoming)
    gathers[1].second()
    gathers[2].second()
    for h in range(2):
        lanes = slice(h * 128, (h + 1) * 128)
        state = incoming[h]
        states[h, 0] = state
        for c in range(CHUNKS):
            state = state * decay[c, 0:1, lanes] + inner_update[h, c]
            states[h, c + 1] = state

    @pl.loop(0, CHUNKS)
    def _(c):
        rows = pl.ds(pl.multiple_of(c * CHUNK, CHUNK), CHUNK)
        carried = jnp.where(segments.column(c) == segments.before(c), 1.0, 0.0)
        for h in range(2):
            lanes = slice(h * 128, (h + 1) * 128)
            query_raw = raw[rows, h * 128 : (h + 1) * 128]
            query = (query_raw * sigmoid(query_raw)).astype(BF16).astype(F32)
            reach = query * jnp.exp(run[rows, lanes]) * carried
            x = mixed[rows, lanes] + mm3(halves(reach), halves(states[h, c]), NT)
            mixed[rows, lanes] = x
            scale = lax.rsqrt(jnp.mean(x * x, axis=-1, keepdims=True) + EPS)
            gate = raw[rows, 768 + h * 128 : 768 + (h + 1) * 128]
            gated[rows, lanes] = (x * scale * group_gain[...] * (gate * sigmoid(gate))).astype(BF16)

    later.last()
    keep(wt, wt_out)

    scatter = HeadSum(p, ps, slots, rs_s, rs_r)
    for start, send in ((HALF, scatter.send_right), (0, scatter.send_left)):

        @pl.loop(0, 4)
        def _(j):
            columns = pl.ds(pl.multiple_of(start + j * 256, 256), 256)
            ps[:, columns] = mm(gated[...], wt[:, columns], NN).astype(BF16)

        send()
    scatter.middle()
    for g in gathers:
        g.third()
    scatter.collect()
    own = pl.multiple_of(p.head * ROWS, ROWS)

    @pl.loop(0, 4)
    def _(i):
        rows = pl.ds(pl.multiple_of(i * 16, 16), 16)
        here = pl.ds(pl.multiple_of(own + i * 16, 16), 16)
        x = hid[here, :].astype(F32) + scatter.rows(i * 16, 16)
        resid[rows, :] = x
        scale = lax.rsqrt(jnp.mean(x * x, axis=-1, keepdims=True) + EPS)
        hn[here, :] = (x * scale * ffn_gain[...]).astype(BF16)

    spread = HeadGather(p, hn, ag_s, ag_r)
    spread.send()
    spread.middle()
    for g in gathers:
        g.fourth()
    for g, full, out in zip(gathers, (g0, g1, g2), (wg_out, wu_out, wd_out)):
        g.last()
        keep(full, out)
    exchange.finish()
    scatter.finish()
    spread.collect()
    keep(hn, hn_out)
    spread.finish()
    for move in keeps:
        move.wait()


def call_forward(*arrays):
    out = jax.ShapeDtypeStruct
    return pl.pallas_call(
        forward,
        name="forward",
        out_shape=(
            out((TOK, 1024), F32),
            out((TOK, D), BF16),
            out((TOK, HERE), BF16),
            out((TOK, HERE), F32),
            out((2, CHUNKS + 1, 128, 128), F32),
            out((TOK, HERE), F32),
            out((1, HERE), F32),
            out((D, 1024), BF16),
            out((HERE, D), BF16),
            out((TOK, D), BF16),
            out((ROWS, D), F32),
            out((FFH, D), BF16),
            out((FFH, D), BF16),
            out((FFH, D), BF16),
        ),
        in_specs=[VM] * 8 + [SM, SM] + [VM] * 5,
        out_specs=(VM, HB, VM, VM, VM, VM, VM, HB, HB, HB, VM, HB, HB, HB),
        scratch_shapes=[
            pltpu.VMEM((TOK, D), BF16),
            pltpu.VMEM((D, 1024), BF16),
            pltpu.VMEM((HERE, D), BF16),
            *[pltpu.VMEM((FFH, D), BF16)] * 3,
            *[pltpu.VMEM((TOK, D), BF16)] * 3,
            pltpu.VMEM((2, CHUNKS, 128, 128), F32),
            pltpu.VMEM((CHUNKS, 8, HERE), F32),
            pltpu.VMEM((2, 128, 128), F32),
            *exchange_scratch(),
            *sixteen(),
            *sixteen(),
            *gather_semaphores(),
            *gather_semaphores(),
            *gather_semaphores(),
            *gather_semaphores(),
            *gather_semaphores(),
            pltpu.SemaphoreType.DMA((7,)),
        ],
        compiler_params=pltpu.CompilerParams(
            collective_id=0, has_side_effects=True, vmem_limit_bytes=58 * 1024 * 1024
        ),
    )(*arrays)


def backward(
    hn_in, dy_in, wg_in, wu_in, wd_in, resid, ffn_gain, wt, raw_in, run, mixed, states, gated, xn_in, w_in, hid,
    total, gain, group_gain, lb, layer, seq,
    block_out, grad_in, out_query, out_forget, out_input, out_outgate, out_output, out_bounds,
    out_norm, out_group, out_ffn, out_mean, out_gate, out_up, out_down,
    hn, dy, wg, wu, wd, hidden, dg, du, hidden_t, dg_t, du_t, gated_t, ps, slots, db, d_resid, hid_rows, raw,
    draw, d_mixed, d_query, d_keys, d_values, back_update, decay, incoming, vec,
    norm_terms, ffn_terms, group_total, bound_total,
    msg, sib, slots3, give, take, ex_send, ex_recv, rs_s, rs_r, ag_s, ag_r, rs1_s, rs1_r, rs2_s, rs2_r,
    a0, a1, a2, a3, a4, a5, a6, b0, b1, b2, b3, b4, b5, b6, c0, c1, c2, c3, c4, c5, c6,
    e0, e1, e2, e3, e4, e5, e6, f3, f4, f5, f6, g3, g4, g5, g6,
    t0, t1, t2, t3, t4, t5, t6, t7, t8, t9, local_sem,
):
    def load(source, to, k):
        move = pltpu.make_async_copy(source, to, local_sem.at[k])
        move.start()
        return move

    def quarter(ref, j):
        return ref.at[pl.ds(256 * j, 256), :]

    def place(ref, j):
        row, column = lax.rem(j, 2) * 256, lax.div(j, 2) * 1024
        return ref.at[pl.ds(pl.multiple_of(row, 256), 256), pl.ds(pl.multiple_of(column, 1024), 1024)]

    def put(low, high):
        def write_four(x):
            low[:, 0:128], low[:, 128:256] = x[0:128], x[128:256]
            high[:, 0:128], high[:, 128:256] = x[256:384], x[384:512]

        return write_four

    def add_to(low, high):
        def add(x):
            low[:, 0:128] += x[0:128]
            low[:, 128:256] += x[128:256]
            high[:, 0:128] += x[256:384]
            high[:, 128:256] += x[384:512]

        return add

    p = Spot()
    own = pl.multiple_of(p.head * ROWS, ROWS)
    loads = [load(one, full, k) for k, (one, full) in enumerate(((wg_in, wg), (hn_in, hn), (wu_in, wu), (wd_in, wd), (dy_in, dy)))]
    late = [load(hid.at[pl.ds(own, ROWS), :], hid_rows, 5), load(raw_in, raw, 6)]
    arrive = greet(p.chips() + [p.sibling] + p.heads())
    for move in loads:
        move.wait()
    for low, high in ((0, 256), (256, 512), (512, FFH)):
        gate = mm(hn[...], wg[low:high, :], NT)
        up = mm(hn[...], wu[low:high, :], NT)
        dh = mm(dy[...], wd[low:high, :], NT)
        s = sigmoid(gate)
        silu = gate * s
        hidden[:, low:high] = (silu * up).astype(BF16)
        dg[:, low:high] = (dh * up * slope(gate, s)).astype(BF16)
        du[:, low:high] = (dh * silu).astype(BF16)

    arrive()
    scatter = HeadSum(p, ps, slots, rs_s, rs_r)
    for start, send in ((HALF, scatter.send_right), (0, scatter.send_left)):

        @pl.loop(0, 4)
        def _(j):
            columns = pl.ds(pl.multiple_of(start + j * 256, 256), 256)
            ps[:, columns] = (mm(dg[...], wg[:, columns], NN) + mm(du[...], wu[:, columns], NN)).astype(BF16)

        send()
    sums = [
        DpSum(p, FFH, a0, a1, a2, a3, a4, a5, a6),
        DpSum(p, FFH, b0, b1, b2, b3, b4, b5, b6),
        DpSum(p, FFH, c0, c1, c2, c3, c4, c5, c6),
    ]
    dg_t[...] = dg[...].T
    products(dg_t, hn, a0)
    sums[0].to_sibling()
    du_t[...] = du[...].T
    products(du_t, hn, b0)
    sums[0].to_z()
    sums[1].to_sibling()
    scatter.middle()
    hidden_t[...] = hidden[...].T
    products(hidden_t, dy, c0)
    sums[1].to_z()
    sums[2].to_sibling()
    sums[0].join()

    @pl.loop(0, 8)
    def _(j):
        columns = pl.ds(pl.multiple_of(j * 256, 256), 256)
        wu[0:TOK, columns] = mm(hidden[...], wd[:, columns], NN).astype(BF16)

    sums[2].to_z()
    late.append(load(xn_in, hn, 7))
    late += [load(quarter(w_in, j), place(wd, j), 8 + j) for j in range(4)]
    scatter.collect()
    ffn_terms[...] = jnp.zeros_like(ffn_terms)

    @pl.loop(0, 4)
    def _(i):
        rows = pl.ds(pl.multiple_of(i * 16, 16), 16)
        here = pl.ds(pl.multiple_of(own + i * 16, 16), 16)
        grad, x = scatter.rows(i * 16, 16), resid[rows, :]
        inverse = lax.rsqrt(jnp.mean(x * x, axis=-1, keepdims=True) + EPS)
        scaled, normed = grad * ffn_gain[...], x * inverse
        back = inverse * (scaled - normed * jnp.mean(scaled * normed, axis=-1, keepdims=True))
        ffn_terms[...] += jnp.sum(grad * normed, axis=0, keepdims=True)
        both = dy[here, :].astype(F32) + back
        d_resid[rows, :] = both
        db[here, :] = both.astype(BF16)

    scatter.finish()
    spread = HeadGather(p, db, ag_s, ag_r)
    spread.send()
    spread.middle()
    sums[1].join()
    late += [load(quarter(w_in, 4 + j), place(dy, j), 12 + j) for j in range(4)]
    segments = Segments(p, seq)
    soft, picked, bound = lower_bound(lb, layer[0])
    group_total[...] = jnp.zeros_like(group_total)
    gated_t[...] = gated[...].T
    for move in late:
        move.wait()
    sums[2].join()
    spread.collect()
    scatter1 = LateHeadSum(p, wu, wg, rs1_s, rs1_r)
    scatter1.send()

    @pl.loop(0, CHUNKS)
    def _(c):
        rows = pl.ds(pl.multiple_of(c * CHUNK, CHUNK), CHUNK)
        d_gated = mm(db[rows, :], wt[...], NT)
        before, final = segments.before(c), segments.final(c)
        carried = jnp.where(segments.column(c) == before, 1.0, 0.0)
        running = run[rows, :]
        rate = jnp.exp(running[127:128]) * jnp.where(final == before, 1.0, 0.0)
        decay[c] = jnp.broadcast_to(rate, (8, HERE))
        for h in range(2):
            lanes = slice(h * 128, (h + 1) * 128)
            x, grad = mixed[rows, lanes], d_gated[:, lanes]
            gate = raw[rows, 768 + h * 128 : 768 + (h + 1) * 128]
            s = sigmoid(gate)
            inverse = lax.rsqrt(jnp.mean(x * x, axis=-1, keepdims=True) + EPS)
            normed = x * inverse
            draw[rows, 768 + h * 128 : 768 + (h + 1) * 128] = (
                grad * (normed * group_gain[...]) * slope(gate, s)
            ).astype(BF16)
            inner = grad * (gate * s)
            scaled = inner * group_gain[...]
            back = inverse * (scaled - normed * jnp.mean(scaled * normed, axis=-1, keepdims=True))
            group_total[...] += jnp.sum(inner * normed, axis=0, keepdims=True)
            back = back.astype(BF16)
            d_mixed[rows, lanes] = back
            query_raw = raw[rows, lanes]
            query = (query_raw * sigmoid(query_raw)).astype(BF16).astype(F32)
            high, low = halves(query * jnp.exp(running[:, lanes]) * carried)
            back_update[h, c] = mm(back, high, TN) + mm(back, low, TN)

    for h in range(2):
        lanes = slice(h * 128, (h + 1) * 128)
        state, rate = back_update[h, CHUNKS - 1], decay[CHUNKS - 1, 0:1, lanes]
        for c in range(CHUNKS - 2, -1, -1):
            state = state * decay[c, 0:1, lanes] + back_update[h, c]
            rate = rate * decay[c, 0:1, lanes]
        msg[h, 0:128, :] = state
        msg[h, 128:136, :] = jnp.broadcast_to(rate, (8, 128))
    exchange = Exchange(p, msg, sib, slots3, give, take, ex_send, ex_recv, True)
    exchange.to_sibling()
    results = (out_gate, out_up, out_down)
    for one, out in zip(sums[:2], results):
        one.to_x(write(out))
    exchange.to_chips()

    @pl.loop(0, CHUNKS)
    def _(c):
        rows = pl.ds(pl.multiple_of(c * CHUNK, CHUNK), CHUNK)
        running = run[rows, :]
        middle = running[63:64]
        _, _, query, keys, values = gates(raw, bound, rows)
        up, down_ = jnp.exp(running - middle), jnp.exp(middle - running)
        lifted = query.astype(F32) * up
        lowered = keys.astype(F32) * down_
        column, row = segments.column(c), segments.row(c)
        carried = jnp.where(column == segments.before(c), 1.0, 0.0)
        linked = (column == row) & (
            lax.broadcasted_iota(jnp.int32, (CHUNK, CHUNK), 0)
            >= lax.broadcasted_iota(jnp.int32, (CHUNK, CHUNK), 1)
        )
        for h in range(2):
            lanes = slice(h * 128, (h + 1) * 128)
            lift, lower = halves(lifted[:, lanes]), halves(lowered[:, lanes])
            scores = halves(jnp.where(linked, mm3(lift, lower, NT), 0.0))
            grad = d_mixed[rows, lanes]
            d_scores = halves(jnp.where(linked, mm(grad, values[:, lanes], NT), 0.0))
            d_values[rows, lanes] = mm(scores[0], grad, TN) + mm(scores[1], grad, TN)
            state = halves(states[h, c])
            outer = mm(grad, state[0], NN) + mm(grad, state[1], NN)
            query_grad = mm3(d_scores, lower, NN) * up[:, lanes] + outer * jnp.exp(running[:, lanes]) * carried
            d_query[rows, lanes] = query_grad
            query_raw = raw[rows, lanes]
            draw[rows, lanes] = (query_grad * slope(query_raw, sigmoid(query_raw))).astype(BF16)
            d_keys[rows, lanes] = mm3(d_scores, lift, TN) * down_[:, lanes]

    for one in sums[:2]:
        one.finish()
    first = DpSum(p, 512, a0, a1, a2, f3, f4, f5, f6)
    second = DpSum(p, 512, b0, b1, b2, g3, g4, g5, g6)
    third = DpSum(p, HERE, e0, e1, e2, e3, e4, e5, e6)
    products_turned(hn, draw.at[:, 0:256], draw.at[:, 768:1024], a0)
    exchange.result(incoming)
    first.to_sibling()
    sums[2].to_x(write(out_down))
    for one, out in zip(sums[:2], results):
        one.end(accumulate(out))
    first.to_z()
    bound_total[...] = jnp.zeros_like(bound_total)

    @pl.loop(0, CHUNKS)
    def _(i):
        c = CHUNKS - 1 - i
        rows = pl.ds(pl.multiple_of(c * CHUNK, CHUNK), CHUNK)
        running = run[rows, :]
        logistic, forget, query, keys, values = gates(raw, bound, rows)
        keys = keys.astype(F32)
        fade = jnp.exp(running[127:128] - running)
        column, final = segments.column(c), segments.final(c)
        ends = jnp.where(column == final, 1.0, 0.0)
        for h in range(2):
            lanes = slice(h * 128, (h + 1) * 128)
            state = incoming[h]
            pair = halves(state)
            tail = halves(keys[:, lanes] * fade[:, lanes] * ends)
            value_grad = d_values[rows, lanes] + mm3(tail, pair, NT)
            draw[rows, 512 + h * 128 : 512 + (h + 1) * 128] = value_grad.astype(BF16)
            lift = mm(values[:, lanes], pair[0], NN) + mm(values[:, lanes], pair[1], NN)
            key_grad = d_keys[rows, lanes] + lift * fade[:, lanes] * ends
            at_end = jnp.sum(states[h, c + 1] * state, axis=0, keepdims=True)
            query_grad = d_query[rows, lanes]
            step = query[:, lanes].astype(F32) * query_grad - keys[:, lanes] * key_grad
            log_grad = summed_rows(False, step) + at_end
            forget_grad = log_grad / forget[:, lanes] - key_grad
            rest = 1.0 - logistic[:, lanes]
            draw[rows, 256 + h * 128 : 256 + (h + 1) * 128] = (
                forget_grad * (1.0 - bound[:, lanes]) * logistic[:, lanes] * rest
            ).astype(BF16)
            bound_total[:, lanes] += jnp.sum(forget_grad * rest, axis=0, keepdims=True)
            incoming[h] = state * decay[c, 0:1, lanes] + back_update[h, c]

    scatter2 = HeadSum(p, ps, slots, rs2_s, rs2_r)
    for start, part, send in ((HALF, dy, scatter2.send_right), (0, wd, scatter2.send_left)):

        @pl.loop(0, 4)
        def _(j):
            columns = pl.ds(pl.multiple_of(start + j * 256, 256), 256)
            ps[:, columns] = mm(draw[...], place(part, j)[...], NT).astype(BF16)

        send()
    products_turned(hn, draw.at[:, 256:512], draw.at[:, 512:768], b0)
    second.to_sibling()
    first.join()

    @pl.loop(0, 8)
    def _(j):
        columns = pl.ds(pl.multiple_of(j * 256, 256), 256)
        terms = ps[:, columns].astype(F32) * hn[:, columns].astype(F32)
        norm_terms[:, columns] = jnp.sum(terms, axis=0, keepdims=True) / gain[:, columns]

    vec[...] = jnp.zeros_like(vec)
    for i in range(16):
        vec[i : i + 1, :] = norm_terms[:, i * 128 : (i + 1) * 128]
        vec[16 + i : 17 + i, :] = ffn_terms[:, i * 128 : (i + 1) * 128]
    vec[32:33, :] = group_total[...]
    vec[33:34, :] = total[:, 0:128] + total[:, 128:256]
    vec[34:35, :] = bound_total[:, 0:128]
    vec[35:36, :] = bound_total[:, 128:256]
    everywhere = Total(p, vec, t0, t1, t2, t3, t4, t5, t6, t7, t8.at[0], t9.at[0])
    everywhere.send()
    second.to_z()
    scatter2.middle()
    products(gated_t, db, e0)
    third.to_sibling()
    everywhere.middle()
    third.to_z()
    everywhere.late()
    scatter1.middle()
    second.join()
    sums[2].end(accumulate(out_down))
    first.to_x(put(out_query, out_outgate))
    third.join()
    scatter2.collect()

    @pl.loop(0, 4)
    def _(i):
        rows = pl.ds(pl.multiple_of(i * 16, 16), 16)
        grad, x = scatter2.rows(i * 16, 16), hid_rows[rows, :].astype(F32)
        inverse = lax.rsqrt(jnp.mean(x * x, axis=-1, keepdims=True) + EPS)
        scaled, normed = grad * gain[...], x * inverse
        back = inverse * (scaled - normed * jnp.mean(scaled * normed, axis=-1, keepdims=True))
        grad_in[rows, :] = d_resid[rows, :] + back

    scatter1.collect()

    @pl.loop(0, 4)
    def _(i):
        rows = pl.ds(pl.multiple_of(i * 16, 16), 16)
        block_out[rows, :] = (resid[rows, :] + scatter1.rows(i * 16, 16)).astype(BF16)

    second.to_x(put(out_forget, out_input))
    third.to_x(write(out_output))
    all_of = everywhere.result()
    out_norm[...] = all_of[0:16]
    out_ffn[...] = all_of[16:32]
    out_group[...] = all_of[32:33]
    mean = jnp.sum(all_of[33:34], axis=-1, keepdims=True) / float(8192 * D)
    out_mean[...] = jnp.broadcast_to(mean, (1, 128))
    for h in range(2):
        lanes = slice(h * 128, (h + 1) * 128)
        out_bounds[:, lanes] = soft[:, lanes] * (picked[:, lanes] - bound[:, lanes]) * all_of[34 + h : 35 + h]

    first.end(add_to(out_query, out_outgate))
    second.end(add_to(out_forget, out_input))
    third.end(accumulate(out_output))
    spread.finish()
    scatter1.finish()
    scatter2.finish()
    exchange.finish()
    everywhere.finish()
    for one in (first, second, third, sums[2]):
        one.finish()


OUTS = (
    ((ROWS, D), BF16),
    ((ROWS, D), F32),
    ((128, HERE), F32),
    ((128, HERE), F32),
    ((128, HERE), F32),
    ((128, HERE), F32),
    ((HERE, 128), F32),
    ((24, HERE), F32),
    ((16, 128), F32),
    ((1, KDIM), F32),
    ((16, 128), F32),
    ((1, 128), F32),
    ((FFH, 128), F32),
    ((FFH, 128), F32),
    ((FFH, 128), F32),
)


def call_backward(*arrays):
    sums = dp_sum_scratch(FFH)
    again = [pltpu.VMEM((512, 128), BF16)] * 2 + sixteen()
    return pl.pallas_call(
        backward,
        name="backward",
        out_shape=[jax.ShapeDtypeStruct(*one) for one in OUTS],
        in_specs=[HB, HB, HB, HB, HB, VM, VM, VM, HB, VM, VM, VM, VM, HB, HB, HB, VM, VM, VM, VM, SM, SM],
        out_specs=[VM] * len(OUTS),
        scratch_shapes=[
            *[pltpu.VMEM((TOK, D), BF16)] * 2,
            *[pltpu.VMEM((FFH, D), BF16)] * 3,
            *[pltpu.VMEM((TOK, FFH), BF16)] * 3,
            *[pltpu.VMEM((FFH, TOK), BF16)] * 3,
            pltpu.VMEM((HERE, TOK), BF16),
            *[pltpu.VMEM((TOK, D), BF16)] * 3,
            pltpu.VMEM((ROWS, D), F32),
            pltpu.VMEM((ROWS, D), BF16),
            pltpu.VMEM((TOK, 1024), F32),
            pltpu.VMEM((TOK, 1024), BF16),
            pltpu.VMEM((TOK, HERE), BF16),
            *[pltpu.VMEM((TOK, HERE), F32)] * 3,
            pltpu.VMEM((2, CHUNKS, 128, 128), F32),
            pltpu.VMEM((CHUNKS, 8, HERE), F32),
            pltpu.VMEM((2, 128, 128), F32),
            pltpu.VMEM((VEC, 128), F32),
            pltpu.VMEM((1, D), F32),
            pltpu.VMEM((1, D), F32),
            pltpu.VMEM((1, 128), F32),
            pltpu.VMEM((1, HERE), F32),
            *exchange_scratch(),
            *sixteen(),
            *sixteen(),
            *eight(),
            *sixteen(),
            *sums,
            *sums,
            *sums,
            *dp_sum_scratch(HERE),
            *again,
            *again,
            pltpu.VMEM((8, VEC, 128), F32),
            pltpu.VMEM((8, VEC, 128), F32),
            pltpu.VMEM((VEC, 128), F32),
            pltpu.VMEM((VEC, 128), F32),
            *eight(),
            *eight(),
            pltpu.SemaphoreType.DMA((1,)),
            pltpu.SemaphoreType.DMA((1,)),
            pltpu.SemaphoreType.DMA((16,)),
        ],
        compiler_params=pltpu.CompilerParams(
            collective_id=1, has_side_effects=True, vmem_limit_bytes=60 * 1024 * 1024
        ),
    )(*arrays)


def results(*refs):
    half = len(refs) // 2
    for one, out in zip(refs[:half], refs[half:]):
        out[...] = one[...]


def call_results(arrays):
    return pl.pallas_call(
        results,
        name="results",
        out_shape=[jax.ShapeDtypeStruct(*one) for one in OUTS],
        in_specs=[VM] * len(OUTS),
        out_specs=[VM] * len(OUTS),
    )(*arrays)


def local(
    hidden_in, norm_gain, w_query, w_forget, w_input, w_outgate, lower_bounds, layer_index, group_gain,
    w_output, ffn_gain, w_gate, w_up, w_down, seq_lengths, grad_out,
):
    norm_row, ffn_row, group_row = norm_gain.reshape(1, D), ffn_gain.reshape(1, D), group_gain.reshape(1, KDIM)
    raw, xn, gated, mixed, states, run, total, w_all, wt_all, hn, resid, wg, wu, wd = call_forward(
        hidden_in, norm_row, w_query, w_forget, w_input, w_outgate, w_output, lower_bounds, layer_index, seq_lengths,
        group_row, ffn_row, w_gate.T, w_up.T, w_down,
    )
    (
        block_out, grad_in, grad_query, grad_forget, grad_input, grad_outgate, grad_output, grad_bounds,
        grad_norm, grad_group, grad_ffn, mean, grad_gate, grad_up, grad_down,
    ) = call_results(call_backward(
        hn, grad_out, wg, wu, wd, resid, ffn_row, wt_all, raw, run, mixed, states, gated, xn, w_all, hidden_in,
        total, norm_row, group_row, lower_bounds, layer_index, seq_lengths,
    ))
    return (
        block_out,
        grad_in,
        grad_norm.reshape(D),
        grad_query,
        grad_forget,
        grad_input,
        grad_outgate,
        grad_bounds,
        grad_group.reshape(KDIM),
        grad_output,
        grad_ffn.reshape(D),
        grad_gate.T,
        grad_up.T,
        grad_down,
        mean[0, 0:1],
    )


def solution(mesh):
    return jax.shard_map(
        local,
        mesh=mesh,
        in_specs=(
            P("dp", None),
            P(),
            P("dp", "head"),
            P("dp", "head"),
            P("dp", "head"),
            P("dp", "head"),
            P(None, "head"),
            P(),
            P(),
            P("head", "dp"),
            P(),
            P("dp", "head"),
            P("dp", "head"),
            P("head", "dp"),
            P(),
            P("dp", None),
        ),
        out_specs=(
            P(("dp", "head"), None),
            P(("dp", "head"), None),
            P(),
            P("dp", "head"),
            P("dp", "head"),
            P("dp", "head"),
            P("dp", "head"),
            P(None, "head"),
            P(),
            P("head", "dp"),
            P(),
            P("dp", "head"),
            P("dp", "head"),
            P("head", "dp"),
            P(),
        ),
        check_vma=False,
    )
```

```python
from functools import partial

import jax
import jax.numpy as jnp
from jax import lax
from jax.experimental import pallas as pl
from jax.experimental.pallas import tpu as pltpu
from jax.sharding import PartitionSpec as P

D = 2048
KDIM = 128
CHUNK = 128
TOK = 512
CHUNKS = TOK // CHUNK
HERE = 256
FFH = 704
NSEQ = 12
NHEAD = 8
ROWS = TOK // NHEAD
EPS = 1e-06
F32 = jnp.float32
BF16 = jnp.bfloat16
MESH = pl.DeviceIdType.MESH
VM = pl.BlockSpec(memory_space=pltpu.VMEM)
SM = pl.BlockSpec(memory_space=pltpu.SMEM)
HB = pl.BlockSpec(memory_space=pl.ANY)


class Spot:
    def __init__(self):
        self.dp = lax.axis_index("dp")
        self.head = lax.axis_index("head")
        self.core = lax.rem(self.dp, 2)
        self.chip = lax.div(self.dp, 2)
        self.xh = lax.rem(self.chip, 2)
        self.z = lax.div(self.chip, 2)
        self.xl = lax.rem(self.head, 2)
        self.y = lax.div(self.head, 2)

    def at(self, dz, xh, core):
        return (lax.rem(self.z + dz, 4) * 2 + xh) * 2 + core

    def y_at(self, k):
        return lax.rem(self.y + k, 4)

    @property
    def beside(self):
        return {"head": self.y * 2 + 1 - self.xl}

    def lines(self):
        return [self.beside] + [{"head": self.y_at(k) * 2 + self.xl} for k in (1, 2, 3)]

    @property
    def sibling(self):
        return {"dp": self.chip * 2 + 1 - self.core}

    def chips(self):
        return [{"dp": lax.rem(self.chip + k, 8) * 2 + self.core} for k in range(1, 8)]

    def heads(self):
        return [{"head": lax.rem(self.head + k, NHEAD)} for k in range(1, NHEAD)]


def greet(ids):
    barrier = pltpu.get_barrier_semaphore()
    for one in ids:
        pl.semaphore_signal(barrier, inc=1, device_id=one, device_id_type=MESH)
    return lambda: pl.semaphore_wait(barrier, len(ids))


def rcopy(src, dst, send, recv, where):
    return pltpu.make_async_remote_copy(
        src_ref=src, dst_ref=dst, send_sem=send, recv_sem=recv, device_id=where, device_id_type=MESH
    )


GATHER_SENDS = 17


class Gather:
    def __init__(self, spot, g, send, recv, half, columns=0):
        self.spot, self.g, self.s, self.r, self.h = spot, g, send, recv, half
        self.columns, self.middle = columns, (columns or 128) // 2

    def block(self, d, start=0, rows=0):
        if self.columns:
            rows = rows or self.columns
            return self.g.at[pl.ds(start, rows), pl.ds(pl.multiple_of(d * 128, 128), 128)]
        return self.g.at[pl.ds(pl.multiple_of(d * 128 + start, 64), rows or 128), :]

    def push(self, d, to, k):
        rcopy(self.block(d), self.block(d), self.s.at[k], self.r.at[d], {"dp": to}).start()

    def push_half(self, d, to, k, xh, part):
        b = self.block(d, part * self.middle, self.middle)
        rcopy(b, b, self.s.at[k], self.h.at[2 * xh + part], {"dp": to}).start()

    def arrived(self, d):
        b = self.block(d)
        rcopy(b, b, self.s.at[0], self.r.at[d], self.spot.sibling).wait_recv()

    def arrived_halves(self, d, xh):
        for part in range(2):
            b = self.block(d, part * self.middle, self.middle)
            rcopy(b, b, self.s.at[0], self.h.at[2 * xh + part], self.spot.sibling).wait_recv()

    def first(self):
        p = self.spot
        self.push(p.dp, p.at(0, 1 - p.xh, p.core), 0)
        self.push(p.dp, p.at(1, p.xh, p.core), 1)
        self.push(p.dp, p.at(3, p.xh, p.core), 2)
        self.push(p.dp, p.at(0, p.xh, 1 - p.core), 3)

    def second(self):
        p = self.spot
        b = p.at(0, 1 - p.xh, p.core)
        self.arrived(b)
        self.push(b, p.at(1, p.xh, p.core), 4)
        self.push(b, p.at(3, p.xh, p.core), 5)
        self.push(b, p.at(0, p.xh, 1 - p.core), 6)

    def third(self):
        p = self.spot
        for i, h in enumerate((p.xh, 1 - p.xh)):
            b = p.at(3, h, p.core)
            self.arrived(b)
            self.push_half(b, p.at(1, p.xh, p.core), 7 + i, h, 0)
            self.push(b, p.at(0, p.xh, 1 - p.core), 9 + i)
            b = p.at(1, h, p.core)
            self.arrived(b)
            self.push_half(b, p.at(3, p.xh, p.core), 11 + i, h, 1)
            self.push(b, p.at(0, p.xh, 1 - p.core), 13 + i)

    def fourth(self):
        p = self.spot
        for i, h in enumerate((p.xh, 1 - p.xh)):
            b = p.at(2, h, p.core)
            self.arrived_halves(b, h)
            self.push(b, p.at(0, p.xh, 1 - p.core), 15 + i)

    def last(self):
        p = self.spot
        for dz in range(4):
            for h in range(2):
                self.arrived(p.at(dz, h, 1 - p.core))
        half = self.block(0, 0, self.middle)
        for k in range(GATHER_SENDS):
            b = half if k in (7, 8, 11, 12) else self.block(0)
            rcopy(b, b, self.s.at[k], self.r.at[0], p.sibling).wait_send()


class WideGather(Gather):
    def block(self, d, start=0, rows=0):
        row, column = lax.rem(d, 8) * 128 + start, lax.div(d, 8) * 1024
        return self.g.at[pl.ds(pl.multiple_of(row, 64), rows or 128), pl.ds(pl.multiple_of(column, 1024), 1024)]

    def tile(self, d, k):
        row, column = lax.rem(d, 8) * 128, lax.div(d, 8) * 1024 + 256 * k
        return self.g.at[pl.ds(pl.multiple_of(row, 128), 128), pl.ds(pl.multiple_of(column, 256), 256)]


def gather_semaphores():
    return [
        pltpu.SemaphoreType.DMA((GATHER_SENDS,)),
        pltpu.SemaphoreType.DMA((16,)),
        pltpu.SemaphoreType.DMA((4,)),
    ]


NN = (((1,), (0,)), ((), ()))
NT = (((1,), (1,)), ((), ()))
TN = (((0,), (0,)), ((), ()))


def mm(a, b, dims):
    return lax.dot_general(a, b, dims, preferred_element_type=F32)


def halves(a):
    high = a.astype(BF16)
    return high, (a - high.astype(F32)).astype(BF16)


def mm2(a, b, dims):
    return mm(a[0], b, dims) + mm(a[1], b, dims)


def mm3(a, b, dims):
    return mm(a[0], b[0], dims) + (mm(a[0], b[1], dims) + mm(a[1], b[0], dims))


def triangle(lower):
    rows = lax.broadcasted_iota(jnp.int32, (CHUNK, CHUNK), 0)
    columns = lax.broadcasted_iota(jnp.int32, (CHUNK, CHUNK), 1)
    return (rows >= columns if lower else rows <= columns).astype(BF16)


def summed_rows(lower, x):
    high = x.astype(BF16)
    rest = x - high.astype(F32)
    middle = rest.astype(BF16)
    low = (rest - middle.astype(F32)).astype(BF16)
    t = triangle(lower)
    return mm(t, high, NN) + (mm(t, middle, NN) + mm(t, low, NN))


class Segments:
    def __init__(self, spot, seq):
        self.starts = []
        total = jnp.int32(0)
        for i in range(NSEQ):
            self.starts.append(total)
            total = total + seq[i]
        self.first = spot.dp * TOK

    def of(self, position):
        found = jnp.where(position >= self.starts[0], 1, 0)
        for s in self.starts[1:]:
            found = found + jnp.where(position >= s, 1, 0)
        return found - 1

    def column(self, c):
        return self.of(self.first + c * CHUNK + lax.broadcasted_iota(jnp.int32, (CHUNK, KDIM), 0))

    def row(self, c):
        return self.of(self.first + c * CHUNK + lax.broadcasted_iota(jnp.int32, (CHUNK, KDIM), 1))

    def before(self, c):
        return self.of(self.first + c * CHUNK - 1)

    def final(self, c):
        return self.of(self.first + (c + 1) * CHUNK - 1)


def lower_bound(lb, layer):
    x = lb[...]
    e = jnp.exp(x - jnp.max(x, axis=0, keepdims=True))
    soft = e / jnp.sum(e, axis=0, keepdims=True)
    depth = lax.broadcasted_iota(jnp.int32, x.shape, 0)
    picked = jnp.where((depth >= 1) & (depth <= layer), 1.0, 0.0)
    return soft, picked, jnp.sum(soft * picked, axis=0, keepdims=True)


def sigmoid(x):
    return lax.logistic(x)


def slope(x, s):
    return s * (1.0 + x * (1.0 - s))


class Exchange:
    def __init__(self, spot, msg, sib, slots, give, take, send, recv, backward):
        self.p, self.msg, self.sib, self.slots = spot, msg, sib, slots
        self.give, self.take, self.s, self.r, self.back = give, take, send, recv, backward

    def to_sibling(self):
        p = self.p
        rcopy(self.msg.at[1 - p.core], self.sib, self.s.at[7], self.r.at[8], p.sibling).start()

    def to_chips(self):
        p = self.p
        rcopy(self.sib, self.sib, self.s.at[7], self.r.at[8], p.sibling).wait_recv()
        mine, other = self.msg[p.core], self.sib[...]
        zero = p.core == 0
        one, two = jnp.where(zero, mine, other), jnp.where(zero, other, mine)
        near, far = (two, one) if self.back else (one, two)
        self.near = near
        state = near[0:128] * far[128:129] + far[0:128]
        rate = near[128:136] * far[128:136]
        high = rate.astype(BF16).astype(F32)
        self.slots[p.chip, 0:128, :] = state.astype(BF16)
        self.slots[p.chip, 128:144, :] = jnp.concatenate([high, rate - high], axis=0).astype(BF16)
        for k, to in enumerate(p.chips()):
            rcopy(self.slots.at[p.chip], self.slots.at[p.chip], self.s.at[k], self.r.at[p.chip], to).start()

    def result(self, out):
        p = self.p
        for k in range(1, 8):
            chip = lax.rem(p.chip + k, 8)
            rcopy(self.slots.at[chip], self.slots.at[chip], self.s.at[0], self.r.at[chip], p.sibling).wait_recv()
        state = jnp.zeros((128, 128), F32)
        for k in range(7, 0, -1) if self.back else range(7):
            m = self.slots[k].astype(F32)
            after = state * (m[128:129] + m[136:137]) + m[0:128]
            state = jnp.where(k > p.chip if self.back else k < p.chip, after, state)
        second = state * self.near[128:129] + self.near[0:128]
        is_first = p.core == (1 if self.back else 0)
        self.give[...] = jnp.where(is_first, second, state)
        move = rcopy(self.give, self.take, self.s.at[8], self.r.at[9], p.sibling)
        move.start()
        out[p.core] = jnp.where(is_first, state, second)
        move.wait_recv()
        out[1 - p.core] = self.take[...]

    def finish(self):
        p = self.p
        for k in range(7):
            rcopy(self.slots.at[0], self.slots.at[0], self.s.at[k], self.r.at[0], p.sibling).wait_send()
        rcopy(self.sib, self.sib, self.s.at[7], self.r.at[8], p.sibling).wait_send()
        rcopy(self.give, self.take, self.s.at[8], self.r.at[9], p.sibling).wait_send()


def exchange_scratch():
    return [
        pltpu.VMEM((2, 136, 128), F32),
        pltpu.VMEM((136, 128), F32),
        pltpu.VMEM((8, 144, 128), BF16),
        pltpu.VMEM((128, 128), F32),
        pltpu.VMEM((128, 128), F32),
        pltpu.SemaphoreType.DMA((9,)),
        pltpu.SemaphoreType.DMA((10,)),
    ]


def gates(raw, bound, rows):
    query_raw = raw[rows, 0:256]
    logistic = sigmoid(raw[rows, 256:512])
    forget = bound + (1.0 - bound) * logistic
    query = (query_raw * sigmoid(query_raw)).astype(BF16)
    keys = (1.0 - forget).astype(BF16)
    values = raw[rows, 512:768].astype(BF16)
    return logistic, forget, query, keys, values


HALF = D // 2


class HeadSum:
    def __init__(self, spot, ps, slots, send, recv):
        self.p, self.ps, self.slots, self.s, self.r = spot, ps, slots, send, recv

    def left_of(self, start, rows=ROWS):
        return self.slots.at[pl.ds(start, rows), pl.ds(0, HALF)]

    def right_of(self, start, rows=ROWS):
        return self.slots.at[pl.ds(start, rows), pl.ds(HALF, HALF)]

    def part(self, h, rows, right):
        return self.ps.at[pl.ds(pl.multiple_of(h * ROWS, ROWS), rows), pl.ds(HALF if right else 0, HALF)]

    def left_x(self, k):
        p = self.p
        h = p.y_at(k) * 2 + 1 - p.xl
        return rcopy(self.part(h, ROWS, False), self.left_of(64 * k), self.s.at[k], self.r.at[k], p.beside)

    def left_y(self, k):
        p = self.p
        to = {"head": p.y_at(k) * 2 + p.xl}
        return rcopy(self.left_of(64 * k), self.left_of(192 + 64 * k), self.s.at[3 + k], self.r.at[3 + k], to)

    def right_y(self, k):
        p = self.p
        to = {"head": p.y_at(k) * 2 + p.xl}
        return rcopy(
            self.part(p.y_at(k) * 2, 128, True), self.right_of(128 * k - 128, 128), self.s.at[6 + k], self.r.at[6 + k], to
        )

    def right_x(self):
        return rcopy(self.right_of(384), self.right_of(448), self.s.at[10], self.r.at[10], self.p.beside)

    def send_left(self):
        for k in (2, 1, 3, 0):
            self.left_x(k).start()

    def send_right(self):
        for k in (2, 1, 3):
            self.right_y(k).start()

    def send(self):
        self.send_right()
        self.send_left()

    def middle(self):
        p = self.p
        for k in (2, 1, 3, 0):
            self.left_x(k).wait_recv()
            mine = self.part(p.y_at(k) * 2 + p.xl, ROWS, False)
            one = self.left_of(64 * k)
            one[...] = (one[...].astype(F32) + mine[...].astype(F32)).astype(BF16)
            if k:
                self.left_y(k).start()
        for k in (1, 3, 2):
            self.right_y(k).wait_recv()

        def total(xl):
            one = self.part(p.y * 2 + xl, ROWS, True)[...].astype(F32)
            for k in range(3):
                rows = pl.ds(pl.multiple_of(128 * k + xl * ROWS, ROWS), ROWS)
                one = one + self.slots[rows, HALF:].astype(F32)
            return one.astype(BF16)

        self.slots[384:448, HALF:] = total(1 - p.xl)
        self.right_x().start()
        self.slots[448:512, 0:HALF] = total(p.xl)

    def collect(self):
        for k in (1, 3, 2):
            self.left_y(k).wait_recv()
        self.right_x().wait_recv()

    def rows(self, start, count):
        def at(row, left):
            rows = pl.ds(pl.multiple_of(row + start, 16), count)
            return self.slots[rows, 0:HALF].astype(F32) if left else self.slots[rows, HALF:].astype(F32)

        left = (at(0, True) + at(256, True)) + (at(320, True) + at(384, True))
        return jnp.concatenate([left, at(448, True) + at(448, False)], axis=1)

    def finish(self):
        for k in range(4):
            self.left_x(k).wait_send()
        for k in (1, 2, 3):
            self.left_y(k).wait_send()
            self.right_y(k).wait_send()
        self.right_x().wait_send()


class LateHeadSum:
    def __init__(self, spot, ps, slots, send, recv):
        self.p, self.ps, self.slots, self.s, self.r = spot, ps, slots, send, recv

    def block(self, ref, start, rows=ROWS):
        return ref.at[pl.ds(pl.multiple_of(start, ROWS), rows), :]

    def along_y(self, k):
        p = self.p
        y = p.y_at(k)
        return rcopy(
            self.block(self.ps, y * 128, 128), self.block(self.slots, 128 * k - 128, 128),
            self.s.at[k], self.r.at[k], {"head": y * 2 + p.xl},
        )

    def along_x(self):
        return rcopy(self.block(self.slots, 384), self.block(self.slots, 448), self.s.at[0], self.r.at[0], self.p.beside)

    def send(self):
        for k in (2, 1, 3):
            self.along_y(k).start()

    def part(self, xl, start, count):
        p = self.p
        one = self.ps[pl.ds(pl.multiple_of((p.y * 2 + xl) * ROWS + start, 16), count), :].astype(F32)
        for k in range(3):
            rows = pl.ds(pl.multiple_of(128 * k + xl * ROWS + start, 16), count)
            one = one + self.slots[rows, :].astype(F32)
        return one

    def middle(self):
        for k in (1, 3, 2):
            self.along_y(k).wait_recv()

        @pl.loop(0, 4)
        def _(i):
            rows = pl.ds(pl.multiple_of(384 + i * 16, 16), 16)
            self.slots[rows, :] = self.part(1 - self.p.xl, i * 16, 16).astype(BF16)

        self.along_x().start()

    def collect(self):
        self.along_x().wait_recv()

    def rows(self, start, count):
        rows = pl.ds(pl.multiple_of(448 + start, 16), count)
        return self.part(self.p.xl, start, count) + self.slots[rows, :].astype(F32)

    def finish(self):
        for k in (1, 2, 3):
            self.along_y(k).wait_send()
        self.along_x().wait_send()


class HeadGather:
    def __init__(self, spot, full, send, recv):
        self.p, self.full, self.s, self.r = spot, full, send, recv

    def block(self, h, right):
        return self.full.at[pl.ds(pl.multiple_of(h * ROWS, ROWS), ROWS), pl.ds(HALF if right else 0, HALF)]

    def along_y(self, k, xl, right, i):
        p = self.p
        b = self.block(p.y * 2 + xl, right)
        return rcopy(b, b, self.s.at[i + k], self.r.at[i + k], {"head": p.y_at(k) * 2 + p.xl})

    def beside(self, k, right, i):
        p = self.p
        b = self.block(p.y_at(k) * 2 + p.xl, right)
        return rcopy(b, b, self.s.at[i + k], self.r.at[i + k], p.beside)

    def send(self):
        p = self.p
        self.beside(0, False, 0).start()
        for k in (2, 1, 3):
            self.along_y(k, p.xl, True, 0).start()
        self.beside(0, True, 4).start()
        for k in (2, 1, 3):
            self.along_y(k, p.xl, False, 8).start()

    def middle(self):
        p = self.p
        self.beside(0, False, 0).wait_recv()
        for k in (2, 1, 3):
            self.along_y(k, 1 - p.xl, False, 11).start()
        for k in (1, 3, 2):
            self.along_y(4 - k, p.xl, True, 0).wait_recv()
            self.beside(k, True, 4).start()

    def collect(self):
        p = self.p
        self.beside(0, True, 4).wait_recv()
        for k in (1, 3, 2):
            self.along_y(k, p.xl, False, 8).wait_recv()
            self.along_y(k, 1 - p.xl, False, 11).wait_recv()
            self.beside(k, True, 4).wait_recv()

    def finish(self):
        p = self.p
        self.beside(0, False, 0).wait_send()
        for k in range(4):
            self.beside(k, True, 4).wait_send()
        for k in (1, 2, 3):
            self.along_y(k, p.xl, True, 0).wait_send()
            self.along_y(k, p.xl, False, 8).wait_send()
            self.along_y(k, 1 - p.xl, False, 11).wait_send()


def sixteen():
    return [pltpu.SemaphoreType.DMA((16,)), pltpu.SemaphoreType.DMA((16,))]


def eight():
    return [pltpu.SemaphoreType.DMA((8,)), pltpu.SemaphoreType.DMA((8,))]


class DpSum:
    def __init__(self, spot, rows, gs, cr, zr, xs, xr, send, recv):
        n = pl.ds(0, rows)
        self.rows, self.p = rows, spot
        self.gs, self.cr, self.zr = gs.at[:, :, n, :], cr.at[:, n, :], zr.at[:, :, n, :]
        self.xs, self.xr, self.s, self.r = xs.at[n, :], xr.at[n, :], send, recv

    def pair(self, i):
        p = self.p
        two = pl.ds(2 * i, 2)
        return rcopy(self.gs.at[1 - p.core, two], self.cr.at[two], self.s.at[i], self.r.at[i], p.sibling)

    def to_sibling(self):
        for i in range(4):
            self.pair(i).start()

    def half(self, part):
        return pl.ds(part * (self.rows // 2), self.rows // 2)

    def along_z(self, d, block, part, slot, i):
        p = self.p
        z = lax.rem(p.z + block, 4)
        where = {"dp": (lax.rem(p.z + d, 4) * 2 + p.xh) * 2 + p.core}
        source = self.gs.at[p.core, pl.ds(z * 2, 2), self.half(part), :]
        return rcopy(source, self.zr.at[slot, :, self.half(part), :], self.s.at[4 + i], self.r.at[4 + i], where)

    def far(self, part):
        return self.along_z(3 if part else 1, 2, part, 2, part)

    def near(self, part):
        return self.along_z(3, 3, 0, 1, 2) if part else self.along_z(1, 1, 1, 0, 3)

    def joined(self, part):
        return self.along_z(3, 3, 1, 1, 4) if part else self.along_z(1, 1, 0, 0, 5)

    def to_z(self):
        p = self.p
        for i in range(4):
            self.pair(i).wait_recv()

        @pl.loop(0, 8)
        def _(k):
            self.gs[p.core, k] = (self.gs[p.core, k].astype(F32) + self.cr[k].astype(F32)).astype(BF16)

        for part in range(2):
            self.far(part).start()
        for part in range(2):
            self.near(part).start()

    def join(self):
        p = self.p
        for part in range(2):
            self.far(part).wait_recv()
            z = lax.rem(p.z + (3 if part else 1), 4)
            for h in range(2):
                mine = self.gs.at[p.core, z * 2 + h, self.half(part), :]
                other = self.zr.at[2, h, self.half(part), :]
                mine[...] = (mine[...].astype(F32) + other[...].astype(F32)).astype(BF16)
            self.joined(part).start()

    def last_move(self):
        p = self.p
        where = {"dp": (p.z * 2 + 1 - p.xh) * 2 + p.core}
        return rcopy(self.xs, self.xr, self.s.at[10], self.r.at[10], where)

    def to_x(self, put):
        p = self.p
        for part in range(2):
            self.near(part).wait_recv()
            self.joined(part).wait_recv()

        def total(h):
            one = self.gs[p.core, 2 * p.z + h].astype(F32)
            for i in range(2):
                one = one + self.zr[i, h].astype(F32)
            return one

        self.xs[...] = total(1 - p.xh).astype(BF16)
        self.last_move().start()
        put(total(p.xh))

    def end(self, add):
        self.last_move().wait_recv()
        add(self.xr[...].astype(F32))

    def finish(self):
        for i in range(4):
            self.pair(i).wait_send()
        for part in range(2):
            self.far(part).wait_send()
            self.near(part).wait_send()
            self.joined(part).wait_send()
        self.last_move().wait_send()


def dp_sum_scratch(rows):
    return [
        pltpu.VMEM((2, 8, rows, 128), BF16),
        pltpu.VMEM((8, rows, 128), BF16),
        pltpu.VMEM((3, 2, rows, 128), BF16),
        pltpu.VMEM((rows, 128), BF16),
        pltpu.VMEM((rows, 128), BF16),
        *sixteen(),
    ]


def products(left_turned, right, gs):
    @pl.loop(0, 8)
    def _(k):
        columns = pl.ds(pl.multiple_of(k * 256, 256), 256)
        both = mm(left_turned[...], right[:, columns], NN).astype(BF16)
        gs[0, k] = both[:, 0:128]
        gs[1, k] = both[:, 128:256]


def products_turned(left, first, second, gs):
    @pl.loop(0, 8)
    def _(k):
        turned = left[:, pl.ds(pl.multiple_of(k * 256, 256), 256)]
        for i, right in enumerate((first, second)):
            both = mm(turned, right[...], TN).astype(BF16)
            for q in range(2):
                rows = slice(256 * i + 128 * q, 256 * i + 128 * (q + 1))
                gs[0, k, rows, :] = both[0:128, 128 * q : 128 * (q + 1)]
                gs[1, k, rows, :] = both[128:256, 128 * q : 128 * (q + 1)]


def write(ref):
    def put(x):
        ref[...] = x

    return put


def accumulate(ref):
    def add(x):
        ref[...] += x

    return add


VEC = 40


class Total:
    def __init__(self, spot, vec, h_slots, c_slots, own, other, h_s, h_r, c_s, c_r, k_s, k_r):
        self.p, self.vec, self.hs, self.cs, self.own, self.other = spot, vec, h_slots, c_slots, own, other
        self.h_s, self.h_r, self.c_s, self.c_r, self.k_s, self.k_r = h_s, h_r, c_s, c_r, k_s, k_r

    def send(self):
        p = self.p
        self.cs[p.chip] = self.vec[...]
        for k, to in enumerate(p.chips()):
            rcopy(self.cs.at[p.chip], self.cs.at[p.chip], self.c_s.at[k], self.c_r.at[p.chip], to).start()

    def middle(self):
        p = self.p
        for k in range(1, 8):
            chip = lax.rem(p.chip + k, 8)
            rcopy(self.cs.at[chip], self.cs.at[chip], self.c_s.at[0], self.c_r.at[chip], p.sibling).wait_recv()
        total = self.cs[0]
        for k in range(1, 8):
            total = total + self.cs[k]
        self.own[...] = total
        rcopy(self.own, self.other, self.k_s, self.k_r, p.sibling).start()

    def late(self):
        p = self.p
        rcopy(self.own, self.other, self.k_s, self.k_r, p.sibling).wait_recv()
        self.hs[p.head] = self.own[...] + self.other[...]
        for k in range(1, NHEAD):
            h = lax.rem(p.head + k, NHEAD)
            rcopy(self.hs.at[p.head], self.hs.at[p.head], self.h_s.at[k], self.h_r.at[p.head], {"head": h}).start()

    def result(self):
        p = self.p
        for k in range(1, NHEAD):
            h = lax.rem(p.head + k, NHEAD)
            rcopy(self.hs.at[h], self.hs.at[h], self.h_s.at[0], self.h_r.at[h], p.sibling).wait_recv()
        total = self.hs[0]
        for h in range(1, NHEAD):
            total = total + self.hs[h]
        per_head = lax.broadcasted_iota(jnp.int32, (VEC, 128), 0) >= 34
        return jnp.where(per_head, self.hs[p.head], total)

    def finish(self):
        p = self.p
        for k in range(1, NHEAD):
            rcopy(self.hs.at[0], self.hs.at[0], self.h_s.at[k], self.h_r.at[0], p.sibling).wait_send()
        for k in range(7):
            rcopy(self.cs.at[0], self.cs.at[0], self.c_s.at[k], self.c_r.at[0], p.sibling).wait_send()
        rcopy(self.own, self.other, self.k_s, self.k_r, p.sibling).wait_send()


def layer_block(
    hid, dy_in, wq, wf, wi, wo, w_output, wg_in, wu_in, wd_in, gain, lb, group_gain, ffn_gain, layer, seq,
    block_out, grad_in, out_query, out_forget, out_input, out_outgate, out_output, out_bounds,
    out_norm, out_group, out_ffn, out_mean, out_gate, out_up, out_down, xn_out, w_out,
    ps, slots, hn, wide, wg, wu, wd, wt, raw, hid_rows, gated, gated_t, mixed, run, states, update, resid, d_resid,
    hidden, dg, du, hidden_t, dg_t, du_t, draw, d_mixed, d_query, d_keys, d_values, decay, incoming, vec,
    norm_terms, ffn_terms, group_total, bound_total, total,
    msg, sib, slots3, give, take, ex_send, ex_recv, msg2, sib2, slots4, give2, take2, ex2_send, ex2_recv,
    rs0_s, rs0_r, ag0_s, ag0_r, rs_s, rs_r, ag_s, ag_r, rs1_s, rs1_r, rs2_s, rs2_r,
    ws, wr, wh, os, or_, oh, s0, r0, h0, s1, r1, h1, s2, r2, h2,
    a0, a1, a2, a3, a4, a5, a6, b0, b1, b2, b3, b4, b5, b6, c0, c1, c2, c3, c4, c5, c6,
    e0, e1, e2, e3, e4, e5, e6, f3, f4, f5, f6, g3, g4, g5, g6,
    t0, t1, t2, t3, t4, t5, t6, t7, t8, t9, local_sem,
):
    dy, db, xn = wide.at[0:TOK], wide.at[TOK : 2 * TOK], hn
    used = []

    def load(source, to):
        move = pltpu.make_async_copy(source, to, local_sem.at[len(used)])
        move.start()
        used.append(move)
        return move

    def put(low, high):
        def write_four(x):
            low[:, 0:128], low[:, 128:256] = x[0:128], x[128:256]
            high[:, 0:128], high[:, 128:256] = x[256:384], x[384:512]

        return write_four

    def add_to(low, high):
        def add(x):
            low[:, 0:128] += x[0:128]
            low[:, 128:256] += x[128:256]
            high[:, 0:128] += x[256:384]
            high[:, 128:256] += x[384:512]

        return add

    p = Spot()
    arrive = greet(p.chips() + [p.sibling] + p.heads())
    own = pl.multiple_of(p.head * ROWS, ROWS)
    mine = pl.ds(pl.multiple_of(p.dp * 128, 128), 128)
    gather = WideGather(p, wide, ws, wr, wh)
    loads = [load(one, gather.tile(p.dp, k)) for k, one in enumerate((wq, wf, wi, wo))]
    loads.append(load(hid, ps))
    own_blocks = [load(w_output, wt.at[:, mine])]
    own_blocks += [load(one, full.at[:, mine]) for one, full in ((wg_in, wg), (wu_in, wu), (wd_in, wd))]
    own_rows = load(hid.at[pl.ds(own, ROWS), :], hid_rows)
    for move in loads[:4]:
        move.wait()
    arrive()
    gather.first()
    loads[4].wait()
    later = Gather(p, wt, os, or_, oh, HERE)
    gathers = [Gather(p, wg, s0, r0, h0, FFH), Gather(p, wu, s1, r1, h1, FFH), Gather(p, wd, s2, r2, h2, FFH)]

    @pl.loop(0, 8)
    def _(i):
        rows = pl.ds(pl.multiple_of(i * 64, 64), 64)
        x = ps[rows, :].astype(F32)
        scale = lax.rsqrt(jnp.mean(x * x, axis=-1, keepdims=True) + EPS)
        xn[rows, :] = (x * scale * gain[...]).astype(BF16)

    gather.second()
    gather.third()
    gather.fourth()
    for move in own_blocks:
        move.wait()
    later.first()
    gathers[0].first()
    gather.last()
    spills = [load(xn, xn_out), load(wide, w_out)]

    @pl.loop(0, 4)
    def _(j):
        columns = pl.ds(pl.multiple_of(j * 256, 256), 256)
        other = pl.ds(pl.multiple_of(1024 + j * 256, 256), 256)
        raw[:, columns] = mm(xn[:, 0:1024], wide[:, columns], NN) + mm(xn[:, 1024:2048], wide[:, other], NN)

    later.second()
    segments = Segments(p, seq)
    soft, picked, bound = lower_bound(lb, layer[0])
    total[...] = jnp.zeros_like(total)

    @pl.loop(0, CHUNKS)
    def _(c):
        rows = pl.ds(pl.multiple_of(c * CHUNK, CHUNK), CHUNK)
        logistic, forget, query, keys, values = gates(raw, bound, rows)
        total[...] += jnp.sum(forget, axis=0, keepdims=True)
        running = summed_rows(True, jnp.log(forget))
        run[rows, :] = running
        middle, ending = running[63:64], running[127:128]
        lifted = query.astype(F32) * jnp.exp(running - middle)
        lowered = keys.astype(F32) * jnp.exp(middle - running)
        tail = keys.astype(F32) * jnp.exp(ending - running)
        column, row = segments.column(c), segments.row(c)
        linked = (column == row) & (
            lax.broadcasted_iota(jnp.int32, (CHUNK, CHUNK), 0)
            >= lax.broadcasted_iota(jnp.int32, (CHUNK, CHUNK), 1)
        )
        final = segments.final(c)
        rate = jnp.exp(ending) * jnp.where(final == segments.before(c), 1.0, 0.0)
        decay[c] = jnp.broadcast_to(rate, (8, HERE))
        ends = jnp.where(column == final, 1.0, 0.0)
        for h in range(2):
            lanes = slice(h * 128, (h + 1) * 128)
            scores = mm3(halves(lifted[:, lanes]), halves(lowered[:, lanes]), NT)
            scores = jnp.where(linked, scores, 0.0)
            mixed[rows, lanes] = mm2(halves(scores), values[:, lanes], NN)
            high, low = halves(tail[:, lanes] * ends)
            update[h, c] = mm(values[:, lanes], high, TN) + mm(values[:, lanes], low, TN)

    for h in range(2):
        lanes = slice(h * 128, (h + 1) * 128)
        state, rate = update[h, 0], decay[0, 0:1, lanes]
        for c in range(1, CHUNKS):
            state = state * decay[c, 0:1, lanes] + update[h, c]
            rate = rate * decay[c, 0:1, lanes]
        msg[h, 0:128, :] = state
        msg[h, 128:136, :] = jnp.broadcast_to(rate, (8, 128))
    exchange = Exchange(p, msg, sib, slots3, give, take, ex_send, ex_recv, False)
    exchange.to_sibling()
    exchange.to_chips()
    later.third()
    gathers[1].first()
    gathers[2].first()
    gathers[0].second()
    later.fourth()
    exchange.result(incoming)
    gathers[1].second()
    gathers[2].second()
    for h in range(2):
        lanes = slice(h * 128, (h + 1) * 128)
        state = incoming[h]
        states[h, 0] = state
        for c in range(CHUNKS):
            state = state * decay[c, 0:1, lanes] + update[h, c]
            states[h, c + 1] = state

    @pl.loop(0, CHUNKS)
    def _(c):
        rows = pl.ds(pl.multiple_of(c * CHUNK, CHUNK), CHUNK)
        carried = jnp.where(segments.column(c) == segments.before(c), 1.0, 0.0)
        for h in range(2):
            lanes = slice(h * 128, (h + 1) * 128)
            query_raw = raw[rows, h * 128 : (h + 1) * 128]
            query = (query_raw * sigmoid(query_raw)).astype(BF16).astype(F32)
            reach = query * jnp.exp(run[rows, lanes]) * carried
            x = mixed[rows, lanes] + mm3(halves(reach), halves(states[h, c]), NT)
            mixed[rows, lanes] = x
            scale = lax.rsqrt(jnp.mean(x * x, axis=-1, keepdims=True) + EPS)
            gate = raw[rows, 768 + h * 128 : 768 + (h + 1) * 128]
            gated[rows, lanes] = (x * scale * group_gain[...] * (gate * sigmoid(gate))).astype(BF16)

    later.last()

    for move in spills:
        move.wait()
    dy_load = load(dy_in, dy)
    scatter0 = HeadSum(p, ps, slots, rs0_s, rs0_r)
    for start, send in ((HALF, scatter0.send_right), (0, scatter0.send_left)):

        @pl.loop(0, 4)
        def _(j):
            columns = pl.ds(pl.multiple_of(start + j * 256, 256), 256)
            ps[:, columns] = mm(gated[...], wt[:, columns], NN).astype(BF16)

        send()
    scatter0.middle()
    for g in gathers:
        g.third()
    scatter0.collect()
    own_rows.wait()

    @pl.loop(0, 4)
    def _(i):
        rows = pl.ds(pl.multiple_of(i * 16, 16), 16)
        here = pl.ds(pl.multiple_of(own + i * 16, 16), 16)
        x = hid_rows[rows, :].astype(F32) + scatter0.rows(i * 16, 16)
        resid[rows, :] = x
        scale = lax.rsqrt(jnp.mean(x * x, axis=-1, keepdims=True) + EPS)
        hn[here, :] = (x * scale * ffn_gain[...]).astype(BF16)

    scatter0.finish()
    spread0 = HeadGather(p, hn, ag0_s, ag0_r)
    spread0.send()
    spread0.middle()
    for g in gathers:
        g.fourth()
    for g in gathers:
        g.last()
    dy_load.wait()
    gated_t[...] = gated[...].T
    exchange.finish()
    spread0.collect()

    for low, high in ((0, 256), (256, 512), (512, FFH)):
        gate = mm(hn[...], wg[low:high, :], NT)
        up = mm(hn[...], wu[low:high, :], NT)
        dh = mm(dy[...], wd[low:high, :], NT)
        s = sigmoid(gate)
        silu = gate * s
        hidden[:, low:high] = (silu * up).astype(BF16)
        dg[:, low:high] = (dh * up * slope(gate, s)).astype(BF16)
        du[:, low:high] = (dh * silu).astype(BF16)

    scatter = HeadSum(p, ps, slots, rs_s, rs_r)
    for start, send in ((HALF, scatter.send_right), (0, scatter.send_left)):

        @pl.loop(0, 4)
        def _(j):
            columns = pl.ds(pl.multiple_of(start + j * 256, 256), 256)
            ps[:, columns] = (mm(dg[...], wg[:, columns], NN) + mm(du[...], wu[:, columns], NN)).astype(BF16)

        send()
    sums = [
        DpSum(p, FFH, a0, a1, a2, a3, a4, a5, a6),
        DpSum(p, FFH, b0, b1, b2, b3, b4, b5, b6),
        DpSum(p, FFH, c0, c1, c2, c3, c4, c5, c6),
    ]
    dg_t[...] = dg[...].T
    products(dg_t, hn, a0)
    sums[0].to_sibling()
    du_t[...] = du[...].T
    products(du_t, hn, b0)
    sums[0].to_z()
    sums[1].to_sibling()
    scatter.middle()
    hidden_t[...] = hidden[...].T
    products(hidden_t, dy, c0)
    sums[1].to_z()
    sums[2].to_sibling()
    sums[0].join()

    @pl.loop(0, 8)
    def _(j):
        columns = pl.ds(pl.multiple_of(j * 256, 256), 256)
        wu[0:TOK, columns] = mm(hidden[...], wd[:, columns], NN).astype(BF16)

    sums[2].to_z()
    spread0.finish()
    late = [load(xn_out, hn), load(w_out.at[0:TOK], wd.at[0:TOK])]
    scatter.collect()
    ffn_terms[...] = jnp.zeros_like(ffn_terms)

    @pl.loop(0, 4)
    def _(i):
        rows = pl.ds(pl.multiple_of(i * 16, 16), 16)
        here = pl.ds(pl.multiple_of(own + i * 16, 16), 16)
        grad, x = scatter.rows(i * 16, 16), resid[rows, :]
        inverse = lax.rsqrt(jnp.mean(x * x, axis=-1, keepdims=True) + EPS)
        scaled, normed = grad * ffn_gain[...], x * inverse
        back = inverse * (scaled - normed * jnp.mean(scaled * normed, axis=-1, keepdims=True))
        ffn_terms[...] += jnp.sum(grad * normed, axis=0, keepdims=True)
        both = dy[here, :].astype(F32) + back
        d_resid[rows, :] = both
        db[here, :] = both.astype(BF16)

    scatter.finish()
    spread = HeadGather(p, db, ag_s, ag_r)
    spread.send()
    spread.middle()
    sums[1].join()
    late.append(load(w_out.at[TOK : 2 * TOK], dy))
    group_total[...] = jnp.zeros_like(group_total)
    for move in late:
        move.wait()
    sums[2].join()
    spread.collect()
    scatter1 = LateHeadSum(p, wu, wg, rs1_s, rs1_r)
    scatter1.send()

    @pl.loop(0, CHUNKS)
    def _(c):
        rows = pl.ds(pl.multiple_of(c * CHUNK, CHUNK), CHUNK)
        d_gated = mm(db[rows, :], wt[...], NT)
        carried = jnp.where(segments.column(c) == segments.before(c), 1.0, 0.0)
        running = run[rows, :]
        for h in range(2):
            lanes = slice(h * 128, (h + 1) * 128)
            x, grad = mixed[rows, lanes], d_gated[:, lanes]
            gate = raw[rows, 768 + h * 128 : 768 + (h + 1) * 128]
            s = sigmoid(gate)
            inverse = lax.rsqrt(jnp.mean(x * x, axis=-1, keepdims=True) + EPS)
            normed = x * inverse
            draw[rows, 768 + h * 128 : 768 + (h + 1) * 128] = (
                grad * (normed * group_gain[...]) * slope(gate, s)
            ).astype(BF16)
            inner = grad * (gate * s)
            scaled = inner * group_gain[...]
            back = inverse * (scaled - normed * jnp.mean(scaled * normed, axis=-1, keepdims=True))
            group_total[...] += jnp.sum(inner * normed, axis=0, keepdims=True)
            back = back.astype(BF16)
            d_mixed[rows, lanes] = back
            query_raw = raw[rows, lanes]
            query = (query_raw * sigmoid(query_raw)).astype(BF16).astype(F32)
            high, low = halves(query * jnp.exp(running[:, lanes]) * carried)
            update[h, c] = mm(back, high, TN) + mm(back, low, TN)

    for h in range(2):
        lanes = slice(h * 128, (h + 1) * 128)
        state, rate = update[h, CHUNKS - 1], decay[CHUNKS - 1, 0:1, lanes]
        for c in range(CHUNKS - 2, -1, -1):
            state = state * decay[c, 0:1, lanes] + update[h, c]
            rate = rate * decay[c, 0:1, lanes]
        msg2[h, 0:128, :] = state
        msg2[h, 128:136, :] = jnp.broadcast_to(rate, (8, 128))
    exchange2 = Exchange(p, msg2, sib2, slots4, give2, take2, ex2_send, ex2_recv, True)
    exchange2.to_sibling()
    results = (out_gate, out_up, out_down)
    for one, out in zip(sums[:2], results):
        one.to_x(write(out))
    exchange2.to_chips()

    @pl.loop(0, CHUNKS)
    def _(c):
        rows = pl.ds(pl.multiple_of(c * CHUNK, CHUNK), CHUNK)
        running = run[rows, :]
        middle = running[63:64]
        _, _, query, keys, values = gates(raw, bound, rows)
        up, down_ = jnp.exp(running - middle), jnp.exp(middle - running)
        lifted = query.astype(F32) * up
        lowered = keys.astype(F32) * down_
        column, row = segments.column(c), segments.row(c)
        carried = jnp.where(column == segments.before(c), 1.0, 0.0)
        linked = (column == row) & (
            lax.broadcasted_iota(jnp.int32, (CHUNK, CHUNK), 0)
            >= lax.broadcasted_iota(jnp.int32, (CHUNK, CHUNK), 1)
        )
        for h in range(2):
            lanes = slice(h * 128, (h + 1) * 128)
            lift, lower = halves(lifted[:, lanes]), halves(lowered[:, lanes])
            scores = halves(jnp.where(linked, mm3(lift, lower, NT), 0.0))
            grad = d_mixed[rows, lanes]
            d_scores = halves(jnp.where(linked, mm(grad, values[:, lanes], NT), 0.0))
            d_values[rows, lanes] = mm(scores[0], grad, TN) + mm(scores[1], grad, TN)
            state = halves(states[h, c])
            outer = mm(grad, state[0], NN) + mm(grad, state[1], NN)
            query_grad = mm3(d_scores, lower, NN) * up[:, lanes] + outer * jnp.exp(running[:, lanes]) * carried
            d_query[rows, lanes] = query_grad
            query_raw = raw[rows, lanes]
            draw[rows, lanes] = (query_grad * slope(query_raw, sigmoid(query_raw))).astype(BF16)
            d_keys[rows, lanes] = mm3(d_scores, lift, TN) * down_[:, lanes]

    for one in sums[:2]:
        one.finish()
    first = DpSum(p, 512, a0, a1, a2, f3, f4, f5, f6)
    second = DpSum(p, 512, b0, b1, b2, g3, g4, g5, g6)
    third = DpSum(p, HERE, e0, e1, e2, e3, e4, e5, e6)
    products_turned(hn, draw.at[:, 0:256], draw.at[:, 768:1024], a0)
    exchange2.result(incoming)
    first.to_sibling()
    sums[2].to_x(write(out_down))
    for one, out in zip(sums[:2], results):
        one.end(accumulate(out))
    first.to_z()
    bound_total[...] = jnp.zeros_like(bound_total)

    @pl.loop(0, CHUNKS)
    def _(i):
        c = CHUNKS - 1 - i
        rows = pl.ds(pl.multiple_of(c * CHUNK, CHUNK), CHUNK)
        running = run[rows, :]
        logistic, forget, query, keys, values = gates(raw, bound, rows)
        keys = keys.astype(F32)
        fade = jnp.exp(running[127:128] - running)
        column, final = segments.column(c), segments.final(c)
        ends = jnp.where(column == final, 1.0, 0.0)
        for h in range(2):
            lanes = slice(h * 128, (h + 1) * 128)
            state = incoming[h]
            pair = halves(state)
            tail = halves(keys[:, lanes] * fade[:, lanes] * ends)
            value_grad = d_values[rows, lanes] + mm3(tail, pair, NT)
            draw[rows, 512 + h * 128 : 512 + (h + 1) * 128] = value_grad.astype(BF16)
            lift = mm(values[:, lanes], pair[0], NN) + mm(values[:, lanes], pair[1], NN)
            key_grad = d_keys[rows, lanes] + lift * fade[:, lanes] * ends
            at_end = jnp.sum(states[h, c + 1] * state, axis=0, keepdims=True)
            query_grad = d_query[rows, lanes]
            step = query[:, lanes].astype(F32) * query_grad - keys[:, lanes] * key_grad
            log_grad = summed_rows(False, step) + at_end
            forget_grad = log_grad / forget[:, lanes] - key_grad
            rest = 1.0 - logistic[:, lanes]
            draw[rows, 256 + h * 128 : 256 + (h + 1) * 128] = (
                forget_grad * (1.0 - bound[:, lanes]) * logistic[:, lanes] * rest
            ).astype(BF16)
            bound_total[:, lanes] += jnp.sum(forget_grad * rest, axis=0, keepdims=True)
            incoming[h] = state * decay[c, 0:1, lanes] + update[h, c]

    scatter2 = HeadSum(p, ps, slots, rs2_s, rs2_r)
    for start, send in ((HALF, scatter2.send_right), (0, scatter2.send_left)):
        for first_row, part in ((0, wd), (TOK, dy)):

            @pl.loop(0, 2)
            def _(j):
                rows = pl.ds(pl.multiple_of(j * 256, 256), 256)
                columns = pl.ds(pl.multiple_of(start + first_row + j * 256, 256), 256)
                ps[:, columns] = mm(draw[...], part[rows, start : start + HALF], NT).astype(BF16)

        send()
    products_turned(hn, draw.at[:, 256:512], draw.at[:, 512:768], b0)
    second.to_sibling()
    first.join()

    @pl.loop(0, 8)
    def _(j):
        columns = pl.ds(pl.multiple_of(j * 256, 256), 256)
        terms = ps[:, columns].astype(F32) * hn[:, columns].astype(F32)
        norm_terms[:, columns] = jnp.sum(terms, axis=0, keepdims=True) / gain[:, columns]

    vec[...] = jnp.zeros_like(vec)
    for i in range(16):
        vec[i : i + 1, :] = norm_terms[:, i * 128 : (i + 1) * 128]
        vec[16 + i : 17 + i, :] = ffn_terms[:, i * 128 : (i + 1) * 128]
    vec[32:33, :] = group_total[...]
    vec[33:34, :] = total[:, 0:128] + total[:, 128:256]
    vec[34:35, :] = bound_total[:, 0:128]
    vec[35:36, :] = bound_total[:, 128:256]
    everywhere = Total(p, vec, t0, t1, t2, t3, t4, t5, t6, t7, t8.at[0], t9.at[0])
    everywhere.send()
    second.to_z()
    scatter2.middle()
    products(gated_t, db, e0)
    third.to_sibling()
    everywhere.middle()
    third.to_z()
    everywhere.late()
    scatter1.middle()
    second.join()
    sums[2].end(accumulate(out_down))
    first.to_x(put(out_query, out_outgate))
    third.join()
    scatter2.collect()

    @pl.loop(0, 4)
    def _(i):
        rows = pl.ds(pl.multiple_of(i * 16, 16), 16)
        grad, x = scatter2.rows(i * 16, 16), hid_rows[rows, :].astype(F32)
        inverse = lax.rsqrt(jnp.mean(x * x, axis=-1, keepdims=True) + EPS)
        scaled, normed = grad * gain[...], x * inverse
        back = inverse * (scaled - normed * jnp.mean(scaled * normed, axis=-1, keepdims=True))
        grad_in[rows, :] = d_resid[rows, :] + back

    scatter1.collect()

    @pl.loop(0, 4)
    def _(i):
        rows = pl.ds(pl.multiple_of(i * 16, 16), 16)
        block_out[rows, :] = (resid[rows, :] + scatter1.rows(i * 16, 16)).astype(BF16)

    second.to_x(put(out_forget, out_input))
    third.to_x(write(out_output))
    all_of = everywhere.result()
    out_norm[...] = all_of[0:16]
    out_ffn[...] = all_of[16:32]
    out_group[...] = all_of[32:33]
    mean = jnp.sum(all_of[33:34], axis=-1, keepdims=True) / float(8192 * D)
    out_mean[...] = jnp.broadcast_to(mean, (1, 128))
    for h in range(2):
        lanes = slice(h * 128, (h + 1) * 128)
        out_bounds[:, lanes] = soft[:, lanes] * (picked[:, lanes] - bound[:, lanes]) * all_of[34 + h : 35 + h]

    first.end(add_to(out_query, out_outgate))
    second.end(add_to(out_forget, out_input))
    third.end(accumulate(out_output))
    spread.finish()
    scatter1.finish()
    scatter2.finish()
    exchange2.finish()
    everywhere.finish()
    for one in (first, second, third, sums[2]):
        one.finish()


OUTS = (
    ((ROWS, D), BF16),
    ((ROWS, D), F32),
    ((128, HERE), F32),
    ((128, HERE), F32),
    ((128, HERE), F32),
    ((128, HERE), F32),
    ((HERE, 128), F32),
    ((24, HERE), F32),
    ((16, 128), F32),
    ((1, KDIM), F32),
    ((16, 128), F32),
    ((1, 128), F32),
    ((FFH, 128), F32),
    ((FFH, 128), F32),
    ((FFH, 128), F32),
)


def call_block(*arrays):
    sums = dp_sum_scratch(FFH)
    again = [pltpu.VMEM((512, 128), BF16)] * 2 + sixteen()
    shapes = [*OUTS, ((TOK, D), BF16), ((2 * TOK, D), BF16)]
    return pl.pallas_call(
        layer_block,
        name="layer_block",
        out_shape=[jax.ShapeDtypeStruct(*one) for one in shapes],
        in_specs=[HB] * 10 + [VM] * 4 + [SM, SM],
        out_specs=[VM] * len(OUTS) + [HB, HB],
        scratch_shapes=[
            *[pltpu.VMEM((TOK, D), BF16)] * 3,
            pltpu.VMEM((2 * TOK, D), BF16),
            *[pltpu.VMEM((FFH, D), BF16)] * 3,
            pltpu.VMEM((HERE, D), BF16),
            pltpu.VMEM((TOK, 1024), F32),
            pltpu.VMEM((ROWS, D), BF16),
            pltpu.VMEM((TOK, HERE), BF16),
            pltpu.VMEM((HERE, TOK), BF16),
            *[pltpu.VMEM((TOK, HERE), F32)] * 2,
            pltpu.VMEM((2, CHUNKS + 1, 128, 128), F32),
            pltpu.VMEM((2, CHUNKS, 128, 128), F32),
            *[pltpu.VMEM((ROWS, D), F32)] * 2,
            *[pltpu.VMEM((TOK, FFH), BF16)] * 3,
            *[pltpu.VMEM((FFH, TOK), BF16)] * 3,
            pltpu.VMEM((TOK, 1024), BF16),
            pltpu.VMEM((TOK, HERE), BF16),
            *[pltpu.VMEM((TOK, HERE), F32)] * 3,
            pltpu.VMEM((CHUNKS, 8, HERE), F32),
            pltpu.VMEM((2, 128, 128), F32),
            pltpu.VMEM((VEC, 128), F32),
            pltpu.VMEM((1, D), F32),
            pltpu.VMEM((1, D), F32),
            pltpu.VMEM((1, 128), F32),
            pltpu.VMEM((1, HERE), F32),
            pltpu.VMEM((1, HERE), F32),
            *exchange_scratch(),
            *exchange_scratch(),
            *sixteen(),
            *sixteen(),
            *sixteen(),
            *sixteen(),
            *eight(),
            *sixteen(),
            *gather_semaphores(),
            *gather_semaphores(),
            *gather_semaphores(),
            *gather_semaphores(),
            *gather_semaphores(),
            *sums,
            *sums,
            *sums,
            *dp_sum_scratch(HERE),
            *again,
            *again,
            pltpu.VMEM((8, VEC, 128), F32),
            pltpu.VMEM((8, VEC, 128), F32),
            pltpu.VMEM((VEC, 128), F32),
            pltpu.VMEM((VEC, 128), F32),
            *eight(),
            *eight(),
            pltpu.SemaphoreType.DMA((1,)),
            pltpu.SemaphoreType.DMA((1,)),
            pltpu.SemaphoreType.DMA((20,)),
        ],
        compiler_params=pltpu.CompilerParams(
            collective_id=0, has_side_effects=True, vmem_limit_bytes=60 * 1024 * 1024
        ),
    )(*arrays)


def results(*refs):
    half = len(refs) // 2
    for one, out in zip(refs[:half], refs[half:]):
        out[...] = one[...]


def call_results(arrays):
    return pl.pallas_call(
        results,
        name="results",
        out_shape=[jax.ShapeDtypeStruct(*one) for one in OUTS],
        in_specs=[VM] * len(OUTS),
        out_specs=[VM] * len(OUTS),
    )(*arrays)


def local(
    hidden_in, norm_gain, w_query, w_forget, w_input, w_outgate, lower_bounds, layer_index, group_gain,
    w_output, ffn_gain, w_gate, w_up, w_down, seq_lengths, grad_out,
):
    arrays = call_block(
        hidden_in, grad_out, w_query, w_forget, w_input, w_outgate, w_output, w_gate.T, w_up.T, w_down,
        norm_gain.reshape(1, D), lower_bounds, group_gain.reshape(1, KDIM), ffn_gain.reshape(1, D), layer_index, seq_lengths,
    )
    (
        block_out, grad_in, grad_query, grad_forget, grad_input, grad_outgate, grad_output, grad_bounds,
        grad_norm, grad_group, grad_ffn, mean, grad_gate, grad_up, grad_down,
    ) = call_results(arrays[: len(OUTS)])
    return (
        block_out,
        grad_in,
        grad_norm.reshape(D),
        grad_query,
        grad_forget,
        grad_input,
        grad_outgate,
        grad_bounds,
        grad_group.reshape(KDIM),
        grad_output,
        grad_ffn.reshape(D),
        grad_gate.T,
        grad_up.T,
        grad_down,
        mean[0, 0:1],
    )


def solution(mesh):
    return jax.shard_map(
        local,
        mesh=mesh,
        in_specs=(
            P("dp", None),
            P(),
            P("dp", "head"),
            P("dp", "head"),
            P("dp", "head"),
            P("dp", "head"),
            P(None, "head"),
            P(),
            P(),
            P("head", "dp"),
            P(),
            P("dp", "head"),
            P("dp", "head"),
            P("head", "dp"),
            P(),
            P("dp", None),
        ),
        out_specs=(
            P(("dp", "head"), None),
            P(("dp", "head"), None),
            P(),
            P("dp", "head"),
            P("dp", "head"),
            P("dp", "head"),
            P("dp", "head"),
            P(None, "head"),
            P(),
            P("head", "dp"),
            P(),
            P("dp", "head"),
            P("dp", "head"),
            P("head", "dp"),
            P(),
        ),
        check_vma=False,
    )
```

```python
from functools import partial

import jax
import jax.numpy as jnp
from jax import lax
from jax.experimental import pallas as pl
from jax.experimental.pallas import tpu as pltpu
from jax.sharding import PartitionSpec as P

D = 2048
KDIM = 128
CHUNK = 128
TOK = 512
CHUNKS = TOK // CHUNK
HERE = 256
FFH = 704
NSEQ = 12
NHEAD = 8
ROWS = TOK // NHEAD
EPS = 1e-06
F32 = jnp.float32
BF16 = jnp.bfloat16
MESH = pl.DeviceIdType.MESH
VM = pl.BlockSpec(memory_space=pltpu.VMEM)
SM = pl.BlockSpec(memory_space=pltpu.SMEM)
HB = pl.BlockSpec(memory_space=pl.ANY)


class Spot:
    def __init__(self):
        self.dp = lax.axis_index("dp")
        self.head = lax.axis_index("head")
        self.core = lax.rem(self.dp, 2)
        self.chip = lax.div(self.dp, 2)
        self.xh = lax.rem(self.chip, 2)
        self.z = lax.div(self.chip, 2)
        self.xl = lax.rem(self.head, 2)
        self.y = lax.div(self.head, 2)

    def at(self, dz, xh, core):
        return (lax.rem(self.z + dz, 4) * 2 + xh) * 2 + core

    def y_at(self, k):
        return lax.rem(self.y + k, 4)

    @property
    def beside(self):
        return {"head": self.y * 2 + 1 - self.xl}

    def lines(self):
        return [self.beside] + [{"head": self.y_at(k) * 2 + self.xl} for k in (1, 2, 3)]

    @property
    def sibling(self):
        return {"dp": self.chip * 2 + 1 - self.core}

    def chips(self):
        return [{"dp": lax.rem(self.chip + k, 8) * 2 + self.core} for k in range(1, 8)]

    def heads(self):
        return [{"head": lax.rem(self.head + k, NHEAD)} for k in range(1, NHEAD)]


def greet(ids):
    barrier = pltpu.get_barrier_semaphore()
    for one in ids:
        pl.semaphore_signal(barrier, inc=1, device_id=one, device_id_type=MESH)
    return lambda: pl.semaphore_wait(barrier, len(ids))


def rcopy(src, dst, send, recv, where):
    return pltpu.make_async_remote_copy(
        src_ref=src, dst_ref=dst, send_sem=send, recv_sem=recv, device_id=where, device_id_type=MESH
    )


GATHER_SENDS = 17


class Gather:
    def __init__(self, spot, g, send, recv, half, columns=0):
        self.spot, self.g, self.s, self.r, self.h = spot, g, send, recv, half
        self.columns, self.middle = columns, (columns or 128) // 2

    def block(self, d, start=0, rows=0):
        if self.columns:
            rows = rows or self.columns
            return self.g.at[pl.ds(start, rows), pl.ds(pl.multiple_of(d * 128, 128), 128)]
        return self.g.at[pl.ds(pl.multiple_of(d * 128 + start, 64), rows or 128), :]

    def push(self, d, to, k):
        rcopy(self.block(d), self.block(d), self.s.at[k], self.r.at[d], {"dp": to}).start()

    def push_half(self, d, to, k, xh, part):
        b = self.block(d, part * self.middle, self.middle)
        rcopy(b, b, self.s.at[k], self.h.at[2 * xh + part], {"dp": to}).start()

    def arrived(self, d):
        b = self.block(d)
        rcopy(b, b, self.s.at[0], self.r.at[d], self.spot.sibling).wait_recv()

    def arrived_halves(self, d, xh):
        for part in range(2):
            b = self.block(d, part * self.middle, self.middle)
            rcopy(b, b, self.s.at[0], self.h.at[2 * xh + part], self.spot.sibling).wait_recv()

    def first(self):
        p = self.spot
        self.push(p.dp, p.at(0, 1 - p.xh, p.core), 0)
        self.push(p.dp, p.at(1, p.xh, p.core), 1)
        self.push(p.dp, p.at(3, p.xh, p.core), 2)
        self.push(p.dp, p.at(0, p.xh, 1 - p.core), 3)

    def second(self):
        p = self.spot
        b = p.at(0, 1 - p.xh, p.core)
        self.arrived(b)
        self.push(b, p.at(1, p.xh, p.core), 4)
        self.push(b, p.at(3, p.xh, p.core), 5)
        self.push(b, p.at(0, p.xh, 1 - p.core), 6)

    def third(self):
        p = self.spot
        for i, h in enumerate((p.xh, 1 - p.xh)):
            b = p.at(3, h, p.core)
            self.arrived(b)
            self.push_half(b, p.at(1, p.xh, p.core), 7 + i, h, 0)
            self.push(b, p.at(0, p.xh, 1 - p.core), 9 + i)
            b = p.at(1, h, p.core)
            self.arrived(b)
            self.push_half(b, p.at(3, p.xh, p.core), 11 + i, h, 1)
            self.push(b, p.at(0, p.xh, 1 - p.core), 13 + i)

    def fourth(self):
        p = self.spot
        for i, h in enumerate((p.xh, 1 - p.xh)):
            b = p.at(2, h, p.core)
            self.arrived_halves(b, h)
            self.push(b, p.at(0, p.xh, 1 - p.core), 15 + i)

    def last(self):
        p = self.spot
        for dz in range(4):
            for h in range(2):
                self.arrived(p.at(dz, h, 1 - p.core))
        half = self.block(0, 0, self.middle)
        for k in range(GATHER_SENDS):
            b = half if k in (7, 8, 11, 12) else self.block(0)
            rcopy(b, b, self.s.at[k], self.r.at[0], p.sibling).wait_send()


class WideGather(Gather):
    def block(self, d, start=0, rows=0):
        row, column = lax.rem(d, 8) * 128 + start, lax.div(d, 8) * 1024
        return self.g.at[pl.ds(pl.multiple_of(row, 64), rows or 128), pl.ds(pl.multiple_of(column, 1024), 1024)]

    def tile(self, d, k):
        row, column = lax.rem(d, 8) * 128, lax.div(d, 8) * 1024 + 256 * k
        return self.g.at[pl.ds(pl.multiple_of(row, 128), 128), pl.ds(pl.multiple_of(column, 256), 256)]


def gather_semaphores():
    return [
        pltpu.SemaphoreType.DMA((GATHER_SENDS,)),
        pltpu.SemaphoreType.DMA((16,)),
        pltpu.SemaphoreType.DMA((4,)),
    ]


NN = (((1,), (0,)), ((), ()))
NT = (((1,), (1,)), ((), ()))
TN = (((0,), (0,)), ((), ()))


def mm(a, b, dims):
    return lax.dot_general(a, b, dims, preferred_element_type=F32)


def halves(a):
    high = a.astype(BF16)
    return high, (a - high.astype(F32)).astype(BF16)


def mm2(a, b, dims):
    return mm(a[0], b, dims) + mm(a[1], b, dims)


def mm3(a, b, dims):
    return mm(a[0], b[0], dims) + (mm(a[0], b[1], dims) + mm(a[1], b[0], dims))


def triangle(lower):
    rows = lax.broadcasted_iota(jnp.int32, (CHUNK, CHUNK), 0)
    columns = lax.broadcasted_iota(jnp.int32, (CHUNK, CHUNK), 1)
    return (rows >= columns if lower else rows <= columns).astype(BF16)


def summed_rows(lower, x):
    high = x.astype(BF16)
    rest = x - high.astype(F32)
    middle = rest.astype(BF16)
    low = (rest - middle.astype(F32)).astype(BF16)
    t = triangle(lower)
    return mm(t, high, NN) + (mm(t, middle, NN) + mm(t, low, NN))


class Segments:
    def __init__(self, spot, seq):
        self.starts = []
        total = jnp.int32(0)
        for i in range(NSEQ):
            self.starts.append(total)
            total = total + seq[i]
        self.first = spot.dp * TOK

    def of(self, position):
        found = jnp.where(position >= self.starts[0], 1, 0)
        for s in self.starts[1:]:
            found = found + jnp.where(position >= s, 1, 0)
        return found - 1

    def column(self, c):
        return self.of(self.first + c * CHUNK + lax.broadcasted_iota(jnp.int32, (CHUNK, KDIM), 0))

    def row(self, c):
        return self.of(self.first + c * CHUNK + lax.broadcasted_iota(jnp.int32, (CHUNK, KDIM), 1))

    def before(self, c):
        return self.of(self.first + c * CHUNK - 1)

    def final(self, c):
        return self.of(self.first + (c + 1) * CHUNK - 1)


def lower_bound(lb, layer):
    x = lb[...]
    e = jnp.exp(x - jnp.max(x, axis=0, keepdims=True))
    soft = e / jnp.sum(e, axis=0, keepdims=True)
    depth = lax.broadcasted_iota(jnp.int32, x.shape, 0)
    picked = jnp.where((depth >= 1) & (depth <= layer), 1.0, 0.0)
    return soft, picked, jnp.sum(soft * picked, axis=0, keepdims=True)


def sigmoid(x):
    return lax.logistic(x)


def slope(x, s):
    return s * (1.0 + x * (1.0 - s))


class Exchange:
    def __init__(self, spot, msg, sib, slots, give, take, send, recv, backward):
        self.p, self.msg, self.sib, self.slots = spot, msg, sib, slots
        self.give, self.take, self.s, self.r, self.back = give, take, send, recv, backward

    def to_sibling(self):
        p = self.p
        rcopy(self.msg.at[1 - p.core], self.sib, self.s.at[7], self.r.at[8], p.sibling).start()

    def to_chips(self):
        p = self.p
        rcopy(self.sib, self.sib, self.s.at[7], self.r.at[8], p.sibling).wait_recv()
        mine, other = self.msg[p.core], self.sib[...]
        zero = p.core == 0
        one, two = jnp.where(zero, mine, other), jnp.where(zero, other, mine)
        near, far = (two, one) if self.back else (one, two)
        self.near = near
        state = near[0:128] * far[128:129] + far[0:128]
        rate = near[128:136] * far[128:136]
        high = rate.astype(BF16).astype(F32)
        self.slots[p.chip, 0:128, :] = state.astype(BF16)
        self.slots[p.chip, 128:144, :] = jnp.concatenate([high, rate - high], axis=0).astype(BF16)
        for k, to in enumerate(p.chips()):
            rcopy(self.slots.at[p.chip], self.slots.at[p.chip], self.s.at[k], self.r.at[p.chip], to).start()

    def result(self, out):
        p = self.p
        for k in range(1, 8):
            chip = lax.rem(p.chip + k, 8)
            rcopy(self.slots.at[chip], self.slots.at[chip], self.s.at[0], self.r.at[chip], p.sibling).wait_recv()
        state = jnp.zeros((128, 128), F32)
        for k in range(7, 0, -1) if self.back else range(7):
            m = self.slots[k].astype(F32)
            after = state * (m[128:129] + m[136:137]) + m[0:128]
            state = jnp.where(k > p.chip if self.back else k < p.chip, after, state)
        second = state * self.near[128:129] + self.near[0:128]
        is_first = p.core == (1 if self.back else 0)
        self.give[...] = jnp.where(is_first, second, state)
        move = rcopy(self.give, self.take, self.s.at[8], self.r.at[9], p.sibling)
        move.start()
        out[p.core] = jnp.where(is_first, state, second)
        move.wait_recv()
        out[1 - p.core] = self.take[...]

    def finish(self):
        p = self.p
        for k in range(7):
            rcopy(self.slots.at[0], self.slots.at[0], self.s.at[k], self.r.at[0], p.sibling).wait_send()
        rcopy(self.sib, self.sib, self.s.at[7], self.r.at[8], p.sibling).wait_send()
        rcopy(self.give, self.take, self.s.at[8], self.r.at[9], p.sibling).wait_send()


def exchange_scratch():
    return [
        pltpu.VMEM((2, 136, 128), F32),
        pltpu.VMEM((136, 128), F32),
        pltpu.VMEM((8, 144, 128), BF16),
        pltpu.VMEM((128, 128), F32),
        pltpu.VMEM((128, 128), F32),
        pltpu.SemaphoreType.DMA((9,)),
        pltpu.SemaphoreType.DMA((10,)),
    ]


def gates(raw, bound, rows):
    query_raw = raw[rows, 0:256]
    logistic = sigmoid(raw[rows, 256:512])
    forget = bound + (1.0 - bound) * logistic
    query = (query_raw * sigmoid(query_raw)).astype(BF16)
    keys = (1.0 - forget).astype(BF16)
    values = raw[rows, 512:768].astype(BF16)
    return logistic, forget, query, keys, values


HALF = D // 2


class HeadSum:
    def __init__(self, spot, ps, slots, send, recv):
        self.p, self.ps, self.slots, self.s, self.r = spot, ps, slots, send, recv

    def left_of(self, start, rows=ROWS):
        return self.slots.at[pl.ds(start, rows), pl.ds(0, HALF)]

    def right_of(self, start, rows=ROWS):
        return self.slots.at[pl.ds(start, rows), pl.ds(HALF, HALF)]

    def part(self, h, rows, right):
        return self.ps.at[pl.ds(pl.multiple_of(h * ROWS, ROWS), rows), pl.ds(HALF if right else 0, HALF)]

    def left_x(self, k):
        p = self.p
        h = p.y_at(k) * 2 + 1 - p.xl
        return rcopy(self.part(h, ROWS, False), self.left_of(64 * k), self.s.at[k], self.r.at[k], p.beside)

    def left_y(self, k):
        p = self.p
        to = {"head": p.y_at(k) * 2 + p.xl}
        return rcopy(self.left_of(64 * k), self.left_of(192 + 64 * k), self.s.at[3 + k], self.r.at[3 + k], to)

    def right_y(self, k):
        p = self.p
        to = {"head": p.y_at(k) * 2 + p.xl}
        return rcopy(
            self.part(p.y_at(k) * 2, 128, True), self.right_of(128 * k - 128, 128), self.s.at[6 + k], self.r.at[6 + k], to
        )

    def right_x(self):
        return rcopy(self.right_of(384), self.right_of(448), self.s.at[10], self.r.at[10], self.p.beside)

    def send_left(self):
        for k in (2, 1, 3, 0):
            self.left_x(k).start()

    def send_right(self):
        for k in (2, 1, 3):
            self.right_y(k).start()

    def send(self):
        self.send_right()
        self.send_left()

    def join(self, k):
        p = self.p
        self.left_x(k).wait_recv()
        mine = self.part(p.y_at(k) * 2 + p.xl, ROWS, False)
        one = self.left_of(64 * k)
        one[...] = (one[...].astype(F32) + mine[...].astype(F32)).astype(BF16)
        if k:
            self.left_y(k).start()

    def middle(self):
        p = self.p
        for k in (2, 1, 3):
            self.join(k)
        for k in (1, 3, 2):
            self.right_y(k).wait_recv()

        def total(xl):
            one = self.part(p.y * 2 + xl, ROWS, True)[...].astype(F32)
            for k in range(3):
                rows = pl.ds(pl.multiple_of(128 * k + xl * ROWS, ROWS), ROWS)
                one = one + self.slots[rows, HALF:].astype(F32)
            return one.astype(BF16)

        self.slots[384:448, HALF:] = total(1 - p.xl)
        self.right_x().start()
        self.slots[448:512, 0:HALF] = total(p.xl)
        self.join(0)

    def collect(self):
        for k in (1, 3, 2):
            self.left_y(k).wait_recv()
        self.right_x().wait_recv()

    def rows(self, start, count):
        def at(row, left):
            rows = pl.ds(pl.multiple_of(row + start, 16), count)
            return self.slots[rows, 0:HALF].astype(F32) if left else self.slots[rows, HALF:].astype(F32)

        left = (at(0, True) + at(256, True)) + (at(320, True) + at(384, True))
        return jnp.concatenate([left, at(448, True) + at(448, False)], axis=1)

    def finish(self):
        for k in range(4):
            self.left_x(k).wait_send()
        for k in (1, 2, 3):
            self.left_y(k).wait_send()
            self.right_y(k).wait_send()
        self.right_x().wait_send()


class LateHeadSum:
    def __init__(self, spot, ps, slots, send, recv):
        self.p, self.ps, self.slots, self.s, self.r = spot, ps, slots, send, recv

    def block(self, ref, start, rows=ROWS):
        return ref.at[pl.ds(pl.multiple_of(start, ROWS), rows), :]

    def along_y(self, k):
        p = self.p
        y = p.y_at(k)
        return rcopy(
            self.block(self.ps, y * 128, 128), self.block(self.slots, 128 * k - 128, 128),
            self.s.at[k], self.r.at[k], {"head": y * 2 + p.xl},
        )

    def along_x(self):
        return rcopy(self.block(self.slots, 384), self.block(self.slots, 448), self.s.at[0], self.r.at[0], self.p.beside)

    def send(self):
        for k in (2, 1, 3):
            self.along_y(k).start()

    def part(self, xl, start, count):
        p = self.p
        one = self.ps[pl.ds(pl.multiple_of((p.y * 2 + xl) * ROWS + start, 16), count), :].astype(F32)
        for k in range(3):
            rows = pl.ds(pl.multiple_of(128 * k + xl * ROWS + start, 16), count)
            one = one + self.slots[rows, :].astype(F32)
        return one

    def middle(self):
        for k in (1, 3, 2):
            self.along_y(k).wait_recv()

        @pl.loop(0, 4)
        def _(i):
            rows = pl.ds(pl.multiple_of(384 + i * 16, 16), 16)
            self.slots[rows, :] = self.part(1 - self.p.xl, i * 16, 16).astype(BF16)

        self.along_x().start()

    def collect(self):
        self.along_x().wait_recv()

    def rows(self, start, count):
        rows = pl.ds(pl.multiple_of(448 + start, 16), count)
        return self.part(self.p.xl, start, count) + self.slots[rows, :].astype(F32)

    def finish(self):
        for k in (1, 2, 3):
            self.along_y(k).wait_send()
        self.along_x().wait_send()


class HeadGather:
    def __init__(self, spot, full, send, recv):
        self.p, self.full, self.s, self.r = spot, full, send, recv

    def block(self, h, right):
        return self.full.at[pl.ds(pl.multiple_of(h * ROWS, ROWS), ROWS), pl.ds(HALF if right else 0, HALF)]

    def along_y(self, k, xl, right, i):
        p = self.p
        b = self.block(p.y * 2 + xl, right)
        return rcopy(b, b, self.s.at[i + k], self.r.at[i + k], {"head": p.y_at(k) * 2 + p.xl})

    def beside(self, k, right, i):
        p = self.p
        b = self.block(p.y_at(k) * 2 + p.xl, right)
        return rcopy(b, b, self.s.at[i + k], self.r.at[i + k], p.beside)

    def send(self):
        p = self.p
        self.beside(0, False, 0).start()
        for k in (2, 1, 3):
            self.along_y(k, p.xl, True, 0).start()
        self.beside(0, True, 4).start()
        for k in (2, 1, 3):
            self.along_y(k, p.xl, False, 8).start()

    def middle(self):
        p = self.p
        self.beside(0, False, 0).wait_recv()
        for k in (2, 1, 3):
            self.along_y(k, 1 - p.xl, False, 11).start()
        for k in (1, 3, 2):
            self.along_y(4 - k, p.xl, True, 0).wait_recv()
            self.beside(k, True, 4).start()

    def collect(self):
        p = self.p
        self.beside(0, True, 4).wait_recv()
        for k in (1, 3, 2):
            self.along_y(k, p.xl, False, 8).wait_recv()
            self.along_y(k, 1 - p.xl, False, 11).wait_recv()
            self.beside(k, True, 4).wait_recv()

    def finish(self):
        p = self.p
        self.beside(0, False, 0).wait_send()
        for k in range(4):
            self.beside(k, True, 4).wait_send()
        for k in (1, 2, 3):
            self.along_y(k, p.xl, True, 0).wait_send()
            self.along_y(k, p.xl, False, 8).wait_send()
            self.along_y(k, 1 - p.xl, False, 11).wait_send()


def sixteen():
    return [pltpu.SemaphoreType.DMA((16,)), pltpu.SemaphoreType.DMA((16,))]


def eight():
    return [pltpu.SemaphoreType.DMA((8,)), pltpu.SemaphoreType.DMA((8,))]


class DpSum:
    def __init__(self, spot, rows, gs, cr, zr, xs, xr, send, recv):
        n = pl.ds(0, rows)
        self.rows, self.p = rows, spot
        self.gs, self.cr, self.zr = gs.at[:, :, n, :], cr.at[:, n, :], zr.at[:, :, n, :]
        self.xs, self.xr, self.s, self.r = xs.at[n, :], xr.at[n, :], send, recv

    def pair(self, i):
        p = self.p
        two = pl.ds(2 * i, 2)
        return rcopy(self.gs.at[1 - p.core, two], self.cr.at[two], self.s.at[i], self.r.at[i], p.sibling)

    def to_sibling(self):
        for i in range(4):
            self.pair(i).start()

    def half(self, part):
        return pl.ds(part * (self.rows // 2), self.rows // 2)

    def along_z(self, d, block, part, slot, i):
        p = self.p
        z = lax.rem(p.z + block, 4)
        where = {"dp": (lax.rem(p.z + d, 4) * 2 + p.xh) * 2 + p.core}
        source = self.gs.at[p.core, pl.ds(z * 2, 2), self.half(part), :]
        return rcopy(source, self.zr.at[slot, :, self.half(part), :], self.s.at[4 + i], self.r.at[4 + i], where)

    def far(self, part):
        return self.along_z(3 if part else 1, 2, part, 2, part)

    def near(self, part):
        return self.along_z(3, 3, 0, 1, 2) if part else self.along_z(1, 1, 1, 0, 3)

    def joined(self, part):
        return self.along_z(3, 3, 1, 1, 4) if part else self.along_z(1, 1, 0, 0, 5)

    def to_z(self):
        p = self.p
        for i in range(4):
            self.pair(i).wait_recv()

        @pl.loop(0, 8)
        def _(k):
            self.gs[p.core, k] = (self.gs[p.core, k].astype(F32) + self.cr[k].astype(F32)).astype(BF16)

        for part in range(2):
            self.far(part).start()
        for part in range(2):
            self.near(part).start()

    def join(self):
        p = self.p
        for part in range(2):
            self.far(part).wait_recv()
            z = lax.rem(p.z + (3 if part else 1), 4)
            for h in range(2):
                mine = self.gs.at[p.core, z * 2 + h, self.half(part), :]
                other = self.zr.at[2, h, self.half(part), :]
                mine[...] = (mine[...].astype(F32) + other[...].astype(F32)).astype(BF16)
            self.joined(part).start()

    def last_move(self):
        p = self.p
        where = {"dp": (p.z * 2 + 1 - p.xh) * 2 + p.core}
        return rcopy(self.xs, self.xr, self.s.at[10], self.r.at[10], where)

    def to_x(self, put):
        p = self.p
        for part in range(2):
            self.near(part).wait_recv()
            self.joined(part).wait_recv()

        def total(h):
            one = self.gs[p.core, 2 * p.z + h].astype(F32)
            for i in range(2):
                one = one + self.zr[i, h].astype(F32)
            return one

        self.xs[...] = total(1 - p.xh).astype(BF16)
        self.last_move().start()
        put(total(p.xh))

    def end(self, add):
        self.last_move().wait_recv()
        add(self.xr[...].astype(F32))

    def finish(self):
        for i in range(4):
            self.pair(i).wait_send()
        for part in range(2):
            self.far(part).wait_send()
            self.near(part).wait_send()
            self.joined(part).wait_send()
        self.last_move().wait_send()


def dp_sum_scratch(rows):
    return [
        pltpu.VMEM((2, 8, rows, 128), BF16),
        pltpu.VMEM((8, rows, 128), BF16),
        pltpu.VMEM((3, 2, rows, 128), BF16),
        pltpu.VMEM((rows, 128), BF16),
        pltpu.VMEM((rows, 128), BF16),
        *sixteen(),
    ]


def products(left_turned, right, gs):
    @pl.loop(0, 8)
    def _(k):
        columns = pl.ds(pl.multiple_of(k * 256, 256), 256)
        both = mm(left_turned[...], right[:, columns], NN).astype(BF16)
        gs[0, k] = both[:, 0:128]
        gs[1, k] = both[:, 128:256]


def products_turned(left, first, second, gs):
    @pl.loop(0, 8)
    def _(k):
        turned = left[:, pl.ds(pl.multiple_of(k * 256, 256), 256)]
        for i, right in enumerate((first, second)):
            both = mm(turned, right[...], TN).astype(BF16)
            for q in range(2):
                rows = slice(256 * i + 128 * q, 256 * i + 128 * (q + 1))
                gs[0, k, rows, :] = both[0:128, 128 * q : 128 * (q + 1)]
                gs[1, k, rows, :] = both[128:256, 128 * q : 128 * (q + 1)]


def write(ref):
    def put(x):
        ref[...] = x

    return put


def accumulate(ref):
    def add(x):
        ref[...] += x

    return add


VEC = 40


class Total:
    def __init__(self, spot, vec, h_slots, c_slots, own, other, h_s, h_r, c_s, c_r, k_s, k_r):
        self.p, self.vec, self.hs, self.cs, self.own, self.other = spot, vec, h_slots, c_slots, own, other
        self.h_s, self.h_r, self.c_s, self.c_r, self.k_s, self.k_r = h_s, h_r, c_s, c_r, k_s, k_r

    def send(self):
        p = self.p
        self.cs[p.chip] = self.vec[...]
        for k, to in enumerate(p.chips()):
            rcopy(self.cs.at[p.chip], self.cs.at[p.chip], self.c_s.at[k], self.c_r.at[p.chip], to).start()

    def middle(self):
        p = self.p
        for k in range(1, 8):
            chip = lax.rem(p.chip + k, 8)
            rcopy(self.cs.at[chip], self.cs.at[chip], self.c_s.at[0], self.c_r.at[chip], p.sibling).wait_recv()
        total = self.cs[0]
        for k in range(1, 8):
            total = total + self.cs[k]
        self.own[...] = total
        rcopy(self.own, self.other, self.k_s, self.k_r, p.sibling).start()

    def late(self):
        p = self.p
        rcopy(self.own, self.other, self.k_s, self.k_r, p.sibling).wait_recv()
        self.hs[p.head] = self.own[...] + self.other[...]
        for k in range(1, NHEAD):
            h = lax.rem(p.head + k, NHEAD)
            rcopy(self.hs.at[p.head], self.hs.at[p.head], self.h_s.at[k], self.h_r.at[p.head], {"head": h}).start()

    def result(self):
        p = self.p
        for k in range(1, NHEAD):
            h = lax.rem(p.head + k, NHEAD)
            rcopy(self.hs.at[h], self.hs.at[h], self.h_s.at[0], self.h_r.at[h], p.sibling).wait_recv()
        total = self.hs[0]
        for h in range(1, NHEAD):
            total = total + self.hs[h]
        per_head = lax.broadcasted_iota(jnp.int32, (VEC, 128), 0) >= 34
        return jnp.where(per_head, self.hs[p.head], total)

    def finish(self):
        p = self.p
        for k in range(1, NHEAD):
            rcopy(self.hs.at[0], self.hs.at[0], self.h_s.at[k], self.h_r.at[0], p.sibling).wait_send()
        for k in range(7):
            rcopy(self.cs.at[0], self.cs.at[0], self.c_s.at[k], self.c_r.at[0], p.sibling).wait_send()
        rcopy(self.own, self.other, self.k_s, self.k_r, p.sibling).wait_send()


def layer_block(
    hid, dy_in, wq, wf, wi, wo, w_output, wg_in, wu_in, wd_in, gain, lb, group_gain, ffn_gain, layer, seq,
    i0, i1, i2, i3, i4, i5, i6, i7, i8, i9, i10, i11, i12, i13, i14, xn_out, w_out,
    block_out, grad_in, out_query, out_forget, out_input, out_outgate, out_output, out_bounds,
    out_norm, out_group, out_ffn, out_mean, out_gate, out_up, out_down,
    ps, slots, hn, wide, wg, wu, wd, wt, raw, hid_rows, gated, gated_t, mixed, run, states, update, resid, d_resid,
    hidden, dg, du, hidden_t, dg_t, du_t, draw, d_mixed, d_query, d_keys, d_values, decay, incoming, vec,
    norm_terms, ffn_terms, group_total, bound_total, total,
    msg, sib, slots3, give, take, ex_send, ex_recv, sib2, slots4, take2, ex2_send, ex2_recv,
    rs0_s, rs0_r, ag0_s, ag0_r, rs_s, rs_r, ag_s, ag_r, rs1_s, rs1_r, rs2_s, rs2_r,
    ws, wr, wh, os, or_, oh, s0, r0, h0, s1, r1, h1, s2, r2, h2,
    a0, a1, a2, a3, a4, a5, a6, b0, b1, b2, b3, b4, b5, b6, c0, c1, c2, c3, c4, c5, c6,
    e0, e1, e2, e3, e4, e5, e6, f3, f4, f5, f6, g3, g4, g5, g6,
    t0, t1, t2, t3, t4, t5, t6, t7, t8, t9, local_sem,
):
    dy, db, xn = wide.at[0:TOK], wide.at[TOK : 2 * TOK], hn
    used = []

    def load(source, to):
        move = pltpu.make_async_copy(source, to, local_sem.at[len(used)])
        move.start()
        used.append(move)
        return move

    emitted = []
    made = (
        block_out, grad_in, out_query, out_forget, out_input, out_outgate, out_output, out_bounds,
        out_norm, out_group, out_ffn, out_mean, out_gate, out_up, out_down,
    )
    to_emit = (i0, i1, i2, i3, i4, i5, i6, i7, i8, i9, i10, i11, i12, i13, i14)

    def emit(*which):
        for k in which:
            emitted.append(load(made[k], to_emit[k]))

    def put(low, high):
        def write_four(x):
            low[:, 0:128], low[:, 128:256] = x[0:128], x[128:256]
            high[:, 0:128], high[:, 128:256] = x[256:384], x[384:512]

        return write_four

    def add_to(low, high):
        def add(x):
            low[:, 0:128] += x[0:128]
            low[:, 128:256] += x[128:256]
            high[:, 0:128] += x[256:384]
            high[:, 128:256] += x[384:512]

        return add

    p = Spot()
    arrive = greet(p.chips() + [p.sibling] + p.heads())
    own = pl.multiple_of(p.head * ROWS, ROWS)
    mine = pl.ds(pl.multiple_of(p.dp * 128, 128), 128)
    gather = WideGather(p, wide, ws, wr, wh)
    loads = [load(one, gather.tile(p.dp, k)) for k, one in enumerate((wq, wf, wi, wo))]
    loads.append(load(hid, ps))
    own_blocks = [load(w_output, wt.at[:, mine])]
    own_blocks += [load(one, full.at[:, mine]) for one, full in ((wg_in, wg), (wu_in, wu), (wd_in, wd))]
    own_rows = load(hid.at[pl.ds(own, ROWS), :], hid_rows)
    for move in loads[:4]:
        move.wait()
    arrive()
    gather.first()
    loads[4].wait()
    later = Gather(p, wt, os, or_, oh, HERE)
    gathers = [Gather(p, wg, s0, r0, h0, FFH), Gather(p, wu, s1, r1, h1, FFH), Gather(p, wd, s2, r2, h2, FFH)]

    @pl.loop(0, 8)
    def _(i):
        rows = pl.ds(pl.multiple_of(i * 64, 64), 64)
        x = ps[rows, :].astype(F32)
        scale = lax.rsqrt(jnp.mean(x * x, axis=-1, keepdims=True) + EPS)
        xn[rows, :] = (x * scale * gain[...]).astype(BF16)

    gather.second()
    gather.third()
    gather.fourth()
    for move in own_blocks:
        move.wait()
    later.first()
    gathers[0].first()
    gather.last()
    spills = [load(xn, xn_out), load(wide, w_out)]

    for j in range(4):
        columns = slice(j * 256, (j + 1) * 256)
        other = slice(1024 + j * 256, 1024 + (j + 1) * 256)
        raw[:, columns] = mm(xn[:, 0:1024], wide[:, columns], NN) + mm(xn[:, 1024:2048], wide[:, other], NN)

    later.second()
    segments = Segments(p, seq)
    soft, picked, bound = lower_bound(lb, layer[0])
    total[...] = jnp.zeros_like(total)

    @pl.loop(0, CHUNKS)
    def _(c):
        rows = pl.ds(pl.multiple_of(c * CHUNK, CHUNK), CHUNK)
        logistic, forget, query, keys, values = gates(raw, bound, rows)
        total[...] += jnp.sum(forget, axis=0, keepdims=True)
        running = summed_rows(True, jnp.log(forget))
        run[rows, :] = running
        middle, ending = running[63:64], running[127:128]
        lifted = query.astype(F32) * jnp.exp(running - middle)
        lowered = keys.astype(F32) * jnp.exp(middle - running)
        tail = keys.astype(F32) * jnp.exp(ending - running)
        column, row = segments.column(c), segments.row(c)
        linked = (column == row) & (
            lax.broadcasted_iota(jnp.int32, (CHUNK, CHUNK), 0)
            >= lax.broadcasted_iota(jnp.int32, (CHUNK, CHUNK), 1)
        )
        final = segments.final(c)
        rate = jnp.exp(ending) * jnp.where(final == segments.before(c), 1.0, 0.0)
        decay[c] = jnp.broadcast_to(rate, (8, HERE))
        ends = jnp.where(column == final, 1.0, 0.0)
        for h in range(2):
            lanes = slice(h * 128, (h + 1) * 128)
            scores = mm3(halves(lifted[:, lanes]), halves(lowered[:, lanes]), NT)
            scores = jnp.where(linked, scores, 0.0)
            mixed[rows, lanes] = mm2(halves(scores), values[:, lanes], NN)
            high, low = halves(tail[:, lanes] * ends)
            update[h, c] = mm(values[:, lanes], high, TN) + mm(values[:, lanes], low, TN)

    for h in range(2):
        lanes = slice(h * 128, (h + 1) * 128)
        state, rate = update[h, 0], decay[0, 0:1, lanes]
        for c in range(1, CHUNKS):
            state = state * decay[c, 0:1, lanes] + update[h, c]
            rate = rate * decay[c, 0:1, lanes]
        msg[h, 0:128, :] = state
        msg[h, 128:136, :] = jnp.broadcast_to(rate, (8, 128))
    exchange = Exchange(p, msg, sib, slots3, give, take, ex_send, ex_recv, False)
    exchange.to_sibling()
    exchange.to_chips()
    later.third()
    gathers[1].first()
    gathers[2].first()
    gathers[0].second()
    later.fourth()
    exchange.result(incoming)
    for h in range(2):
        lanes = slice(h * 128, (h + 1) * 128)
        state = incoming[h]
        states[h, 0] = state
        for c in range(CHUNKS):
            state = state * decay[c, 0:1, lanes] + update[h, c]
            states[h, c + 1] = state

    @pl.loop(0, CHUNKS)
    def _(c):
        rows = pl.ds(pl.multiple_of(c * CHUNK, CHUNK), CHUNK)
        carried = jnp.where(segments.column(c) == segments.before(c), 1.0, 0.0)
        for h in range(2):
            lanes = slice(h * 128, (h + 1) * 128)
            query_raw = raw[rows, h * 128 : (h + 1) * 128]
            query = (query_raw * sigmoid(query_raw)).astype(BF16).astype(F32)
            reach = query * jnp.exp(run[rows, lanes]) * carried
            x = mixed[rows, lanes] + mm3(halves(reach), halves(states[h, c]), NT)
            mixed[rows, lanes] = x
            scale = lax.rsqrt(jnp.mean(x * x, axis=-1, keepdims=True) + EPS)
            gate = raw[rows, 768 + h * 128 : 768 + (h + 1) * 128]
            gated[rows, lanes] = (x * scale * group_gain[...] * (gate * sigmoid(gate))).astype(BF16)

    gathers[1].second()
    later.last()

    for move in spills:
        move.wait()
    dy_load = load(dy_in, dy)
    scatter0 = HeadSum(p, ps, slots, rs0_s, rs0_r)
    for start, send in ((HALF, scatter0.send_right), (0, scatter0.send_left)):
        for j in range(4):
            columns = slice(start + j * 256, start + (j + 1) * 256)
            ps[:, columns] = mm(gated[...], wt[:, columns], NN).astype(BF16)

        send()
    gathers[2].second()
    gathers[0].third()
    scatter0.middle()
    gathers[1].third()
    gathers[2].third()
    scatter0.collect()
    own_rows.wait()

    @pl.loop(0, 4)
    def _(i):
        rows = pl.ds(pl.multiple_of(i * 16, 16), 16)
        here = pl.ds(pl.multiple_of(own + i * 16, 16), 16)
        x = hid_rows[rows, :].astype(F32) + scatter0.rows(i * 16, 16)
        resid[rows, :] = x
        scale = lax.rsqrt(jnp.mean(x * x, axis=-1, keepdims=True) + EPS)
        hn[here, :] = (x * scale * ffn_gain[...]).astype(BF16)

    scatter0.finish()
    spread0 = HeadGather(p, hn, ag0_s, ag0_r)
    spread0.send()
    spread0.middle()
    for g in gathers:
        g.fourth()
    for g in gathers:
        g.last()
    dy_load.wait()
    gated_t[...] = gated[...].T
    exchange.finish()
    spread0.collect()

    for low, high in ((0, 256), (256, 512), (512, FFH)):
        gate = mm(hn[...], wg[low:high, :], NT)
        up = mm(hn[...], wu[low:high, :], NT)
        dh = mm(dy[...], wd[low:high, :], NT)
        s = sigmoid(gate)
        silu = gate * s
        hidden[:, low:high] = (silu * up).astype(BF16)
        dg[:, low:high] = (dh * up * slope(gate, s)).astype(BF16)
        du[:, low:high] = (dh * silu).astype(BF16)

    scatter = HeadSum(p, ps, slots, rs_s, rs_r)
    for start, send in ((HALF, scatter.send_right), (0, scatter.send_left)):
        for j in range(4):
            columns = slice(start + j * 256, start + (j + 1) * 256)
            ps[:, columns] = (mm(dg[...], wg[:, columns], NN) + mm(du[...], wu[:, columns], NN)).astype(BF16)

        send()
    sums = [
        DpSum(p, FFH, a0, a1, a2, a3, a4, a5, a6),
        DpSum(p, FFH, b0, b1, b2, b3, b4, b5, b6),
        DpSum(p, FFH, c0, c1, c2, c3, c4, c5, c6),
    ]
    dg_t[...] = dg[...].T
    products(dg_t, hn, a0)
    sums[0].to_sibling()
    du_t[...] = du[...].T
    products(du_t, hn, b0)
    sums[0].to_z()
    sums[1].to_sibling()
    scatter.middle()
    hidden_t[...] = hidden[...].T
    products(hidden_t, dy, c0)
    sums[1].to_z()
    sums[2].to_sibling()
    scatter.collect()
    ffn_terms[...] = jnp.zeros_like(ffn_terms)

    @pl.loop(0, 4)
    def _(i):
        rows = pl.ds(pl.multiple_of(i * 16, 16), 16)
        here = pl.ds(pl.multiple_of(own + i * 16, 16), 16)
        grad, x = scatter.rows(i * 16, 16), resid[rows, :]
        inverse = lax.rsqrt(jnp.mean(x * x, axis=-1, keepdims=True) + EPS)
        scaled, normed = grad * ffn_gain[...], x * inverse
        back = inverse * (scaled - normed * jnp.mean(scaled * normed, axis=-1, keepdims=True))
        ffn_terms[...] += jnp.sum(grad * normed, axis=0, keepdims=True)
        both = dy[here, :].astype(F32) + back
        d_resid[rows, :] = both
        db[here, :] = both.astype(BF16)

    scatter.finish()
    spread = HeadGather(p, db, ag_s, ag_r)
    spread.send()
    sums[2].to_z()
    spread.middle()
    sums[0].join()

    @pl.loop(0, 8)
    def _(j):
        columns = pl.ds(pl.multiple_of(j * 256, 256), 256)
        wu[0:TOK, columns] = mm(hidden[...], wd[:, columns], NN).astype(BF16)

    sums[1].join()
    spread0.finish()
    late = [load(xn_out, hn), load(w_out.at[0:TOK], wd.at[0:TOK]), load(w_out.at[TOK : 2 * TOK], dy)]
    group_total[...] = jnp.zeros_like(group_total)
    for move in late:
        move.wait()
    sums[2].join()
    spread.collect()
    scatter1 = LateHeadSum(p, wu, wg, rs1_s, rs1_r)
    scatter1.send()

    @pl.loop(0, CHUNKS)
    def _(c):
        rows = pl.ds(pl.multiple_of(c * CHUNK, CHUNK), CHUNK)
        d_gated = mm(db[rows, :], wt[...], NT)
        carried = jnp.where(segments.column(c) == segments.before(c), 1.0, 0.0)
        running = run[rows, :]
        for h in range(2):
            lanes = slice(h * 128, (h + 1) * 128)
            x, grad = mixed[rows, lanes], d_gated[:, lanes]
            gate = raw[rows, 768 + h * 128 : 768 + (h + 1) * 128]
            s = sigmoid(gate)
            inverse = lax.rsqrt(jnp.mean(x * x, axis=-1, keepdims=True) + EPS)
            normed = x * inverse
            draw[rows, 768 + h * 128 : 768 + (h + 1) * 128] = (
                grad * (normed * group_gain[...]) * slope(gate, s)
            ).astype(BF16)
            inner = grad * (gate * s)
            scaled = inner * group_gain[...]
            back = inverse * (scaled - normed * jnp.mean(scaled * normed, axis=-1, keepdims=True))
            group_total[...] += jnp.sum(inner * normed, axis=0, keepdims=True)
            back = back.astype(BF16)
            d_mixed[rows, lanes] = back
            query_raw = raw[rows, lanes]
            query = (query_raw * sigmoid(query_raw)).astype(BF16).astype(F32)
            high, low = halves(query * jnp.exp(running[:, lanes]) * carried)
            update[h, c] = mm(back, high, TN) + mm(back, low, TN)

    for h in range(2):
        lanes = slice(h * 128, (h + 1) * 128)
        state, rate = update[h, CHUNKS - 1], decay[CHUNKS - 1, 0:1, lanes]
        for c in range(CHUNKS - 2, -1, -1):
            state = state * decay[c, 0:1, lanes] + update[h, c]
            rate = rate * decay[c, 0:1, lanes]
        msg[h, 0:128, :] = state
        msg[h, 128:136, :] = jnp.broadcast_to(rate, (8, 128))
    exchange2 = Exchange(p, msg, sib2, slots4, give, take2, ex2_send, ex2_recv, True)
    exchange2.to_sibling()
    results = (out_gate, out_up, out_down)
    for one, out in zip(sums[:2], results):
        one.to_x(write(out))
    exchange2.to_chips()

    @pl.loop(0, CHUNKS)
    def _(c):
        rows = pl.ds(pl.multiple_of(c * CHUNK, CHUNK), CHUNK)
        running = run[rows, :]
        middle = running[63:64]
        _, _, query, keys, values = gates(raw, bound, rows)
        up, down_ = jnp.exp(running - middle), jnp.exp(middle - running)
        lifted = query.astype(F32) * up
        lowered = keys.astype(F32) * down_
        column, row = segments.column(c), segments.row(c)
        carried = jnp.where(column == segments.before(c), 1.0, 0.0)
        linked = (column == row) & (
            lax.broadcasted_iota(jnp.int32, (CHUNK, CHUNK), 0)
            >= lax.broadcasted_iota(jnp.int32, (CHUNK, CHUNK), 1)
        )
        for h in range(2):
            lanes = slice(h * 128, (h + 1) * 128)
            lift, lower = halves(lifted[:, lanes]), halves(lowered[:, lanes])
            scores = halves(jnp.where(linked, mm3(lift, lower, NT), 0.0))
            grad = d_mixed[rows, lanes]
            d_scores = halves(jnp.where(linked, mm(grad, values[:, lanes], NT), 0.0))
            d_values[rows, lanes] = mm(scores[0], grad, TN) + mm(scores[1], grad, TN)
            state = halves(states[h, c])
            outer = mm(grad, state[0], NN) + mm(grad, state[1], NN)
            query_grad = mm3(d_scores, lower, NN) * up[:, lanes] + outer * jnp.exp(running[:, lanes]) * carried
            d_query[rows, lanes] = query_grad
            query_raw = raw[rows, lanes]
            draw[rows, lanes] = (query_grad * slope(query_raw, sigmoid(query_raw))).astype(BF16)
            d_keys[rows, lanes] = mm3(d_scores, lift, TN) * down_[:, lanes]

    for one in sums[:2]:
        one.finish()
    first = DpSum(p, 512, a0, a1, a2, f3, f4, f5, f6)
    second = DpSum(p, 512, b0, b1, b2, g3, g4, g5, g6)
    third = DpSum(p, HERE, e0, e1, e2, e3, e4, e5, e6)
    products_turned(hn, draw.at[:, 0:256], draw.at[:, 768:1024], a0)
    exchange2.result(incoming)
    first.to_sibling()
    sums[2].to_x(write(out_down))
    for one, out in zip(sums[:2], results):
        one.end(accumulate(out))
    emit(12, 13)
    first.to_z()
    bound_total[...] = jnp.zeros_like(bound_total)

    @pl.loop(0, CHUNKS)
    def _(i):
        c = CHUNKS - 1 - i
        rows = pl.ds(pl.multiple_of(c * CHUNK, CHUNK), CHUNK)
        running = run[rows, :]
        logistic, forget, query, keys, values = gates(raw, bound, rows)
        keys = keys.astype(F32)
        fade = jnp.exp(running[127:128] - running)
        column, final = segments.column(c), segments.final(c)
        ends = jnp.where(column == final, 1.0, 0.0)
        for h in range(2):
            lanes = slice(h * 128, (h + 1) * 128)
            state = incoming[h]
            pair = halves(state)
            tail = halves(keys[:, lanes] * fade[:, lanes] * ends)
            value_grad = d_values[rows, lanes] + mm3(tail, pair, NT)
            draw[rows, 512 + h * 128 : 512 + (h + 1) * 128] = value_grad.astype(BF16)
            lift = mm(values[:, lanes], pair[0], NN) + mm(values[:, lanes], pair[1], NN)
            key_grad = d_keys[rows, lanes] + lift * fade[:, lanes] * ends
            at_end = jnp.sum(states[h, c + 1] * state, axis=0, keepdims=True)
            query_grad = d_query[rows, lanes]
            step = query[:, lanes].astype(F32) * query_grad - keys[:, lanes] * key_grad
            log_grad = summed_rows(False, step) + at_end
            forget_grad = log_grad / forget[:, lanes] - key_grad
            rest = 1.0 - logistic[:, lanes]
            draw[rows, 256 + h * 128 : 256 + (h + 1) * 128] = (
                forget_grad * (1.0 - bound[:, lanes]) * logistic[:, lanes] * rest
            ).astype(BF16)
            bound_total[:, lanes] += jnp.sum(forget_grad * rest, axis=0, keepdims=True)
            incoming[h] = state * decay[c, 0:1, lanes] + update[h, c]

    scatter2 = HeadSum(p, ps, slots, rs2_s, rs2_r)
    for start, send in ((HALF, scatter2.send_right), (0, scatter2.send_left)):
        for first_row, part in ((0, wd), (TOK, dy)):
            for j in range(2):
                rows = slice(j * 256, (j + 1) * 256)
                columns = slice(start + first_row + j * 256, start + first_row + (j + 1) * 256)
                ps[:, columns] = mm(draw[...], part[rows, start : start + HALF], NT).astype(BF16)

        send()
    products_turned(hn, draw.at[:, 256:512], draw.at[:, 512:768], b0)
    second.to_sibling()
    first.join()
    products(gated_t, db, e0)
    second.to_z()
    third.to_sibling()

    @pl.loop(0, 8)
    def _(j):
        columns = pl.ds(pl.multiple_of(j * 256, 256), 256)
        terms = ps[:, columns].astype(F32) * hn[:, columns].astype(F32)
        norm_terms[:, columns] = jnp.sum(terms, axis=0, keepdims=True) / gain[:, columns]

    vec[...] = jnp.zeros_like(vec)
    for i in range(16):
        vec[i : i + 1, :] = norm_terms[:, i * 128 : (i + 1) * 128]
        vec[16 + i : 17 + i, :] = ffn_terms[:, i * 128 : (i + 1) * 128]
    vec[32:33, :] = group_total[...]
    vec[33:34, :] = total[:, 0:128] + total[:, 128:256]
    vec[34:35, :] = bound_total[:, 0:128]
    vec[35:36, :] = bound_total[:, 128:256]
    everywhere = Total(p, vec, t0, t1, t2, t3, t4, t5, t6, t7, t8.at[0], t9.at[0])
    everywhere.send()
    second.join()
    third.to_z()
    scatter2.middle()
    everywhere.middle()
    third.join()
    everywhere.late()
    scatter1.middle()
    sums[2].end(accumulate(out_down))
    emit(14)
    first.to_x(put(out_query, out_outgate))
    second.to_x(put(out_forget, out_input))
    scatter2.collect()

    @pl.loop(0, 4)
    def _(i):
        rows = pl.ds(pl.multiple_of(i * 16, 16), 16)
        grad, x = scatter2.rows(i * 16, 16), hid_rows[rows, :].astype(F32)
        inverse = lax.rsqrt(jnp.mean(x * x, axis=-1, keepdims=True) + EPS)
        scaled, normed = grad * gain[...], x * inverse
        back = inverse * (scaled - normed * jnp.mean(scaled * normed, axis=-1, keepdims=True))
        grad_in[rows, :] = d_resid[rows, :] + back

    emit(1)

    third.to_x(write(out_output))
    scatter1.collect()

    @pl.loop(0, 4)
    def _(i):
        rows = pl.ds(pl.multiple_of(i * 16, 16), 16)
        block_out[rows, :] = (resid[rows, :] + scatter1.rows(i * 16, 16)).astype(BF16)

    emit(0)

    all_of = everywhere.result()
    out_norm[...] = all_of[0:16]
    out_ffn[...] = all_of[16:32]
    out_group[...] = all_of[32:33]
    mean = jnp.sum(all_of[33:34], axis=-1, keepdims=True) / float(8192 * D)
    out_mean[...] = jnp.broadcast_to(mean, (1, 128))
    for h in range(2):
        lanes = slice(h * 128, (h + 1) * 128)
        out_bounds[:, lanes] = soft[:, lanes] * (picked[:, lanes] - bound[:, lanes]) * all_of[34 + h : 35 + h]
    emit(7, 8, 9, 10, 11)

    first.end(add_to(out_query, out_outgate))
    emit(2, 5)
    second.end(add_to(out_forget, out_input))
    emit(3, 4)
    third.end(accumulate(out_output))
    emit(6)
    spread.finish()
    scatter1.finish()
    scatter2.finish()
    exchange2.finish()
    everywhere.finish()
    for one in (first, second, third, sums[2]):
        one.finish()
    for move in emitted:
        move.wait()


OUTS = (
    ((ROWS, D), BF16),
    ((ROWS, D), F32),
    ((128, HERE), F32),
    ((128, HERE), F32),
    ((128, HERE), F32),
    ((128, HERE), F32),
    ((HERE, 128), F32),
    ((24, HERE), F32),
    ((16, 128), F32),
    ((1, KDIM), F32),
    ((16, 128), F32),
    ((1, 128), F32),
    ((FFH, 128), F32),
    ((FFH, 128), F32),
    ((FFH, 128), F32),
)


def call_block(*arrays):
    sums = dp_sum_scratch(FFH)
    again = [pltpu.VMEM((512, 128), BF16)] * 2 + sixteen()
    shapes = [*OUTS, ((TOK, D), BF16), ((2 * TOK, D), BF16)]
    return pl.pallas_call(
        layer_block,
        name="layer_block",
        out_shape=[jax.ShapeDtypeStruct(*one) for one in shapes],
        in_specs=[HB] * 10 + [VM] * 4 + [SM, SM],
        out_specs=[HB] * (len(OUTS) + 2),
        scratch_shapes=[
            *[pltpu.VMEM(*one) for one in OUTS],
            *[pltpu.VMEM((TOK, D), BF16)] * 3,
            pltpu.VMEM((2 * TOK, D), BF16),
            *[pltpu.VMEM((FFH, D), BF16)] * 3,
            pltpu.VMEM((HERE, D), BF16),
            pltpu.VMEM((TOK, 1024), F32),
            pltpu.VMEM((ROWS, D), BF16),
            pltpu.VMEM((TOK, HERE), BF16),
            pltpu.VMEM((HERE, TOK), BF16),
            *[pltpu.VMEM((TOK, HERE), F32)] * 2,
            pltpu.VMEM((2, CHUNKS + 1, 128, 128), F32),
            pltpu.VMEM((2, CHUNKS, 128, 128), F32),
            *[pltpu.VMEM((ROWS, D), F32)] * 2,
            *[pltpu.VMEM((TOK, FFH), BF16)] * 3,
            *[pltpu.VMEM((FFH, TOK), BF16)] * 3,
            pltpu.VMEM((TOK, 1024), BF16),
            pltpu.VMEM((TOK, HERE), BF16),
            *[pltpu.VMEM((TOK, HERE), F32)] * 3,
            pltpu.VMEM((CHUNKS, 8, HERE), F32),
            pltpu.VMEM((2, 128, 128), F32),
            pltpu.VMEM((VEC, 128), F32),
            pltpu.VMEM((1, D), F32),
            pltpu.VMEM((1, D), F32),
            pltpu.VMEM((1, 128), F32),
            pltpu.VMEM((1, HERE), F32),
            pltpu.VMEM((1, HERE), F32),
            *exchange_scratch(),
            *[one for k, one in enumerate(exchange_scratch()) if k not in (0, 3)],
            *sixteen(),
            *sixteen(),
            *sixteen(),
            *sixteen(),
            *eight(),
            *sixteen(),
            *gather_semaphores(),
            *gather_semaphores(),
            *gather_semaphores(),
            *gather_semaphores(),
            *gather_semaphores(),
            *sums,
            *sums,
            *sums,
            *dp_sum_scratch(HERE),
            *again,
            *again,
            pltpu.VMEM((8, VEC, 128), F32),
            pltpu.VMEM((8, VEC, 128), F32),
            pltpu.VMEM((VEC, 128), F32),
            pltpu.VMEM((VEC, 128), F32),
            *eight(),
            *eight(),
            pltpu.SemaphoreType.DMA((1,)),
            pltpu.SemaphoreType.DMA((1,)),
            pltpu.SemaphoreType.DMA((32,)),
        ],
        compiler_params=pltpu.CompilerParams(
            collective_id=0, has_side_effects=True, vmem_limit_bytes=60 * 1024 * 1024
        ),
    )(*arrays)


def results(*refs):
    count, sems = len(OUTS), refs[-1]
    ins, outs, held = refs[:count], refs[count : 2 * count], refs[2 * count : 3 * count]
    reads = [pltpu.make_async_copy(ins[k], held[k], sems.at[0, k]) for k in range(count)]
    writes = [pltpu.make_async_copy(held[k], outs[k], sems.at[1, k]) for k in range(count)]
    for move in reads:
        move.start()
    for read, move in zip(reads, writes):
        read.wait()
        move.start()
    for move in writes:
        move.wait()


def call_results(arrays):
    return pl.pallas_call(
        results,
        name="results",
        out_shape=[jax.ShapeDtypeStruct(*one) for one in OUTS],
        in_specs=[HB] * len(OUTS),
        out_specs=[HB] * len(OUTS),
        scratch_shapes=[*[pltpu.VMEM(*one) for one in OUTS], pltpu.SemaphoreType.DMA((2, len(OUTS)))],
    )(*arrays)


def local(
    hidden_in, norm_gain, w_query, w_forget, w_input, w_outgate, lower_bounds, layer_index, group_gain,
    w_output, ffn_gain, w_gate, w_up, w_down, seq_lengths, grad_out,
):
    arrays = call_block(
        hidden_in, grad_out, w_query, w_forget, w_input, w_outgate, w_output, w_gate.T, w_up.T, w_down,
        norm_gain.reshape(1, D), lower_bounds, group_gain.reshape(1, KDIM), ffn_gain.reshape(1, D), layer_index, seq_lengths,
    )
    (
        block_out, grad_in, grad_query, grad_forget, grad_input, grad_outgate, grad_output, grad_bounds,
        grad_norm, grad_group, grad_ffn, mean, grad_gate, grad_up, grad_down,
    ) = call_results(arrays[: len(OUTS)])
    return (
        block_out,
        grad_in,
        grad_norm.reshape(D),
        grad_query,
        grad_forget,
        grad_input,
        grad_outgate,
        grad_bounds,
        grad_group.reshape(KDIM),
        grad_output,
        grad_ffn.reshape(D),
        grad_gate.T,
        grad_up.T,
        grad_down,
        mean[0, 0:1],
    )


def solution(mesh):
    return jax.shard_map(
        local,
        mesh=mesh,
        in_specs=(
            P("dp", None),
            P(),
            P("dp", "head"),
            P("dp", "head"),
            P("dp", "head"),
            P("dp", "head"),
            P(None, "head"),
            P(),
            P(),
            P("head", "dp"),
            P(),
            P("dp", "head"),
            P("dp", "head"),
            P("head", "dp"),
            P(),
            P("dp", None),
        ),
        out_specs=(
            P(("dp", "head"), None),
            P(("dp", "head"), None),
            P(),
            P("dp", "head"),
            P("dp", "head"),
            P("dp", "head"),
            P("dp", "head"),
            P(None, "head"),
            P(),
            P("head", "dp"),
            P(),
            P("dp", "head"),
            P("dp", "head"),
            P("head", "dp"),
            P(),
        ),
        check_vma=False,
    )
```

```python
from functools import partial

import jax
import jax.numpy as jnp
from jax import lax
from jax.experimental import pallas as pl
from jax.experimental.pallas import tpu as pltpu
from jax.sharding import PartitionSpec as P

D = 2048
KDIM = 128
CHUNK = 128
TOK = 512
CHUNKS = TOK // CHUNK
HERE = 256
FFH = 704
NSEQ = 12
NHEAD = 8
ROWS = TOK // NHEAD
EPS = 1e-06
F32 = jnp.float32
BF16 = jnp.bfloat16
MESH = pl.DeviceIdType.MESH
VM = pl.BlockSpec(memory_space=pltpu.VMEM)
SM = pl.BlockSpec(memory_space=pltpu.SMEM)
HB = pl.BlockSpec(memory_space=pl.ANY)


class Spot:
    def __init__(self):
        self.dp = lax.axis_index("dp")
        self.head = lax.axis_index("head")
        self.core = lax.rem(self.dp, 2)
        self.chip = lax.div(self.dp, 2)
        self.xh = lax.rem(self.chip, 2)
        self.z = lax.div(self.chip, 2)
        self.xl = lax.rem(self.head, 2)
        self.y = lax.div(self.head, 2)

    def at(self, dz, xh, core):
        return (lax.rem(self.z + dz, 4) * 2 + xh) * 2 + core

    def y_at(self, k):
        return lax.rem(self.y + k, 4)

    @property
    def beside(self):
        return {"head": self.y * 2 + 1 - self.xl}

    def lines(self):
        return [self.beside] + [{"head": self.y_at(k) * 2 + self.xl} for k in (1, 2, 3)]

    @property
    def sibling(self):
        return {"dp": self.chip * 2 + 1 - self.core}

    def chips(self):
        return [{"dp": lax.rem(self.chip + k, 8) * 2 + self.core} for k in range(1, 8)]

    def heads(self):
        return [{"head": lax.rem(self.head + k, NHEAD)} for k in range(1, NHEAD)]


def greet(ids):
    barrier = pltpu.get_barrier_semaphore()
    for one in ids:
        pl.semaphore_signal(barrier, inc=1, device_id=one, device_id_type=MESH)
    return lambda: pl.semaphore_wait(barrier, len(ids))


def rcopy(src, dst, send, recv, where):
    return pltpu.make_async_remote_copy(
        src_ref=src, dst_ref=dst, send_sem=send, recv_sem=recv, device_id=where, device_id_type=MESH
    )


GATHER_SENDS = 17


class Gather:
    def __init__(self, spot, g, send, recv, half, columns=0):
        self.spot, self.g, self.s, self.r, self.h = spot, g, send, recv, half
        self.columns, self.middle = columns, (columns or 128) // 2

    def block(self, d, start=0, rows=0):
        if self.columns:
            rows = rows or self.columns
            return self.g.at[pl.ds(start, rows), pl.ds(pl.multiple_of(d * 128, 128), 128)]
        return self.g.at[pl.ds(pl.multiple_of(d * 128 + start, 64), rows or 128), :]

    def push(self, d, to, k):
        rcopy(self.block(d), self.block(d), self.s.at[k], self.r.at[d], {"dp": to}).start()

    def push_half(self, d, to, k, xh, part):
        b = self.block(d, part * self.middle, self.middle)
        rcopy(b, b, self.s.at[k], self.h.at[2 * xh + part], {"dp": to}).start()

    def arrived(self, d):
        b = self.block(d)
        rcopy(b, b, self.s.at[0], self.r.at[d], self.spot.sibling).wait_recv()

    def arrived_halves(self, d, xh):
        for part in range(2):
            b = self.block(d, part * self.middle, self.middle)
            rcopy(b, b, self.s.at[0], self.h.at[2 * xh + part], self.spot.sibling).wait_recv()

    def first(self):
        p = self.spot
        self.push(p.dp, p.at(0, 1 - p.xh, p.core), 0)
        self.push(p.dp, p.at(1, p.xh, p.core), 1)
        self.push(p.dp, p.at(3, p.xh, p.core), 2)
        self.push(p.dp, p.at(0, p.xh, 1 - p.core), 3)

    def second(self):
        p = self.spot
        b = p.at(0, 1 - p.xh, p.core)
        self.arrived(b)
        self.push(b, p.at(1, p.xh, p.core), 4)
        self.push(b, p.at(3, p.xh, p.core), 5)
        self.push(b, p.at(0, p.xh, 1 - p.core), 6)

    def third(self):
        p = self.spot
        for i, h in enumerate((p.xh, 1 - p.xh)):
            b = p.at(3, h, p.core)
            self.arrived(b)
            self.push_half(b, p.at(1, p.xh, p.core), 7 + i, h, 0)
            self.push(b, p.at(0, p.xh, 1 - p.core), 9 + i)
            b = p.at(1, h, p.core)
            self.arrived(b)
            self.push_half(b, p.at(3, p.xh, p.core), 11 + i, h, 1)
            self.push(b, p.at(0, p.xh, 1 - p.core), 13 + i)

    def fourth(self):
        p = self.spot
        for i, h in enumerate((p.xh, 1 - p.xh)):
            b = p.at(2, h, p.core)
            self.arrived_halves(b, h)
            self.push(b, p.at(0, p.xh, 1 - p.core), 15 + i)

    def last(self):
        p = self.spot
        for dz in range(4):
            for h in range(2):
                self.arrived(p.at(dz, h, 1 - p.core))
        half = self.block(0, 0, self.middle)
        for k in range(GATHER_SENDS):
            b = half if k in (7, 8, 11, 12) else self.block(0)
            rcopy(b, b, self.s.at[k], self.r.at[0], p.sibling).wait_send()


class WideGather(Gather):
    def __init__(self, spot, g, send, recv, half, offset=0):
        super().__init__(spot, g, send, recv, half)
        self.offset, self.middle = offset, 32

    def block(self, d, start=0, rows=0):
        row, column = lax.rem(d, 8) * 128 + (self.offset + start), lax.div(d, 8) * 1024
        return self.g.at[pl.ds(pl.multiple_of(row, 32), rows or 64), pl.ds(pl.multiple_of(column, 1024), 1024)]

    def tile(self, d, k):
        row, column = lax.rem(d, 8) * 128, lax.div(d, 8) * 1024 + 256 * k
        return self.g.at[pl.ds(pl.multiple_of(row, 128), 128), pl.ds(pl.multiple_of(column, 256), 256)]


class LowerGather(WideGather):
    def first(self):
        p = self.spot
        self.push(p.dp, p.at(1, p.xh, p.core), 0)
        self.push(p.dp, p.at(3, p.xh, p.core), 1)
        self.push(p.dp, p.at(0, 1 - p.xh, p.core), 2)
        self.push(p.dp, p.at(0, p.xh, 1 - p.core), 3)

    def second(self):
        p = self.spot
        for part, (source, to) in enumerate(((3, 1), (1, 3))):
            b = p.at(source, p.xh, p.core)
            self.arrived(b)
            self.push_half(b, p.at(to, p.xh, p.core), 4 + part, 0, part)
            self.push(b, p.at(0, 1 - p.xh, p.core), 6 + part)
            self.push(b, p.at(0, p.xh, 1 - p.core), 8 + part)

    def third(self):
        p = self.spot
        b = p.at(2, p.xh, p.core)
        self.arrived_halves(b, 0)
        self.push(b, p.at(0, 1 - p.xh, p.core), 10)
        self.push(b, p.at(0, p.xh, 1 - p.core), 11)

    def fourth(self):
        p = self.spot
        for k, dz in enumerate((0, 3, 1, 2)):
            b = p.at(dz, 1 - p.xh, p.core)
            self.arrived(b)
            self.push(b, p.at(0, p.xh, 1 - p.core), 12 + k)

    def last(self):
        p = self.spot
        for dz in range(4):
            for h in range(2):
                self.arrived(p.at(dz, h, 1 - p.core))
        for k in range(16):
            b = self.block(0, 0, self.middle) if k in (4, 5) else self.block(0)
            rcopy(b, b, self.s.at[k], self.r.at[0], p.sibling).wait_send()


def gather_semaphores():
    return [
        pltpu.SemaphoreType.DMA((GATHER_SENDS,)),
        pltpu.SemaphoreType.DMA((16,)),
        pltpu.SemaphoreType.DMA((4,)),
    ]


NN = (((1,), (0,)), ((), ()))
NT = (((1,), (1,)), ((), ()))
TN = (((0,), (0,)), ((), ()))


def mm(a, b, dims):
    return lax.dot_general(a, b, dims, preferred_element_type=F32)


def halves(a):
    high = a.astype(BF16)
    return high, (a - high.astype(F32)).astype(BF16)


def mm2(a, b, dims):
    return mm(a[0], b, dims) + mm(a[1], b, dims)


def mm3(a, b, dims):
    return mm(a[0], b[0], dims) + (mm(a[0], b[1], dims) + mm(a[1], b[0], dims))


def triangle(lower):
    rows = lax.broadcasted_iota(jnp.int32, (CHUNK, CHUNK), 0)
    columns = lax.broadcasted_iota(jnp.int32, (CHUNK, CHUNK), 1)
    return (rows >= columns if lower else rows <= columns).astype(BF16)


def summed_rows(lower, x):
    high = x.astype(BF16)
    rest = x - high.astype(F32)
    middle = rest.astype(BF16)
    low = (rest - middle.astype(F32)).astype(BF16)
    t = triangle(lower)
    return mm(t, high, NN) + (mm(t, middle, NN) + mm(t, low, NN))


class Segments:
    def __init__(self, spot, seq):
        self.starts = []
        total = jnp.int32(0)
        for i in range(NSEQ):
            self.starts.append(total)
            total = total + seq[i]
        self.first = spot.dp * TOK

    def of(self, position):
        found = jnp.where(position >= self.starts[0], 1, 0)
        for s in self.starts[1:]:
            found = found + jnp.where(position >= s, 1, 0)
        return found - 1

    def column(self, c):
        return self.of(self.first + c * CHUNK + lax.broadcasted_iota(jnp.int32, (CHUNK, KDIM), 0))

    def row(self, c):
        return self.of(self.first + c * CHUNK + lax.broadcasted_iota(jnp.int32, (CHUNK, KDIM), 1))

    def before(self, c):
        return self.of(self.first + c * CHUNK - 1)

    def final(self, c):
        return self.of(self.first + (c + 1) * CHUNK - 1)


def lower_bound(lb, layer):
    x = lb[...]
    e = jnp.exp(x - jnp.max(x, axis=0, keepdims=True))
    soft = e / jnp.sum(e, axis=0, keepdims=True)
    depth = lax.broadcasted_iota(jnp.int32, x.shape, 0)
    picked = jnp.where((depth >= 1) & (depth <= layer), 1.0, 0.0)
    return soft, picked, jnp.sum(soft * picked, axis=0, keepdims=True)


def sigmoid(x):
    return lax.logistic(x)


def slope(x, s):
    return s * (1.0 + x * (1.0 - s))


class Exchange:
    def __init__(self, spot, msg, sib, slots, give, take, send, recv, backward):
        self.p, self.msg, self.sib, self.slots = spot, msg, sib, slots
        self.give, self.take, self.s, self.r, self.back = give, take, send, recv, backward

    def to_sibling(self):
        p = self.p
        rcopy(self.msg.at[1 - p.core], self.sib, self.s.at[7], self.r.at[8], p.sibling).start()

    def to_chips(self):
        p = self.p
        rcopy(self.sib, self.sib, self.s.at[7], self.r.at[8], p.sibling).wait_recv()
        mine, other = self.msg[p.core], self.sib[...]
        zero = p.core == 0
        one, two = jnp.where(zero, mine, other), jnp.where(zero, other, mine)
        near, far = (two, one) if self.back else (one, two)
        self.near = near
        state = near[0:128] * far[128:129] + far[0:128]
        rate = near[128:136] * far[128:136]
        high = rate.astype(BF16).astype(F32)
        self.slots[p.chip, 0:128, :] = state.astype(BF16)
        self.slots[p.chip, 128:144, :] = jnp.concatenate([high, rate - high], axis=0).astype(BF16)
        for k, to in enumerate(p.chips()):
            rcopy(self.slots.at[p.chip], self.slots.at[p.chip], self.s.at[k], self.r.at[p.chip], to).start()

    def result(self, out):
        p = self.p
        for k in range(1, 8):
            chip = lax.rem(p.chip + k, 8)
            rcopy(self.slots.at[chip], self.slots.at[chip], self.s.at[0], self.r.at[chip], p.sibling).wait_recv()
        state = jnp.zeros((128, 128), F32)
        for k in range(7, 0, -1) if self.back else range(7):
            m = self.slots[k].astype(F32)
            after = state * (m[128:129] + m[136:137]) + m[0:128]
            state = jnp.where(k > p.chip if self.back else k < p.chip, after, state)
        second = state * self.near[128:129] + self.near[0:128]
        is_first = p.core == (1 if self.back else 0)
        self.give[...] = jnp.where(is_first, second, state)
        move = rcopy(self.give, self.take, self.s.at[8], self.r.at[9], p.sibling)
        move.start()
        out[p.core] = jnp.where(is_first, state, second)
        move.wait_recv()
        out[1 - p.core] = self.take[...]

    def finish(self):
        p = self.p
        for k in range(7):
            rcopy(self.slots.at[0], self.slots.at[0], self.s.at[k], self.r.at[0], p.sibling).wait_send()
        rcopy(self.sib, self.sib, self.s.at[7], self.r.at[8], p.sibling).wait_send()
        rcopy(self.give, self.take, self.s.at[8], self.r.at[9], p.sibling).wait_send()


def exchange_scratch():
    return [
        pltpu.VMEM((2, 136, 128), F32),
        pltpu.VMEM((136, 128), F32),
        pltpu.VMEM((8, 144, 128), BF16),
        pltpu.VMEM((128, 128), F32),
        pltpu.VMEM((128, 128), F32),
        pltpu.SemaphoreType.DMA((9,)),
        pltpu.SemaphoreType.DMA((10,)),
    ]


def gates(raw, bound, rows):
    query_raw = raw[rows, 0:256]
    logistic = sigmoid(raw[rows, 256:512])
    forget = bound + (1.0 - bound) * logistic
    query = (query_raw * sigmoid(query_raw)).astype(BF16)
    keys = (1.0 - forget).astype(BF16)
    values = raw[rows, 512:768].astype(BF16)
    return logistic, forget, query, keys, values


HALF = D // 2


class HeadSum:
    def __init__(self, spot, ps, slots, send, recv):
        self.p, self.ps, self.slots, self.s, self.r = spot, ps, slots, send, recv

    def left_of(self, start, rows=ROWS):
        return self.slots.at[pl.ds(start, rows), pl.ds(0, HALF)]

    def right_of(self, start, rows=ROWS):
        return self.slots.at[pl.ds(start, rows), pl.ds(HALF, HALF)]

    def part(self, h, rows, right):
        return self.ps.at[pl.ds(pl.multiple_of(h * ROWS, ROWS), rows), pl.ds(HALF if right else 0, HALF)]

    def left_x(self, k):
        p = self.p
        h = p.y_at(k) * 2 + 1 - p.xl
        return rcopy(self.part(h, ROWS, False), self.left_of(64 * k), self.s.at[k], self.r.at[k], p.beside)

    def left_y(self, k):
        p = self.p
        to = {"head": p.y_at(k) * 2 + p.xl}
        return rcopy(self.left_of(64 * k), self.left_of(192 + 64 * k), self.s.at[3 + k], self.r.at[3 + k], to)

    def right_y(self, k):
        p = self.p
        to = {"head": p.y_at(k) * 2 + p.xl}
        return rcopy(
            self.part(p.y_at(k) * 2, 128, True), self.right_of(128 * k - 128, 128), self.s.at[6 + k], self.r.at[6 + k], to
        )

    def right_x(self):
        return rcopy(self.right_of(384), self.right_of(448), self.s.at[10], self.r.at[10], self.p.beside)

    def send_left(self):
        for k in (2, 1, 3, 0):
            self.left_x(k).start()

    def send_right(self):
        for k in (2, 1, 3):
            self.right_y(k).start()

    def send(self):
        self.send_right()
        self.send_left()

    def join(self, k):
        p = self.p
        self.left_x(k).wait_recv()
        mine = self.part(p.y_at(k) * 2 + p.xl, ROWS, False)
        one = self.left_of(64 * k)
        one[...] = (one[...].astype(F32) + mine[...].astype(F32)).astype(BF16)
        if k:
            self.left_y(k).start()

    def middle(self):
        p = self.p
        for k in (2, 1, 3):
            self.join(k)
        for k in (1, 3, 2):
            self.right_y(k).wait_recv()

        def total(xl):
            one = self.part(p.y * 2 + xl, ROWS, True)[...].astype(F32)
            for k in range(3):
                rows = pl.ds(pl.multiple_of(128 * k + xl * ROWS, ROWS), ROWS)
                one = one + self.slots[rows, HALF:].astype(F32)
            return one.astype(BF16)

        self.slots[384:448, HALF:] = total(1 - p.xl)
        self.right_x().start()
        self.slots[448:512, 0:HALF] = total(p.xl)
        self.join(0)

    def collect(self):
        for k in (1, 3, 2):
            self.left_y(k).wait_recv()
        self.right_x().wait_recv()

    def rows(self, start, count):
        def at(row, left):
            rows = pl.ds(pl.multiple_of(row + start, 16), count)
            return self.slots[rows, 0:HALF].astype(F32) if left else self.slots[rows, HALF:].astype(F32)

        left = (at(0, True) + at(256, True)) + (at(320, True) + at(384, True))
        return jnp.concatenate([left, at(448, True) + at(448, False)], axis=1)

    def finish(self):
        for k in range(4):
            self.left_x(k).wait_send()
        for k in (1, 2, 3):
            self.left_y(k).wait_send()
            self.right_y(k).wait_send()
        self.right_x().wait_send()


class LateHeadSum:
    def __init__(self, spot, ps, slots, send, recv):
        self.p, self.ps, self.slots, self.s, self.r = spot, ps, slots, send, recv

    def block(self, ref, start, rows=ROWS):
        return ref.at[pl.ds(pl.multiple_of(start, ROWS), rows), :]

    def along_y(self, k):
        p = self.p
        y = p.y_at(k)
        return rcopy(
            self.block(self.ps, y * 128, 128), self.block(self.slots, 128 * k - 128, 128),
            self.s.at[k], self.r.at[k], {"head": y * 2 + p.xl},
        )

    def along_x(self):
        return rcopy(self.block(self.slots, 384), self.block(self.slots, 448), self.s.at[0], self.r.at[0], self.p.beside)

    def send(self):
        for k in (2, 1, 3):
            self.along_y(k).start()

    def part(self, xl, start, count):
        p = self.p
        one = self.ps[pl.ds(pl.multiple_of((p.y * 2 + xl) * ROWS + start, 16), count), :].astype(F32)
        for k in range(3):
            rows = pl.ds(pl.multiple_of(128 * k + xl * ROWS + start, 16), count)
            one = one + self.slots[rows, :].astype(F32)
        return one

    def middle(self):
        for k in (1, 3, 2):
            self.along_y(k).wait_recv()

        @pl.loop(0, 4)
        def _(i):
            rows = pl.ds(pl.multiple_of(384 + i * 16, 16), 16)
            self.slots[rows, :] = self.part(1 - self.p.xl, i * 16, 16).astype(BF16)

        self.along_x().start()

    def collect(self):
        self.along_x().wait_recv()

    def rows(self, start, count):
        rows = pl.ds(pl.multiple_of(448 + start, 16), count)
        return self.part(self.p.xl, start, count) + self.slots[rows, :].astype(F32)

    def finish(self):
        for k in (1, 2, 3):
            self.along_y(k).wait_send()
        self.along_x().wait_send()


class HeadGather:
    def __init__(self, spot, full, send, recv):
        self.p, self.full, self.s, self.r = spot, full, send, recv

    def block(self, h, right):
        return self.full.at[pl.ds(pl.multiple_of(h * ROWS, ROWS), ROWS), pl.ds(HALF if right else 0, HALF)]

    def along_y(self, k, xl, right, i):
        p = self.p
        b = self.block(p.y * 2 + xl, right)
        return rcopy(b, b, self.s.at[i + k], self.r.at[i + k], {"head": p.y_at(k) * 2 + p.xl})

    def beside(self, k, right, i):
        p = self.p
        b = self.block(p.y_at(k) * 2 + p.xl, right)
        return rcopy(b, b, self.s.at[i + k], self.r.at[i + k], p.beside)

    def send(self):
        p = self.p
        self.beside(0, False, 0).start()
        for k in (2, 1, 3):
            self.along_y(k, p.xl, True, 0).start()
        self.beside(0, True, 4).start()
        for k in (2, 1, 3):
            self.along_y(k, p.xl, False, 8).start()

    def middle(self):
        p = self.p
        self.beside(0, False, 0).wait_recv()
        for k in (2, 1, 3):
            self.along_y(k, 1 - p.xl, False, 11).start()
        for k in (1, 3, 2):
            self.along_y(4 - k, p.xl, True, 0).wait_recv()
            self.beside(k, True, 4).start()

    def collect(self):
        p = self.p
        self.beside(0, True, 4).wait_recv()
        for k in (1, 3, 2):
            self.along_y(k, p.xl, False, 8).wait_recv()
            self.along_y(k, 1 - p.xl, False, 11).wait_recv()
            self.beside(k, True, 4).wait_recv()

    def finish(self):
        p = self.p
        self.beside(0, False, 0).wait_send()
        for k in range(4):
            self.beside(k, True, 4).wait_send()
        for k in (1, 2, 3):
            self.along_y(k, p.xl, True, 0).wait_send()
            self.along_y(k, p.xl, False, 8).wait_send()
            self.along_y(k, 1 - p.xl, False, 11).wait_send()


def sixteen():
    return [pltpu.SemaphoreType.DMA((16,)), pltpu.SemaphoreType.DMA((16,))]


def eight():
    return [pltpu.SemaphoreType.DMA((8,)), pltpu.SemaphoreType.DMA((8,))]


class DpSum:
    def __init__(self, spot, rows, gs, cr, zr, xs, xr, send, recv):
        n = pl.ds(0, rows)
        self.rows, self.p = rows, spot
        self.gs, self.cr, self.zr = gs.at[:, :, n, :], cr.at[:, n, :], zr.at[:, :, n, :]
        self.xs, self.xr, self.s, self.r = xs.at[n, :], xr.at[n, :], send, recv

    def pair(self, i):
        p = self.p
        two = pl.ds(2 * i, 2)
        return rcopy(self.gs.at[1 - p.core, two], self.cr.at[two], self.s.at[i], self.r.at[i], p.sibling)

    def to_sibling(self):
        for i in range(4):
            self.pair(i).start()

    def half(self, part):
        return pl.ds(part * (self.rows // 2), self.rows // 2)

    def along_z(self, d, block, part, slot, i):
        p = self.p
        z = lax.rem(p.z + block, 4)
        where = {"dp": (lax.rem(p.z + d, 4) * 2 + p.xh) * 2 + p.core}
        source = self.gs.at[p.core, pl.ds(z * 2, 2), self.half(part), :]
        return rcopy(source, self.zr.at[slot, :, self.half(part), :], self.s.at[4 + i], self.r.at[4 + i], where)

    def far(self, part):
        return self.along_z(3 if part else 1, 2, part, 2, part)

    def near(self, part):
        return self.along_z(3, 3, 0, 1, 2) if part else self.along_z(1, 1, 1, 0, 3)

    def joined(self, part):
        return self.along_z(3, 3, 1, 1, 4) if part else self.along_z(1, 1, 0, 0, 5)

    def to_z(self):
        p = self.p
        for i in range(4):
            self.pair(i).wait_recv()

        @pl.loop(0, 8)
        def _(k):
            self.gs[p.core, k] = (self.gs[p.core, k].astype(F32) + self.cr[k].astype(F32)).astype(BF16)

        for part in range(2):
            self.far(part).start()
        for part in range(2):
            self.near(part).start()

    def join(self):
        p = self.p
        for part in range(2):
            self.far(part).wait_recv()
            z = lax.rem(p.z + (3 if part else 1), 4)
            for h in range(2):
                mine = self.gs.at[p.core, z * 2 + h, self.half(part), :]
                other = self.zr.at[2, h, self.half(part), :]
                mine[...] = (mine[...].astype(F32) + other[...].astype(F32)).astype(BF16)
            self.joined(part).start()

    def last_move(self):
        p = self.p
        where = {"dp": (p.z * 2 + 1 - p.xh) * 2 + p.core}
        return rcopy(self.xs, self.xr, self.s.at[10], self.r.at[10], where)

    def to_x(self, put, go=True):
        p = self.p
        for part in range(2):
            self.near(part).wait_recv()
            self.joined(part).wait_recv()

        def total(h):
            one = self.gs[p.core, 2 * p.z + h].astype(F32)
            for i in range(2):
                one = one + self.zr[i, h].astype(F32)
            return one

        self.xs[...] = total(1 - p.xh).astype(BF16)
        if go:
            self.go()
        put(total(p.xh))

    def go(self):
        self.last_move().start()

    def end(self, add):
        self.last_move().wait_recv()
        add(self.xr[...].astype(F32))

    def finish(self):
        for i in range(4):
            self.pair(i).wait_send()
        for part in range(2):
            self.far(part).wait_send()
            self.near(part).wait_send()
            self.joined(part).wait_send()
        self.last_move().wait_send()


def dp_sum_scratch(rows):
    return [
        pltpu.VMEM((2, 8, rows, 128), BF16),
        pltpu.VMEM((8, rows, 128), BF16),
        pltpu.VMEM((3, 2, rows, 128), BF16),
        pltpu.VMEM((rows, 128), BF16),
        pltpu.VMEM((rows, 128), BF16),
        *sixteen(),
    ]


def products(left_turned, right, gs):
    @pl.loop(0, 8)
    def _(k):
        columns = pl.ds(pl.multiple_of(k * 256, 256), 256)
        both = mm(left_turned[...], right[:, columns], NN).astype(BF16)
        gs[0, k] = both[:, 0:128]
        gs[1, k] = both[:, 128:256]


def products_turned(left, first, second, gs):
    @pl.loop(0, 8)
    def _(k):
        turned = left[:, pl.ds(pl.multiple_of(k * 256, 256), 256)]
        for i, right in enumerate((first, second)):
            both = mm(turned, right[...], TN).astype(BF16)
            for q in range(2):
                rows = slice(256 * i + 128 * q, 256 * i + 128 * (q + 1))
                gs[0, k, rows, :] = both[0:128, 128 * q : 128 * (q + 1)]
                gs[1, k, rows, :] = both[128:256, 128 * q : 128 * (q + 1)]


def write(ref):
    def put(x):
        ref[...] = x

    return put


def accumulate(ref):
    def add(x):
        ref[...] += x

    return add


VEC = 40


class Total:
    def __init__(self, spot, vec, h_slots, c_slots, own, other, h_s, h_r, c_s, c_r, k_s, k_r):
        self.p, self.vec, self.hs, self.cs, self.own, self.other = spot, vec, h_slots, c_slots, own, other
        self.h_s, self.h_r, self.c_s, self.c_r, self.k_s, self.k_r = h_s, h_r, c_s, c_r, k_s, k_r

    def send(self):
        p = self.p
        self.cs[p.chip] = self.vec[...]
        for k, to in enumerate(p.chips()):
            rcopy(self.cs.at[p.chip], self.cs.at[p.chip], self.c_s.at[k], self.c_r.at[p.chip], to).start()

    def middle(self):
        p = self.p
        for k in range(1, 8):
            chip = lax.rem(p.chip + k, 8)
            rcopy(self.cs.at[chip], self.cs.at[chip], self.c_s.at[0], self.c_r.at[chip], p.sibling).wait_recv()
        total = self.cs[0]
        for k in range(1, 8):
            total = total + self.cs[k]
        self.own[...] = total
        rcopy(self.own, self.other, self.k_s, self.k_r, p.sibling).start()

    def late(self):
        p = self.p
        rcopy(self.own, self.other, self.k_s, self.k_r, p.sibling).wait_recv()
        self.hs[p.head] = self.own[...] + self.other[...]
        for k in range(1, NHEAD):
            h = lax.rem(p.head + k, NHEAD)
            rcopy(self.hs.at[p.head], self.hs.at[p.head], self.h_s.at[k], self.h_r.at[p.head], {"head": h}).start()

    def result(self):
        p = self.p
        for k in range(1, NHEAD):
            h = lax.rem(p.head + k, NHEAD)
            rcopy(self.hs.at[h], self.hs.at[h], self.h_s.at[0], self.h_r.at[h], p.sibling).wait_recv()
        total = self.hs[0]
        for h in range(1, NHEAD):
            total = total + self.hs[h]
        per_head = lax.broadcasted_iota(jnp.int32, (VEC, 128), 0) >= 34
        return jnp.where(per_head, self.hs[p.head], total)

    def finish(self):
        p = self.p
        for k in range(1, NHEAD):
            rcopy(self.hs.at[0], self.hs.at[0], self.h_s.at[k], self.h_r.at[0], p.sibling).wait_send()
        for k in range(7):
            rcopy(self.cs.at[0], self.cs.at[0], self.c_s.at[k], self.c_r.at[0], p.sibling).wait_send()
        rcopy(self.own, self.other, self.k_s, self.k_r, p.sibling).wait_send()


def layer_block(
    hid, dy_in, wq, wf, wi, wo, w_output, wg_in, wu_in, wd_in, gain, lb, group_gain, ffn_gain, layer, seq,
    i0, i1, i2, i3, i4, i5, i6, i7, i8, i9, i10, i11, i12, i13, i14, xn_out, w_out,
    block_out, grad_in, out_query, out_forget, out_input, out_outgate, out_output, out_bounds,
    out_norm, out_group, out_ffn, out_mean, out_gate, out_up, out_down,
    ps, slots, hn, wide, wg, wu, wd, wt, raw, hid_rows, gated, gated_t, mixed, run, states, update, resid, d_resid,
    hidden, dg, du, hidden_t, dg_t, du_t, draw, d_mixed, d_query, d_keys, d_values, decay, incoming, vec,
    norm_terms, ffn_terms, group_total, bound_total, total,
    msg, sib, slots3, give, take, ex_send, ex_recv, sib2, slots4, take2, ex2_send, ex2_recv,
    rs0_s, rs0_r, ag0_s, ag0_r, rs_s, rs_r, ag_s, ag_r, rs1_s, rs1_r, rs2_s, rs2_r,
    ws, wr, wh, vs, vr, vh, os, or_, oh, s0, r0, h0, s1, r1, h1, s2, r2, h2,
    a0, a1, a2, a3, a4, a5, a6, b0, b1, b2, b3, b4, b5, b6, c0, c1, c2, c3, c4, c5, c6,
    e0, e1, e2, e3, e4, e5, e6, f3, f4, f5, f6, g3, g4, g5, g6,
    t0, t1, t2, t3, t4, t5, t6, t7, t8, t9, local_sem,
):
    dy, db, xn = wide.at[0:TOK], wide.at[TOK : 2 * TOK], hn
    used = []

    def load(source, to):
        move = pltpu.make_async_copy(source, to, local_sem.at[len(used)])
        move.start()
        used.append(move)
        return move

    emitted = []
    made = (
        block_out, grad_in, out_query, out_forget, out_input, out_outgate, out_output, out_bounds,
        out_norm, out_group, out_ffn, out_mean, out_gate, out_up, out_down,
    )
    to_emit = (i0, i1, i2, i3, i4, i5, i6, i7, i8, i9, i10, i11, i12, i13, i14)

    def emit(*which):
        for k in which:
            emitted.append(load(made[k], to_emit[k]))

    def put(low, high):
        def write_four(x):
            low[:, 0:128], low[:, 128:256] = x[0:128], x[128:256]
            high[:, 0:128], high[:, 128:256] = x[256:384], x[384:512]

        return write_four

    def add_to(low, high):
        def add(x):
            low[:, 0:128] += x[0:128]
            low[:, 128:256] += x[128:256]
            high[:, 0:128] += x[256:384]
            high[:, 128:256] += x[384:512]

        return add

    p = Spot()
    arrive = greet(p.chips() + [p.sibling] + p.heads())
    own = pl.multiple_of(p.head * ROWS, ROWS)
    mine = pl.ds(pl.multiple_of(p.dp * 128, 128), 128)
    gather = WideGather(p, wide, ws, wr, wh)
    lower = LowerGather(p, wide, vs, vr, vh, 64)
    loads = [load(one, gather.tile(p.dp, k)) for k, one in enumerate((wq, wf, wi, wo))]
    loads.append(load(hid, ps))
    own_blocks = [load(w_output, wt.at[:, mine])]
    own_blocks += [load(one, full.at[:, mine]) for one, full in ((wg_in, wg), (wu_in, wu), (wd_in, wd))]
    own_rows = load(hid.at[pl.ds(own, ROWS), :], hid_rows)
    for move in loads[:4]:
        move.wait()
    arrive()
    gather.first()
    lower.first()
    loads[4].wait()
    later = Gather(p, wt, os, or_, oh, HERE)
    gathers = [Gather(p, wg, s0, r0, h0, FFH), Gather(p, wu, s1, r1, h1, FFH), Gather(p, wd, s2, r2, h2, FFH)]

    @pl.loop(0, 8)
    def _(i):
        rows = pl.ds(pl.multiple_of(i * 64, 64), 64)
        x = ps[rows, :].astype(F32)
        scale = lax.rsqrt(jnp.mean(x * x, axis=-1, keepdims=True) + EPS)
        xn[rows, :] = (x * scale * gain[...]).astype(BF16)

    gather.second()
    lower.second()
    gather.third()
    lower.third()
    gather.fourth()
    lower.fourth()
    for move in own_blocks:
        move.wait()
    later.first()
    gathers[0].first()
    gather.last()
    lower.last()
    spills = [load(xn, xn_out), load(wide, w_out)]

    for j in range(4):
        columns = slice(j * 256, (j + 1) * 256)
        other = slice(1024 + j * 256, 1024 + (j + 1) * 256)
        raw[:, columns] = mm(xn[:, 0:1024], wide[:, columns], NN) + mm(xn[:, 1024:2048], wide[:, other], NN)

    later.second()
    segments = Segments(p, seq)
    soft, picked, bound = lower_bound(lb, layer[0])
    total[...] = jnp.zeros_like(total)

    @pl.loop(0, CHUNKS)
    def _(c):
        rows = pl.ds(pl.multiple_of(c * CHUNK, CHUNK), CHUNK)
        logistic, forget, query, keys, values = gates(raw, bound, rows)
        total[...] += jnp.sum(forget, axis=0, keepdims=True)
        running = summed_rows(True, jnp.log(forget))
        run[rows, :] = running
        middle, ending = running[63:64], running[127:128]
        lifted = query.astype(F32) * jnp.exp(running - middle)
        lowered = keys.astype(F32) * jnp.exp(middle - running)
        tail = keys.astype(F32) * jnp.exp(ending - running)
        column, row = segments.column(c), segments.row(c)
        linked = (column == row) & (
            lax.broadcasted_iota(jnp.int32, (CHUNK, CHUNK), 0)
            >= lax.broadcasted_iota(jnp.int32, (CHUNK, CHUNK), 1)
        )
        final = segments.final(c)
        rate = jnp.exp(ending) * jnp.where(final == segments.before(c), 1.0, 0.0)
        decay[c] = jnp.broadcast_to(rate, (8, HERE))
        ends = jnp.where(column == final, 1.0, 0.0)
        for h in range(2):
            lanes = slice(h * 128, (h + 1) * 128)
            scores = mm3(halves(lifted[:, lanes]), halves(lowered[:, lanes]), NT)
            scores = jnp.where(linked, scores, 0.0)
            mixed[rows, lanes] = mm2(halves(scores), values[:, lanes], NN)
            high, low = halves(tail[:, lanes] * ends)
            update[h, c] = mm(values[:, lanes], high, TN) + mm(values[:, lanes], low, TN)

    for h in range(2):
        lanes = slice(h * 128, (h + 1) * 128)
        state, rate = update[h, 0], decay[0, 0:1, lanes]
        for c in range(1, CHUNKS):
            state = state * decay[c, 0:1, lanes] + update[h, c]
            rate = rate * decay[c, 0:1, lanes]
        msg[h, 0:128, :] = state
        msg[h, 128:136, :] = jnp.broadcast_to(rate, (8, 128))
    exchange = Exchange(p, msg, sib, slots3, give, take, ex_send, ex_recv, False)
    exchange.to_sibling()
    exchange.to_chips()
    later.third()
    gathers[1].first()
    gathers[2].first()
    gathers[0].second()
    later.fourth()
    exchange.result(incoming)
    for h in range(2):
        lanes = slice(h * 128, (h + 1) * 128)
        state = incoming[h]
        states[h, 0] = state
        for c in range(CHUNKS):
            state = state * decay[c, 0:1, lanes] + update[h, c]
            states[h, c + 1] = state

    @pl.loop(0, CHUNKS)
    def _(c):
        rows = pl.ds(pl.multiple_of(c * CHUNK, CHUNK), CHUNK)
        carried = jnp.where(segments.column(c) == segments.before(c), 1.0, 0.0)
        for h in range(2):
            lanes = slice(h * 128, (h + 1) * 128)
            query_raw = raw[rows, h * 128 : (h + 1) * 128]
            query = (query_raw * sigmoid(query_raw)).astype(BF16).astype(F32)
            reach = query * jnp.exp(run[rows, lanes]) * carried
            x = mixed[rows, lanes] + mm3(halves(reach), halves(states[h, c]), NT)
            mixed[rows, lanes] = x
            scale = lax.rsqrt(jnp.mean(x * x, axis=-1, keepdims=True) + EPS)
            gate = raw[rows, 768 + h * 128 : 768 + (h + 1) * 128]
            gated[rows, lanes] = (x * scale * group_gain[...] * (gate * sigmoid(gate))).astype(BF16)

    gathers[1].second()
    later.last()

    for move in spills:
        move.wait()
    dy_load = load(dy_in, dy)
    scatter0 = HeadSum(p, ps, slots, rs0_s, rs0_r)
    for start, send in ((HALF, scatter0.send_right), (0, scatter0.send_left)):
        for j in range(4):
            columns = slice(start + j * 256, start + (j + 1) * 256)
            ps[:, columns] = mm(gated[...], wt[:, columns], NN).astype(BF16)

        send()
    gathers[2].second()
    gathers[0].third()
    scatter0.middle()
    gathers[1].third()
    gathers[2].third()
    scatter0.collect()
    own_rows.wait()

    @pl.loop(0, 4)
    def _(i):
        rows = pl.ds(pl.multiple_of(i * 16, 16), 16)
        here = pl.ds(pl.multiple_of(own + i * 16, 16), 16)
        x = hid_rows[rows, :].astype(F32) + scatter0.rows(i * 16, 16)
        resid[rows, :] = x
        scale = lax.rsqrt(jnp.mean(x * x, axis=-1, keepdims=True) + EPS)
        hn[here, :] = (x * scale * ffn_gain[...]).astype(BF16)

    scatter0.finish()
    spread0 = HeadGather(p, hn, ag0_s, ag0_r)
    spread0.send()
    spread0.middle()
    for g in gathers:
        g.fourth()
    for g in gathers:
        g.last()
    dy_load.wait()
    gated_t[...] = gated[...].T
    exchange.finish()
    spread0.collect()

    for low, high in ((0, 256), (256, 512), (512, FFH)):
        gate = mm(hn[...], wg[low:high, :], NT)
        up = mm(hn[...], wu[low:high, :], NT)
        dh = mm(dy[...], wd[low:high, :], NT)
        s = sigmoid(gate)
        silu = gate * s
        hidden[:, low:high] = (silu * up).astype(BF16)
        dg[:, low:high] = (dh * up * slope(gate, s)).astype(BF16)
        du[:, low:high] = (dh * silu).astype(BF16)

    scatter = HeadSum(p, ps, slots, rs_s, rs_r)
    for start, send in ((HALF, scatter.send_right), (0, scatter.send_left)):
        for j in range(4):
            columns = slice(start + j * 256, start + (j + 1) * 256)
            ps[:, columns] = (mm(dg[...], wg[:, columns], NN) + mm(du[...], wu[:, columns], NN)).astype(BF16)

        send()
    sums = [
        DpSum(p, FFH, a0, a1, a2, a3, a4, a5, a6),
        DpSum(p, FFH, b0, b1, b2, b3, b4, b5, b6),
        DpSum(p, FFH, c0, c1, c2, c3, c4, c5, c6),
    ]
    dg_t[...] = dg[...].T
    products(dg_t, hn, a0)
    sums[0].to_sibling()
    du_t[...] = du[...].T
    products(du_t, hn, b0)
    sums[0].to_z()
    sums[1].to_sibling()
    scatter.middle()
    hidden_t[...] = hidden[...].T
    products(hidden_t, dy, c0)
    sums[1].to_z()
    sums[2].to_sibling()
    scatter.collect()
    ffn_terms[...] = jnp.zeros_like(ffn_terms)

    @pl.loop(0, 4)
    def _(i):
        rows = pl.ds(pl.multiple_of(i * 16, 16), 16)
        here = pl.ds(pl.multiple_of(own + i * 16, 16), 16)
        grad, x = scatter.rows(i * 16, 16), resid[rows, :]
        inverse = lax.rsqrt(jnp.mean(x * x, axis=-1, keepdims=True) + EPS)
        scaled, normed = grad * ffn_gain[...], x * inverse
        back = inverse * (scaled - normed * jnp.mean(scaled * normed, axis=-1, keepdims=True))
        ffn_terms[...] += jnp.sum(grad * normed, axis=0, keepdims=True)
        both = dy[here, :].astype(F32) + back
        d_resid[rows, :] = both
        db[here, :] = both.astype(BF16)

    scatter.finish()
    spread = HeadGather(p, db, ag_s, ag_r)
    spread.send()
    sums[2].to_z()
    spread.middle()
    sums[0].join()

    @pl.loop(0, 8)
    def _(j):
        columns = pl.ds(pl.multiple_of(j * 256, 256), 256)
        wu[0:TOK, columns] = mm(hidden[...], wd[:, columns], NN).astype(BF16)

    sums[1].join()
    spread0.finish()
    late = [load(xn_out, hn), load(w_out.at[0:TOK], wd.at[0:TOK]), load(w_out.at[TOK : 2 * TOK], dy)]
    group_total[...] = jnp.zeros_like(group_total)
    for move in late:
        move.wait()
    sums[2].join()
    spread.collect()
    scatter1 = LateHeadSum(p, wu, wg, rs1_s, rs1_r)
    scatter1.send()

    @pl.loop(0, CHUNKS)
    def _(c):
        rows = pl.ds(pl.multiple_of(c * CHUNK, CHUNK), CHUNK)
        d_gated = mm(db[rows, :], wt[...], NT)
        carried = jnp.where(segments.column(c) == segments.before(c), 1.0, 0.0)
        running = run[rows, :]
        for h in range(2):
            lanes = slice(h * 128, (h + 1) * 128)
            x, grad = mixed[rows, lanes], d_gated[:, lanes]
            gate = raw[rows, 768 + h * 128 : 768 + (h + 1) * 128]
            s = sigmoid(gate)
            inverse = lax.rsqrt(jnp.mean(x * x, axis=-1, keepdims=True) + EPS)
            normed = x * inverse
            draw[rows, 768 + h * 128 : 768 + (h + 1) * 128] = (
                grad * (normed * group_gain[...]) * slope(gate, s)
            ).astype(BF16)
            inner = grad * (gate * s)
            scaled = inner * group_gain[...]
            back = inverse * (scaled - normed * jnp.mean(scaled * normed, axis=-1, keepdims=True))
            group_total[...] += jnp.sum(inner * normed, axis=0, keepdims=True)
            back = back.astype(BF16)
            d_mixed[rows, lanes] = back
            query_raw = raw[rows, lanes]
            query = (query_raw * sigmoid(query_raw)).astype(BF16).astype(F32)
            high, low = halves(query * jnp.exp(running[:, lanes]) * carried)
            update[h, c] = mm(back, high, TN) + mm(back, low, TN)

    for h in range(2):
        lanes = slice(h * 128, (h + 1) * 128)
        state, rate = update[h, CHUNKS - 1], decay[CHUNKS - 1, 0:1, lanes]
        for c in range(CHUNKS - 2, -1, -1):
            state = state * decay[c, 0:1, lanes] + update[h, c]
            rate = rate * decay[c, 0:1, lanes]
        msg[h, 0:128, :] = state
        msg[h, 128:136, :] = jnp.broadcast_to(rate, (8, 128))
    exchange2 = Exchange(p, msg, sib2, slots4, give, take2, ex2_send, ex2_recv, True)
    exchange2.to_sibling()
    results = (out_gate, out_up, out_down)
    for one, out in zip(sums[:2], results):
        one.to_x(write(out), go=False)
    exchange2.to_chips()
    for one in sums[:2]:
        one.go()

    @pl.loop(0, CHUNKS)
    def _(c):
        rows = pl.ds(pl.multiple_of(c * CHUNK, CHUNK), CHUNK)
        running = run[rows, :]
        middle = running[63:64]
        _, _, query, keys, values = gates(raw, bound, rows)
        up, down_ = jnp.exp(running - middle), jnp.exp(middle - running)
        lifted = query.astype(F32) * up
        lowered = keys.astype(F32) * down_
        column, row = segments.column(c), segments.row(c)
        carried = jnp.where(column == segments.before(c), 1.0, 0.0)
        linked = (column == row) & (
            lax.broadcasted_iota(jnp.int32, (CHUNK, CHUNK), 0)
            >= lax.broadcasted_iota(jnp.int32, (CHUNK, CHUNK), 1)
        )
        for h in range(2):
            lanes = slice(h * 128, (h + 1) * 128)
            lift, lower = halves(lifted[:, lanes]), halves(lowered[:, lanes])
            scores = halves(jnp.where(linked, mm3(lift, lower, NT), 0.0))
            grad = d_mixed[rows, lanes]
            d_scores = halves(jnp.where(linked, mm(grad, values[:, lanes], NT), 0.0))
            d_values[rows, lanes] = mm(scores[0], grad, TN) + mm(scores[1], grad, TN)
            state = halves(states[h, c])
            outer = mm(grad, state[0], NN) + mm(grad, state[1], NN)
            query_grad = mm3(d_scores, lower, NN) * up[:, lanes] + outer * jnp.exp(running[:, lanes]) * carried
            d_query[rows, lanes] = query_grad
            query_raw = raw[rows, lanes]
            draw[rows, lanes] = (query_grad * slope(query_raw, sigmoid(query_raw))).astype(BF16)
            d_keys[rows, lanes] = mm3(d_scores, lift, TN) * down_[:, lanes]

    for one in sums[:2]:
        one.finish()
    first = DpSum(p, 512, a0, a1, a2, f3, f4, f5, f6)
    second = DpSum(p, 512, b0, b1, b2, g3, g4, g5, g6)
    third = DpSum(p, HERE, e0, e1, e2, e3, e4, e5, e6)
    products_turned(hn, draw.at[:, 0:256], draw.at[:, 768:1024], a0)
    exchange2.result(incoming)
    first.to_sibling()
    sums[2].to_x(write(out_down))
    for one, out in zip(sums[:2], results):
        one.end(accumulate(out))
    emit(12, 13)
    first.to_z()
    bound_total[...] = jnp.zeros_like(bound_total)

    @pl.loop(0, CHUNKS)
    def _(i):
        c = CHUNKS - 1 - i
        rows = pl.ds(pl.multiple_of(c * CHUNK, CHUNK), CHUNK)
        running = run[rows, :]
        logistic, forget, query, keys, values = gates(raw, bound, rows)
        keys = keys.astype(F32)
        fade = jnp.exp(running[127:128] - running)
        column, final = segments.column(c), segments.final(c)
        ends = jnp.where(column == final, 1.0, 0.0)
        for h in range(2):
            lanes = slice(h * 128, (h + 1) * 128)
            state = incoming[h]
            pair = halves(state)
            tail = halves(keys[:, lanes] * fade[:, lanes] * ends)
            value_grad = d_values[rows, lanes] + mm3(tail, pair, NT)
            draw[rows, 512 + h * 128 : 512 + (h + 1) * 128] = value_grad.astype(BF16)
            lift = mm(values[:, lanes], pair[0], NN) + mm(values[:, lanes], pair[1], NN)
            key_grad = d_keys[rows, lanes] + lift * fade[:, lanes] * ends
            at_end = jnp.sum(states[h, c + 1] * state, axis=0, keepdims=True)
            query_grad = d_query[rows, lanes]
            step = query[:, lanes].astype(F32) * query_grad - keys[:, lanes] * key_grad
            log_grad = summed_rows(False, step) + at_end
            forget_grad = log_grad / forget[:, lanes] - key_grad
            rest = 1.0 - logistic[:, lanes]
            draw[rows, 256 + h * 128 : 256 + (h + 1) * 128] = (
                forget_grad * (1.0 - bound[:, lanes]) * logistic[:, lanes] * rest
            ).astype(BF16)
            bound_total[:, lanes] += jnp.sum(forget_grad * rest, axis=0, keepdims=True)
            incoming[h] = state * decay[c, 0:1, lanes] + update[h, c]

    scatter2 = HeadSum(p, ps, slots, rs2_s, rs2_r)
    for start, send in ((HALF, scatter2.send_right), (0, scatter2.send_left)):
        for first_row, part in ((0, wd), (TOK, dy)):
            for j in range(2):
                rows = slice(j * 256, (j + 1) * 256)
                columns = slice(start + first_row + j * 256, start + first_row + (j + 1) * 256)
                ps[:, columns] = mm(draw[...], part[rows, start : start + HALF], NT).astype(BF16)

        send()
    first.join()
    products_turned(hn, draw.at[:, 256:512], draw.at[:, 512:768], b0)
    second.to_sibling()

    @pl.loop(0, 8)
    def _(j):
        columns = pl.ds(pl.multiple_of(j * 256, 256), 256)
        terms = ps[:, columns].astype(F32) * hn[:, columns].astype(F32)
        norm_terms[:, columns] = jnp.sum(terms, axis=0, keepdims=True) / gain[:, columns]

    vec[...] = jnp.zeros_like(vec)
    for i in range(16):
        vec[i : i + 1, :] = norm_terms[:, i * 128 : (i + 1) * 128]
        vec[16 + i : 17 + i, :] = ffn_terms[:, i * 128 : (i + 1) * 128]
    vec[32:33, :] = group_total[...]
    vec[33:34, :] = total[:, 0:128] + total[:, 128:256]
    vec[34:35, :] = bound_total[:, 0:128]
    vec[35:36, :] = bound_total[:, 128:256]
    everywhere = Total(p, vec, t0, t1, t2, t3, t4, t5, t6, t7, t8.at[0], t9.at[0])
    everywhere.send()
    second.to_z()
    products(gated_t, db, e0)
    third.to_sibling()
    second.join()
    scatter2.middle()
    third.to_z()
    everywhere.middle()
    first.to_x(put(out_query, out_outgate))
    scatter1.middle()
    everywhere.late()
    second.to_x(put(out_forget, out_input))
    third.join()
    sums[2].end(accumulate(out_down))
    emit(14)
    scatter2.collect()

    @pl.loop(0, 4)
    def _(i):
        rows = pl.ds(pl.multiple_of(i * 16, 16), 16)
        grad, x = scatter2.rows(i * 16, 16), hid_rows[rows, :].astype(F32)
        inverse = lax.rsqrt(jnp.mean(x * x, axis=-1, keepdims=True) + EPS)
        scaled, normed = grad * gain[...], x * inverse
        back = inverse * (scaled - normed * jnp.mean(scaled * normed, axis=-1, keepdims=True))
        grad_in[rows, :] = d_resid[rows, :] + back

    emit(1)

    third.to_x(write(out_output))
    scatter1.collect()

    @pl.loop(0, 4)
    def _(i):
        rows = pl.ds(pl.multiple_of(i * 16, 16), 16)
        block_out[rows, :] = (resid[rows, :] + scatter1.rows(i * 16, 16)).astype(BF16)

    emit(0)

    all_of = everywhere.result()
    out_norm[...] = all_of[0:16]
    out_ffn[...] = all_of[16:32]
    out_group[...] = all_of[32:33]
    mean = jnp.sum(all_of[33:34], axis=-1, keepdims=True) / float(8192 * D)
    out_mean[...] = jnp.broadcast_to(mean, (1, 128))
    for h in range(2):
        lanes = slice(h * 128, (h + 1) * 128)
        out_bounds[:, lanes] = soft[:, lanes] * (picked[:, lanes] - bound[:, lanes]) * all_of[34 + h : 35 + h]
    emit(7, 8, 9, 10, 11)

    first.end(add_to(out_query, out_outgate))
    emit(2, 5)
    second.end(add_to(out_forget, out_input))
    emit(3, 4)
    third.end(accumulate(out_output))
    emit(6)
    spread.finish()
    scatter1.finish()
    scatter2.finish()
    exchange2.finish()
    everywhere.finish()
    for one in (first, second, third, sums[2]):
        one.finish()
    for move in emitted:
        move.wait()


OUTS = (
    ((ROWS, D), BF16),
    ((ROWS, D), F32),
    ((128, HERE), F32),
    ((128, HERE), F32),
    ((128, HERE), F32),
    ((128, HERE), F32),
    ((HERE, 128), F32),
    ((24, HERE), F32),
    ((16, 128), F32),
    ((1, KDIM), F32),
    ((16, 128), F32),
    ((1, 128), F32),
    ((FFH, 128), F32),
    ((FFH, 128), F32),
    ((FFH, 128), F32),
)


def call_block(*arrays):
    sums = dp_sum_scratch(FFH)
    again = [pltpu.VMEM((512, 128), BF16)] * 2 + sixteen()
    shapes = [*OUTS, ((TOK, D), BF16), ((2 * TOK, D), BF16)]
    return pl.pallas_call(
        layer_block,
        name="layer_block",
        out_shape=[jax.ShapeDtypeStruct(*one) for one in shapes],
        in_specs=[HB] * 10 + [VM] * 4 + [SM, SM],
        out_specs=[HB] * (len(OUTS) + 2),
        scratch_shapes=[
            *[pltpu.VMEM(*one) for one in OUTS],
            *[pltpu.VMEM((TOK, D), BF16)] * 3,
            pltpu.VMEM((2 * TOK, D), BF16),
            *[pltpu.VMEM((FFH, D), BF16)] * 3,
            pltpu.VMEM((HERE, D), BF16),
            pltpu.VMEM((TOK, 1024), F32),
            pltpu.VMEM((ROWS, D), BF16),
            pltpu.VMEM((TOK, HERE), BF16),
            pltpu.VMEM((HERE, TOK), BF16),
            *[pltpu.VMEM((TOK, HERE), F32)] * 2,
            pltpu.VMEM((2, CHUNKS + 1, 128, 128), F32),
            pltpu.VMEM((2, CHUNKS, 128, 128), F32),
            *[pltpu.VMEM((ROWS, D), F32)] * 2,
            *[pltpu.VMEM((TOK, FFH), BF16)] * 3,
            *[pltpu.VMEM((FFH, TOK), BF16)] * 3,
            pltpu.VMEM((TOK, 1024), BF16),
            pltpu.VMEM((TOK, HERE), BF16),
            *[pltpu.VMEM((TOK, HERE), F32)] * 3,
            pltpu.VMEM((CHUNKS, 8, HERE), F32),
            pltpu.VMEM((2, 128, 128), F32),
            pltpu.VMEM((VEC, 128), F32),
            pltpu.VMEM((1, D), F32),
            pltpu.VMEM((1, D), F32),
            pltpu.VMEM((1, 128), F32),
            pltpu.VMEM((1, HERE), F32),
            pltpu.VMEM((1, HERE), F32),
            *exchange_scratch(),
            *[one for k, one in enumerate(exchange_scratch()) if k not in (0, 3)],
            *sixteen(),
            *sixteen(),
            *sixteen(),
            *sixteen(),
            *eight(),
            *sixteen(),
            *gather_semaphores(),
            *gather_semaphores(),
            *gather_semaphores(),
            *gather_semaphores(),
            *gather_semaphores(),
            *gather_semaphores(),
            *sums,
            *sums,
            *sums,
            *dp_sum_scratch(HERE),
            *again,
            *again,
            pltpu.VMEM((8, VEC, 128), F32),
            pltpu.VMEM((8, VEC, 128), F32),
            pltpu.VMEM((VEC, 128), F32),
            pltpu.VMEM((VEC, 128), F32),
            *eight(),
            *eight(),
            pltpu.SemaphoreType.DMA((1,)),
            pltpu.SemaphoreType.DMA((1,)),
            pltpu.SemaphoreType.DMA((32,)),
        ],
        compiler_params=pltpu.CompilerParams(
            collective_id=0, has_side_effects=True, vmem_limit_bytes=60 * 1024 * 1024
        ),
    )(*arrays)


def results(*refs):
    count, sems = len(OUTS), refs[-1]
    ins, outs, held = refs[:count], refs[count : 2 * count], refs[2 * count : 3 * count]
    reads = [pltpu.make_async_copy(ins[k], held[k], sems.at[0, k]) for k in range(count)]
    writes = [pltpu.make_async_copy(held[k], outs[k], sems.at[1, k]) for k in range(count)]
    for move in reads:
        move.start()
    for read, move in zip(reads, writes):
        read.wait()
        move.start()
    for move in writes:
        move.wait()


def call_results(arrays):
    return pl.pallas_call(
        results,
        name="results",
        out_shape=[jax.ShapeDtypeStruct(*one) for one in OUTS],
        in_specs=[HB] * len(OUTS),
        out_specs=[HB] * len(OUTS),
        scratch_shapes=[*[pltpu.VMEM(*one) for one in OUTS], pltpu.SemaphoreType.DMA((2, len(OUTS)))],
    )(*arrays)


def local(
    hidden_in, norm_gain, w_query, w_forget, w_input, w_outgate, lower_bounds, layer_index, group_gain,
    w_output, ffn_gain, w_gate, w_up, w_down, seq_lengths, grad_out,
):
    arrays = call_block(
        hidden_in, grad_out, w_query, w_forget, w_input, w_outgate, w_output, w_gate.T, w_up.T, w_down,
        norm_gain.reshape(1, D), lower_bounds, group_gain.reshape(1, KDIM), ffn_gain.reshape(1, D), layer_index, seq_lengths,
    )
    (
        block_out, grad_in, grad_query, grad_forget, grad_input, grad_outgate, grad_output, grad_bounds,
        grad_norm, grad_group, grad_ffn, mean, grad_gate, grad_up, grad_down,
    ) = call_results(arrays[: len(OUTS)])
    return (
        block_out,
        grad_in,
        grad_norm.reshape(D),
        grad_query,
        grad_forget,
        grad_input,
        grad_outgate,
        grad_bounds,
        grad_group.reshape(KDIM),
        grad_output,
        grad_ffn.reshape(D),
        grad_gate.T,
        grad_up.T,
        grad_down,
        mean[0, 0:1],
    )


def solution(mesh):
    return jax.shard_map(
        local,
        mesh=mesh,
        in_specs=(
            P("dp", None),
            P(),
            P("dp", "head"),
            P("dp", "head"),
            P("dp", "head"),
            P("dp", "head"),
            P(None, "head"),
            P(),
            P(),
            P("head", "dp"),
            P(),
            P("dp", "head"),
            P("dp", "head"),
            P("head", "dp"),
            P(),
            P("dp", None),
        ),
        out_specs=(
            P(("dp", "head"), None),
            P(("dp", "head"), None),
            P(),
            P("dp", "head"),
            P("dp", "head"),
            P("dp", "head"),
            P("dp", "head"),
            P(None, "head"),
            P(),
            P("head", "dp"),
            P(),
            P("dp", "head"),
            P("dp", "head"),
            P("head", "dp"),
            P(),
        ),
        check_vma=False,
    )
```

```python
from functools import partial

import jax
import jax.numpy as jnp
from jax import lax
from jax.experimental import pallas as pl
from jax.experimental.pallas import tpu as pltpu
from jax.sharding import PartitionSpec as P

D = 2048
KDIM = 128
CHUNK = 128
TOK = 512
CHUNKS = TOK // CHUNK
HERE = 256
FFH = 704
NSEQ = 12
NHEAD = 8
ROWS = TOK // NHEAD
EPS = 1e-06
F32 = jnp.float32
BF16 = jnp.bfloat16
MESH = pl.DeviceIdType.MESH
VM = pl.BlockSpec(memory_space=pltpu.VMEM)
SM = pl.BlockSpec(memory_space=pltpu.SMEM)
HB = pl.BlockSpec(memory_space=pl.ANY)


class Spot:
    def __init__(self):
        self.dp = lax.axis_index("dp")
        self.head = lax.axis_index("head")
        self.core = lax.rem(self.dp, 2)
        self.chip = lax.div(self.dp, 2)
        self.xh = lax.rem(self.chip, 2)
        self.z = lax.div(self.chip, 2)
        self.xl = lax.rem(self.head, 2)
        self.y = lax.div(self.head, 2)

    def at(self, dz, xh, core):
        return (lax.rem(self.z + dz, 4) * 2 + xh) * 2 + core

    def y_at(self, k):
        return lax.rem(self.y + k, 4)

    @property
    def beside(self):
        return {"head": self.y * 2 + 1 - self.xl}

    def lines(self):
        return [self.beside] + [{"head": self.y_at(k) * 2 + self.xl} for k in (1, 2, 3)]

    @property
    def sibling(self):
        return {"dp": self.chip * 2 + 1 - self.core}

    def chips(self):
        return [{"dp": lax.rem(self.chip + k, 8) * 2 + self.core} for k in range(1, 8)]

    def heads(self):
        return [{"head": lax.rem(self.head + k, NHEAD)} for k in range(1, NHEAD)]


def greet(ids):
    barrier = pltpu.get_barrier_semaphore()
    for one in ids:
        pl.semaphore_signal(barrier, inc=1, device_id=one, device_id_type=MESH)
    return lambda: pl.semaphore_wait(barrier, len(ids))


def rcopy(src, dst, send, recv, where):
    return pltpu.make_async_remote_copy(
        src_ref=src, dst_ref=dst, send_sem=send, recv_sem=recv, device_id=where, device_id_type=MESH
    )


GATHER_SENDS = 17


class Gather:
    def __init__(self, spot, g, send, recv, half, columns=0):
        self.spot, self.g, self.s, self.r, self.h = spot, g, send, recv, half
        self.columns, self.middle = columns, (columns or 128) // 2

    def block(self, d, start=0, rows=0):
        if self.columns:
            rows = rows or self.columns
            return self.g.at[pl.ds(start, rows), pl.ds(pl.multiple_of(d * 128, 128), 128)]
        return self.g.at[pl.ds(pl.multiple_of(d * 128 + start, 64), rows or 128), :]

    def push(self, d, to, k):
        rcopy(self.block(d), self.block(d), self.s.at[k], self.r.at[d], {"dp": to}).start()

    def push_half(self, d, to, k, xh, part):
        b = self.block(d, part * self.middle, self.middle)
        rcopy(b, b, self.s.at[k], self.h.at[2 * xh + part], {"dp": to}).start()

    def arrived(self, d):
        b = self.block(d)
        rcopy(b, b, self.s.at[0], self.r.at[d], self.spot.sibling).wait_recv()

    def arrived_halves(self, d, xh):
        for part in range(2):
            b = self.block(d, part * self.middle, self.middle)
            rcopy(b, b, self.s.at[0], self.h.at[2 * xh + part], self.spot.sibling).wait_recv()

    def first(self):
        p = self.spot
        self.push(p.dp, p.at(0, 1 - p.xh, p.core), 0)
        self.push(p.dp, p.at(1, p.xh, p.core), 1)
        self.push(p.dp, p.at(3, p.xh, p.core), 2)
        self.push(p.dp, p.at(0, p.xh, 1 - p.core), 3)

    def second(self):
        p = self.spot
        b = p.at(0, 1 - p.xh, p.core)
        self.arrived(b)
        self.push(b, p.at(1, p.xh, p.core), 4)
        self.push(b, p.at(3, p.xh, p.core), 5)
        self.push(b, p.at(0, p.xh, 1 - p.core), 6)

    def third(self):
        p = self.spot
        for i, h in enumerate((p.xh, 1 - p.xh)):
            b = p.at(3, h, p.core)
            self.arrived(b)
            self.push_half(b, p.at(1, p.xh, p.core), 7 + i, h, 0)
            self.push(b, p.at(0, p.xh, 1 - p.core), 9 + i)
            b = p.at(1, h, p.core)
            self.arrived(b)
            self.push_half(b, p.at(3, p.xh, p.core), 11 + i, h, 1)
            self.push(b, p.at(0, p.xh, 1 - p.core), 13 + i)

    def fourth(self):
        p = self.spot
        for i, h in enumerate((p.xh, 1 - p.xh)):
            b = p.at(2, h, p.core)
            self.arrived_halves(b, h)
            self.push(b, p.at(0, p.xh, 1 - p.core), 15 + i)

    def last(self):
        p = self.spot
        for dz in range(4):
            for h in range(2):
                self.arrived(p.at(dz, h, 1 - p.core))
        half = self.block(0, 0, self.middle)
        for k in range(GATHER_SENDS):
            b = half if k in (7, 8, 11, 12) else self.block(0)
            rcopy(b, b, self.s.at[k], self.r.at[0], p.sibling).wait_send()


class WideGather(Gather):
    def __init__(self, spot, g, send, recv, half, offset=0):
        super().__init__(spot, g, send, recv, half)
        self.offset, self.middle = offset, 32

    def block(self, d, start=0, rows=0):
        row, column = lax.rem(d, 8) * 128 + (self.offset + start), lax.div(d, 8) * 1024
        return self.g.at[pl.ds(pl.multiple_of(row, 32), rows or 64), pl.ds(pl.multiple_of(column, 1024), 1024)]

    def tile(self, d, k):
        row, column = lax.rem(d, 8) * 128, lax.div(d, 8) * 1024 + 256 * k
        return self.g.at[pl.ds(pl.multiple_of(row, 128), 128), pl.ds(pl.multiple_of(column, 256), 256)]


class LowerGather(WideGather):
    def first(self):
        p = self.spot
        self.push(p.dp, p.at(1, p.xh, p.core), 0)
        self.push(p.dp, p.at(3, p.xh, p.core), 1)
        self.push(p.dp, p.at(0, 1 - p.xh, p.core), 2)
        self.push(p.dp, p.at(0, p.xh, 1 - p.core), 3)

    def second(self):
        p = self.spot
        for part, (source, to) in enumerate(((3, 1), (1, 3))):
            b = p.at(source, p.xh, p.core)
            self.arrived(b)
            self.push_half(b, p.at(to, p.xh, p.core), 4 + part, 0, part)
            self.push(b, p.at(0, 1 - p.xh, p.core), 6 + part)
            self.push(b, p.at(0, p.xh, 1 - p.core), 8 + part)

    def third(self):
        p = self.spot
        b = p.at(2, p.xh, p.core)
        self.arrived_halves(b, 0)
        self.push(b, p.at(0, 1 - p.xh, p.core), 10)
        self.push(b, p.at(0, p.xh, 1 - p.core), 11)

    def fourth(self):
        p = self.spot
        for k, dz in enumerate((0, 3, 1, 2)):
            b = p.at(dz, 1 - p.xh, p.core)
            self.arrived(b)
            self.push(b, p.at(0, p.xh, 1 - p.core), 12 + k)

    def last(self):
        p = self.spot
        for dz in range(4):
            for h in range(2):
                self.arrived(p.at(dz, h, 1 - p.core))
        for k in range(16):
            b = self.block(0, 0, self.middle) if k in (4, 5) else self.block(0)
            rcopy(b, b, self.s.at[k], self.r.at[0], p.sibling).wait_send()


def gather_semaphores():
    return [
        pltpu.SemaphoreType.DMA((GATHER_SENDS,)),
        pltpu.SemaphoreType.DMA((16,)),
        pltpu.SemaphoreType.DMA((4,)),
    ]


NN = (((1,), (0,)), ((), ()))
NT = (((1,), (1,)), ((), ()))
TN = (((0,), (0,)), ((), ()))


def mm(a, b, dims):
    return lax.dot_general(a, b, dims, preferred_element_type=F32)


def halves(a):
    high = a.astype(BF16)
    return high, (a - high.astype(F32)).astype(BF16)


def mm2(a, b, dims):
    return mm(a[0], b, dims) + mm(a[1], b, dims)


def mm3(a, b, dims):
    return mm(a[0], b[0], dims) + (mm(a[0], b[1], dims) + mm(a[1], b[0], dims))


def triangle(lower):
    rows = lax.broadcasted_iota(jnp.int32, (CHUNK, CHUNK), 0)
    columns = lax.broadcasted_iota(jnp.int32, (CHUNK, CHUNK), 1)
    return (rows >= columns if lower else rows <= columns).astype(BF16)


def summed_rows(lower, x):
    high = x.astype(BF16)
    rest = x - high.astype(F32)
    middle = rest.astype(BF16)
    low = (rest - middle.astype(F32)).astype(BF16)
    t = triangle(lower)
    return mm(t, high, NN) + (mm(t, middle, NN) + mm(t, low, NN))


class Segments:
    def __init__(self, spot, seq):
        self.starts = []
        total = jnp.int32(0)
        for i in range(NSEQ):
            self.starts.append(total)
            total = total + seq[i]
        self.first = spot.dp * TOK

    def of(self, position):
        found = jnp.where(position >= self.starts[0], 1, 0)
        for s in self.starts[1:]:
            found = found + jnp.where(position >= s, 1, 0)
        return found - 1

    def column(self, c):
        return self.of(self.first + c * CHUNK + lax.broadcasted_iota(jnp.int32, (CHUNK, KDIM), 0))

    def row(self, c):
        return self.of(self.first + c * CHUNK + lax.broadcasted_iota(jnp.int32, (CHUNK, KDIM), 1))

    def before(self, c):
        return self.of(self.first + c * CHUNK - 1)

    def final(self, c):
        return self.of(self.first + (c + 1) * CHUNK - 1)


def lower_bound(lb, layer):
    x = lb[...]
    e = jnp.exp(x - jnp.max(x, axis=0, keepdims=True))
    soft = e / jnp.sum(e, axis=0, keepdims=True)
    depth = lax.broadcasted_iota(jnp.int32, x.shape, 0)
    picked = jnp.where((depth >= 1) & (depth <= layer), 1.0, 0.0)
    return soft, picked, jnp.sum(soft * picked, axis=0, keepdims=True)


def sigmoid(x):
    return lax.logistic(x)


def slope(x, s):
    return s * (1.0 + x * (1.0 - s))


class Exchange:
    def __init__(self, spot, msg, sib, slots, give, take, send, recv, backward):
        self.p, self.msg, self.sib, self.slots = spot, msg, sib, slots
        self.give, self.take, self.s, self.r, self.back = give, take, send, recv, backward

    def to_sibling(self):
        p = self.p
        rcopy(self.msg.at[1 - p.core], self.sib, self.s.at[7], self.r.at[8], p.sibling).start()

    def to_chips(self):
        p = self.p
        rcopy(self.sib, self.sib, self.s.at[7], self.r.at[8], p.sibling).wait_recv()
        mine, other = self.msg[p.core], self.sib[...]
        zero = p.core == 0
        one, two = jnp.where(zero, mine, other), jnp.where(zero, other, mine)
        near, far = (two, one) if self.back else (one, two)
        self.near = near
        state = near[0:128] * far[128:129] + far[0:128]
        rate = near[128:136] * far[128:136]
        high = rate.astype(BF16).astype(F32)
        self.slots[p.chip, 0:128, :] = state.astype(BF16)
        self.slots[p.chip, 128:144, :] = jnp.concatenate([high, rate - high], axis=0).astype(BF16)
        for k, to in enumerate(p.chips()):
            rcopy(self.slots.at[p.chip], self.slots.at[p.chip], self.s.at[k], self.r.at[p.chip], to).start()

    def result(self, out):
        p = self.p
        for k in range(1, 8):
            chip = lax.rem(p.chip + k, 8)
            rcopy(self.slots.at[chip], self.slots.at[chip], self.s.at[0], self.r.at[chip], p.sibling).wait_recv()
        state = jnp.zeros((128, 128), F32)
        for k in range(7, 0, -1) if self.back else range(7):
            m = self.slots[k].astype(F32)
            after = state * (m[128:129] + m[136:137]) + m[0:128]
            state = jnp.where(k > p.chip if self.back else k < p.chip, after, state)
        second = state * self.near[128:129] + self.near[0:128]
        is_first = p.core == (1 if self.back else 0)
        self.give[...] = jnp.where(is_first, second, state)
        move = rcopy(self.give, self.take, self.s.at[8], self.r.at[9], p.sibling)
        move.start()
        out[p.core] = jnp.where(is_first, state, second)
        move.wait_recv()
        out[1 - p.core] = self.take[...]

    def finish(self):
        p = self.p
        for k in range(7):
            rcopy(self.slots.at[0], self.slots.at[0], self.s.at[k], self.r.at[0], p.sibling).wait_send()
        rcopy(self.sib, self.sib, self.s.at[7], self.r.at[8], p.sibling).wait_send()
        rcopy(self.give, self.take, self.s.at[8], self.r.at[9], p.sibling).wait_send()


def exchange_scratch():
    return [
        pltpu.VMEM((2, 136, 128), F32),
        pltpu.VMEM((136, 128), F32),
        pltpu.VMEM((8, 144, 128), BF16),
        pltpu.VMEM((128, 128), F32),
        pltpu.VMEM((128, 128), F32),
        pltpu.SemaphoreType.DMA((9,)),
        pltpu.SemaphoreType.DMA((10,)),
    ]


def gates(raw, bound, rows):
    query_raw = raw[rows, 0:256]
    logistic = sigmoid(raw[rows, 256:512])
    forget = bound + (1.0 - bound) * logistic
    query = (query_raw * sigmoid(query_raw)).astype(BF16)
    keys = (1.0 - forget).astype(BF16)
    values = raw[rows, 512:768].astype(BF16)
    return logistic, forget, query, keys, values


HALF = D // 2


class HeadSum:
    def __init__(self, spot, ps, slots, send, recv):
        self.p, self.ps, self.slots, self.s, self.r = spot, ps, slots, send, recv

    def left_of(self, start, rows=ROWS):
        return self.slots.at[pl.ds(start, rows), pl.ds(0, HALF)]

    def right_of(self, start, rows=ROWS):
        return self.slots.at[pl.ds(start, rows), pl.ds(HALF, HALF)]

    def part(self, h, rows, right):
        return self.ps.at[pl.ds(pl.multiple_of(h * ROWS, ROWS), rows), pl.ds(HALF if right else 0, HALF)]

    def left_x(self, k):
        p = self.p
        h = p.y_at(k) * 2 + 1 - p.xl
        return rcopy(self.part(h, ROWS, False), self.left_of(64 * k), self.s.at[k], self.r.at[k], p.beside)

    def left_y(self, k):
        p = self.p
        to = {"head": p.y_at(k) * 2 + p.xl}
        return rcopy(self.left_of(64 * k), self.left_of(192 + 64 * k), self.s.at[3 + k], self.r.at[3 + k], to)

    def right_y(self, k):
        p = self.p
        to = {"head": p.y_at(k) * 2 + p.xl}
        return rcopy(
            self.part(p.y_at(k) * 2, 128, True), self.right_of(128 * k - 128, 128), self.s.at[6 + k], self.r.at[6 + k], to
        )

    def right_x(self):
        return rcopy(self.right_of(384), self.right_of(448), self.s.at[10], self.r.at[10], self.p.beside)

    def send_left(self):
        for k in (2, 1, 3, 0):
            self.left_x(k).start()

    def send_right(self):
        for k in (2, 1, 3):
            self.right_y(k).start()

    def send(self):
        self.send_right()
        self.send_left()

    def join(self, k):
        p = self.p
        self.left_x(k).wait_recv()
        mine = self.part(p.y_at(k) * 2 + p.xl, ROWS, False)
        one = self.left_of(64 * k)
        one[...] = (one[...].astype(F32) + mine[...].astype(F32)).astype(BF16)
        if k:
            self.left_y(k).start()

    def middle(self):
        p = self.p
        for k in (2, 1, 3):
            self.join(k)
        for k in (1, 3, 2):
            self.right_y(k).wait_recv()

        def total(xl):
            one = self.part(p.y * 2 + xl, ROWS, True)[...].astype(F32)
            for k in range(3):
                rows = pl.ds(pl.multiple_of(128 * k + xl * ROWS, ROWS), ROWS)
                one = one + self.slots[rows, HALF:].astype(F32)
            return one.astype(BF16)

        self.slots[384:448, HALF:] = total(1 - p.xl)
        self.right_x().start()
        self.slots[448:512, 0:HALF] = total(p.xl)
        self.join(0)

    def collect(self):
        for k in (1, 3, 2):
            self.left_y(k).wait_recv()
        self.right_x().wait_recv()

    def rows(self, start, count):
        def at(row, left):
            rows = pl.ds(pl.multiple_of(row + start, 16), count)
            return self.slots[rows, 0:HALF].astype(F32) if left else self.slots[rows, HALF:].astype(F32)

        left = (at(0, True) + at(256, True)) + (at(320, True) + at(384, True))
        return jnp.concatenate([left, at(448, True) + at(448, False)], axis=1)

    def finish(self):
        for k in range(4):
            self.left_x(k).wait_send()
        for k in (1, 2, 3):
            self.left_y(k).wait_send()
            self.right_y(k).wait_send()
        self.right_x().wait_send()


class LateHeadSum:
    def __init__(self, spot, ps, slots, send, recv):
        self.p, self.ps, self.slots, self.s, self.r = spot, ps, slots, send, recv

    def block(self, ref, start, rows=ROWS):
        return ref.at[pl.ds(pl.multiple_of(start, ROWS), rows), :]

    def along_y(self, k):
        p = self.p
        y = p.y_at(k)
        return rcopy(
            self.block(self.ps, y * 128, 128), self.block(self.slots, 128 * k - 128, 128),
            self.s.at[k], self.r.at[k], {"head": y * 2 + p.xl},
        )

    def along_x(self):
        return rcopy(self.block(self.slots, 384), self.block(self.slots, 448), self.s.at[0], self.r.at[0], self.p.beside)

    def send(self):
        for k in (2, 1, 3):
            self.along_y(k).start()

    def part(self, xl, start, count):
        p = self.p
        one = self.ps[pl.ds(pl.multiple_of((p.y * 2 + xl) * ROWS + start, 16), count), :].astype(F32)
        for k in range(3):
            rows = pl.ds(pl.multiple_of(128 * k + xl * ROWS + start, 16), count)
            one = one + self.slots[rows, :].astype(F32)
        return one

    def middle(self):
        for k in (1, 3, 2):
            self.along_y(k).wait_recv()

        @pl.loop(0, 4)
        def _(i):
            rows = pl.ds(pl.multiple_of(384 + i * 16, 16), 16)
            self.slots[rows, :] = self.part(1 - self.p.xl, i * 16, 16).astype(BF16)

        self.along_x().start()

    def collect(self):
        self.along_x().wait_recv()

    def rows(self, start, count):
        rows = pl.ds(pl.multiple_of(448 + start, 16), count)
        return self.part(self.p.xl, start, count) + self.slots[rows, :].astype(F32)

    def finish(self):
        for k in (1, 2, 3):
            self.along_y(k).wait_send()
        self.along_x().wait_send()


class HeadGather:
    def __init__(self, spot, full, send, recv):
        self.p, self.full, self.s, self.r = spot, full, send, recv

    def block(self, dy, stream, start=0, rows=ROWS):
        p = self.p
        h = p.y_at(dy) * 2 + (1 - p.xl if stream == 2 else p.xl)
        columns = pl.ds(0 if stream else HALF, HALF)
        return self.full.at[pl.ds(pl.multiple_of(h * ROWS + start, 32), rows), columns]

    def along_y(self, stream, k):
        p = self.p
        b, i = self.block(0, stream), 4 * stream + (k == 3)
        return rcopy(b, b, self.s.at[i], self.r.at[i], {"head": p.y_at(k) * 2 + p.xl})

    def onward(self, stream, part):
        p = self.p
        b, i = self.block(1 if part else 3, stream, 32 * part, 32), 4 * stream + 2 + part
        return rcopy(b, b, self.s.at[i], self.r.at[i], {"head": p.y_at(3 if part else 1) * 2 + p.xl})

    def beside(self, dy, stream):
        b, i = self.block(dy, stream), 12 if stream else 13 + dy
        return rcopy(b, b, self.s.at[i], self.r.at[i], self.p.beside)

    def send(self):
        self.beside(0, 1).start()
        for k in (1, 3):
            self.along_y(0, k).start()
        self.beside(0, 0).start()
        for k in (1, 3):
            self.along_y(1, k).start()

    def middle(self):
        self.beside(0, 1).wait_recv()
        for k in (1, 3):
            self.along_y(2, k).start()
        for part in range(2):
            self.along_y(0, 3 if part else 1).wait_recv()
            self.onward(0, part).start()
            self.beside(1 if part else 3, 0).start()
        for part in range(2):
            self.along_y(1, 3 if part else 1).wait_recv()
            self.onward(1, part).start()

    def late(self):
        for part in range(2):
            self.along_y(2, 3 if part else 1).wait_recv()
            self.onward(2, part).start()
        for part in range(2):
            self.onward(0, part).wait_recv()
        self.beside(2, 0).start()

    def collect(self):
        for dy in range(4):
            self.beside(dy, 0).wait_recv()
        for stream in (1, 2):
            for part in range(2):
                self.onward(stream, part).wait_recv()

    def finish(self):
        self.beside(0, 1).wait_send()
        for dy in range(4):
            self.beside(dy, 0).wait_send()
        for stream in range(3):
            for part in range(2):
                self.along_y(stream, 3 if part else 1).wait_send()
                self.onward(stream, part).wait_send()


def twenty():
    return [pltpu.SemaphoreType.DMA((20,)), pltpu.SemaphoreType.DMA((20,))]


def sixteen():
    return [pltpu.SemaphoreType.DMA((16,)), pltpu.SemaphoreType.DMA((16,))]


def eight():
    return [pltpu.SemaphoreType.DMA((8,)), pltpu.SemaphoreType.DMA((8,))]


class DpSum:
    def __init__(self, spot, rows, gs, cr, zr, xs, xr, send, recv):
        n = pl.ds(0, rows)
        self.rows, self.p = rows, spot
        self.gs, self.cr, self.zr = gs.at[:, :, n, :], cr.at[:, n, :], zr.at[:, :, n, :]
        self.xs, self.xr, self.s, self.r = xs.at[n, :], xr.at[n, :], send, recv

    def pair(self, i):
        p = self.p
        two = pl.ds(2 * i, 2)
        return rcopy(self.gs.at[1 - p.core, two], self.cr.at[two], self.s.at[i], self.r.at[i], p.sibling)

    def to_sibling(self):
        for i in range(4):
            self.pair(i).start()

    def half(self, part):
        return pl.ds(part * (self.rows // 2), self.rows // 2)

    def along_z(self, d, block, part, slot, i):
        p = self.p
        z = lax.rem(p.z + block, 4)
        where = {"dp": (lax.rem(p.z + d, 4) * 2 + p.xh) * 2 + p.core}
        source = self.gs.at[p.core, pl.ds(z * 2, 2), self.half(part), :]
        return rcopy(source, self.zr.at[slot, :, self.half(part), :], self.s.at[4 + i], self.r.at[4 + i], where)

    def far(self, part):
        return self.along_z(3 if part else 1, 2, part, 2, part)

    def near(self, part):
        return self.along_z(3, 3, 0, 1, 2) if part else self.along_z(1, 1, 1, 0, 3)

    def joined(self, part):
        return self.along_z(3, 3, 1, 1, 4) if part else self.along_z(1, 1, 0, 0, 5)

    def to_z(self):
        p = self.p
        for i in range(4):
            self.pair(i).wait_recv()

        @pl.loop(0, 8)
        def _(k):
            self.gs[p.core, k] = (self.gs[p.core, k].astype(F32) + self.cr[k].astype(F32)).astype(BF16)

        for part in range(2):
            self.far(part).start()
        for part in range(2):
            self.near(part).start()

    def join(self):
        p = self.p
        for part in range(2):
            self.far(part).wait_recv()
            z = lax.rem(p.z + (3 if part else 1), 4)
            for h in range(2):
                mine = self.gs.at[p.core, z * 2 + h, self.half(part), :]
                other = self.zr.at[2, h, self.half(part), :]
                mine[...] = (mine[...].astype(F32) + other[...].astype(F32)).astype(BF16)
            self.joined(part).start()

    def last_move(self):
        p = self.p
        where = {"dp": (p.z * 2 + 1 - p.xh) * 2 + p.core}
        return rcopy(self.xs, self.xr, self.s.at[10], self.r.at[10], where)

    def to_x(self, put, go=True):
        p = self.p
        for part in range(2):
            self.near(part).wait_recv()
            self.joined(part).wait_recv()

        def total(h):
            one = self.gs[p.core, 2 * p.z + h].astype(F32)
            for i in range(2):
                one = one + self.zr[i, h].astype(F32)
            return one

        self.xs[...] = total(1 - p.xh).astype(BF16)
        if go:
            self.go()
        put(total(p.xh))

    def go(self):
        self.last_move().start()

    def end(self, add):
        self.last_move().wait_recv()
        add(self.xr[...].astype(F32))

    def finish(self):
        for i in range(4):
            self.pair(i).wait_send()
        for part in range(2):
            self.far(part).wait_send()
            self.near(part).wait_send()
            self.joined(part).wait_send()
        self.last_move().wait_send()


def dp_sum_scratch(rows):
    return [
        pltpu.VMEM((2, 8, rows, 128), BF16),
        pltpu.VMEM((8, rows, 128), BF16),
        pltpu.VMEM((3, 2, rows, 128), BF16),
        pltpu.VMEM((rows, 128), BF16),
        pltpu.VMEM((rows, 128), BF16),
        *sixteen(),
    ]


def products(left_turned, right, gs):
    @pl.loop(0, 8)
    def _(k):
        columns = pl.ds(pl.multiple_of(k * 256, 256), 256)
        both = mm(left_turned[...], right[:, columns], NN).astype(BF16)
        gs[0, k] = both[:, 0:128]
        gs[1, k] = both[:, 128:256]


def products_turned(left, first, second, gs):
    @pl.loop(0, 8)
    def _(k):
        turned = left[:, pl.ds(pl.multiple_of(k * 256, 256), 256)]
        for i, right in enumerate((first, second)):
            both = mm(turned, right[...], TN).astype(BF16)
            for q in range(2):
                rows = slice(256 * i + 128 * q, 256 * i + 128 * (q + 1))
                gs[0, k, rows, :] = both[0:128, 128 * q : 128 * (q + 1)]
                gs[1, k, rows, :] = both[128:256, 128 * q : 128 * (q + 1)]


def write(ref):
    def put(x):
        ref[...] = x

    return put


def accumulate(ref):
    def add(x):
        ref[...] += x

    return add


VEC = 40


class Total:
    def __init__(self, spot, vec, h_slots, c_slots, own, other, h_s, h_r, c_s, c_r, k_s, k_r):
        self.p, self.vec, self.hs, self.cs, self.own, self.other = spot, vec, h_slots, c_slots, own, other
        self.h_s, self.h_r, self.c_s, self.c_r, self.k_s, self.k_r = h_s, h_r, c_s, c_r, k_s, k_r

    def send(self):
        p = self.p
        self.cs[p.chip] = self.vec[...]
        for k, to in enumerate(p.chips()):
            rcopy(self.cs.at[p.chip], self.cs.at[p.chip], self.c_s.at[k], self.c_r.at[p.chip], to).start()

    def middle(self):
        p = self.p
        for k in range(1, 8):
            chip = lax.rem(p.chip + k, 8)
            rcopy(self.cs.at[chip], self.cs.at[chip], self.c_s.at[0], self.c_r.at[chip], p.sibling).wait_recv()
        total = self.cs[0]
        for k in range(1, 8):
            total = total + self.cs[k]
        self.own[...] = total
        rcopy(self.own, self.other, self.k_s, self.k_r, p.sibling).start()

    def late(self):
        p = self.p
        rcopy(self.own, self.other, self.k_s, self.k_r, p.sibling).wait_recv()
        self.hs[p.head] = self.own[...] + self.other[...]
        for k in range(1, NHEAD):
            h = lax.rem(p.head + k, NHEAD)
            rcopy(self.hs.at[p.head], self.hs.at[p.head], self.h_s.at[k], self.h_r.at[p.head], {"head": h}).start()

    def result(self):
        p = self.p
        for k in range(1, NHEAD):
            h = lax.rem(p.head + k, NHEAD)
            rcopy(self.hs.at[h], self.hs.at[h], self.h_s.at[0], self.h_r.at[h], p.sibling).wait_recv()
        total = self.hs[0]
        for h in range(1, NHEAD):
            total = total + self.hs[h]
        per_head = lax.broadcasted_iota(jnp.int32, (VEC, 128), 0) >= 34
        return jnp.where(per_head, self.hs[p.head], total)

    def finish(self):
        p = self.p
        for k in range(1, NHEAD):
            rcopy(self.hs.at[0], self.hs.at[0], self.h_s.at[k], self.h_r.at[0], p.sibling).wait_send()
        for k in range(7):
            rcopy(self.cs.at[0], self.cs.at[0], self.c_s.at[k], self.c_r.at[0], p.sibling).wait_send()
        rcopy(self.own, self.other, self.k_s, self.k_r, p.sibling).wait_send()


def layer_block(
    hid, dy_in, wq, wf, wi, wo, w_output, wg_in, wu_in, wd_in, gain, lb, group_gain, ffn_gain, layer, seq,
    i0, i1, i2, i3, i4, i5, i6, i7, i8, i9, i10, i11, i12, i13, i14, xn_out, w_out,
    block_out, grad_in, out_query, out_forget, out_input, out_outgate, out_output, out_bounds,
    out_norm, out_group, out_ffn, out_mean, out_gate, out_up, out_down,
    ps, slots, hn, wide, wg, wu, wd, wt, raw, hid_rows, gated, gated_t, mixed, run, states, update, resid, d_resid,
    hidden, dg, du, hidden_t, dg_t, du_t, draw, d_mixed, d_query, d_keys, d_values, decay, incoming, vec,
    norm_terms, ffn_terms, group_total, bound_total, total,
    msg, sib, slots3, give, take, ex_send, ex_recv, sib2, slots4, take2, ex2_send, ex2_recv,
    rs0_s, rs0_r, ag0_s, ag0_r, rs_s, rs_r, ag_s, ag_r, rs1_s, rs1_r, rs2_s, rs2_r,
    ws, wr, wh, vs, vr, vh, os, or_, oh, s0, r0, h0, s1, r1, h1, s2, r2, h2,
    a0, a1, a2, a3, a4, a5, a6, b0, b1, b2, b3, b4, b5, b6, c0, c1, c2, c3, c4, c5, c6,
    e0, e1, e2, e3, e4, e5, e6, f3, f4, f5, f6, g3, g4, g5, g6,
    t0, t1, t2, t3, t4, t5, t6, t7, t8, t9, local_sem,
):
    dy, db, xn = wide.at[0:TOK], wide.at[TOK : 2 * TOK], hn
    used = []

    def load(source, to):
        move = pltpu.make_async_copy(source, to, local_sem.at[len(used)])
        move.start()
        used.append(move)
        return move

    emitted = []
    made = (
        block_out, grad_in, out_query, out_forget, out_input, out_outgate, out_output, out_bounds,
        out_norm, out_group, out_ffn, out_mean, out_gate, out_up, out_down,
    )
    to_emit = (i0, i1, i2, i3, i4, i5, i6, i7, i8, i9, i10, i11, i12, i13, i14)

    def emit(*which):
        for k in which:
            emitted.append(load(made[k], to_emit[k]))

    def put(low, high):
        def write_four(x):
            low[:, 0:128], low[:, 128:256] = x[0:128], x[128:256]
            high[:, 0:128], high[:, 128:256] = x[256:384], x[384:512]

        return write_four

    def add_to(low, high):
        def add(x):
            low[:, 0:128] += x[0:128]
            low[:, 128:256] += x[128:256]
            high[:, 0:128] += x[256:384]
            high[:, 128:256] += x[384:512]

        return add

    p = Spot()
    arrive = greet(p.chips() + [p.sibling] + p.heads())
    own = pl.multiple_of(p.head * ROWS, ROWS)
    mine = pl.ds(pl.multiple_of(p.dp * 128, 128), 128)
    gather = WideGather(p, wide, ws, wr, wh)
    lower = LowerGather(p, wide, vs, vr, vh, 64)
    loads = [load(one, gather.tile(p.dp, k)) for k, one in enumerate((wq, wf, wi, wo))]
    loads.append(load(hid, ps))
    own_blocks = [load(w_output, wt.at[:, mine])]
    own_blocks += [load(one, full.at[:, mine]) for one, full in ((wg_in, wg), (wu_in, wu), (wd_in, wd))]
    own_rows = load(hid.at[pl.ds(own, ROWS), :], hid_rows)
    for move in loads[:4]:
        move.wait()
    arrive()
    gather.first()
    lower.first()
    loads[4].wait()
    later = Gather(p, wt, os, or_, oh, HERE)
    gathers = [Gather(p, wg, s0, r0, h0, FFH), Gather(p, wu, s1, r1, h1, FFH), Gather(p, wd, s2, r2, h2, FFH)]

    @pl.loop(0, 8)
    def _(i):
        rows = pl.ds(pl.multiple_of(i * 64, 64), 64)
        x = ps[rows, :].astype(F32)
        scale = lax.rsqrt(jnp.mean(x * x, axis=-1, keepdims=True) + EPS)
        xn[rows, :] = (x * scale * gain[...]).astype(BF16)

    gather.second()
    lower.second()
    gather.third()
    lower.third()
    gather.fourth()
    lower.fourth()
    for move in own_blocks:
        move.wait()
    later.first()
    gathers[0].first()
    gather.last()
    lower.last()
    spills = [load(xn, xn_out), load(wide, w_out)]

    for j in range(4):
        columns = slice(j * 256, (j + 1) * 256)
        other = slice(1024 + j * 256, 1024 + (j + 1) * 256)
        raw[:, columns] = mm(xn[:, 0:1024], wide[:, columns], NN) + mm(xn[:, 1024:2048], wide[:, other], NN)

    later.second()
    segments = Segments(p, seq)
    soft, picked, bound = lower_bound(lb, layer[0])
    total[...] = jnp.zeros_like(total)

    @pl.loop(0, CHUNKS)
    def _(c):
        rows = pl.ds(pl.multiple_of(c * CHUNK, CHUNK), CHUNK)
        logistic, forget, query, keys, values = gates(raw, bound, rows)
        total[...] += jnp.sum(forget, axis=0, keepdims=True)
        running = summed_rows(True, jnp.log(forget))
        run[rows, :] = running
        ending = running[127:128]
        tail = keys.astype(F32) * jnp.exp(ending - running)
        final = segments.final(c)
        rate = jnp.exp(ending) * jnp.where(final == segments.before(c), 1.0, 0.0)
        decay[c] = jnp.broadcast_to(rate, (8, HERE))
        ends = jnp.where(segments.column(c) == final, 1.0, 0.0)
        for h in range(2):
            lanes = slice(h * 128, (h + 1) * 128)
            high, low = halves(tail[:, lanes] * ends)
            update[h, c] = mm(values[:, lanes], high, TN) + mm(values[:, lanes], low, TN)

    for h in range(2):
        lanes = slice(h * 128, (h + 1) * 128)
        state, rate = update[h, 0], decay[0, 0:1, lanes]
        for c in range(1, CHUNKS):
            state = state * decay[c, 0:1, lanes] + update[h, c]
            rate = rate * decay[c, 0:1, lanes]
        msg[h, 0:128, :] = state
        msg[h, 128:136, :] = jnp.broadcast_to(rate, (8, 128))
    exchange = Exchange(p, msg, sib, slots3, give, take, ex_send, ex_recv, False)
    exchange.to_sibling()
    exchange.to_chips()

    @pl.loop(0, CHUNKS)
    def _(c):
        rows = pl.ds(pl.multiple_of(c * CHUNK, CHUNK), CHUNK)
        _, _, query, keys, values = gates(raw, bound, rows)
        running = run[rows, :]
        middle = running[63:64]
        lifted = query.astype(F32) * jnp.exp(running - middle)
        lowered = keys.astype(F32) * jnp.exp(middle - running)
        linked = (segments.column(c) == segments.row(c)) & (
            lax.broadcasted_iota(jnp.int32, (CHUNK, CHUNK), 0)
            >= lax.broadcasted_iota(jnp.int32, (CHUNK, CHUNK), 1)
        )
        for h in range(2):
            lanes = slice(h * 128, (h + 1) * 128)
            scores = mm3(halves(lifted[:, lanes]), halves(lowered[:, lanes]), NT)
            scores = jnp.where(linked, scores, 0.0)
            mixed[rows, lanes] = mm2(halves(scores), values[:, lanes], NN)

    later.third()
    gathers[1].first()
    gathers[2].first()
    gathers[0].second()
    later.fourth()
    exchange.result(incoming)
    for h in range(2):
        lanes = slice(h * 128, (h + 1) * 128)
        state = incoming[h]
        states[h, 0] = state
        for c in range(CHUNKS):
            state = state * decay[c, 0:1, lanes] + update[h, c]
            states[h, c + 1] = state

    @pl.loop(0, CHUNKS)
    def _(c):
        rows = pl.ds(pl.multiple_of(c * CHUNK, CHUNK), CHUNK)
        carried = jnp.where(segments.column(c) == segments.before(c), 1.0, 0.0)
        for h in range(2):
            lanes = slice(h * 128, (h + 1) * 128)
            query_raw = raw[rows, h * 128 : (h + 1) * 128]
            query = (query_raw * sigmoid(query_raw)).astype(BF16).astype(F32)
            reach = query * jnp.exp(run[rows, lanes]) * carried
            x = mixed[rows, lanes] + mm3(halves(reach), halves(states[h, c]), NT)
            mixed[rows, lanes] = x
            scale = lax.rsqrt(jnp.mean(x * x, axis=-1, keepdims=True) + EPS)
            gate = raw[rows, 768 + h * 128 : 768 + (h + 1) * 128]
            gated[rows, lanes] = (x * scale * group_gain[...] * (gate * sigmoid(gate))).astype(BF16)

    gathers[1].second()
    later.last()

    for move in spills:
        move.wait()
    dy_load = load(dy_in, dy)
    scatter0 = HeadSum(p, ps, slots, rs0_s, rs0_r)
    for start, send in ((HALF, scatter0.send_right), (0, scatter0.send_left)):
        for j in range(4):
            columns = slice(start + j * 256, start + (j + 1) * 256)
            ps[:, columns] = mm(gated[...], wt[:, columns], NN).astype(BF16)

        send()
    gathers[2].second()
    gathers[0].third()
    scatter0.middle()
    gathers[1].third()
    gathers[2].third()
    scatter0.collect()
    own_rows.wait()

    @pl.loop(0, 4)
    def _(i):
        rows = pl.ds(pl.multiple_of(i * 16, 16), 16)
        here = pl.ds(pl.multiple_of(own + i * 16, 16), 16)
        x = hid_rows[rows, :].astype(F32) + scatter0.rows(i * 16, 16)
        resid[rows, :] = x
        scale = lax.rsqrt(jnp.mean(x * x, axis=-1, keepdims=True) + EPS)
        hn[here, :] = (x * scale * ffn_gain[...]).astype(BF16)

    scatter0.finish()
    spread0 = HeadGather(p, hn, ag0_s, ag0_r)
    spread0.send()
    spread0.middle()
    for g in gathers:
        g.fourth()
    spread0.late()
    for g in gathers:
        g.last()
    dy_load.wait()
    gated_t[...] = gated[...].T
    exchange.finish()
    spread0.collect()

    for low, high in ((0, 256), (256, 512), (512, FFH)):
        gate = mm(hn[...], wg[low:high, :], NT)
        up = mm(hn[...], wu[low:high, :], NT)
        dh = mm(dy[...], wd[low:high, :], NT)
        s = sigmoid(gate)
        silu = gate * s
        hidden[:, low:high] = (silu * up).astype(BF16)
        dg[:, low:high] = (dh * up * slope(gate, s)).astype(BF16)
        du[:, low:high] = (dh * silu).astype(BF16)

    scatter = HeadSum(p, ps, slots, rs_s, rs_r)
    for start, send in ((HALF, scatter.send_right), (0, scatter.send_left)):
        for j in range(4):
            columns = slice(start + j * 256, start + (j + 1) * 256)
            ps[:, columns] = (mm(dg[...], wg[:, columns], NN) + mm(du[...], wu[:, columns], NN)).astype(BF16)

        send()
    sums = [
        DpSum(p, FFH, a0, a1, a2, a3, a4, a5, a6),
        DpSum(p, FFH, b0, b1, b2, b3, b4, b5, b6),
        DpSum(p, FFH, c0, c1, c2, c3, c4, c5, c6),
    ]
    dg_t[...] = dg[...].T
    products(dg_t, hn, a0)
    sums[0].to_sibling()
    du_t[...] = du[...].T
    products(du_t, hn, b0)
    sums[0].to_z()
    sums[1].to_sibling()
    scatter.middle()
    hidden_t[...] = hidden[...].T
    products(hidden_t, dy, c0)
    sums[1].to_z()
    sums[2].to_sibling()
    scatter.collect()
    ffn_terms[...] = jnp.zeros_like(ffn_terms)

    @pl.loop(0, 4)
    def _(i):
        rows = pl.ds(pl.multiple_of(i * 16, 16), 16)
        here = pl.ds(pl.multiple_of(own + i * 16, 16), 16)
        grad, x = scatter.rows(i * 16, 16), resid[rows, :]
        inverse = lax.rsqrt(jnp.mean(x * x, axis=-1, keepdims=True) + EPS)
        scaled, normed = grad * ffn_gain[...], x * inverse
        back = inverse * (scaled - normed * jnp.mean(scaled * normed, axis=-1, keepdims=True))
        ffn_terms[...] += jnp.sum(grad * normed, axis=0, keepdims=True)
        both = dy[here, :].astype(F32) + back
        d_resid[rows, :] = both
        db[here, :] = both.astype(BF16)

    scatter.finish()
    spread = HeadGather(p, db, ag_s, ag_r)
    spread.send()
    sums[2].to_z()
    spread.middle()
    sums[0].join()
    spread.late()

    @pl.loop(0, 8)
    def _(j):
        columns = pl.ds(pl.multiple_of(j * 256, 256), 256)
        wu[0:TOK, columns] = mm(hidden[...], wd[:, columns], NN).astype(BF16)

    sums[1].join()
    spread0.finish()
    late = [load(xn_out, hn), load(w_out.at[0:TOK], wd.at[0:TOK]), load(w_out.at[TOK : 2 * TOK], dy)]
    group_total[...] = jnp.zeros_like(group_total)
    for move in late:
        move.wait()
    sums[2].join()
    spread.collect()
    scatter1 = LateHeadSum(p, wu, wg, rs1_s, rs1_r)
    scatter1.send()
    d_query[...] = mm(db[...], wt[...], NT)

    @pl.loop(0, CHUNKS)
    def _(c):
        rows = pl.ds(pl.multiple_of(c * CHUNK, CHUNK), CHUNK)
        carried = jnp.where(segments.column(c) == segments.before(c), 1.0, 0.0)
        running = run[rows, :]
        for h in range(2):
            lanes = slice(h * 128, (h + 1) * 128)
            x, grad = mixed[rows, lanes], d_query[rows, lanes]
            gate = raw[rows, 768 + h * 128 : 768 + (h + 1) * 128]
            s = sigmoid(gate)
            inverse = lax.rsqrt(jnp.mean(x * x, axis=-1, keepdims=True) + EPS)
            normed = x * inverse
            draw[rows, 768 + h * 128 : 768 + (h + 1) * 128] = (
                grad * (normed * group_gain[...]) * slope(gate, s)
            ).astype(BF16)
            inner = grad * (gate * s)
            scaled = inner * group_gain[...]
            back = inverse * (scaled - normed * jnp.mean(scaled * normed, axis=-1, keepdims=True))
            group_total[...] += jnp.sum(inner * normed, axis=0, keepdims=True)
            back = back.astype(BF16)
            d_mixed[rows, lanes] = back
            query_raw = raw[rows, lanes]
            query = (query_raw * sigmoid(query_raw)).astype(BF16).astype(F32)
            high, low = halves(query * jnp.exp(running[:, lanes]) * carried)
            update[h, c] = mm(back, high, TN) + mm(back, low, TN)

    for h in range(2):
        lanes = slice(h * 128, (h + 1) * 128)
        state, rate = update[h, CHUNKS - 1], decay[CHUNKS - 1, 0:1, lanes]
        for c in range(CHUNKS - 2, -1, -1):
            state = state * decay[c, 0:1, lanes] + update[h, c]
            rate = rate * decay[c, 0:1, lanes]
        msg[h, 0:128, :] = state
        msg[h, 128:136, :] = jnp.broadcast_to(rate, (8, 128))
    exchange2 = Exchange(p, msg, sib2, slots4, give, take2, ex2_send, ex2_recv, True)
    exchange2.to_sibling()
    results = (out_gate, out_up, out_down)
    for one, out in zip(sums[:2], results):
        one.to_x(write(out), go=False)
    exchange2.to_chips()
    for one in sums[:2]:
        one.go()

    @pl.loop(0, CHUNKS)
    def _(c):
        rows = pl.ds(pl.multiple_of(c * CHUNK, CHUNK), CHUNK)
        running = run[rows, :]
        middle = running[63:64]
        _, _, query, keys, values = gates(raw, bound, rows)
        up, down_ = jnp.exp(running - middle), jnp.exp(middle - running)
        lifted = query.astype(F32) * up
        lowered = keys.astype(F32) * down_
        column, row = segments.column(c), segments.row(c)
        carried = jnp.where(column == segments.before(c), 1.0, 0.0)
        linked = (column == row) & (
            lax.broadcasted_iota(jnp.int32, (CHUNK, CHUNK), 0)
            >= lax.broadcasted_iota(jnp.int32, (CHUNK, CHUNK), 1)
        )
        for h in range(2):
            lanes = slice(h * 128, (h + 1) * 128)
            lift, lower = halves(lifted[:, lanes]), halves(lowered[:, lanes])
            scores = halves(jnp.where(linked, mm3(lift, lower, NT), 0.0))
            grad = d_mixed[rows, lanes]
            d_scores = halves(jnp.where(linked, mm(grad, values[:, lanes], NT), 0.0))
            d_values[rows, lanes] = mm(scores[0], grad, TN) + mm(scores[1], grad, TN)
            state = halves(states[h, c])
            outer = mm(grad, state[0], NN) + mm(grad, state[1], NN)
            query_grad = mm3(d_scores, lower, NN) * up[:, lanes] + outer * jnp.exp(running[:, lanes]) * carried
            d_query[rows, lanes] = query_grad
            query_raw = raw[rows, lanes]
            draw[rows, lanes] = (query_grad * slope(query_raw, sigmoid(query_raw))).astype(BF16)
            d_keys[rows, lanes] = mm3(d_scores, lift, TN) * down_[:, lanes]

    for one in sums[:2]:
        one.finish()
    first = DpSum(p, 512, a0, a1, a2, f3, f4, f5, f6)
    second = DpSum(p, 512, b0, b1, b2, g3, g4, g5, g6)
    third = DpSum(p, HERE, e0, e1, e2, e3, e4, e5, e6)
    products_turned(hn, draw.at[:, 0:256], draw.at[:, 768:1024], a0)
    exchange2.result(incoming)
    first.to_sibling()
    sums[2].to_x(write(out_down))
    for one, out in zip(sums[:2], results):
        one.end(accumulate(out))
    emit(12, 13)
    first.to_z()
    bound_total[...] = jnp.zeros_like(bound_total)

    @pl.loop(0, CHUNKS)
    def _(i):
        c = CHUNKS - 1 - i
        rows = pl.ds(pl.multiple_of(c * CHUNK, CHUNK), CHUNK)
        running = run[rows, :]
        logistic, forget, query, keys, values = gates(raw, bound, rows)
        keys = keys.astype(F32)
        fade = jnp.exp(running[127:128] - running)
        column, final = segments.column(c), segments.final(c)
        ends = jnp.where(column == final, 1.0, 0.0)
        for h in range(2):
            lanes = slice(h * 128, (h + 1) * 128)
            state = incoming[h]
            pair = halves(state)
            tail = halves(keys[:, lanes] * fade[:, lanes] * ends)
            value_grad = d_values[rows, lanes] + mm3(tail, pair, NT)
            draw[rows, 512 + h * 128 : 512 + (h + 1) * 128] = value_grad.astype(BF16)
            lift = mm(values[:, lanes], pair[0], NN) + mm(values[:, lanes], pair[1], NN)
            key_grad = d_keys[rows, lanes] + lift * fade[:, lanes] * ends
            at_end = jnp.sum(states[h, c + 1] * state, axis=0, keepdims=True)
            query_grad = d_query[rows, lanes]
            step = query[:, lanes].astype(F32) * query_grad - keys[:, lanes] * key_grad
            log_grad = summed_rows(False, step) + at_end
            forget_grad = log_grad / forget[:, lanes] - key_grad
            rest = 1.0 - logistic[:, lanes]
            draw[rows, 256 + h * 128 : 256 + (h + 1) * 128] = (
                forget_grad * (1.0 - bound[:, lanes]) * logistic[:, lanes] * rest
            ).astype(BF16)
            bound_total[:, lanes] += jnp.sum(forget_grad * rest, axis=0, keepdims=True)
            incoming[h] = state * decay[c, 0:1, lanes] + update[h, c]

    scatter2 = HeadSum(p, ps, slots, rs2_s, rs2_r)
    for start, send in ((HALF, scatter2.send_right), (0, scatter2.send_left)):
        for first_row, part in ((0, wd), (TOK, dy)):
            for j in range(2):
                rows = slice(j * 256, (j + 1) * 256)
                columns = slice(start + first_row + j * 256, start + first_row + (j + 1) * 256)
                ps[:, columns] = mm(draw[...], part[rows, start : start + HALF], NT).astype(BF16)

        send()
    first.join()
    products_turned(hn, draw.at[:, 256:512], draw.at[:, 512:768], b0)
    second.to_sibling()

    @pl.loop(0, 8)
    def _(j):
        columns = pl.ds(pl.multiple_of(j * 256, 256), 256)
        terms = ps[:, columns].astype(F32) * hn[:, columns].astype(F32)
        norm_terms[:, columns] = jnp.sum(terms, axis=0, keepdims=True) / gain[:, columns]

    vec[...] = jnp.zeros_like(vec)
    for i in range(16):
        vec[i : i + 1, :] = norm_terms[:, i * 128 : (i + 1) * 128]
        vec[16 + i : 17 + i, :] = ffn_terms[:, i * 128 : (i + 1) * 128]
    vec[32:33, :] = group_total[...]
    vec[33:34, :] = total[:, 0:128] + total[:, 128:256]
    vec[34:35, :] = bound_total[:, 0:128]
    vec[35:36, :] = bound_total[:, 128:256]
    everywhere = Total(p, vec, t0, t1, t2, t3, t4, t5, t6, t7, t8.at[0], t9.at[0])
    everywhere.send()
    second.to_z()
    products(gated_t, db, e0)
    third.to_sibling()
    second.join()
    scatter2.middle()
    third.to_z()
    everywhere.middle()
    first.to_x(put(out_query, out_outgate))
    scatter1.middle()
    everywhere.late()
    second.to_x(put(out_forget, out_input))
    third.join()
    sums[2].end(accumulate(out_down))
    emit(14)
    scatter2.collect()

    @pl.loop(0, 4)
    def _(i):
        rows = pl.ds(pl.multiple_of(i * 16, 16), 16)
        grad, x = scatter2.rows(i * 16, 16), hid_rows[rows, :].astype(F32)
        inverse = lax.rsqrt(jnp.mean(x * x, axis=-1, keepdims=True) + EPS)
        scaled, normed = grad * gain[...], x * inverse
        back = inverse * (scaled - normed * jnp.mean(scaled * normed, axis=-1, keepdims=True))
        grad_in[rows, :] = d_resid[rows, :] + back

    emit(1)

    third.to_x(write(out_output))
    scatter1.collect()

    @pl.loop(0, 4)
    def _(i):
        rows = pl.ds(pl.multiple_of(i * 16, 16), 16)
        block_out[rows, :] = (resid[rows, :] + scatter1.rows(i * 16, 16)).astype(BF16)

    emit(0)

    all_of = everywhere.result()
    out_norm[...] = all_of[0:16]
    out_ffn[...] = all_of[16:32]
    out_group[...] = all_of[32:33]
    mean = jnp.sum(all_of[33:34], axis=-1, keepdims=True) / float(8192 * D)
    out_mean[...] = jnp.broadcast_to(mean, (1, 128))
    for h in range(2):
        lanes = slice(h * 128, (h + 1) * 128)
        out_bounds[:, lanes] = soft[:, lanes] * (picked[:, lanes] - bound[:, lanes]) * all_of[34 + h : 35 + h]
    emit(7, 8, 9, 10, 11)

    first.end(add_to(out_query, out_outgate))
    emit(2, 5)
    second.end(add_to(out_forget, out_input))
    emit(3, 4)
    third.end(accumulate(out_output))
    emit(6)
    spread.finish()
    scatter1.finish()
    scatter2.finish()
    exchange2.finish()
    everywhere.finish()
    for one in (first, second, third, sums[2]):
        one.finish()
    for move in emitted:
        move.wait()


OUTS = (
    ((ROWS, D), BF16),
    ((ROWS, D), F32),
    ((128, HERE), F32),
    ((128, HERE), F32),
    ((128, HERE), F32),
    ((128, HERE), F32),
    ((HERE, 128), F32),
    ((24, HERE), F32),
    ((16, 128), F32),
    ((1, KDIM), F32),
    ((16, 128), F32),
    ((1, 128), F32),
    ((FFH, 128), F32),
    ((FFH, 128), F32),
    ((FFH, 128), F32),
)


def call_block(*arrays):
    sums = dp_sum_scratch(FFH)
    again = [pltpu.VMEM((512, 128), BF16)] * 2 + sixteen()
    shapes = [*OUTS, ((TOK, D), BF16), ((2 * TOK, D), BF16)]
    return pl.pallas_call(
        layer_block,
        name="layer_block",
        out_shape=[jax.ShapeDtypeStruct(*one) for one in shapes],
        in_specs=[HB] * 10 + [VM] * 4 + [SM, SM],
        out_specs=[HB] * (len(OUTS) + 2),
        scratch_shapes=[
            *[pltpu.VMEM(*one) for one in OUTS],
            *[pltpu.VMEM((TOK, D), BF16)] * 3,
            pltpu.VMEM((2 * TOK, D), BF16),
            *[pltpu.VMEM((FFH, D), BF16)] * 3,
            pltpu.VMEM((HERE, D), BF16),
            pltpu.VMEM((TOK, 1024), F32),
            pltpu.VMEM((ROWS, D), BF16),
            pltpu.VMEM((TOK, HERE), BF16),
            pltpu.VMEM((HERE, TOK), BF16),
            *[pltpu.VMEM((TOK, HERE), F32)] * 2,
            pltpu.VMEM((2, CHUNKS + 1, 128, 128), F32),
            pltpu.VMEM((2, CHUNKS, 128, 128), F32),
            *[pltpu.VMEM((ROWS, D), F32)] * 2,
            *[pltpu.VMEM((TOK, FFH), BF16)] * 3,
            *[pltpu.VMEM((FFH, TOK), BF16)] * 3,
            pltpu.VMEM((TOK, 1024), BF16),
            pltpu.VMEM((TOK, HERE), BF16),
            *[pltpu.VMEM((TOK, HERE), F32)] * 3,
            pltpu.VMEM((CHUNKS, 8, HERE), F32),
            pltpu.VMEM((2, 128, 128), F32),
            pltpu.VMEM((VEC, 128), F32),
            pltpu.VMEM((1, D), F32),
            pltpu.VMEM((1, D), F32),
            pltpu.VMEM((1, 128), F32),
            pltpu.VMEM((1, HERE), F32),
            pltpu.VMEM((1, HERE), F32),
            *exchange_scratch(),
            *[one for k, one in enumerate(exchange_scratch()) if k not in (0, 3)],
            *sixteen(),
            *twenty(),
            *sixteen(),
            *twenty(),
            *eight(),
            *sixteen(),
            *gather_semaphores(),
            *gather_semaphores(),
            *gather_semaphores(),
            *gather_semaphores(),
            *gather_semaphores(),
            *gather_semaphores(),
            *sums,
            *sums,
            *sums,
            *dp_sum_scratch(HERE),
            *again,
            *again,
            pltpu.VMEM((8, VEC, 128), F32),
            pltpu.VMEM((8, VEC, 128), F32),
            pltpu.VMEM((VEC, 128), F32),
            pltpu.VMEM((VEC, 128), F32),
            *eight(),
            *eight(),
            pltpu.SemaphoreType.DMA((1,)),
            pltpu.SemaphoreType.DMA((1,)),
            pltpu.SemaphoreType.DMA((32,)),
        ],
        compiler_params=pltpu.CompilerParams(
            collective_id=0, has_side_effects=True, vmem_limit_bytes=60 * 1024 * 1024
        ),
    )(*arrays)


def results(*refs):
    count, sems = len(OUTS), refs[-1]
    ins, outs, held = refs[:count], refs[count : 2 * count], refs[2 * count : 3 * count]
    reads = [pltpu.make_async_copy(ins[k], held[k], sems.at[0, k]) for k in range(count)]
    writes = [pltpu.make_async_copy(held[k], outs[k], sems.at[1, k]) for k in range(count)]
    for move in reads:
        move.start()
    for read, move in zip(reads, writes):
        read.wait()
        move.start()
    for move in writes:
        move.wait()


def call_results(arrays):
    return pl.pallas_call(
        results,
        name="results",
        out_shape=[jax.ShapeDtypeStruct(*one) for one in OUTS],
        in_specs=[HB] * len(OUTS),
        out_specs=[HB] * len(OUTS),
        scratch_shapes=[*[pltpu.VMEM(*one) for one in OUTS], pltpu.SemaphoreType.DMA((2, len(OUTS)))],
    )(*arrays)


def local(
    hidden_in, norm_gain, w_query, w_forget, w_input, w_outgate, lower_bounds, layer_index, group_gain,
    w_output, ffn_gain, w_gate, w_up, w_down, seq_lengths, grad_out,
):
    arrays = call_block(
        hidden_in, grad_out, w_query, w_forget, w_input, w_outgate, w_output, w_gate.T, w_up.T, w_down,
        norm_gain.reshape(1, D), lower_bounds, group_gain.reshape(1, KDIM), ffn_gain.reshape(1, D), layer_index, seq_lengths,
    )
    (
        block_out, grad_in, grad_query, grad_forget, grad_input, grad_outgate, grad_output, grad_bounds,
        grad_norm, grad_group, grad_ffn, mean, grad_gate, grad_up, grad_down,
    ) = call_results(arrays[: len(OUTS)])
    return (
        block_out,
        grad_in,
        grad_norm.reshape(D),
        grad_query,
        grad_forget,
        grad_input,
        grad_outgate,
        grad_bounds,
        grad_group.reshape(KDIM),
        grad_output,
        grad_ffn.reshape(D),
        grad_gate.T,
        grad_up.T,
        grad_down,
        mean[0, 0:1],
    )


def solution(mesh):
    return jax.shard_map(
        local,
        mesh=mesh,
        in_specs=(
            P("dp", None),
            P(),
            P("dp", "head"),
            P("dp", "head"),
            P("dp", "head"),
            P("dp", "head"),
            P(None, "head"),
            P(),
            P(),
            P("head", "dp"),
            P(),
            P("dp", "head"),
            P("dp", "head"),
            P("head", "dp"),
            P(),
            P("dp", None),
        ),
        out_specs=(
            P(("dp", "head"), None),
            P(("dp", "head"), None),
            P(),
            P("dp", "head"),
            P("dp", "head"),
            P("dp", "head"),
            P("dp", "head"),
            P(None, "head"),
            P(),
            P("head", "dp"),
            P(),
            P("dp", "head"),
            P("dp", "head"),
            P("head", "dp"),
            P(),
        ),
        check_vma=False,
    )
```

```python
from functools import partial

import jax
import jax.numpy as jnp
from jax import lax
from jax.experimental import pallas as pl
from jax.experimental.pallas import tpu as pltpu
from jax.sharding import PartitionSpec as P

D = 2048
KDIM = 128
CHUNK = 128
TOK = 512
CHUNKS = TOK // CHUNK
HERE = 256
FFH = 704
NSEQ = 12
NHEAD = 8
ROWS = TOK // NHEAD
EPS = 1e-06
F32 = jnp.float32
BF16 = jnp.bfloat16
MESH = pl.DeviceIdType.MESH
VM = pl.BlockSpec(memory_space=pltpu.VMEM)
SM = pl.BlockSpec(memory_space=pltpu.SMEM)
HB = pl.BlockSpec(memory_space=pl.ANY)


class Spot:
    def __init__(self):
        self.dp = lax.axis_index("dp")
        self.head = lax.axis_index("head")
        self.core = lax.rem(self.dp, 2)
        self.chip = lax.div(self.dp, 2)
        self.xh = lax.rem(self.chip, 2)
        self.z = lax.div(self.chip, 2)
        self.xl = lax.rem(self.head, 2)
        self.y = lax.div(self.head, 2)

    def at(self, dz, xh, core):
        return (lax.rem(self.z + dz, 4) * 2 + xh) * 2 + core

    def y_at(self, k):
        return lax.rem(self.y + k, 4)

    @property
    def beside(self):
        return {"head": self.y * 2 + 1 - self.xl}

    def lines(self):
        return [self.beside] + [{"head": self.y_at(k) * 2 + self.xl} for k in (1, 2, 3)]

    @property
    def sibling(self):
        return {"dp": self.chip * 2 + 1 - self.core}

    def chips(self):
        return [{"dp": lax.rem(self.chip + k, 8) * 2 + self.core} for k in range(1, 8)]

    def heads(self):
        return [{"head": lax.rem(self.head + k, NHEAD)} for k in range(1, NHEAD)]


def greet(ids):
    barrier = pltpu.get_barrier_semaphore()
    for one in ids:
        pl.semaphore_signal(barrier, inc=1, device_id=one, device_id_type=MESH)
    return lambda: pl.semaphore_wait(barrier, len(ids))


def rcopy(src, dst, send, recv, where):
    return pltpu.make_async_remote_copy(
        src_ref=src, dst_ref=dst, send_sem=send, recv_sem=recv, device_id=where, device_id_type=MESH
    )


GATHER_SENDS = 17


class Gather:
    def __init__(self, spot, g, send, recv, half, columns=0):
        self.spot, self.g, self.s, self.r, self.h = spot, g, send, recv, half
        self.columns, self.middle = columns, (columns or 128) // 2

    def block(self, d, start=0, rows=0):
        if self.columns:
            rows = rows or self.columns
            return self.g.at[pl.ds(start, rows), pl.ds(pl.multiple_of(d * 128, 128), 128)]
        return self.g.at[pl.ds(pl.multiple_of(d * 128 + start, 64), rows or 128), :]

    def push(self, d, to, k):
        rcopy(self.block(d), self.block(d), self.s.at[k], self.r.at[d], {"dp": to}).start()

    def push_half(self, d, to, k, xh, part):
        b = self.block(d, part * self.middle, self.middle)
        rcopy(b, b, self.s.at[k], self.h.at[2 * xh + part], {"dp": to}).start()

    def arrived(self, d):
        b = self.block(d)
        rcopy(b, b, self.s.at[0], self.r.at[d], self.spot.sibling).wait_recv()

    def arrived_halves(self, d, xh):
        for part in range(2):
            b = self.block(d, part * self.middle, self.middle)
            rcopy(b, b, self.s.at[0], self.h.at[2 * xh + part], self.spot.sibling).wait_recv()

    def first(self):
        p = self.spot
        self.push(p.dp, p.at(0, 1 - p.xh, p.core), 0)
        self.push(p.dp, p.at(1, p.xh, p.core), 1)
        self.push(p.dp, p.at(3, p.xh, p.core), 2)
        self.push(p.dp, p.at(0, p.xh, 1 - p.core), 3)

    def second(self):
        p = self.spot
        b = p.at(0, 1 - p.xh, p.core)
        self.arrived(b)
        self.push(b, p.at(1, p.xh, p.core), 4)
        self.push(b, p.at(3, p.xh, p.core), 5)
        self.push(b, p.at(0, p.xh, 1 - p.core), 6)

    def third(self):
        p = self.spot
        for i, h in enumerate((p.xh, 1 - p.xh)):
            b = p.at(3, h, p.core)
            self.arrived(b)
            self.push_half(b, p.at(1, p.xh, p.core), 7 + i, h, 0)
            self.push(b, p.at(0, p.xh, 1 - p.core), 9 + i)
            b = p.at(1, h, p.core)
            self.arrived(b)
            self.push_half(b, p.at(3, p.xh, p.core), 11 + i, h, 1)
            self.push(b, p.at(0, p.xh, 1 - p.core), 13 + i)

    def fourth(self):
        p = self.spot
        for i, h in enumerate((p.xh, 1 - p.xh)):
            b = p.at(2, h, p.core)
            self.arrived_halves(b, h)
            self.push(b, p.at(0, p.xh, 1 - p.core), 15 + i)

    def last(self):
        p = self.spot
        for dz in range(4):
            for h in range(2):
                self.arrived(p.at(dz, h, 1 - p.core))
        half = self.block(0, 0, self.middle)
        for k in range(GATHER_SENDS):
            b = half if k in (7, 8, 11, 12) else self.block(0)
            rcopy(b, b, self.s.at[k], self.r.at[0], p.sibling).wait_send()


class WideGather(Gather):
    def __init__(self, spot, g, send, recv, half, offset=0):
        super().__init__(spot, g, send, recv, half)
        self.offset, self.middle = offset, 32

    def block(self, d, start=0, rows=0):
        row, column = lax.rem(d, 8) * 128 + (self.offset + start), lax.div(d, 8) * 1024
        return self.g.at[pl.ds(pl.multiple_of(row, 32), rows or 64), pl.ds(pl.multiple_of(column, 1024), 1024)]

    def tile(self, d, k):
        row, column = lax.rem(d, 8) * 128, lax.div(d, 8) * 1024 + 256 * k
        return self.g.at[pl.ds(pl.multiple_of(row, 128), 128), pl.ds(pl.multiple_of(column, 256), 256)]


class LowerGather(WideGather):
    def first(self):
        p = self.spot
        self.push(p.dp, p.at(1, p.xh, p.core), 0)
        self.push(p.dp, p.at(3, p.xh, p.core), 1)
        self.push(p.dp, p.at(0, 1 - p.xh, p.core), 2)
        self.push(p.dp, p.at(0, p.xh, 1 - p.core), 3)

    def second(self):
        p = self.spot
        for part, (source, to) in enumerate(((3, 1), (1, 3))):
            b = p.at(source, p.xh, p.core)
            self.arrived(b)
            self.push_half(b, p.at(to, p.xh, p.core), 4 + part, 0, part)
            self.push(b, p.at(0, 1 - p.xh, p.core), 6 + part)
            self.push(b, p.at(0, p.xh, 1 - p.core), 8 + part)

    def third(self):
        p = self.spot
        b = p.at(2, p.xh, p.core)
        self.arrived_halves(b, 0)
        self.push(b, p.at(0, 1 - p.xh, p.core), 10)
        self.push(b, p.at(0, p.xh, 1 - p.core), 11)

    def fourth(self):
        p = self.spot
        for k, dz in enumerate((0, 3, 1, 2)):
            b = p.at(dz, 1 - p.xh, p.core)
            self.arrived(b)
            self.push(b, p.at(0, p.xh, 1 - p.core), 12 + k)

    def last(self):
        p = self.spot
        for dz in range(4):
            for h in range(2):
                self.arrived(p.at(dz, h, 1 - p.core))
        for k in range(16):
            b = self.block(0, 0, self.middle) if k in (4, 5) else self.block(0)
            rcopy(b, b, self.s.at[k], self.r.at[0], p.sibling).wait_send()


def gather_semaphores():
    return [
        pltpu.SemaphoreType.DMA((GATHER_SENDS,)),
        pltpu.SemaphoreType.DMA((16,)),
        pltpu.SemaphoreType.DMA((4,)),
    ]


NN = (((1,), (0,)), ((), ()))
NT = (((1,), (1,)), ((), ()))
TN = (((0,), (0,)), ((), ()))


def mm(a, b, dims):
    return lax.dot_general(a, b, dims, preferred_element_type=F32)


def halves(a):
    high = a.astype(BF16)
    return high, (a - high.astype(F32)).astype(BF16)


def mm2(a, b, dims):
    return mm(a[0], b, dims) + mm(a[1], b, dims)


def mm3(a, b, dims):
    return mm(a[0], b[0], dims) + (mm(a[0], b[1], dims) + mm(a[1], b[0], dims))


def triangle(lower):
    rows = lax.broadcasted_iota(jnp.int32, (CHUNK, CHUNK), 0)
    columns = lax.broadcasted_iota(jnp.int32, (CHUNK, CHUNK), 1)
    return (rows >= columns if lower else rows <= columns).astype(BF16)


def summed_rows(lower, x):
    high = x.astype(BF16)
    rest = x - high.astype(F32)
    middle = rest.astype(BF16)
    low = (rest - middle.astype(F32)).astype(BF16)
    t = triangle(lower)
    return mm(t, high, NN) + (mm(t, middle, NN) + mm(t, low, NN))


class Segments:
    def __init__(self, spot, seq):
        self.starts = []
        total = jnp.int32(0)
        for i in range(NSEQ):
            self.starts.append(total)
            total = total + seq[i]
        self.first = spot.dp * TOK

    def of(self, position):
        found = jnp.where(position >= self.starts[0], 1, 0)
        for s in self.starts[1:]:
            found = found + jnp.where(position >= s, 1, 0)
        return found - 1

    def column(self, c):
        return self.of(self.first + c * CHUNK + lax.broadcasted_iota(jnp.int32, (CHUNK, KDIM), 0))

    def row(self, c):
        return self.of(self.first + c * CHUNK + lax.broadcasted_iota(jnp.int32, (CHUNK, KDIM), 1))

    def before(self, c):
        return self.of(self.first + c * CHUNK - 1)

    def final(self, c):
        return self.of(self.first + (c + 1) * CHUNK - 1)


def lower_bound(lb, layer):
    x = lb[...]
    e = jnp.exp(x - jnp.max(x, axis=0, keepdims=True))
    soft = e / jnp.sum(e, axis=0, keepdims=True)
    depth = lax.broadcasted_iota(jnp.int32, x.shape, 0)
    picked = jnp.where((depth >= 1) & (depth <= layer), 1.0, 0.0)
    return soft, picked, jnp.sum(soft * picked, axis=0, keepdims=True)


def sigmoid(x):
    return lax.logistic(x)


def slope(x, s):
    return s * (1.0 + x * (1.0 - s))


class Exchange:
    def __init__(self, spot, msg, sib, slots, give, take, send, recv, backward):
        self.p, self.msg, self.sib, self.slots = spot, msg, sib, slots
        self.give, self.take, self.s, self.r, self.back = give, take, send, recv, backward

    def to_sibling(self):
        p = self.p
        rcopy(self.msg.at[1 - p.core], self.sib, self.s.at[7], self.r.at[8], p.sibling).start()

    def to_chips(self):
        p = self.p
        rcopy(self.sib, self.sib, self.s.at[7], self.r.at[8], p.sibling).wait_recv()
        mine, other = self.msg[p.core], self.sib[...]
        zero = p.core == 0
        one, two = jnp.where(zero, mine, other), jnp.where(zero, other, mine)
        near, far = (two, one) if self.back else (one, two)
        self.near = near
        state = near[0:128] * far[128:129] + far[0:128]
        rate = near[128:136] * far[128:136]
        high = rate.astype(BF16).astype(F32)
        self.slots[p.chip, 0:128, :] = state.astype(BF16)
        self.slots[p.chip, 128:144, :] = jnp.concatenate([high, rate - high], axis=0).astype(BF16)
        for k, to in enumerate(p.chips()):
            rcopy(self.slots.at[p.chip], self.slots.at[p.chip], self.s.at[k], self.r.at[p.chip], to).start()

    def result(self, out):
        p = self.p
        for k in range(1, 8):
            chip = lax.rem(p.chip + k, 8)
            rcopy(self.slots.at[chip], self.slots.at[chip], self.s.at[0], self.r.at[chip], p.sibling).wait_recv()
        state = jnp.zeros((128, 128), F32)
        for k in range(7, 0, -1) if self.back else range(7):
            m = self.slots[k].astype(F32)
            after = state * (m[128:129] + m[136:137]) + m[0:128]
            state = jnp.where(k > p.chip if self.back else k < p.chip, after, state)
        second = state * self.near[128:129] + self.near[0:128]
        is_first = p.core == (1 if self.back else 0)
        self.give[...] = jnp.where(is_first, second, state)
        move = rcopy(self.give, self.take, self.s.at[8], self.r.at[9], p.sibling)
        move.start()
        out[p.core] = jnp.where(is_first, state, second)
        move.wait_recv()
        out[1 - p.core] = self.take[...]

    def finish(self):
        p = self.p
        for k in range(7):
            rcopy(self.slots.at[0], self.slots.at[0], self.s.at[k], self.r.at[0], p.sibling).wait_send()
        rcopy(self.sib, self.sib, self.s.at[7], self.r.at[8], p.sibling).wait_send()
        rcopy(self.give, self.take, self.s.at[8], self.r.at[9], p.sibling).wait_send()


def exchange_scratch():
    return [
        pltpu.VMEM((2, 136, 128), F32),
        pltpu.VMEM((136, 128), F32),
        pltpu.VMEM((8, 144, 128), BF16),
        pltpu.VMEM((128, 128), F32),
        pltpu.VMEM((128, 128), F32),
        pltpu.SemaphoreType.DMA((9,)),
        pltpu.SemaphoreType.DMA((10,)),
    ]


def gates(raw, bound, rows):
    query_raw = raw[rows, 0:256]
    logistic = sigmoid(raw[rows, 256:512])
    forget = bound + (1.0 - bound) * logistic
    query = (query_raw * sigmoid(query_raw)).astype(BF16)
    keys = (1.0 - forget).astype(BF16)
    values = raw[rows, 512:768].astype(BF16)
    return logistic, forget, query, keys, values


HALF = D // 2


class HeadSum:
    def __init__(self, spot, ps, slots, send, recv):
        self.p, self.ps, self.slots, self.s, self.r = spot, ps, slots, send, recv

    def left_of(self, start, rows=ROWS):
        return self.slots.at[pl.ds(start, rows), pl.ds(0, HALF)]

    def right_of(self, start, rows=ROWS):
        return self.slots.at[pl.ds(start, rows), pl.ds(HALF, HALF)]

    def part(self, h, rows, right):
        return self.ps.at[pl.ds(pl.multiple_of(h * ROWS, ROWS), rows), pl.ds(HALF if right else 0, HALF)]

    def left_x(self, k):
        p = self.p
        h = p.y_at(k) * 2 + 1 - p.xl
        return rcopy(self.part(h, ROWS, False), self.left_of(64 * k), self.s.at[k], self.r.at[k], p.beside)

    def left_y(self, k):
        p = self.p
        to = {"head": p.y_at(k) * 2 + p.xl}
        return rcopy(self.left_of(64 * k), self.left_of(192 + 64 * k), self.s.at[3 + k], self.r.at[3 + k], to)

    def right_y(self, k):
        p = self.p
        to = {"head": p.y_at(k) * 2 + p.xl}
        return rcopy(
            self.part(p.y_at(k) * 2, 128, True), self.right_of(128 * k - 128, 128), self.s.at[6 + k], self.r.at[6 + k], to
        )

    def right_x(self):
        return rcopy(self.right_of(384), self.right_of(448), self.s.at[10], self.r.at[10], self.p.beside)

    def send_left(self):
        for k in (2, 1, 3, 0):
            self.left_x(k).start()

    def send_right(self):
        for k in (2, 1, 3):
            self.right_y(k).start()

    def send(self):
        self.send_right()
        self.send_left()

    def join(self, k):
        p = self.p
        self.left_x(k).wait_recv()
        mine = self.part(p.y_at(k) * 2 + p.xl, ROWS, False)
        one = self.left_of(64 * k)
        one[...] = (one[...].astype(F32) + mine[...].astype(F32)).astype(BF16)
        if k:
            self.left_y(k).start()

    def middle(self):
        p = self.p
        for k in (2, 1, 3):
            self.join(k)
        for k in (1, 3, 2):
            self.right_y(k).wait_recv()

        def total(xl):
            one = self.part(p.y * 2 + xl, ROWS, True)[...].astype(F32)
            for k in range(3):
                rows = pl.ds(pl.multiple_of(128 * k + xl * ROWS, ROWS), ROWS)
                one = one + self.slots[rows, HALF:].astype(F32)
            return one.astype(BF16)

        self.slots[384:448, HALF:] = total(1 - p.xl)
        self.right_x().start()
        self.slots[448:512, 0:HALF] = total(p.xl)
        self.join(0)

    def collect(self):
        for k in (1, 3, 2):
            self.left_y(k).wait_recv()
        self.right_x().wait_recv()

    def rows(self, start, count):
        def at(row, left):
            rows = pl.ds(pl.multiple_of(row + start, 16), count)
            return self.slots[rows, 0:HALF].astype(F32) if left else self.slots[rows, HALF:].astype(F32)

        left = (at(0, True) + at(256, True)) + (at(320, True) + at(384, True))
        return jnp.concatenate([left, at(448, True) + at(448, False)], axis=1)

    def finish(self):
        for k in range(4):
            self.left_x(k).wait_send()
        for k in (1, 2, 3):
            self.left_y(k).wait_send()
            self.right_y(k).wait_send()
        self.right_x().wait_send()


class LateHeadSum:
    def __init__(self, spot, ps, slots, send, recv):
        self.p, self.ps, self.slots, self.s, self.r = spot, ps, slots, send, recv

    def block(self, ref, start, rows=ROWS):
        return ref.at[pl.ds(pl.multiple_of(start, ROWS), rows), :]

    def along_y(self, k):
        p = self.p
        y = p.y_at(k)
        return rcopy(
            self.block(self.ps, y * 128, 128), self.block(self.slots, 128 * k - 128, 128),
            self.s.at[k], self.r.at[k], {"head": y * 2 + p.xl},
        )

    def along_x(self):
        return rcopy(self.block(self.slots, 384), self.block(self.slots, 448), self.s.at[0], self.r.at[0], self.p.beside)

    def send(self):
        for k in (2, 1, 3):
            self.along_y(k).start()

    def part(self, xl, start, count):
        p = self.p
        one = self.ps[pl.ds(pl.multiple_of((p.y * 2 + xl) * ROWS + start, 16), count), :].astype(F32)
        for k in range(3):
            rows = pl.ds(pl.multiple_of(128 * k + xl * ROWS + start, 16), count)
            one = one + self.slots[rows, :].astype(F32)
        return one

    def middle(self):
        for k in (1, 3, 2):
            self.along_y(k).wait_recv()

        @pl.loop(0, 4)
        def _(i):
            rows = pl.ds(pl.multiple_of(384 + i * 16, 16), 16)
            self.slots[rows, :] = self.part(1 - self.p.xl, i * 16, 16).astype(BF16)

        self.along_x().start()

    def collect(self):
        self.along_x().wait_recv()

    def rows(self, start, count):
        rows = pl.ds(pl.multiple_of(448 + start, 16), count)
        return self.part(self.p.xl, start, count) + self.slots[rows, :].astype(F32)

    def finish(self):
        for k in (1, 2, 3):
            self.along_y(k).wait_send()
        self.along_x().wait_send()


class HeadGather:
    def __init__(self, spot, full, send, recv):
        self.p, self.full, self.s, self.r = spot, full, send, recv

    def block(self, dy, stream, start=0, rows=ROWS):
        p = self.p
        h = p.y_at(dy) * 2 + (1 - p.xl if stream == 2 else p.xl)
        columns = pl.ds(0 if stream else HALF, HALF)
        return self.full.at[pl.ds(pl.multiple_of(h * ROWS + start, 32), rows), columns]

    def along_y(self, stream, k):
        p = self.p
        b, i = self.block(0, stream), 4 * stream + (k == 3)
        return rcopy(b, b, self.s.at[i], self.r.at[i], {"head": p.y_at(k) * 2 + p.xl})

    def onward(self, stream, part):
        p = self.p
        b, i = self.block(1 if part else 3, stream, 32 * part, 32), 4 * stream + 2 + part
        return rcopy(b, b, self.s.at[i], self.r.at[i], {"head": p.y_at(3 if part else 1) * 2 + p.xl})

    def beside(self, dy, stream):
        b, i = self.block(dy, stream), 12 if stream else 13 + dy
        return rcopy(b, b, self.s.at[i], self.r.at[i], self.p.beside)

    def send(self):
        self.beside(0, 1).start()
        for k in (1, 3):
            self.along_y(0, k).start()
        self.beside(0, 0).start()
        for k in (1, 3):
            self.along_y(1, k).start()

    def middle(self):
        self.beside(0, 1).wait_recv()
        for k in (1, 3):
            self.along_y(2, k).start()
        for part in range(2):
            self.along_y(0, 3 if part else 1).wait_recv()
            self.onward(0, part).start()
            self.beside(1 if part else 3, 0).start()
        for part in range(2):
            self.along_y(1, 3 if part else 1).wait_recv()
            self.onward(1, part).start()

    def late(self):
        for part in range(2):
            self.along_y(2, 3 if part else 1).wait_recv()
            self.onward(2, part).start()
        for part in range(2):
            self.onward(0, part).wait_recv()
        self.beside(2, 0).start()

    def collect(self):
        for dy in range(4):
            self.beside(dy, 0).wait_recv()
        for stream in (1, 2):
            for part in range(2):
                self.onward(stream, part).wait_recv()

    def finish(self):
        self.beside(0, 1).wait_send()
        for dy in range(4):
            self.beside(dy, 0).wait_send()
        for stream in range(3):
            for part in range(2):
                self.along_y(stream, 3 if part else 1).wait_send()
                self.onward(stream, part).wait_send()


def twenty():
    return [pltpu.SemaphoreType.DMA((20,)), pltpu.SemaphoreType.DMA((20,))]


def sixteen():
    return [pltpu.SemaphoreType.DMA((16,)), pltpu.SemaphoreType.DMA((16,))]


def eight():
    return [pltpu.SemaphoreType.DMA((8,)), pltpu.SemaphoreType.DMA((8,))]


class DpSum:
    def __init__(self, spot, rows, gs, cr, zr, xs, xr, send, recv):
        n = pl.ds(0, rows)
        self.rows, self.p = rows, spot
        self.gs, self.cr, self.zr = gs.at[:, :, n, :], cr.at[:, n, :], zr.at[:, :, n, :]
        self.xs, self.xr, self.s, self.r = xs.at[n, :], xr.at[n, :], send, recv

    def pair(self, i):
        p = self.p
        two = pl.ds(2 * i, 2)
        return rcopy(self.gs.at[1 - p.core, two], self.cr.at[two], self.s.at[i], self.r.at[i], p.sibling)

    def to_sibling(self):
        for i in range(4):
            self.pair(i).start()

    def half(self, part):
        return pl.ds(part * (self.rows // 2), self.rows // 2)

    def along_z(self, d, block, part, slot, i):
        p = self.p
        z = lax.rem(p.z + block, 4)
        where = {"dp": (lax.rem(p.z + d, 4) * 2 + p.xh) * 2 + p.core}
        source = self.gs.at[p.core, pl.ds(z * 2, 2), self.half(part), :]
        return rcopy(source, self.zr.at[slot, :, self.half(part), :], self.s.at[4 + i], self.r.at[4 + i], where)

    def far(self, part):
        return self.along_z(3 if part else 1, 2, part, 2, part)

    def near(self, part):
        return self.along_z(3, 3, 0, 1, 2) if part else self.along_z(1, 1, 1, 0, 3)

    def joined(self, part):
        return self.along_z(3, 3, 1, 1, 4) if part else self.along_z(1, 1, 0, 0, 5)

    def to_z(self):
        p = self.p
        for i in range(4):
            self.pair(i).wait_recv()

        @pl.loop(0, 8)
        def _(k):
            self.gs[p.core, k] = (self.gs[p.core, k].astype(F32) + self.cr[k].astype(F32)).astype(BF16)

        for part in range(2):
            self.far(part).start()
        for part in range(2):
            self.near(part).start()

    def join(self):
        p = self.p
        for part in range(2):
            self.far(part).wait_recv()
            z = lax.rem(p.z + (3 if part else 1), 4)
            for h in range(2):
                mine = self.gs.at[p.core, z * 2 + h, self.half(part), :]
                other = self.zr.at[2, h, self.half(part), :]
                mine[...] = (mine[...].astype(F32) + other[...].astype(F32)).astype(BF16)
            self.joined(part).start()

    def last_move(self):
        p = self.p
        where = {"dp": (p.z * 2 + 1 - p.xh) * 2 + p.core}
        return rcopy(self.xs, self.xr, self.s.at[10], self.r.at[10], where)

    def to_x(self, put, go=True):
        p = self.p
        for part in range(2):
            self.near(part).wait_recv()
            self.joined(part).wait_recv()

        def total(h):
            one = self.gs[p.core, 2 * p.z + h].astype(F32)
            for i in range(2):
                one = one + self.zr[i, h].astype(F32)
            return one

        self.xs[...] = total(1 - p.xh).astype(BF16)
        if go:
            self.go()
        put(total(p.xh))

    def go(self):
        self.last_move().start()

    def end(self, add):
        self.last_move().wait_recv()
        add(self.xr[...].astype(F32))

    def finish(self):
        for i in range(4):
            self.pair(i).wait_send()
        for part in range(2):
            self.far(part).wait_send()
            self.near(part).wait_send()
            self.joined(part).wait_send()
        self.last_move().wait_send()


def dp_sum_scratch(rows):
    return [
        pltpu.VMEM((2, 8, rows, 128), BF16),
        pltpu.VMEM((8, rows, 128), BF16),
        pltpu.VMEM((3, 2, rows, 128), BF16),
        pltpu.VMEM((rows, 128), BF16),
        pltpu.VMEM((rows, 128), BF16),
        *sixteen(),
    ]


def products(left_turned, right, gs):
    @pl.loop(0, 8)
    def _(k):
        columns = pl.ds(pl.multiple_of(k * 256, 256), 256)
        both = mm(left_turned[...], right[:, columns], NN).astype(BF16)
        gs[0, k] = both[:, 0:128]
        gs[1, k] = both[:, 128:256]


def products_turned(left, first, second, gs):
    @pl.loop(0, 8)
    def _(k):
        turned = left[:, pl.ds(pl.multiple_of(k * 256, 256), 256)]
        for i, right in enumerate((first, second)):
            both = mm(turned, right[...], TN).astype(BF16)
            for q in range(2):
                rows = slice(256 * i + 128 * q, 256 * i + 128 * (q + 1))
                gs[0, k, rows, :] = both[0:128, 128 * q : 128 * (q + 1)]
                gs[1, k, rows, :] = both[128:256, 128 * q : 128 * (q + 1)]


def write(ref):
    def put(x):
        ref[...] = x

    return put


def accumulate(ref):
    def add(x):
        ref[...] += x

    return add


VEC = 40


class Total:
    def __init__(self, spot, vec, h_slots, c_slots, own, other, h_s, h_r, c_s, c_r, k_s, k_r):
        self.p, self.vec, self.hs, self.cs, self.own, self.other = spot, vec, h_slots, c_slots, own, other
        self.h_s, self.h_r, self.c_s, self.c_r, self.k_s, self.k_r = h_s, h_r, c_s, c_r, k_s, k_r

    def send(self):
        p = self.p
        self.cs[p.chip] = self.vec[...]
        for k, to in enumerate(p.chips()):
            rcopy(self.cs.at[p.chip], self.cs.at[p.chip], self.c_s.at[k], self.c_r.at[p.chip], to).start()

    def middle(self):
        p = self.p
        for k in range(1, 8):
            chip = lax.rem(p.chip + k, 8)
            rcopy(self.cs.at[chip], self.cs.at[chip], self.c_s.at[0], self.c_r.at[chip], p.sibling).wait_recv()
        total = self.cs[0]
        for k in range(1, 8):
            total = total + self.cs[k]
        self.own[...] = total
        rcopy(self.own, self.other, self.k_s, self.k_r, p.sibling).start()

    def late(self):
        p = self.p
        rcopy(self.own, self.other, self.k_s, self.k_r, p.sibling).wait_recv()
        self.hs[p.head] = self.own[...] + self.other[...]
        for k in range(1, NHEAD):
            h = lax.rem(p.head + k, NHEAD)
            rcopy(self.hs.at[p.head], self.hs.at[p.head], self.h_s.at[k], self.h_r.at[p.head], {"head": h}).start()

    def result(self):
        p = self.p
        for k in range(1, NHEAD):
            h = lax.rem(p.head + k, NHEAD)
            rcopy(self.hs.at[h], self.hs.at[h], self.h_s.at[0], self.h_r.at[h], p.sibling).wait_recv()
        total = self.hs[0]
        for h in range(1, NHEAD):
            total = total + self.hs[h]
        per_head = lax.broadcasted_iota(jnp.int32, (VEC, 128), 0) >= 34
        return jnp.where(per_head, self.hs[p.head], total)

    def finish(self):
        p = self.p
        for k in range(1, NHEAD):
            rcopy(self.hs.at[0], self.hs.at[0], self.h_s.at[k], self.h_r.at[0], p.sibling).wait_send()
        for k in range(7):
            rcopy(self.cs.at[0], self.cs.at[0], self.c_s.at[k], self.c_r.at[0], p.sibling).wait_send()
        rcopy(self.own, self.other, self.k_s, self.k_r, p.sibling).wait_send()


def layer_block(
    hid, dy_in, wq, wf, wi, wo, w_output, wg_in, wu_in, wd_in, gain, lb, group_gain, ffn_gain, layer, seq,
    i0, i1, i2, i3, i4, i5, i6, i7, i8, i9, i10, i11, i12, i13, i14, xn_out, w_out,
    block_out, grad_in, out_query, out_forget, out_input, out_outgate, out_output, out_bounds,
    out_norm, out_group, out_ffn, out_mean, out_gate, out_up, out_down,
    ps, slots, hn, wide, wg, wu, wd, wt, raw, hid_rows, gated, gated_t, mixed, run, states, update, resid, d_resid,
    hidden, dg, du, hidden_t, dg_t, du_t, draw, d_mixed, d_query, d_keys, d_values, decay, incoming, vec,
    norm_terms, ffn_terms, group_total, bound_total, total,
    msg, sib, slots3, give, take, ex_send, ex_recv, sib2, slots4, take2, ex2_send, ex2_recv,
    rs0_s, rs0_r, ag0_s, ag0_r, rs_s, rs_r, ag_s, ag_r, rs1_s, rs1_r, rs2_s, rs2_r,
    ws, wr, wh, vs, vr, vh, os, or_, oh, s0, r0, h0, s1, r1, h1, s2, r2, h2,
    a0, a1, a2, a3, a4, a5, a6, b0, b1, b2, b3, b4, b5, b6, c0, c1, c2, c3, c4, c5, c6,
    e0, e1, e2, e3, e4, e5, e6, f3, f4, f5, f6, g3, g4, g5, g6,
    t0, t1, t2, t3, t4, t5, t6, t7, t8, t9, local_sem,
):
    dy, db, xn = wide.at[0:TOK], wide.at[TOK : 2 * TOK], hn
    used = []

    def load(source, to):
        move = pltpu.make_async_copy(source, to, local_sem.at[len(used)])
        move.start()
        used.append(move)
        return move

    emitted = []
    made = (
        block_out, grad_in, out_query, out_forget, out_input, out_outgate, out_output, out_bounds,
        out_norm, out_group, out_ffn, out_mean, out_gate, out_up, out_down,
    )
    to_emit = (i0, i1, i2, i3, i4, i5, i6, i7, i8, i9, i10, i11, i12, i13, i14)

    def emit(*which):
        for k in which:
            emitted.append(load(made[k], to_emit[k]))

    def put(low, high):
        def write_four(x):
            low[:, 0:128], low[:, 128:256] = x[0:128], x[128:256]
            high[:, 0:128], high[:, 128:256] = x[256:384], x[384:512]

        return write_four

    def add_to(low, high):
        def add(x):
            low[:, 0:128] += x[0:128]
            low[:, 128:256] += x[128:256]
            high[:, 0:128] += x[256:384]
            high[:, 128:256] += x[384:512]

        return add

    p = Spot()
    arrive = greet(p.chips() + [p.sibling] + p.heads())
    own = pl.multiple_of(p.head * ROWS, ROWS)
    mine = pl.ds(pl.multiple_of(p.dp * 128, 128), 128)
    gather = WideGather(p, wide, ws, wr, wh)
    lower = LowerGather(p, wide, vs, vr, vh, 64)
    loads = [load(one, gather.tile(p.dp, k)) for k, one in enumerate((wq, wf, wi, wo))]
    loads.append(load(hid, ps))
    own_blocks = [load(w_output, wt.at[:, mine])]
    own_blocks += [load(one, full.at[:, mine]) for one, full in ((wg_in, wg), (wu_in, wu), (wd_in, wd))]
    own_rows = load(hid.at[pl.ds(own, ROWS), :], hid_rows)
    for move in loads[:4]:
        move.wait()
    arrive()
    gather.first()
    lower.first()
    loads[4].wait()
    later = Gather(p, wt, os, or_, oh, HERE)
    gathers = [Gather(p, wg, s0, r0, h0, FFH), Gather(p, wu, s1, r1, h1, FFH), Gather(p, wd, s2, r2, h2, FFH)]

    @pl.loop(0, 8)
    def _(i):
        rows = pl.ds(pl.multiple_of(i * 64, 64), 64)
        x = ps[rows, :].astype(F32)
        scale = lax.rsqrt(jnp.mean(x * x, axis=-1, keepdims=True) + EPS)
        xn[rows, :] = (x * scale * gain[...]).astype(BF16)

    gather.second()
    lower.second()
    gather.third()
    lower.third()
    gather.fourth()
    lower.fourth()
    for move in own_blocks:
        move.wait()
    later.first()
    gathers[0].first()
    gather.last()
    lower.last()
    spills = [load(xn, xn_out), load(wide, w_out)]

    for j in range(4):
        columns = slice(j * 256, (j + 1) * 256)
        other = slice(1024 + j * 256, 1024 + (j + 1) * 256)
        raw[:, columns] = mm(xn[:, 0:1024], wide[:, columns], NN) + mm(xn[:, 1024:2048], wide[:, other], NN)

    later.second()
    segments = Segments(p, seq)
    soft, picked, bound = lower_bound(lb, layer[0])
    total[...] = jnp.zeros_like(total)

    @pl.loop(0, CHUNKS)
    def _(c):
        rows = pl.ds(pl.multiple_of(c * CHUNK, CHUNK), CHUNK)
        logistic, forget, query, keys, values = gates(raw, bound, rows)
        total[...] += jnp.sum(forget, axis=0, keepdims=True)
        running = summed_rows(True, jnp.log(forget))
        run[rows, :] = running
        ending = running[127:128]
        tail = keys.astype(F32) * jnp.exp(ending - running)
        final = segments.final(c)
        rate = jnp.exp(ending) * jnp.where(final == segments.before(c), 1.0, 0.0)
        decay[c] = jnp.broadcast_to(rate, (8, HERE))
        ends = jnp.where(segments.column(c) == final, 1.0, 0.0)
        for h in range(2):
            lanes = slice(h * 128, (h + 1) * 128)
            high, low = halves(tail[:, lanes] * ends)
            update[h, c] = mm(values[:, lanes], high, TN) + mm(values[:, lanes], low, TN)

    for h in range(2):
        lanes = slice(h * 128, (h + 1) * 128)
        state, rate = update[h, 0], decay[0, 0:1, lanes]
        for c in range(1, CHUNKS):
            state = state * decay[c, 0:1, lanes] + update[h, c]
            rate = rate * decay[c, 0:1, lanes]
        msg[h, 0:128, :] = state
        msg[h, 128:136, :] = jnp.broadcast_to(rate, (8, 128))
    exchange = Exchange(p, msg, sib, slots3, give, take, ex_send, ex_recv, False)
    exchange.to_sibling()
    exchange.to_chips()

    @pl.loop(0, CHUNKS)
    def _(c):
        rows = pl.ds(pl.multiple_of(c * CHUNK, CHUNK), CHUNK)
        _, _, query, keys, values = gates(raw, bound, rows)
        running = run[rows, :]
        middle = running[63:64]
        lifted = query.astype(F32) * jnp.exp(running - middle)
        lowered = keys.astype(F32) * jnp.exp(middle - running)
        linked = (segments.column(c) == segments.row(c)) & (
            lax.broadcasted_iota(jnp.int32, (CHUNK, CHUNK), 0)
            >= lax.broadcasted_iota(jnp.int32, (CHUNK, CHUNK), 1)
        )
        for h in range(2):
            lanes = slice(h * 128, (h + 1) * 128)
            scores = mm3(halves(lifted[:, lanes]), halves(lowered[:, lanes]), NT)
            scores = jnp.where(linked, scores, 0.0)
            mixed[rows, lanes] = mm2(halves(scores), values[:, lanes], NN)

    later.third()
    gathers[1].first()
    gathers[2].first()
    gathers[0].second()
    exchange.result(incoming)
    later.fourth()
    for h in range(2):
        lanes = slice(h * 128, (h + 1) * 128)
        state = incoming[h]
        states[h, 0] = state
        for c in range(CHUNKS):
            state = state * decay[c, 0:1, lanes] + update[h, c]
            states[h, c + 1] = state

    @pl.loop(0, CHUNKS)
    def _(c):
        rows = pl.ds(pl.multiple_of(c * CHUNK, CHUNK), CHUNK)
        carried = jnp.where(segments.column(c) == segments.before(c), 1.0, 0.0)
        for h in range(2):
            lanes = slice(h * 128, (h + 1) * 128)
            query_raw = raw[rows, h * 128 : (h + 1) * 128]
            query = (query_raw * sigmoid(query_raw)).astype(BF16).astype(F32)
            reach = query * jnp.exp(run[rows, lanes]) * carried
            x = mixed[rows, lanes] + mm3(halves(reach), halves(states[h, c]), NT)
            mixed[rows, lanes] = x
            scale = lax.rsqrt(jnp.mean(x * x, axis=-1, keepdims=True) + EPS)
            gate = raw[rows, 768 + h * 128 : 768 + (h + 1) * 128]
            gated[rows, lanes] = (x * scale * group_gain[...] * (gate * sigmoid(gate))).astype(BF16)

    gathers[1].second()
    later.last()

    for move in spills:
        move.wait()
    dy_load = load(dy_in, dy)
    scatter0 = HeadSum(p, ps, slots, rs0_s, rs0_r)
    for start, send in ((HALF, scatter0.send_right), (0, scatter0.send_left)):
        for j in range(4):
            columns = slice(start + j * 256, start + (j + 1) * 256)
            ps[:, columns] = mm(gated[...], wt[:, columns], NN).astype(BF16)

        send()
    gathers[2].second()
    scatter0.middle()
    gathers[0].third()
    gathers[1].third()
    gathers[2].third()
    scatter0.collect()
    own_rows.wait()

    @pl.loop(0, 4)
    def _(i):
        rows = pl.ds(pl.multiple_of(i * 16, 16), 16)
        here = pl.ds(pl.multiple_of(own + i * 16, 16), 16)
        x = hid_rows[rows, :].astype(F32) + scatter0.rows(i * 16, 16)
        resid[rows, :] = x
        scale = lax.rsqrt(jnp.mean(x * x, axis=-1, keepdims=True) + EPS)
        hn[here, :] = (x * scale * ffn_gain[...]).astype(BF16)

    scatter0.finish()
    spread0 = HeadGather(p, hn, ag0_s, ag0_r)
    spread0.send()
    spread0.middle()
    for g in gathers:
        g.fourth()
    spread0.late()
    for g in gathers:
        g.last()
    dy_load.wait()
    gated_t[...] = gated[...].T
    exchange.finish()
    spread0.collect()

    for low, high in ((0, 256), (256, 512), (512, FFH)):
        gate = mm(hn[...], wg[low:high, :], NT)
        up = mm(hn[...], wu[low:high, :], NT)
        dh = mm(dy[...], wd[low:high, :], NT)
        s = sigmoid(gate)
        silu = gate * s
        hidden[:, low:high] = (silu * up).astype(BF16)
        dg[:, low:high] = (dh * up * slope(gate, s)).astype(BF16)
        du[:, low:high] = (dh * silu).astype(BF16)

    scatter = HeadSum(p, ps, slots, rs_s, rs_r)
    for start, send in ((HALF, scatter.send_right), (0, scatter.send_left)):
        for j in range(4):
            columns = slice(start + j * 256, start + (j + 1) * 256)
            ps[:, columns] = (mm(dg[...], wg[:, columns], NN) + mm(du[...], wu[:, columns], NN)).astype(BF16)

        send()
    sums = [
        DpSum(p, FFH, a0, a1, a2, a3, a4, a5, a6),
        DpSum(p, FFH, b0, b1, b2, b3, b4, b5, b6),
        DpSum(p, FFH, c0, c1, c2, c3, c4, c5, c6),
    ]
    dg_t[...] = dg[...].T
    products(dg_t, hn, a0)
    sums[0].to_sibling()
    du_t[...] = du[...].T
    products(du_t, hn, b0)
    sums[0].to_z()
    sums[1].to_sibling()
    scatter.middle()
    hidden_t[...] = hidden[...].T
    products(hidden_t, dy, c0)
    sums[1].to_z()
    sums[2].to_sibling()
    scatter.collect()
    ffn_terms[...] = jnp.zeros_like(ffn_terms)

    @pl.loop(0, 4)
    def _(i):
        rows = pl.ds(pl.multiple_of(i * 16, 16), 16)
        here = pl.ds(pl.multiple_of(own + i * 16, 16), 16)
        grad, x = scatter.rows(i * 16, 16), resid[rows, :]
        inverse = lax.rsqrt(jnp.mean(x * x, axis=-1, keepdims=True) + EPS)
        scaled, normed = grad * ffn_gain[...], x * inverse
        back = inverse * (scaled - normed * jnp.mean(scaled * normed, axis=-1, keepdims=True))
        ffn_terms[...] += jnp.sum(grad * normed, axis=0, keepdims=True)
        both = dy[here, :].astype(F32) + back
        d_resid[rows, :] = both
        db[here, :] = both.astype(BF16)

    scatter.finish()
    spread = HeadGather(p, db, ag_s, ag_r)
    spread.send()
    sums[2].to_z()
    spread.middle()
    sums[0].join()
    spread.late()

    @pl.loop(0, 8)
    def _(j):
        columns = pl.ds(pl.multiple_of(j * 256, 256), 256)
        wu[0:TOK, columns] = mm(hidden[...], wd[:, columns], NN).astype(BF16)

    sums[1].join()
    spread0.finish()
    late = [load(xn_out, hn), load(w_out.at[0:TOK], wd.at[0:TOK]), load(w_out.at[TOK : 2 * TOK], dy)]
    group_total[...] = jnp.zeros_like(group_total)
    for move in late:
        move.wait()
    sums[2].join()
    spread.collect()
    scatter1 = LateHeadSum(p, wu, wg, rs1_s, rs1_r)
    scatter1.send()
    d_query[...] = mm(db[...], wt[...], NT)

    @pl.loop(0, CHUNKS)
    def _(c):
        rows = pl.ds(pl.multiple_of(c * CHUNK, CHUNK), CHUNK)
        carried = jnp.where(segments.column(c) == segments.before(c), 1.0, 0.0)
        running = run[rows, :]
        for h in range(2):
            lanes = slice(h * 128, (h + 1) * 128)
            x, grad = mixed[rows, lanes], d_query[rows, lanes]
            gate = raw[rows, 768 + h * 128 : 768 + (h + 1) * 128]
            s = sigmoid(gate)
            inverse = lax.rsqrt(jnp.mean(x * x, axis=-1, keepdims=True) + EPS)
            normed = x * inverse
            draw[rows, 768 + h * 128 : 768 + (h + 1) * 128] = (
                grad * (normed * group_gain[...]) * slope(gate, s)
            ).astype(BF16)
            inner = grad * (gate * s)
            scaled = inner * group_gain[...]
            back = inverse * (scaled - normed * jnp.mean(scaled * normed, axis=-1, keepdims=True))
            group_total[...] += jnp.sum(inner * normed, axis=0, keepdims=True)
            back = back.astype(BF16)
            d_mixed[rows, lanes] = back
            query_raw = raw[rows, lanes]
            query = (query_raw * sigmoid(query_raw)).astype(BF16).astype(F32)
            high, low = halves(query * jnp.exp(running[:, lanes]) * carried)
            update[h, c] = mm(back, high, TN) + mm(back, low, TN)

    for h in range(2):
        lanes = slice(h * 128, (h + 1) * 128)
        state, rate = update[h, CHUNKS - 1], decay[CHUNKS - 1, 0:1, lanes]
        for c in range(CHUNKS - 2, -1, -1):
            state = state * decay[c, 0:1, lanes] + update[h, c]
            rate = rate * decay[c, 0:1, lanes]
        msg[h, 0:128, :] = state
        msg[h, 128:136, :] = jnp.broadcast_to(rate, (8, 128))
    exchange2 = Exchange(p, msg, sib2, slots4, give, take2, ex2_send, ex2_recv, True)
    exchange2.to_sibling()
    results = (out_gate, out_up, out_down)
    for one, out in zip(sums[:2], results):
        one.to_x(write(out), go=False)
    exchange2.to_chips()
    for one in sums[:2]:
        one.go()

    @pl.loop(0, CHUNKS)
    def _(c):
        rows = pl.ds(pl.multiple_of(c * CHUNK, CHUNK), CHUNK)
        running = run[rows, :]
        middle = running[63:64]
        _, _, query, keys, values = gates(raw, bound, rows)
        up, down_ = jnp.exp(running - middle), jnp.exp(middle - running)
        lifted = query.astype(F32) * up
        lowered = keys.astype(F32) * down_
        column, row = segments.column(c), segments.row(c)
        carried = jnp.where(column == segments.before(c), 1.0, 0.0)
        linked = (column == row) & (
            lax.broadcasted_iota(jnp.int32, (CHUNK, CHUNK), 0)
            >= lax.broadcasted_iota(jnp.int32, (CHUNK, CHUNK), 1)
        )
        for h in range(2):
            lanes = slice(h * 128, (h + 1) * 128)
            lift, lower = halves(lifted[:, lanes]), halves(lowered[:, lanes])
            scores = halves(jnp.where(linked, mm3(lift, lower, NT), 0.0))
            grad = d_mixed[rows, lanes]
            d_scores = halves(jnp.where(linked, mm(grad, values[:, lanes], NT), 0.0))
            d_values[rows, lanes] = mm(scores[0], grad, TN) + mm(scores[1], grad, TN)
            state = halves(states[h, c])
            outer = mm(grad, state[0], NN) + mm(grad, state[1], NN)
            query_grad = mm3(d_scores, lower, NN) * up[:, lanes] + outer * jnp.exp(running[:, lanes]) * carried
            d_query[rows, lanes] = query_grad
            query_raw = raw[rows, lanes]
            draw[rows, lanes] = (query_grad * slope(query_raw, sigmoid(query_raw))).astype(BF16)
            d_keys[rows, lanes] = mm3(d_scores, lift, TN) * down_[:, lanes]

    for one in sums[:2]:
        one.finish()
    first = DpSum(p, 512, a0, a1, a2, f3, f4, f5, f6)
    second = DpSum(p, 512, b0, b1, b2, g3, g4, g5, g6)
    third = DpSum(p, HERE, e0, e1, e2, e3, e4, e5, e6)
    products_turned(hn, draw.at[:, 0:256], draw.at[:, 768:1024], a0)
    exchange2.result(incoming)
    first.to_sibling()
    sums[2].to_x(write(out_down))
    for one, out in zip(sums[:2], results):
        one.end(accumulate(out))
    emit(12, 13)
    first.to_z()
    bound_total[...] = jnp.zeros_like(bound_total)

    @pl.loop(0, CHUNKS)
    def _(i):
        c = CHUNKS - 1 - i
        rows = pl.ds(pl.multiple_of(c * CHUNK, CHUNK), CHUNK)
        running = run[rows, :]
        logistic, forget, query, keys, values = gates(raw, bound, rows)
        keys = keys.astype(F32)
        fade = jnp.exp(running[127:128] - running)
        column, final = segments.column(c), segments.final(c)
        ends = jnp.where(column == final, 1.0, 0.0)
        for h in range(2):
            lanes = slice(h * 128, (h + 1) * 128)
            state = incoming[h]
            pair = halves(state)
            tail = halves(keys[:, lanes] * fade[:, lanes] * ends)
            value_grad = d_values[rows, lanes] + mm3(tail, pair, NT)
            draw[rows, 512 + h * 128 : 512 + (h + 1) * 128] = value_grad.astype(BF16)
            lift = mm(values[:, lanes], pair[0], NN) + mm(values[:, lanes], pair[1], NN)
            key_grad = d_keys[rows, lanes] + lift * fade[:, lanes] * ends
            at_end = jnp.sum(states[h, c + 1] * state, axis=0, keepdims=True)
            query_grad = d_query[rows, lanes]
            step = query[:, lanes].astype(F32) * query_grad - keys[:, lanes] * key_grad
            log_grad = summed_rows(False, step) + at_end
            forget_grad = log_grad / forget[:, lanes] - key_grad
            rest = 1.0 - logistic[:, lanes]
            draw[rows, 256 + h * 128 : 256 + (h + 1) * 128] = (
                forget_grad * (1.0 - bound[:, lanes]) * logistic[:, lanes] * rest
            ).astype(BF16)
            bound_total[:, lanes] += jnp.sum(forget_grad * rest, axis=0, keepdims=True)
            incoming[h] = state * decay[c, 0:1, lanes] + update[h, c]

    scatter2 = HeadSum(p, ps, slots, rs2_s, rs2_r)
    for start, send in ((HALF, scatter2.send_right), (0, scatter2.send_left)):
        for first_row, part in ((0, wd), (TOK, dy)):
            for j in range(2):
                rows = slice(j * 256, (j + 1) * 256)
                columns = slice(start + first_row + j * 256, start + first_row + (j + 1) * 256)
                ps[:, columns] = mm(draw[...], part[rows, start : start + HALF], NT).astype(BF16)

        send()
    first.join()
    products_turned(hn, draw.at[:, 256:512], draw.at[:, 512:768], b0)
    second.to_sibling()

    @pl.loop(0, 8)
    def _(j):
        columns = pl.ds(pl.multiple_of(j * 256, 256), 256)
        terms = ps[:, columns].astype(F32) * hn[:, columns].astype(F32)
        norm_terms[:, columns] = jnp.sum(terms, axis=0, keepdims=True) / gain[:, columns]

    vec[...] = jnp.zeros_like(vec)
    for i in range(16):
        vec[i : i + 1, :] = norm_terms[:, i * 128 : (i + 1) * 128]
        vec[16 + i : 17 + i, :] = ffn_terms[:, i * 128 : (i + 1) * 128]
    vec[32:33, :] = group_total[...]
    vec[33:34, :] = total[:, 0:128] + total[:, 128:256]
    vec[34:35, :] = bound_total[:, 0:128]
    vec[35:36, :] = bound_total[:, 128:256]
    everywhere = Total(p, vec, t0, t1, t2, t3, t4, t5, t6, t7, t8.at[0], t9.at[0])
    everywhere.send()
    second.to_z()
    products(gated_t, db, e0)
    third.to_sibling()
    second.join()
    third.to_z()
    scatter2.middle()
    everywhere.middle()
    first.to_x(put(out_query, out_outgate))
    scatter1.middle()
    everywhere.late()
    second.to_x(put(out_forget, out_input))
    third.join()
    sums[2].end(accumulate(out_down))
    emit(14)
    scatter2.collect()

    @pl.loop(0, 4)
    def _(i):
        rows = pl.ds(pl.multiple_of(i * 16, 16), 16)
        grad, x = scatter2.rows(i * 16, 16), hid_rows[rows, :].astype(F32)
        inverse = lax.rsqrt(jnp.mean(x * x, axis=-1, keepdims=True) + EPS)
        scaled, normed = grad * gain[...], x * inverse
        back = inverse * (scaled - normed * jnp.mean(scaled * normed, axis=-1, keepdims=True))
        grad_in[rows, :] = d_resid[rows, :] + back

    emit(1)

    third.to_x(write(out_output))
    scatter1.collect()

    @pl.loop(0, 4)
    def _(i):
        rows = pl.ds(pl.multiple_of(i * 16, 16), 16)
        block_out[rows, :] = (resid[rows, :] + scatter1.rows(i * 16, 16)).astype(BF16)

    emit(0)

    all_of = everywhere.result()
    out_norm[...] = all_of[0:16]
    out_ffn[...] = all_of[16:32]
    out_group[...] = all_of[32:33]
    mean = jnp.sum(all_of[33:34], axis=-1, keepdims=True) / float(8192 * D)
    out_mean[...] = jnp.broadcast_to(mean, (1, 128))
    for h in range(2):
        lanes = slice(h * 128, (h + 1) * 128)
        out_bounds[:, lanes] = soft[:, lanes] * (picked[:, lanes] - bound[:, lanes]) * all_of[34 + h : 35 + h]
    emit(7, 8, 9, 10, 11)

    first.end(add_to(out_query, out_outgate))
    emit(2, 5)
    second.end(add_to(out_forget, out_input))
    emit(3, 4)
    third.end(accumulate(out_output))
    emit(6)
    spread.finish()
    scatter1.finish()
    scatter2.finish()
    exchange2.finish()
    everywhere.finish()
    for one in (first, second, third, sums[2]):
        one.finish()
    for move in emitted:
        move.wait()


OUTS = (
    ((ROWS, D), BF16),
    ((ROWS, D), F32),
    ((128, HERE), F32),
    ((128, HERE), F32),
    ((128, HERE), F32),
    ((128, HERE), F32),
    ((HERE, 128), F32),
    ((24, HERE), F32),
    ((16, 128), F32),
    ((1, KDIM), F32),
    ((16, 128), F32),
    ((1, 128), F32),
    ((FFH, 128), F32),
    ((FFH, 128), F32),
    ((FFH, 128), F32),
)


def call_block(*arrays):
    sums = dp_sum_scratch(FFH)
    again = [pltpu.VMEM((512, 128), BF16)] * 2 + sixteen()
    shapes = [*OUTS, ((TOK, D), BF16), ((2 * TOK, D), BF16)]
    return pl.pallas_call(
        layer_block,
        name="layer_block",
        out_shape=[jax.ShapeDtypeStruct(*one) for one in shapes],
        in_specs=[HB] * 10 + [VM] * 4 + [SM, SM],
        out_specs=[HB] * (len(OUTS) + 2),
        scratch_shapes=[
            *[pltpu.VMEM(*one) for one in OUTS],
            *[pltpu.VMEM((TOK, D), BF16)] * 3,
            pltpu.VMEM((2 * TOK, D), BF16),
            *[pltpu.VMEM((FFH, D), BF16)] * 3,
            pltpu.VMEM((HERE, D), BF16),
            pltpu.VMEM((TOK, 1024), F32),
            pltpu.VMEM((ROWS, D), BF16),
            pltpu.VMEM((TOK, HERE), BF16),
            pltpu.VMEM((HERE, TOK), BF16),
            *[pltpu.VMEM((TOK, HERE), F32)] * 2,
            pltpu.VMEM((2, CHUNKS + 1, 128, 128), F32),
            pltpu.VMEM((2, CHUNKS, 128, 128), F32),
            *[pltpu.VMEM((ROWS, D), F32)] * 2,
            *[pltpu.VMEM((TOK, FFH), BF16)] * 3,
            *[pltpu.VMEM((FFH, TOK), BF16)] * 3,
            pltpu.VMEM((TOK, 1024), BF16),
            pltpu.VMEM((TOK, HERE), BF16),
            *[pltpu.VMEM((TOK, HERE), F32)] * 3,
            pltpu.VMEM((CHUNKS, 8, HERE), F32),
            pltpu.VMEM((2, 128, 128), F32),
            pltpu.VMEM((VEC, 128), F32),
            pltpu.VMEM((1, D), F32),
            pltpu.VMEM((1, D), F32),
            pltpu.VMEM((1, 128), F32),
            pltpu.VMEM((1, HERE), F32),
            pltpu.VMEM((1, HERE), F32),
            *exchange_scratch(),
            *[one for k, one in enumerate(exchange_scratch()) if k not in (0, 3)],
            *sixteen(),
            *twenty(),
            *sixteen(),
            *twenty(),
            *eight(),
            *sixteen(),
            *gather_semaphores(),
            *gather_semaphores(),
            *gather_semaphores(),
            *gather_semaphores(),
            *gather_semaphores(),
            *gather_semaphores(),
            *sums,
            *sums,
            *sums,
            *dp_sum_scratch(HERE),
            *again,
            *again,
            pltpu.VMEM((8, VEC, 128), F32),
            pltpu.VMEM((8, VEC, 128), F32),
            pltpu.VMEM((VEC, 128), F32),
            pltpu.VMEM((VEC, 128), F32),
            *eight(),
            *eight(),
            pltpu.SemaphoreType.DMA((1,)),
            pltpu.SemaphoreType.DMA((1,)),
            pltpu.SemaphoreType.DMA((32,)),
        ],
        compiler_params=pltpu.CompilerParams(
            collective_id=0, has_side_effects=True, vmem_limit_bytes=60 * 1024 * 1024
        ),
    )(*arrays)


def results(*refs):
    count, sems = len(OUTS), refs[-1]
    ins, outs, held = refs[:count], refs[count : 2 * count], refs[2 * count : 3 * count]
    reads = [pltpu.make_async_copy(ins[k], held[k], sems.at[0, k]) for k in range(count)]
    writes = [pltpu.make_async_copy(held[k], outs[k], sems.at[1, k]) for k in range(count)]
    for move in reads:
        move.start()
    for read, move in zip(reads, writes):
        read.wait()
        move.start()
    for move in writes:
        move.wait()


def call_results(arrays):
    return pl.pallas_call(
        results,
        name="results",
        out_shape=[jax.ShapeDtypeStruct(*one) for one in OUTS],
        in_specs=[HB] * len(OUTS),
        out_specs=[HB] * len(OUTS),
        scratch_shapes=[*[pltpu.VMEM(*one) for one in OUTS], pltpu.SemaphoreType.DMA((2, len(OUTS)))],
    )(*arrays)


def local(
    hidden_in, norm_gain, w_query, w_forget, w_input, w_outgate, lower_bounds, layer_index, group_gain,
    w_output, ffn_gain, w_gate, w_up, w_down, seq_lengths, grad_out,
):
    arrays = call_block(
        hidden_in, grad_out, w_query, w_forget, w_input, w_outgate, w_output, w_gate.T, w_up.T, w_down,
        norm_gain.reshape(1, D), lower_bounds, group_gain.reshape(1, KDIM), ffn_gain.reshape(1, D), layer_index, seq_lengths,
    )
    (
        block_out, grad_in, grad_query, grad_forget, grad_input, grad_outgate, grad_output, grad_bounds,
        grad_norm, grad_group, grad_ffn, mean, grad_gate, grad_up, grad_down,
    ) = call_results(arrays[: len(OUTS)])
    return (
        block_out,
        grad_in,
        grad_norm.reshape(D),
        grad_query,
        grad_forget,
        grad_input,
        grad_outgate,
        grad_bounds,
        grad_group.reshape(KDIM),
        grad_output,
        grad_ffn.reshape(D),
        grad_gate.T,
        grad_up.T,
        grad_down,
        mean[0, 0:1],
    )


def solution(mesh):
    return jax.shard_map(
        local,
        mesh=mesh,
        in_specs=(
            P("dp", None),
            P(),
            P("dp", "head"),
            P("dp", "head"),
            P("dp", "head"),
            P("dp", "head"),
            P(None, "head"),
            P(),
            P(),
            P("head", "dp"),
            P(),
            P("dp", "head"),
            P("dp", "head"),
            P("head", "dp"),
            P(),
            P("dp", None),
        ),
        out_specs=(
            P(("dp", "head"), None),
            P(("dp", "head"), None),
            P(),
            P("dp", "head"),
            P("dp", "head"),
            P("dp", "head"),
            P("dp", "head"),
            P(None, "head"),
            P(),
            P("head", "dp"),
            P(),
            P("dp", "head"),
            P("dp", "head"),
            P("head", "dp"),
            P(),
        ),
        check_vma=False,
    )
```
